32 devices in a mesh: ha: 4 (over y, x), wa: 4 (over z), ta: 2 (over core).
Axes of the slice: x: 2, y: 2, z: 4, core: 2. Of those that a mesh axis runs over, the one named last changes fastest.
Arguments:
- hidden_states: bfloat16 [2, 96, 32, 5120], P(None, 'ha', 'wa', 'ta'), may hold values from -60 to 60
- queries: bfloat16 [2, 96, 32, 5120], P(None, 'ha', 'wa', 'ta'), may hold values from -120 to 120
- keys_values: bfloat16 [2, 2, 96, 32, 5120], P(None, None, 'ha', 'wa', 'ta'), may hold values from -16 to 16
- out_weight: bfloat16 [5120, 5120], P('ta', 'wa'), may hold values from -0.078125 to 0.078125
- mod_table: float32 [50, 3, 5120], P(None, None, 'ta'), may hold values from -4 to 4
- windows: int32 [40, 2], P('ta'), may hold values from 0 to 1, as said below
- step_index: int32 [1], replicated, may hold values from 0 to 49
Outputs:
- residual_out: bfloat16 [2, 96, 32, 5120], P(None, 'ha', 'wa', 'ta')
- ffn_input: bfloat16 [2, 96, 32, 5120], P(None, 'ha', 'wa', 'ta')
The draws below stay inside these ranges and needn't reach their ends.
Inputs may be any that keep to these rules, and one draw needn't show every extreme that they name: `windows`: some head has both radii equal to 1.
All inputs are finite; a program needn't handle non-finite values.
Results may differ from the reference program's by a relative error of at most 0.0085.
Values may be sent and summed in bfloat16 or wider, within the bound.
No kernel may reach another device: no remote copies, remote signals or barrier semaphores. Data moves between devices by JAX's collectives and lax.ppermute only.
A program may use at most 128 MiB of HBM per device.

```python
import math
import jax
import jax.numpy as jnp
from jax import lax

D = 5120
HEADS = 40
HD = 128
TILE = 8
FRAMES = 2
STEPS = 50
H = 96
W = 32
N_TA = 2


def base_keys(key):
    return jnp.clip(jax.random.normal(key, (FRAMES, H, W, HEADS * HD), jnp.float32), -4.0, 4.0)


def draw_queries(key, part):
    shared = base_keys(key)
    key = jax.random.fold_in(key, 5)
    result = jnp.clip(jax.random.normal(key, shared.shape, jnp.float32), -4.0, 4.0)
    return result.astype(jnp.bfloat16)


def draw_keys_values(key, part):
    shared = base_keys(key)
    key = jax.random.fold_in(key, 9)
    keys_part = shared
    values_part = 4.0 * jnp.clip(jax.random.normal(key, shared.shape, jnp.float32), -4.0, 4.0)
    return jnp.stack([keys_part, values_part], 0).astype(jnp.bfloat16)


def draw_hidden_states(key, part):
    key = jax.random.fold_in(key, 21)
    row_key = jax.random.fold_in(key, 1)
    col_key = jax.random.fold_in(key, 2)
    main_key = jax.random.fold_in(key, 4)
    shape = (FRAMES, H, W, D)
    row_scale = 10.0 ** jax.random.uniform(row_key, (FRAMES, H, W, 1), jnp.float32)
    position = lax.broadcasted_iota(jnp.float32, (D,), 0) / D
    col_scale = 0.05 * 3.0 ** position * 10.0 ** jax.random.uniform(col_key, (D,), jnp.float32)
    base = jnp.clip(jax.random.normal(main_key, shape, jnp.float32), -4.0, 4.0)
    return (base * row_scale * col_scale).astype(jnp.bfloat16)


def draw_windows(key, part):
    key = jax.random.fold_in(key, 13)
    radii = jax.random.randint(key, (HEADS, 2), 0, 2)
    picked = jax.random.randint(jax.random.fold_in(key, 1), (), 0, HEADS)
    head_ids = lax.broadcasted_iota(jnp.int32, (HEADS, 2), 0)
    return jnp.where(head_ids == picked, 1, radii).astype(jnp.int32)


def shard_levels(own_key, extent, cuts, smallest, high):
    def one(dim, parts):
        draws = jax.random.uniform(jax.random.fold_in(jax.random.fold_in(own_key, 6), dim), (parts,), jnp.float32, smallest / len(cuts), high / len(cuts))
        return jnp.repeat(jnp.exp(draws), extent[dim] // parts).reshape((-1,) + (1,) * (len(extent) - dim - 1))

    loudness = one(*cuts[0])
    for cut in cuts[1:]:
        loudness = loudness * one(*cut)
    return loudness


def normal_values(key, extent, width, most, cuts=(), held_as=jnp.bfloat16):
    gain = shard_levels(key, extent, cuts, -0.22, 0.18) if cuts else 1.0
    values = jax.random.normal(key, extent, jnp.float32) * width * gain
    return jnp.minimum(jnp.maximum(values, -most), most).astype(held_as)


def setup_inputs(seed: int = 0) -> dict:
    streams_of = jax.random.split(jax.random.key(seed), 8)
    hidden_states = draw_hidden_states(jax.random.fold_in(streams_of[7], 71), 0)
    queries = draw_queries(jax.random.fold_in(streams_of[7], 71), 0)
    keys_values = draw_keys_values(jax.random.fold_in(streams_of[7], 71), 0)
    out_weight = normal_values(streams_of[3], (HEADS * HD, D), (HEADS * HD) ** -0.5, 0.078125, ((0, 2), (1, 4)))
    mod_table = normal_values(streams_of[4], (STEPS, 3, D), 0.7, 4.0, ((2, 2),), jnp.float32)
    windows = draw_windows(jax.random.fold_in(streams_of[7], 71), 0)
    step_index = jax.random.randint(streams_of[6], (1,), 0, STEPS).astype(jnp.int32)
    return dict(hidden_states=hidden_states, queries=queries, keys_values=keys_values, out_weight=out_weight, mod_table=mod_table, windows=windows, step_index=step_index)


EPSILON = 1e-06

def tile_attention(queries, padded, windows, tile_index):
    tile_cols = W // TILE
    tile_rows = H // TILE
    tile_row = (tile_index // tile_cols).astype(jnp.int32)
    tile_col = (tile_index % tile_cols).astype(jnp.int32)
    zero = jnp.int32(0)
    span = 3 * TILE
    block = lax.dynamic_slice(queries, (zero, tile_row * TILE, tile_col * TILE, zero), (FRAMES, TILE, TILE, HEADS * HD))
    query_f = block.reshape(-1, HEADS, HD).astype(jnp.float32)
    near = lax.dynamic_slice(padded, (zero, zero, tile_row * TILE, tile_col * TILE, zero), (2, FRAMES, span, span, HEADS * HD))
    key_f = near[0].reshape(-1, HEADS, HD).astype(jnp.float32)
    value_f = near[1].reshape(-1, HEADS, HD).astype(jnp.float32)
    row_gap = (lax.broadcasted_iota(jnp.int32, (FRAMES, span, span), 1) // TILE - 1).reshape(-1)
    col_gap = (lax.broadcasted_iota(jnp.int32, (FRAMES, span, span), 2) // TILE - 1).reshape(-1)
    inside = (tile_row + row_gap >= 0) & (tile_row + row_gap < tile_rows) & (tile_col + col_gap >= 0) & (tile_col + col_gap < tile_cols)
    allowed = inside[None, :] & (jnp.abs(row_gap)[None, :] <= windows[:, 0:1]) & (jnp.abs(col_gap)[None, :] <= windows[:, 1:2])
    scale = 1.0 / math.sqrt(HD)
    scores = jnp.einsum('qhd,khd->hqk', query_f, key_f) * scale
    scores = jnp.where(allowed[:, None, :], scores, -jnp.inf)
    highest = lax.optimization_barrier(jnp.max(scores, axis=2, keepdims=True))
    expo = jnp.exp(scores - highest)
    total = lax.optimization_barrier(jnp.sum(expo, axis=2, keepdims=True))
    weights = (expo / total).astype(jnp.bfloat16)
    output = jnp.einsum('hqk,khd->qhd', weights.astype(jnp.float32), value_f)
    return output.astype(jnp.bfloat16).reshape(FRAMES * TILE * TILE, HEADS * HD)

def reference(hidden_states, queries, keys_values, out_weight, mod_table, windows, step_index):
    padded = jnp.pad(keys_values, ((0, 0), (0, 0), (TILE, TILE), (TILE, TILE), (0, 0)))
    tile_rows = H // TILE
    tile_cols = W // TILE
    tiles = lax.map(lambda index: tile_attention(queries, padded, windows, index), jnp.arange(tile_rows * tile_cols, dtype=jnp.int32))
    tiles = tiles.reshape(tile_rows, tile_cols, FRAMES, TILE, TILE, HEADS * HD)
    attention = jnp.transpose(tiles, (2, 0, 3, 1, 4, 5)).reshape(FRAMES * H * W, HEADS * HD)
    group_width = HEADS * HD // N_TA
    projected = jnp.zeros((FRAMES * H * W, D), jnp.float32)
    for group in range(N_TA):
        partial_sum = jnp.dot(attention[:, group * group_width:(group + 1) * group_width], out_weight[group * group_width:(group + 1) * group_width], preferred_element_type=jnp.float32).astype(jnp.bfloat16)
        partial_sum = lax.optimization_barrier(partial_sum)
        projected = projected + partial_sum.astype(jnp.float32)
    picked = lax.dynamic_index_in_dim(mod_table, step_index[0].astype(jnp.int32), 0, keepdims=False)
    mixed = hidden_states.reshape(-1, D).astype(jnp.float32) + picked[0] * projected
    average = lax.optimization_barrier(jnp.sum(mixed, axis=1, keepdims=True)) / D
    variance = lax.optimization_barrier(jnp.sum(mixed * mixed, axis=1, keepdims=True)) / D - average * average
    normed = (mixed - average) * lax.rsqrt(variance + EPSILON)
    ffn_input = (normed * (1.0 + picked[2]) + picked[1]).astype(jnp.bfloat16)
    residual_out = mixed.astype(jnp.bfloat16)
    return (residual_out.reshape(FRAMES, H, W, D), ffn_input.reshape(FRAMES, H, W, D))
```

```python
from functools import partial
import math

import jax
import jax.numpy as jnp
from jax import lax
from jax.experimental import pallas as pl
from jax.experimental.pallas import tpu as pltpu
from jax.sharding import PartitionSpec as P

D = 5120
HD = 128
TILE = 8

EPSILON = 1e-06
VMEM_LIMIT = 56 * 1024 * 1024


def kernel_params():
    return pltpu.CompilerParams(
        dimension_semantics=("arbitrary",), vmem_limit_bytes=VMEM_LIMIT
    )


def attention_kernel(windows, edges, *refs, q_count, columns_only):
    q_refs = refs[:q_count]
    kv_ref, top_ref, bottom_ref = refs[q_count : q_count + 3]
    out_refs = refs[q_count + 3 : 2 * q_count + 3]
    stat_refs = refs[2 * q_count + 3 :]
    frames, tokens, head_size = q_refs[0].shape
    span = top_ref.shape[2]
    tiles = tokens // span
    head = pl.program_id(0)
    radius_row = windows[head, 0]
    radius_col = windows[head, 1]
    scale = 1.0 / math.sqrt(HD)

    @pl.when(head == 0)
    def _():
        for stat_ref in stat_refs:
            stat_ref[...] = jnp.zeros_like(stat_ref)

    def near(which, tile, wide):
        if not wide:
            return kv_ref[which, :, tile * span : (tile + 1) * span, :].reshape(-1, head_size)
        pieces = []
        if tile == 0:
            pieces.append(top_ref[which])
        low = max(tile - 1, 0) * span
        high = min(tile + 2, tiles) * span
        pieces.append(kv_ref[which, :, low:high, :])
        if tile == tiles - 1:
            pieces.append(bottom_ref[which])
        block = pieces[0] if len(pieces) == 1 else jnp.concatenate(pieces, axis=1)
        return block.reshape(-1, head_size)

    def attend(wide):
        lane = lax.broadcasted_iota(jnp.int32, (frames, span, stat_refs[0].shape[2]), 2)
        for tile in range(tiles):
            rows = slice(tile * span, (tile + 1) * span)
            keys = near(0, tile, wide)
            values = near(1, tile, wide)
            bias = None
            if wide and (tile == 0 or tile == tiles - 1):
                place = lax.rem(
                    lax.broadcasted_iota(jnp.int32, (1, keys.shape[0]), 1), 3 * span
                )
                low = jnp.where(edges[0] == 0, span, 0) if tile == 0 else 0
                high = jnp.where(edges[1] == 0, 2 * span, 3 * span) if tile == tiles - 1 else 3 * span
                bias = jnp.where((place >= low) & (place < high), 0.0, -jnp.inf)
            for q_ref, out_ref, stat_ref in zip(q_refs, out_refs, stat_refs):
                query = q_ref[:, rows, :].reshape(-1, head_size)
                scores = (
                    lax.dot_general(
                        query, keys, (((1,), (1,)), ((), ())), preferred_element_type=jnp.float32
                    )
                    * scale
                )
                if bias is not None:
                    scores = scores + bias
                highest = jnp.max(scores, axis=1, keepdims=True)
                expo = jnp.exp(scores - highest)
                total = jnp.sum(expo, axis=1, keepdims=True)
                output = jnp.dot(
                    expo.astype(jnp.bfloat16), values, preferred_element_type=jnp.float32
                ) * (1.0 / total)
                out_ref[:, rows, :] = output.astype(jnp.bfloat16).reshape(frames, span, head_size)
                level = (highest + jnp.log(total)).reshape(frames, span, 1)
                stat_ref[:, rows, :] = jnp.where(lane == head, level, stat_ref[:, rows, :])

    if columns_only:

        @pl.when(radius_col == 0)
        def _():
            for out_ref in out_refs:
                out_ref[...] = jnp.zeros_like(out_ref)

        active = radius_col != 0
    else:
        active = True

    @pl.when(jnp.logical_and(active, radius_row == 0))
    def _():
        attend(False)

    @pl.when(jnp.logical_and(active, radius_row != 0))
    def _():
        attend(True)


def attention(windows, edges, query_blocks, keys_values, top, bottom, columns_only):
    frames, tokens, features = query_blocks[0].shape
    head_count = windows.shape[0]
    head_size = features // head_count
    span = top.shape[2]
    q_count = len(query_blocks)
    lanes = 128
    q_spec = pl.BlockSpec((frames, tokens, head_size), lambda h, *_: (0, 0, h))
    kv_spec = pl.BlockSpec((2, frames, tokens, head_size), lambda h, *_: (0, 0, 0, h))
    halo_spec = pl.BlockSpec((2, frames, span, head_size), lambda h, *_: (0, 0, 0, h))
    stat_spec = pl.BlockSpec((frames, tokens, lanes), lambda h, *_: (0, 0, 0))
    flops = 4 * q_count * frames * tokens * 2 * frames * span * head_size * head_count
    outs = pl.pallas_call(
        partial(attention_kernel, q_count=q_count, columns_only=columns_only),
        grid_spec=pltpu.PrefetchScalarGridSpec(
            num_scalar_prefetch=2,
            grid=(head_count,),
            in_specs=[q_spec] * q_count + [kv_spec, halo_spec, halo_spec],
            out_specs=[q_spec] * q_count + [stat_spec] * q_count,
        ),
        out_shape=[jax.ShapeDtypeStruct((frames, tokens, features), jnp.bfloat16)] * q_count
        + [jax.ShapeDtypeStruct((frames, tokens, lanes), jnp.float32)] * q_count,
        compiler_params=kernel_params(),
        cost_estimate=pl.CostEstimate(
            flops=flops, bytes_accessed=12_000_000, transcendentals=flops // 256
        ),
        name="attend_neighbours" if columns_only else "attend_own",
    )(windows, edges, *query_blocks, keys_values, top, bottom)
    return outs[:q_count], outs[q_count:]


def combine_kernel(windows, edges, own, left, right, own_stat, left_stat, right_stat, out):
    head = pl.program_id(0)
    radius_col = windows[head, 1]

    @pl.when(radius_col == 0)
    def _():
        out[...] = own[...]

    @pl.when(radius_col != 0)
    def _():
        lane = lax.broadcasted_iota(jnp.int32, own_stat.shape, 2)

        def level(ref):
            return jnp.sum(jnp.where(lane == head, ref[...], 0.0), axis=2, keepdims=True)

        own_level = level(own_stat)
        left_level = jnp.where(edges[2] == 0, -jnp.inf, level(left_stat))
        right_level = jnp.where(edges[3] == 0, -jnp.inf, level(right_stat))
        highest = jnp.maximum(own_level, jnp.maximum(left_level, right_level))
        weights = [jnp.exp(x - highest) for x in (own_level, left_level, right_level)]
        inverse = 1.0 / (weights[0] + weights[1] + weights[2])
        mixed = sum(
            ref[...].astype(jnp.float32) * (weight * inverse)
            for ref, weight in zip((own, left, right), weights)
        )
        out[...] = mixed.astype(jnp.bfloat16)


def combine(windows, edges, outputs, stats):
    frames, tokens, features = outputs[0].shape
    head_count = windows.shape[0]
    head_size = features // head_count
    spec = pl.BlockSpec((frames, tokens, head_size), lambda h, *_: (0, 0, h))
    stat_spec = pl.BlockSpec(stats[0].shape, lambda h, *_: (0, 0, 0))
    return pl.pallas_call(
        combine_kernel,
        grid_spec=pltpu.PrefetchScalarGridSpec(
            num_scalar_prefetch=2,
            grid=(head_count,),
            in_specs=[spec] * 3 + [stat_spec] * 3,
            out_specs=spec,
        ),
        out_shape=jax.ShapeDtypeStruct((frames, tokens, features), jnp.bfloat16),
        compiler_params=kernel_params(),
        cost_estimate=pl.CostEstimate(
            flops=10 * frames * tokens * features,
            bytes_accessed=8 * frames * tokens * features,
            transcendentals=0,
        ),
        name="combine",
    )(windows, edges, *outputs, *stats)


def project_kernel(first, attended, weight, out):
    depth = weight.shape[2]
    total = None
    for part in range(weight.shape[0]):
        term = jnp.dot(
            attended[:, part * depth : (part + 1) * depth],
            weight[part, 0],
            preferred_element_type=jnp.float32,
        )
        total = term if total is None else total + term
    out[0] = total.astype(jnp.bfloat16)


def project(attended, weights, first, count):
    parts, _, depth, width = weights.shape
    tokens, features = attended.shape
    return pl.pallas_call(
        project_kernel,
        grid_spec=pltpu.PrefetchScalarGridSpec(
            num_scalar_prefetch=1,
            grid=(count,),
            in_specs=[
                pl.BlockSpec((tokens, features), lambda i, first: (0, 0)),
                pl.BlockSpec((parts, 1, depth, width), lambda i, first: (0, first[0] + i, 0, 0)),
            ],
            out_specs=pl.BlockSpec((1, tokens, width), lambda i, first: (i, 0, 0)),
        ),
        out_shape=jax.ShapeDtypeStruct((count, tokens, width), jnp.bfloat16),
        compiler_params=kernel_params(),
        cost_estimate=pl.CostEstimate(
            flops=2 * tokens * features * width * count,
            bytes_accessed=2 * features * width * count,
            transcendentals=0,
        ),
        name="project",
    )(first, attended, weights)


def shift(block, axis, step):
    count = lax.axis_size(axis)
    pairs = [(i, i + step) for i in range(count) if 0 <= i + step < count]
    return lax.ppermute(block, axis, pairs)


def shards(hidden_states, queries, keys_values, out_weight, mod_table, windows, step_index):
    frames, rows, cols, features = queries.shape
    n_ha, n_wa, n_ta = lax.axis_size("ha"), lax.axis_size("wa"), lax.axis_size("ta")
    ha, wa, ta = lax.axis_index("ha"), lax.axis_index("wa"), lax.axis_index("ta")
    tokens = frames * rows * cols

    depth = features // n_ha
    share = lax.dynamic_slice_in_dim(out_weight, ha * depth, depth, 0)
    weights = lax.all_gather(share, ("ha", "wa"), axis=0, tiled=False).reshape(
        n_ha, n_wa, depth, out_weight.shape[1]
    )

    edges = jnp.stack([ha > 0, ha < n_ha - 1, wa > 0, wa < n_wa - 1]).astype(jnp.int32)
    top = shift(keys_values[:, :, rows - TILE :], "ha", 1)
    bottom = shift(keys_values[:, :, :TILE], "ha", -1)
    from_left = shift(queries, "wa", 1)
    from_right = shift(queries, "wa", -1)

    def flat(block):
        return block.reshape(block.shape[:-3] + (-1, features))

    kv, top, bottom = flat(keys_values), flat(top), flat(bottom)
    (own,), (own_stat,) = attention(windows, edges, [flat(queries)], kv, top, bottom, False)
    (for_left, for_right), (left_stat, right_stat) = attention(
        windows, edges, [flat(from_left), flat(from_right)], kv, top, bottom, True
    )
    left, left_level = shift(for_right, "wa", 1), shift(right_stat, "wa", 1)
    right, right_level = shift(for_left, "wa", -1), shift(left_stat, "wa", -1)
    attended = combine(
        windows, edges, [own, left, right], [own_stat, left_level, right_level]
    ).reshape(tokens, features)

    blocks = n_wa // n_ta
    summed = None
    for step in list(range(1, n_ta)) + [0]:
        target = lax.rem(ta + step, n_ta)
        piece = project(attended, weights, (target * blocks).reshape(1), blocks)
        if step:
            piece = lax.ppermute(piece, "ta", [(i, (i + step) % n_ta) for i in range(n_ta)])
        piece = piece.astype(jnp.float32)
        summed = piece if summed is None else summed + piece
    width = hidden_states.shape[3]
    summed = jnp.transpose(summed, (1, 0, 2)).reshape(tokens, width)

    picked = lax.dynamic_index_in_dim(mod_table, step_index[0], 0, keepdims=False)
    mixed = hidden_states.reshape(tokens, width).astype(jnp.float32) + picked[0] * summed
    sum_first, sum_second = lax.psum((jnp.sum(mixed, axis=1), jnp.sum(mixed * mixed, axis=1)), "ta")
    average = (sum_first / D)[:, None]
    variance = (sum_second / D)[:, None] - average * average
    normed = (mixed - average) * lax.rsqrt(variance + EPSILON)
    ffn_input = (normed * (1.0 + picked[2]) + picked[1]).astype(jnp.bfloat16)
    residual_out = mixed.astype(jnp.bfloat16)
    out_shape = (frames, rows, cols, width)
    return (residual_out.reshape(out_shape), ffn_input.reshape(out_shape))


def solution(mesh):
    return jax.shard_map(
        shards,
        mesh=mesh,
        in_specs=(
            P(None, "ha", "wa", "ta"),
            P(None, "ha", "wa", "ta"),
            P(None, None, "ha", "wa", "ta"),
            P("ta", "wa"),
            P(None, None, "ta"),
            P("ta", None),
            P(),
        ),
        out_specs=(P(None, "ha", "wa", "ta"), P(None, "ha", "wa", "ta")),
        check_vma=False,
    )
```

```python
from functools import partial
import math

import jax
import jax.numpy as jnp
from jax import lax
from jax.experimental import pallas as pl
from jax.experimental.pallas import tpu as pltpu
from jax.sharding import PartitionSpec as P

D = 5120
HD = 128
TILE = 8
LANES = 128
LEVEL_STEP = 32

EPSILON = 1e-06
VMEM_LIMIT = 48 * 1024 * 1024
HEAD_GROUPS = 2


def kernel_params():
    return pltpu.CompilerParams(
        dimension_semantics=("arbitrary",), vmem_limit_bytes=VMEM_LIMIT
    )


def attention_kernel(windows, edges, *refs, q_count, columns_only, first_head, group):
    q_refs = refs[:q_count]
    kv_ref, top_ref, bottom_ref = refs[q_count : q_count + 3]
    out_refs = refs[q_count + 3 : 2 * q_count + 3]
    stat_refs = refs[2 * q_count + 3 :]
    frames, tokens, head_size = q_refs[0].shape
    span = top_ref.shape[2]
    tiles = tokens // span
    step = pl.program_id(0)
    head = first_head + jnp.minimum(step, group - 1)
    radius_row = windows[head, 0]
    radius_col = windows[head, 1]
    scale = 1.0 / math.sqrt(HD)

    @pl.when(step == 0)
    def _():
        for stat_ref in stat_refs:
            stat_ref[...] = jnp.zeros_like(stat_ref)

    def near(which, tile, wide):
        if not wide:
            return kv_ref[which, :, tile * span : (tile + 1) * span, :].reshape(-1, head_size)
        pieces = []
        if tile == 0:
            pieces.append(top_ref[which])
        low = max(tile - 1, 0) * span
        high = min(tile + 2, tiles) * span
        pieces.append(kv_ref[which, :, low:high, :])
        if tile == tiles - 1:
            pieces.append(bottom_ref[which])
        block = pieces[0] if len(pieces) == 1 else jnp.concatenate(pieces, axis=1)
        return block.reshape(-1, head_size)

    def attend(wide):
        lane = lax.broadcasted_iota(jnp.int32, (frames, span, LANES), 2)
        for tile in range(tiles):
            rows = slice(tile * span, (tile + 1) * span)
            keys = near(0, tile, wide)
            values = near(1, tile, wide)
            bias = None
            if wide and (tile == 0 or tile == tiles - 1):
                place = lax.rem(
                    lax.broadcasted_iota(jnp.int32, (1, keys.shape[0]), 1), 3 * span
                )
                low = jnp.where(edges[0] == 0, span, 0) if tile == 0 else 0
                high = jnp.where(edges[1] == 0, 2 * span, 3 * span) if tile == tiles - 1 else 3 * span
                bias = jnp.where((place >= low) & (place < high), 0.0, -jnp.inf)
            for q_ref, out_ref, stat_ref in zip(q_refs, out_refs, stat_refs):
                query = q_ref[:, rows, :].reshape(-1, head_size)
                scores = (
                    lax.dot_general(
                        query, keys, (((1,), (1,)), ((), ())), preferred_element_type=jnp.float32
                    )
                    * scale
                )
                if bias is not None:
                    scores = scores + bias
                highest = jnp.max(scores, axis=1, keepdims=True)
                expo = jnp.exp(scores - highest)
                total = jnp.sum(expo, axis=1, keepdims=True)
                output = jnp.dot(
                    expo.astype(jnp.bfloat16), values, preferred_element_type=jnp.float32
                ) * (1.0 / total)
                out_ref[:, rows, :] = output.astype(jnp.bfloat16).reshape(frames, span, head_size)
                level = (highest + jnp.log(total)).reshape(frames, span, 1)
                stat_ref[:, rows, :] = jnp.where(lane == step, level, stat_ref[:, rows, :])

    active = step < group
    if columns_only:

        @pl.when(active & (radius_col == 0))
        def _():
            for out_ref in out_refs:
                out_ref[...] = jnp.zeros_like(out_ref)

        active = active & (radius_col != 0)

    @pl.when(active & (radius_row == 0))
    def _():
        attend(False)

    @pl.when(active & (radius_row != 0))
    def _():
        attend(True)

    @pl.when(step == group)
    def _():
        for out_ref, stat_ref in zip(out_refs, stat_refs):
            level = stat_ref[...]
            high = level.astype(jnp.bfloat16).astype(jnp.float32)
            middle = (level - high).astype(jnp.bfloat16).astype(jnp.float32)
            low = level - high - middle
            packed = high + pltpu.roll(middle, LEVEL_STEP, 2) + pltpu.roll(low, 2 * LEVEL_STEP, 2)
            out_ref[...] = packed.astype(jnp.bfloat16)


def attention(windows, edges, query_blocks, keys_values, top, bottom, columns_only, first_head, group):
    frames, tokens, features = query_blocks[0].shape
    head_size = features // windows.shape[0]
    span = top.shape[2]
    q_count = len(query_blocks)

    def head_of(step):
        return first_head + jnp.minimum(step, group - 1)

    q_spec = pl.BlockSpec((frames, tokens, head_size), lambda h, *_: (0, 0, head_of(h)))
    kv_spec = pl.BlockSpec((2, frames, tokens, head_size), lambda h, *_: (0, 0, 0, head_of(h)))
    halo_spec = pl.BlockSpec((2, frames, span, head_size), lambda h, *_: (0, 0, 0, head_of(h)))
    out_spec = pl.BlockSpec((frames, tokens, head_size), lambda h, *_: (0, 0, h))
    flops = 4 * q_count * frames * tokens * 2 * frames * span * head_size * group
    return pl.pallas_call(
        partial(
            attention_kernel,
            q_count=q_count,
            columns_only=columns_only,
            first_head=first_head,
            group=group,
        ),
        grid_spec=pltpu.PrefetchScalarGridSpec(
            num_scalar_prefetch=2,
            grid=(group + 1,),
            in_specs=[q_spec] * q_count + [kv_spec, halo_spec, halo_spec],
            out_specs=[out_spec] * q_count,
            scratch_shapes=[pltpu.VMEM((frames, tokens, LANES), jnp.float32)] * q_count,
        ),
        out_shape=[jax.ShapeDtypeStruct((frames, tokens, (group + 1) * head_size), jnp.bfloat16)]
        * q_count,
        compiler_params=kernel_params(),
        cost_estimate=pl.CostEstimate(
            flops=flops, bytes_accessed=20_000_000, transcendentals=flops // 256
        ),
        name="attend_neighbours" if columns_only else "attend_own",
    )(windows, edges, *query_blocks, keys_values, top, bottom)


def combine_kernel(windows, edges, own, left, right, own_stat, left_stat, right_stat, *rest, first_head):
    out = rest[-1]
    step = pl.program_id(0)
    frames, tokens, head_size = own.shape
    radius_col = windows[first_head + step, 1]

    @pl.when(radius_col == 0)
    def _():
        out[...] = own[...]

    @pl.when(radius_col != 0)
    def _():
        lane = lax.broadcasted_iota(jnp.int32, (LANES, head_size), 0)
        pick = jnp.where(
            (lax.rem(lane, LEVEL_STEP) == step) & (lane < 3 * LEVEL_STEP), 1.0, 0.0
        ).astype(jnp.bfloat16)

        def level(ref):
            return jnp.dot(
                ref[...].reshape(-1, LANES), pick, preferred_element_type=jnp.float32
            ).reshape(frames, tokens, head_size)

        own_level = level(own_stat)
        left_level = jnp.where(edges[2] == 0, -jnp.inf, level(left_stat))
        right_level = jnp.where(edges[3] == 0, -jnp.inf, level(right_stat))
        highest = jnp.maximum(own_level, jnp.maximum(left_level, right_level))
        weights = [jnp.exp(x - highest) for x in (own_level, left_level, right_level)]
        mixed = sum(
            ref[...].astype(jnp.float32) * weight for ref, weight in zip((own, left, right), weights)
        )
        out[...] = (mixed / (weights[0] + weights[1] + weights[2])).astype(jnp.bfloat16)


def combine(windows, edges, outputs, first_head, group, features, so_far):
    frames, tokens, _ = outputs[0].shape
    head_size = features // windows.shape[0]
    spec = pl.BlockSpec((frames, tokens, head_size), lambda h, *_: (0, 0, h))
    stat_spec = pl.BlockSpec((frames, tokens, head_size), lambda h, *_: (0, 0, group))
    more = [] if so_far is None else [so_far]
    return pl.pallas_call(
        partial(combine_kernel, first_head=first_head),
        grid_spec=pltpu.PrefetchScalarGridSpec(
            num_scalar_prefetch=2,
            grid=(group,),
            in_specs=[spec] * 3 + [stat_spec] * 3 + [pl.BlockSpec(memory_space=pl.ANY)] * len(more),
            out_specs=pl.BlockSpec((frames, tokens, head_size), lambda h, *_: (0, 0, first_head + h)),
        ),
        out_shape=jax.ShapeDtypeStruct((frames, tokens, features), jnp.bfloat16),
        input_output_aliases={8: 0} if more else {},
        compiler_params=kernel_params(),
        cost_estimate=pl.CostEstimate(
            flops=10 * frames * tokens * head_size * group,
            bytes_accessed=8 * frames * tokens * head_size * group,
            transcendentals=0,
        ),
        name="combine",
    )(windows, edges, *outputs, *outputs, *more)


def project_kernel(starts, attended, *refs, count, carried):
    pieces = refs[:count]
    out = refs[-1]
    total = refs[count][...] if carried else None
    for index, piece in enumerate(pieces):
        start = pl.multiple_of(starts[index], LANES)
        term = jnp.dot(
            attended[:, pl.ds(start, piece.shape[0])],
            piece[...],
            preferred_element_type=jnp.float32,
        )
        total = term if total is None else total + term
    out[...] = total.astype(out.dtype)


def project(attended, pieces, starts, carry, dtype):
    tokens, features = attended.shape
    width = pieces[0].shape[1]
    column = 256 if width % 256 == 0 else width
    depth = sum(piece.shape[0] for piece in pieces)
    out_spec = pl.BlockSpec((tokens, column), lambda i, _: (0, i))
    return pl.pallas_call(
        partial(project_kernel, count=len(pieces), carried=carry is not None),
        grid_spec=pltpu.PrefetchScalarGridSpec(
            num_scalar_prefetch=1,
            grid=(width // column,),
            in_specs=[pl.BlockSpec((tokens, features), lambda i, _: (0, 0))]
            + [pl.BlockSpec((piece.shape[0], column), lambda i, _: (0, i)) for piece in pieces]
            + ([] if carry is None else [out_spec]),
            out_specs=out_spec,
        ),
        out_shape=jax.ShapeDtypeStruct((tokens, width), dtype),
        compiler_params=kernel_params(),
        cost_estimate=pl.CostEstimate(
            flops=2 * tokens * depth * width,
            bytes_accessed=2 * depth * width + 2 * tokens * features,
            transcendentals=0,
        ),
        name="project",
    )(jnp.stack(starts).astype(jnp.int32), attended, *pieces, *([] if carry is None else [carry]))


def mix_kernel(place, own_part, other_part, own_hidden, other_hidden, own_gate, other_gate, *refs):
    mixed_ref, sums_ref = refs[-2:]
    mine = place[0] != 0
    hidden = jnp.where(
        mine, own_hidden[...].astype(jnp.float32), other_hidden[...].astype(jnp.float32)
    )
    gate = jnp.where(mine, own_gate[...], other_gate[...])
    mixed = hidden + gate * (
        own_part[...].astype(jnp.float32) + other_part[...].astype(jnp.float32)
    )
    mixed_ref[...] = mixed
    lane = lax.broadcasted_iota(jnp.int32, sums_ref.shape, 1)
    first = jnp.sum(mixed, axis=1, keepdims=True)
    second = jnp.sum(mixed * mixed, axis=1, keepdims=True)
    sums = jnp.where(lane == 0, first, jnp.where(lane == 1, second, 0.0))
    if len(refs) == 4:
        sums = sums + refs[0][...]
    sums_ref[...] = sums


def mix(place, own_part, other_part, own_hidden, other_hidden, own_gate, other_gate, carry):
    tokens, width = own_part.shape
    blocks = own_hidden.shape[1] // width
    rows = 64 if tokens % 64 == 0 else tokens
    part = pl.BlockSpec((rows, width), lambda i, place: (i, 0))
    hidden = pl.BlockSpec((rows, width), lambda i, place: (i, place[1]))
    gate = pl.BlockSpec((1, width), lambda i, place: (0, place[1]))
    sums = pl.BlockSpec((rows, LANES), lambda i, place: (i, 0))
    mixed = pl.BlockSpec((rows, width), lambda i, place: (i, place[2]))
    more = [] if carry is None else [carry[1], carry[0]]
    return pl.pallas_call(
        mix_kernel,
        grid_spec=pltpu.PrefetchScalarGridSpec(
            num_scalar_prefetch=1,
            grid=(tokens // rows,),
            in_specs=[part, part, hidden, hidden, gate, gate]
            + ([sums, pl.BlockSpec(memory_space=pl.ANY)] if more else []),
            out_specs=[mixed, sums],
        ),
        out_shape=[
            jax.ShapeDtypeStruct((tokens, (blocks + 1) * width), jnp.float32),
            jax.ShapeDtypeStruct((tokens, LANES), jnp.float32),
        ],
        input_output_aliases={8: 0} if more else {},
        compiler_params=kernel_params(),
        cost_estimate=pl.CostEstimate(
            flops=10 * tokens * width, bytes_accessed=12 * tokens * width, transcendentals=0
        ),
        name="mix",
    )(place, own_part, other_part, own_hidden, other_hidden, own_gate, other_gate, *more)


def finish_kernel(
    place, own_part, other_part, own_hidden, other_hidden, own_gate, other_gate, scale, shift_by,
    sums, mixed_ref, residual, ffn,
):
    mine = place[0] != 0
    width = own_part.shape[1]
    blocks = residual.shape[1] // width
    hidden = jnp.where(
        mine, own_hidden[...].astype(jnp.float32), other_hidden[...].astype(jnp.float32)
    )
    gate = jnp.where(mine, own_gate[...], other_gate[...])
    last = hidden + gate * (
        own_part[...].astype(jnp.float32) + other_part[...].astype(jnp.float32)
    )
    first = sums[:, 0:1] + jnp.sum(last, axis=1, keepdims=True)
    second = sums[:, 1:2] + jnp.sum(last * last, axis=1, keepdims=True)
    average = first / D
    variance = second / D - average * average
    inverse = lax.rsqrt(variance + EPSILON)
    for block in range(blocks):
        columns = slice(block * width, (block + 1) * width)
        here = mine & (place[1] == block)
        mixed = jnp.where(here, last, mixed_ref[:, columns])
        residual[:, columns] = mixed.astype(jnp.bfloat16)
        ffn[:, columns] = (
            (mixed - average) * inverse * (1.0 + scale[:, columns]) + shift_by[:, columns]
        ).astype(jnp.bfloat16)


def finish(place, own_part, other_part, own_hidden, other_hidden, own_gate, other_gate, scale, shift_by, carry):
    tokens, width = own_part.shape
    features = own_hidden.shape[1]
    rows = 64 if tokens % 64 == 0 else tokens
    part = pl.BlockSpec((rows, width), lambda i, place: (i, 0))
    hidden = pl.BlockSpec((rows, width), lambda i, place: (i, place[1]))
    gate = pl.BlockSpec((1, width), lambda i, place: (0, place[1]))
    whole = pl.BlockSpec((1, features), lambda i, place: (0, 0))
    sums = pl.BlockSpec((rows, LANES), lambda i, place: (i, 0))
    row = pl.BlockSpec((rows, features), lambda i, place: (i, 0))
    return pl.pallas_call(
        finish_kernel,
        grid_spec=pltpu.PrefetchScalarGridSpec(
            num_scalar_prefetch=1,
            grid=(tokens // rows,),
            in_specs=[part, part, hidden, hidden, gate, gate, whole, whole, sums, row],
            out_specs=[row, row],
        ),
        out_shape=[jax.ShapeDtypeStruct((tokens, features), jnp.bfloat16)] * 2,
        compiler_params=kernel_params(),
        cost_estimate=pl.CostEstimate(
            flops=20 * tokens * features, bytes_accessed=12 * tokens * features, transcendentals=0
        ),
        name="finish",
    )(
        place, own_part, other_part, own_hidden, other_hidden, own_gate, other_gate, scale,
        shift_by, carry[1], carry[0],
    )


def shift(block, axis, step):
    count = lax.axis_size(axis)
    pairs = [(i, i + step) for i in range(count) if 0 <= i + step < count]
    return lax.ppermute(block, axis, pairs)


def turn(block, axis, step):
    count = lax.axis_size(axis)
    return lax.ppermute(block, axis, [(i, (i + step) % count) for i in range(count)])


def swap(block, axis, bit):
    count = lax.axis_size(axis)
    return lax.ppermute(block, axis, [(i, i ^ bit) for i in range(count)])


def attend_all(queries, keys_values, windows):
    frames, rows, cols, features = queries.shape
    n_ha, n_wa = lax.axis_size("ha"), lax.axis_size("wa")
    ha, wa = lax.axis_index("ha"), lax.axis_index("wa")
    head_count = windows.shape[0]

    edges = jnp.stack([ha > 0, ha < n_ha - 1, wa > 0, wa < n_wa - 1]).astype(jnp.int32)
    from_left = shift(queries, "wa", 1)
    from_right = shift(queries, "wa", -1)
    top = shift(keys_values[:, :, rows - TILE :], "ha", 1)
    bottom = shift(keys_values[:, :, :TILE], "ha", -1)

    def flat(block):
        return block.reshape(block.shape[:-3] + (-1, features))

    held = flat(keys_values), flat(top), flat(bottom)
    groups = HEAD_GROUPS if head_count % HEAD_GROUPS == 0 else 1
    group = head_count // groups
    far = []
    for first in range(0, head_count, group):
        for_left, for_right = attention(
            windows, edges, [flat(from_left), flat(from_right)], *held, True, first, group
        )
        far.append((shift(for_right, "wa", 1), shift(for_left, "wa", -1)))
    near = [
        attention(windows, edges, [flat(queries)], *held, False, first, group)[0]
        for first in range(0, head_count, group)
    ]
    attended = None
    for index, first in enumerate(range(0, head_count, group)):
        attended = combine(
            windows, edges, [near[index], *far[index]], first, group, features, attended
        )
    return attended.reshape(-1, features)


def gather_slots(out_weight):
    n_wa = lax.axis_size("wa")
    ha = lax.axis_index("ha")
    depth = out_weight.shape[0] // lax.axis_size("ha")
    half = max(depth * 3 // 5 // LANES, 1) * LANES
    cuts = [(0, half), (half, depth)] if half < depth else [(0, depth)]
    held = [
        lax.dynamic_slice_in_dim(out_weight, ha * depth + low, high - low, 0) for low, high in cuts
    ]
    slots = []
    for _ in range(1, n_wa):
        slot = []
        for index, (low, high) in enumerate(cuts):
            held[index] = turn(held[index], "wa", 1)
            mine = held[index]
            by_x = swap(mine, "ha", 1)
            by_y = swap(mine, "ha", 2)
            split = LANES if high - low > LANES else (high - low) // 2
            far_x = swap(by_y[:split], "ha", 1)
            far_y = swap(by_x[split:], "ha", 2)
            slot.append(
                [
                    (mine, ha * depth + low),
                    (by_x, (ha ^ 1) * depth + low),
                    (by_y, (ha ^ 2) * depth + low),
                    (far_x, (ha ^ 3) * depth + low),
                    (far_y, (ha ^ 3) * depth + low + split),
                ]
            )
        slots.append(slot)
    return slots


def paired(hidden, attended, out_weight, picked):
    n_wa = lax.axis_size("wa")
    wa, ta = lax.axis_index("wa"), lax.axis_index("ta")
    blocks = n_wa // 2
    other_hidden = swap(hidden, "ta", 1)
    gate = picked[0:1]
    other_gate = swap(gate, "ta", 1)
    slots = [[[(out_weight, jnp.int32(0))]]] + gather_slots(out_weight)
    carry = None
    for distance, slot in enumerate(slots):
        block = lax.rem(wa - distance + n_wa, n_wa)
        mine = block // blocks == ta
        inner = lax.rem(block, blocks)
        place = jnp.stack([mine.astype(jnp.int32), inner, jnp.where(mine, inner, blocks)])
        total = None
        for index, part in enumerate(slot):
            dtype = jnp.bfloat16 if index == len(slot) - 1 else jnp.float32
            total = project(attended, [p for p, _ in part], [s for _, s in part], total, dtype)
        other = swap(total, "ta", 1)
        operands = (place, total, other, hidden, other_hidden, gate, other_gate)
        if distance < n_wa - 1:
            carry = mix(*operands, carry)
    return finish(*operands, picked[2:3], picked[1:2], carry)


def gathered(hidden, attended, out_weight, picked):
    n_ha, n_wa, n_ta = lax.axis_size("ha"), lax.axis_size("wa"), lax.axis_size("ta")
    ha, ta = lax.axis_index("ha"), lax.axis_index("ta")
    tokens, features = attended.shape
    depth = features // n_ha
    width = out_weight.shape[1]
    share = lax.dynamic_slice_in_dim(out_weight, ha * depth, depth, 0)
    weights = lax.all_gather(share, ("ha", "wa"), axis=0, tiled=False).reshape(
        n_ha, n_wa, depth, width
    )
    partial_sums = jnp.einsum(
        "thk,hwkc->wtc",
        attended.reshape(tokens, n_ha, depth),
        weights,
        preferred_element_type=jnp.float32,
    ).astype(jnp.bfloat16)
    blocks = n_wa // n_ta
    summed = None
    for step in range(n_ta):
        target = lax.rem(ta + step, n_ta)
        piece = lax.dynamic_slice_in_dim(partial_sums, target * blocks, blocks, 0)
        if step:
            piece = turn(piece, "ta", step)
        piece = piece.astype(jnp.float32)
        summed = piece if summed is None else summed + piece
    summed = jnp.transpose(summed, (1, 0, 2)).reshape(tokens, -1)
    mixed = hidden.astype(jnp.float32) + picked[0] * summed
    sum_first, sum_second = lax.psum((jnp.sum(mixed, axis=1), jnp.sum(mixed * mixed, axis=1)), "ta")
    average = (sum_first / D)[:, None]
    variance = (sum_second / D)[:, None] - average * average
    normed = (mixed - average) * lax.rsqrt(variance + EPSILON)
    ffn_input = (normed * (1.0 + picked[2]) + picked[1]).astype(jnp.bfloat16)
    return mixed.astype(jnp.bfloat16), ffn_input


def shards(hidden_states, queries, keys_values, out_weight, mod_table, windows, step_index):
    tokens = math.prod(queries.shape[:3])
    width = hidden_states.shape[3]
    picked = lax.dynamic_index_in_dim(mod_table, step_index[0], 0, keepdims=False)
    attended = attend_all(queries, keys_values, windows)
    regular = lax.axis_size("ta") == 2 and lax.axis_size("ha") == 4 and width % LANES == 0
    residual_out, ffn_input = (paired if regular else gathered)(
        hidden_states.reshape(tokens, width), attended, out_weight, picked
    )
    return residual_out.reshape(hidden_states.shape), ffn_input.reshape(hidden_states.shape)


def solution(mesh):
    return jax.shard_map(
        shards,
        mesh=mesh,
        in_specs=(
            P(None, "ha", "wa", "ta"),
            P(None, "ha", "wa", "ta"),
            P(None, None, "ha", "wa", "ta"),
            P("ta", "wa"),
            P(None, None, "ta"),
            P("ta", None),
            P(),
        ),
        out_specs=(P(None, "ha", "wa", "ta"), P(None, "ha", "wa", "ta")),
        check_vma=False,
    )
```

```python
from functools import partial
import math

import jax
import jax.numpy as jnp
from jax import lax
from jax.experimental import pallas as pl
from jax.experimental.pallas import tpu as pltpu
from jax.sharding import PartitionSpec as P

D = 5120
HD = 128
TILE = 8
LANES = 128
LEVEL_STEP = 32

EPSILON = 1e-06
VMEM_LIMIT = 48 * 1024 * 1024
SMALL = pl.CostEstimate(flops=1, bytes_accessed=1, transcendentals=0)


def kernel_params():
    return pltpu.CompilerParams(
        dimension_semantics=("arbitrary",), vmem_limit_bytes=VMEM_LIMIT
    )


def attention_kernel(windows, edges, *refs, q_count, columns_only, first_head, group, waits):
    q_refs = refs[:q_count]
    kv_ref, top_ref, bottom_ref = refs[q_count : q_count + 3]
    refs = refs[q_count + 3 + waits :]
    out_refs, stat_refs = refs[:q_count], refs[q_count:]
    frames, tokens, head_size = q_refs[0].shape
    span = top_ref.shape[2]
    tiles = tokens // span
    step = pl.program_id(0)
    head = first_head + jnp.minimum(step, group - 1)
    radius_row = windows[head, 0]
    radius_col = windows[head, 1]
    scale = 1.0 / math.sqrt(HD)

    @pl.when(step == 0)
    def _():
        for stat_ref in stat_refs:
            stat_ref[...] = jnp.zeros_like(stat_ref)

    def near(which, tile, wide):
        if not wide:
            return kv_ref[which, :, tile * span : (tile + 1) * span, :].reshape(-1, head_size)
        pieces = []
        if tile == 0:
            pieces.append(top_ref[which])
        low = max(tile - 1, 0) * span
        high = min(tile + 2, tiles) * span
        pieces.append(kv_ref[which, :, low:high, :])
        if tile == tiles - 1:
            pieces.append(bottom_ref[which])
        block = pieces[0] if len(pieces) == 1 else jnp.concatenate(pieces, axis=1)
        return block.reshape(-1, head_size)

    def attend(wide):
        lane = lax.broadcasted_iota(jnp.int32, (frames, span, LANES), 2)
        for tile in range(tiles):
            rows = slice(tile * span, (tile + 1) * span)
            keys = near(0, tile, wide)
            values = near(1, tile, wide)
            bias = None
            if wide and (tile == 0 or tile == tiles - 1):
                place = lax.rem(
                    lax.broadcasted_iota(jnp.int32, (1, keys.shape[0]), 1), 3 * span
                )
                low = jnp.where(edges[0] == 0, span, 0) if tile == 0 else 0
                high = jnp.where(edges[1] == 0, 2 * span, 3 * span) if tile == tiles - 1 else 3 * span
                bias = jnp.where((place >= low) & (place < high), 0.0, -jnp.inf)
            for q_ref, out_ref, stat_ref in zip(q_refs, out_refs, stat_refs):
                query = q_ref[:, rows, :].reshape(-1, head_size)
                scores = (
                    lax.dot_general(
                        query, keys, (((1,), (1,)), ((), ())), preferred_element_type=jnp.float32
                    )
                    * scale
                )
                if bias is not None:
                    scores = scores + bias
                highest = jnp.max(scores, axis=1, keepdims=True)
                expo = jnp.exp(scores - highest)
                total = jnp.sum(expo, axis=1, keepdims=True)
                output = jnp.dot(
                    expo.astype(jnp.bfloat16), values, preferred_element_type=jnp.float32
                ) * (1.0 / total)
                out_ref[:, rows, :] = output.astype(jnp.bfloat16).reshape(frames, span, head_size)
                level = (highest + jnp.log(total)).reshape(frames, span, 1)
                stat_ref[:, rows, :] = jnp.where(lane == step, level, stat_ref[:, rows, :])

    active = step < group
    if columns_only:

        @pl.when(active & (radius_col == 0))
        def _():
            for out_ref in out_refs:
                out_ref[...] = jnp.zeros_like(out_ref)

        active = active & (radius_col != 0)

    @pl.when(active & (radius_row == 0))
    def _():
        attend(False)

    @pl.when(active & (radius_row != 0))
    def _():
        attend(True)

    @pl.when(step == group)
    def _():
        for out_ref, stat_ref in zip(out_refs, stat_refs):
            level = stat_ref[...]
            high = level.astype(jnp.bfloat16).astype(jnp.float32)
            middle = (level - high).astype(jnp.bfloat16).astype(jnp.float32)
            low = level - high - middle
            packed = high + pltpu.roll(middle, LEVEL_STEP, 2) + pltpu.roll(low, 2 * LEVEL_STEP, 2)
            out_ref[...] = packed.astype(jnp.bfloat16)


def attention(windows, edges, query_blocks, keys_values, top, bottom, columns_only, first_head, group, after):
    frames, tokens, features = query_blocks[0].shape
    head_size = features // windows.shape[0]
    span = top.shape[2]
    q_count = len(query_blocks)

    def head_of(step):
        return first_head + jnp.minimum(step, group - 1)

    q_spec = pl.BlockSpec((frames, tokens, head_size), lambda h, *_: (0, 0, head_of(h)))
    kv_spec = pl.BlockSpec((2, frames, tokens, head_size), lambda h, *_: (0, 0, 0, head_of(h)))
    halo_spec = pl.BlockSpec((2, frames, span, head_size), lambda h, *_: (0, 0, 0, head_of(h)))
    out_spec = pl.BlockSpec((frames, tokens, head_size), lambda h, *_: (0, 0, h))
    return pl.pallas_call(
        partial(
            attention_kernel,
            q_count=q_count,
            columns_only=columns_only,
            first_head=first_head,
            group=group,
            waits=len(after),
        ),
        grid_spec=pltpu.PrefetchScalarGridSpec(
            num_scalar_prefetch=2,
            grid=(group + 1,),
            in_specs=[q_spec] * q_count + [kv_spec, halo_spec, halo_spec]
            + [pl.BlockSpec(memory_space=pl.ANY)] * len(after),
            out_specs=[out_spec] * q_count,
            scratch_shapes=[pltpu.VMEM((frames, tokens, LANES), jnp.float32)] * q_count,
        ),
        out_shape=[jax.ShapeDtypeStruct((frames, tokens, (group + 1) * head_size), jnp.bfloat16)]
        * q_count,
        compiler_params=kernel_params(),
        cost_estimate=SMALL,
        name="attend_neighbours" if columns_only else "attend_own",
    )(windows, edges, *query_blocks, keys_values, top, bottom, *after)


def combine_kernel(windows, edges, own, left, right, own_stat, left_stat, right_stat, *rest, first_head):
    out = rest[-1]
    step = pl.program_id(0)
    frames, tokens, head_size = own.shape
    radius_col = windows[first_head + step, 1]

    @pl.when(radius_col == 0)
    def _():
        out[...] = own[...]

    @pl.when(radius_col != 0)
    def _():
        lane = lax.broadcasted_iota(jnp.int32, (LANES, head_size), 0)
        pick = jnp.where(
            (lax.rem(lane, LEVEL_STEP) == step) & (lane < 3 * LEVEL_STEP), 1.0, 0.0
        ).astype(jnp.bfloat16)

        def level(ref):
            return jnp.dot(
                ref[...].reshape(-1, LANES), pick, preferred_element_type=jnp.float32
            ).reshape(frames, tokens, head_size)

        own_level = level(own_stat)
        left_level = jnp.where(edges[2] == 0, -jnp.inf, level(left_stat))
        right_level = jnp.where(edges[3] == 0, -jnp.inf, level(right_stat))
        highest = jnp.maximum(own_level, jnp.maximum(left_level, right_level))
        weights = [jnp.exp(x - highest) for x in (own_level, left_level, right_level)]
        mixed = sum(
            ref[...].astype(jnp.float32) * weight for ref, weight in zip((own, left, right), weights)
        )
        out[...] = (mixed / (weights[0] + weights[1] + weights[2])).astype(jnp.bfloat16)


def combine(windows, edges, outputs, first_head, group, features, so_far, order):
    frames, tokens, _ = outputs[0].shape
    head_size = features // windows.shape[0]
    spec = pl.BlockSpec((frames, tokens, head_size), lambda h, *_: (0, 0, h))
    stat_spec = pl.BlockSpec((frames, tokens, head_size), lambda h, *_: (0, 0, group))
    more = [] if so_far is None else [so_far]
    share = windows.shape[0] // order

    def out_index(h, windows, edges):
        head = first_head + h
        return 0, 0, ((head // share) ^ edges[4]) * share + lax.rem(head, share)

    return pl.pallas_call(
        partial(combine_kernel, first_head=first_head),
        grid_spec=pltpu.PrefetchScalarGridSpec(
            num_scalar_prefetch=2,
            grid=(group,),
            in_specs=[spec] * 3 + [stat_spec] * 3 + [pl.BlockSpec(memory_space=pl.ANY)] * len(more),
            out_specs=pl.BlockSpec((frames, tokens, head_size), out_index),
        ),
        out_shape=jax.ShapeDtypeStruct((frames, tokens, features), jnp.bfloat16),
        input_output_aliases={8: 0} if more else {},
        compiler_params=kernel_params(),
        cost_estimate=SMALL,
        name="combine",
    )(windows, edges, *outputs, *outputs, *more)


def project_kernel(place, attended, *refs, offsets, carried):
    pieces = refs[: len(offsets)]
    out = refs[-1]
    total = refs[len(offsets)][...] if carried else None
    for piece, offset in zip(pieces, offsets):
        term = jnp.dot(
            attended[:, offset : offset + piece.shape[0]],
            piece[...],
            preferred_element_type=jnp.float32,
        )
        total = term if total is None else total + term
    out[...] = total.astype(out.dtype)


def project(place, attended, pieces, carry, dtype):
    tokens, features = attended.shape
    width = pieces[0][0].shape[1]
    column = 640 if width % 640 == 0 else width
    out_spec = pl.BlockSpec((tokens, column), lambda i, _: (0, i))
    piece_specs = [
        pl.BlockSpec((rows, column), lambda i, place, block=block: (block(place), i))
        for _, rows, block, _ in pieces
    ]
    return pl.pallas_call(
        partial(
            project_kernel, offsets=[piece[3] for piece in pieces], carried=carry is not None
        ),
        grid_spec=pltpu.PrefetchScalarGridSpec(
            num_scalar_prefetch=1,
            grid=(width // column,),
            in_specs=[pl.BlockSpec((tokens, features), lambda i, _: (0, 0))]
            + piece_specs
            + ([] if carry is None else [out_spec]),
            out_specs=out_spec,
        ),
        out_shape=jax.ShapeDtypeStruct((tokens, width), dtype),
        compiler_params=kernel_params(),
        cost_estimate=SMALL,
        name="project",
    )(place, attended, *[piece[0] for piece in pieces], *([] if carry is None else [carry]))


def mix_kernel(place, own_part, other_part, own_hidden, other_hidden, own_gate, other_gate, *refs):
    mixed_ref, sums_ref = refs[-2:]
    mine = place[0] != 0
    hidden = jnp.where(
        mine, own_hidden[...].astype(jnp.float32), other_hidden[...].astype(jnp.float32)
    )
    gate = jnp.where(mine, own_gate[...], other_gate[...])
    mixed = hidden + gate * (
        own_part[...].astype(jnp.float32) + other_part[...].astype(jnp.float32)
    )
    mixed_ref[...] = mixed
    lane = lax.broadcasted_iota(jnp.int32, sums_ref.shape, 1)
    first = jnp.sum(mixed, axis=1, keepdims=True)
    second = jnp.sum(mixed * mixed, axis=1, keepdims=True)
    sums = jnp.where(lane == 0, first, jnp.where(lane == 1, second, 0.0))
    if len(refs) == 4:
        sums = sums + refs[0][...]
    sums_ref[...] = sums


def mix(place, own_part, other_part, own_hidden, other_hidden, own_gate, other_gate, carry):
    tokens, width = own_part.shape
    blocks = own_hidden.shape[1] // width
    rows = 128 if tokens % 128 == 0 else tokens
    part = pl.BlockSpec((rows, width), lambda i, place: (i, 0))
    hidden = pl.BlockSpec((rows, width), lambda i, place: (i, place[1]))
    gate = pl.BlockSpec((1, width), lambda i, place: (0, place[1]))
    sums = pl.BlockSpec((rows, LANES), lambda i, place: (i, 0))
    mixed = pl.BlockSpec((rows, width), lambda i, place: (i, place[2]))
    more = [] if carry is None else [carry[1], carry[0]]
    return pl.pallas_call(
        mix_kernel,
        grid_spec=pltpu.PrefetchScalarGridSpec(
            num_scalar_prefetch=1,
            grid=(tokens // rows,),
            in_specs=[part, part, hidden, hidden, gate, gate]
            + ([sums, pl.BlockSpec(memory_space=pl.ANY)] if more else []),
            out_specs=[mixed, sums],
        ),
        out_shape=[
            jax.ShapeDtypeStruct((tokens, (blocks + 1) * width), jnp.float32),
            jax.ShapeDtypeStruct((tokens, LANES), jnp.float32),
        ],
        input_output_aliases={8: 0} if more else {},
        compiler_params=kernel_params(),
        cost_estimate=SMALL,
        name="mix",
    )(place, own_part, other_part, own_hidden, other_hidden, own_gate, other_gate, *more)


def finish_kernel(
    place, own_part, other_part, own_hidden, other_hidden, own_gate, other_gate, scale, shift_by,
    sums, mixed_ref, residual, ffn,
):
    mine = place[0] != 0
    width = own_part.shape[1]
    blocks = residual.shape[1] // width
    hidden = jnp.where(
        mine, own_hidden[...].astype(jnp.float32), other_hidden[...].astype(jnp.float32)
    )
    gate = jnp.where(mine, own_gate[...], other_gate[...])
    last = hidden + gate * (
        own_part[...].astype(jnp.float32) + other_part[...].astype(jnp.float32)
    )
    first = sums[:, 0:1] + jnp.sum(last, axis=1, keepdims=True)
    second = sums[:, 1:2] + jnp.sum(last * last, axis=1, keepdims=True)
    average = first / D
    variance = second / D - average * average
    inverse = lax.rsqrt(variance + EPSILON)
    for block in range(blocks):
        columns = slice(block * width, (block + 1) * width)
        here = mine & (place[1] == block)
        mixed = jnp.where(here, last, mixed_ref[:, columns])
        residual[:, columns] = mixed.astype(jnp.bfloat16)
        ffn[:, columns] = (
            (mixed - average) * inverse * (1.0 + scale[:, columns]) + shift_by[:, columns]
        ).astype(jnp.bfloat16)


def finish(place, own_part, other_part, own_hidden, other_hidden, own_gate, other_gate, scale, shift_by, carry):
    tokens, width = own_part.shape
    features = own_hidden.shape[1]
    rows = 128 if tokens % 128 == 0 else tokens
    part = pl.BlockSpec((rows, width), lambda i, place: (i, 0))
    hidden = pl.BlockSpec((rows, width), lambda i, place: (i, place[1]))
    gate = pl.BlockSpec((1, width), lambda i, place: (0, place[1]))
    whole = pl.BlockSpec((1, features), lambda i, place: (0, 0))
    sums = pl.BlockSpec((rows, LANES), lambda i, place: (i, 0))
    row = pl.BlockSpec((rows, features), lambda i, place: (i, 0))
    return pl.pallas_call(
        finish_kernel,
        grid_spec=pltpu.PrefetchScalarGridSpec(
            num_scalar_prefetch=1,
            grid=(tokens // rows,),
            in_specs=[part, part, hidden, hidden, gate, gate, whole, whole, sums, row],
            out_specs=[row, row],
        ),
        out_shape=[jax.ShapeDtypeStruct((tokens, features), jnp.bfloat16)] * 2,
        compiler_params=kernel_params(),
        cost_estimate=SMALL,
        name="finish",
    )(
        place, own_part, other_part, own_hidden, other_hidden, own_gate, other_gate, scale,
        shift_by, carry[1], carry[0],
    )


def shift(block, axis, step):
    count = lax.axis_size(axis)
    pairs = [(i, i + step) for i in range(count) if 0 <= i + step < count]
    return lax.ppermute(block, axis, pairs)


def turn(block, axis, step):
    count = lax.axis_size(axis)
    return lax.ppermute(block, axis, [(i, (i + step) % count) for i in range(count)])


def swap(block, axis, bit):
    count = lax.axis_size(axis)
    return lax.ppermute(block, axis, [(i, i ^ bit) for i in range(count)])


class Tokens:
    def __init__(self, queries, keys_values, windows, order):
        rows = queries.shape[1]
        features = queries.shape[3]
        n_ha, n_wa = lax.axis_size("ha"), lax.axis_size("wa")
        ha, wa = lax.axis_index("ha"), lax.axis_index("wa")

        def flat(block):
            return block.reshape(block.shape[:-3] + (-1, features))

        turned = ha if order > 1 else 0 * ha
        self.edges = jnp.stack([ha > 0, ha < n_ha - 1, wa > 0, wa < n_wa - 1, turned]).astype(
            jnp.int32
        )
        self.windows = windows
        self.order = order
        self.features = features
        self.queries = flat(queries)
        self.keys_values = flat(keys_values)
        last, first = lax.optimization_barrier(
            (keys_values[:, :, rows - TILE :], keys_values[:, :, :TILE])
        )
        self.halos = [flat(shift(last, "ha", 1)), flat(shift(first, "ha", -1))]
        self.visitors = [flat(shift(queries, "wa", 1)), flat(shift(queries, "wa", -1))]

    def attend(self, query_blocks, columns_only):
        return attention(
            self.windows,
            self.edges,
            query_blocks,
            self.keys_values,
            *self.halos,
            columns_only,
            0,
            self.windows.shape[0],
            [],
        )

    def stay(self):
        self.near = self.attend([self.queries], False)

    def visit(self):
        self.ends = self.attend(self.visitors, True)

    def send_back(self):
        for_left, for_right = self.ends
        self.back = [shift(for_right, "wa", 1), shift(for_left, "wa", -1)]

    def combine(self):
        attended = combine(
            self.windows,
            self.edges,
            [*self.near, *self.back],
            0,
            self.windows.shape[0],
            self.features,
            None,
            self.order,
        )
        return attended.reshape(-1, self.features)


def together(*groups):
    blocks = iter(lax.optimization_barrier(tuple(block for group in groups for block in group)))
    return [[next(blocks) for _ in group] for group in groups]


def paired(hidden, queries, keys_values, windows, out_weight, picked):
    ha, wa, ta = lax.axis_index("ha"), lax.axis_index("wa"), lax.axis_index("ta")
    n_wa = lax.axis_size("wa")
    blocks = n_wa // 2
    depth = out_weight.shape[0] // 4
    cut = depth * 2 // 5

    def swaps(share):
        return [swap(share, "ha", 1), swap(share, "ha", 2)]

    def far_swaps(by_x, by_y):
        return [swap(by_y[:cut], "ha", 1), swap(by_x[cut:], "ha", 2)]

    share = lax.optimization_barrier(lax.dynamic_slice_in_dim(out_weight, ha * depth, depth, 0))
    first = turn(share, "wa", 1)
    tokens = Tokens(queries, keys_values, windows, 4)

    [first], tokens.halos = together([first], tokens.halos)
    first_near = swaps(first)
    second = turn(first, "wa", 1)
    tokens.stay()

    first_near, tokens.near, tokens.visitors = together(first_near, tokens.near, tokens.visitors)
    first_far = far_swaps(*first_near)
    tokens.visit()

    [second], first_far, tokens.ends = together([second], first_far, tokens.ends)
    third = turn(second, "wa", 1)
    second_near = swaps(second)
    tokens.send_back()

    [third], second_near = together([third], second_near)
    third_near = swaps(third)
    second_far = far_swaps(*second_near)

    tokens.back, second_far = together(tokens.back, second_far)
    attended = tokens.combine()

    third_near, [attended] = together(third_near, [attended])
    third_far = far_swaps(*third_near)
    slots = [
        [first, *first_near, *first_far],
        [second, *second_near, *second_far],
        [third, *third_near, *third_far],
    ]

    other_hidden = swap(hidden, "ta", 1)
    gate = picked[0:1]
    other_gate = swap(gate, "ta", 1)

    def pieces(slot, shares):
        starts = [0, depth, 2 * depth, 3 * depth, 3 * depth + cut]
        return [
            (slot[share], slot[share].shape[0], lambda place: 0, starts[share]) for share in shares
        ]

    own = [
        (out_weight, depth, lambda place, share=share: share ^ place[3], share * depth)
        for share in range(4)
    ]
    carry = None
    for distance in range(n_wa):
        block = lax.rem(wa - distance + n_wa, n_wa)
        mine = block // blocks == ta
        inner = lax.rem(block, blocks)
        place = jnp.stack([mine.astype(jnp.int32), inner, jnp.where(mine, inner, blocks), ha])
        if distance == 0:
            total = project(place, attended, own, None, jnp.bfloat16)
        elif distance < n_wa - 1:
            total = project(
                place, attended, pieces(slots[distance - 1], range(5)), None, jnp.bfloat16
            )
        else:
            total = project(
                place, attended, pieces(slots[distance - 1], range(3)), None, jnp.float32
            )
            total = project(
                place, attended, pieces(slots[distance - 1], range(3, 5)), total, jnp.bfloat16
            )
        other = swap(total, "ta", 1)
        operands = (place, total, other, hidden, other_hidden, gate, other_gate)
        if distance < n_wa - 1:
            carry = mix(*operands, carry)
    return finish(*operands, picked[2:3], picked[1:2], carry)


def gathered(hidden, queries, keys_values, windows, out_weight, picked):
    work = Tokens(queries, keys_values, windows, 1)
    work.stay()
    work.visit()
    work.send_back()
    attended = work.combine()
    n_ha, n_wa, n_ta = lax.axis_size("ha"), lax.axis_size("wa"), lax.axis_size("ta")
    ha, ta = lax.axis_index("ha"), lax.axis_index("ta")
    tokens, features = attended.shape
    depth = features // n_ha
    width = out_weight.shape[1]
    share = lax.dynamic_slice_in_dim(out_weight, ha * depth, depth, 0)
    weights = lax.all_gather(share, ("ha", "wa"), axis=0, tiled=False).reshape(
        n_ha, n_wa, depth, width
    )
    partial_sums = jnp.einsum(
        "thk,hwkc->wtc",
        attended.reshape(tokens, n_ha, depth),
        weights,
        preferred_element_type=jnp.float32,
    ).astype(jnp.bfloat16)
    blocks = n_wa // n_ta
    summed = None
    for step in range(n_ta):
        target = lax.rem(ta + step, n_ta)
        piece = lax.dynamic_slice_in_dim(partial_sums, target * blocks, blocks, 0)
        if step:
            piece = turn(piece, "ta", step)
        piece = piece.astype(jnp.float32)
        summed = piece if summed is None else summed + piece
    summed = jnp.transpose(summed, (1, 0, 2)).reshape(tokens, -1)
    mixed = hidden.astype(jnp.float32) + picked[0] * summed
    sum_first, sum_second = lax.psum((jnp.sum(mixed, axis=1), jnp.sum(mixed * mixed, axis=1)), "ta")
    average = (sum_first / D)[:, None]
    variance = (sum_second / D)[:, None] - average * average
    normed = (mixed - average) * lax.rsqrt(variance + EPSILON)
    ffn_input = (normed * (1.0 + picked[2]) + picked[1]).astype(jnp.bfloat16)
    return mixed.astype(jnp.bfloat16), ffn_input


def shards(hidden_states, queries, keys_values, out_weight, mod_table, windows, step_index):
    tokens = math.prod(queries.shape[:3])
    width = hidden_states.shape[3]
    picked = lax.dynamic_index_in_dim(mod_table, step_index[0], 0, keepdims=False)
    sizes = lax.axis_size("ha"), lax.axis_size("wa"), lax.axis_size("ta")
    tuned = sizes == (4, 4, 2) and out_weight.shape[0] % (20 * LANES) == 0
    residual_out, ffn_input = (paired if tuned else gathered)(
        hidden_states.reshape(tokens, width), queries, keys_values, windows, out_weight, picked
    )
    return residual_out.reshape(hidden_states.shape), ffn_input.reshape(hidden_states.shape)


def solution(mesh):
    return jax.shard_map(
        shards,
        mesh=mesh,
        in_specs=(
            P(None, "ha", "wa", "ta"),
            P(None, "ha", "wa", "ta"),
            P(None, None, "ha", "wa", "ta"),
            P("ta", "wa"),
            P(None, None, "ta"),
            P("ta", None),
            P(),
        ),
        out_specs=(P(None, "ha", "wa", "ta"), P(None, "ha", "wa", "ta")),
        check_vma=False,
    )
```

```python
from functools import partial
import math

import jax
import jax.numpy as jnp
from jax import lax
from jax.experimental import pallas as pl
from jax.experimental.pallas import tpu as pltpu
from jax.sharding import PartitionSpec as P

D = 5120
HD = 128
TILE = 8
LANES = 128
LEVEL_STEP = 32

EPSILON = 1e-06
VMEM_LIMIT = 32 * 1024 * 1024
SMALL = pl.CostEstimate(flops=1, bytes_accessed=1, transcendentals=0)


def kernel_params():
    return pltpu.CompilerParams(
        dimension_semantics=("arbitrary",), vmem_limit_bytes=VMEM_LIMIT
    )


def attention_kernel(windows, edges, *refs, q_count, columns_only, group):
    q_refs = refs[:q_count]
    kv_ref, top_ref, bottom_ref = refs[q_count : q_count + 3]
    refs = refs[q_count + 3 :]
    out_refs, stat_refs = refs[:q_count], refs[q_count:]
    frames, tokens, head_size = q_refs[0].shape
    span = top_ref.shape[2]
    tiles = tokens // span
    step = pl.program_id(0)
    head = jnp.minimum(step, group - 1)
    radius_row = windows[head, 0]
    radius_col = windows[head, 1]
    scale = 1.0 / math.sqrt(HD)

    @pl.when(step == 0)
    def _():
        for stat_ref in stat_refs:
            stat_ref[...] = jnp.zeros_like(stat_ref)

    def near(which, tile, wide):
        if not wide:
            return kv_ref[which, :, tile * span : (tile + 1) * span, :].reshape(-1, head_size)
        pieces = []
        if tile == 0:
            pieces.append(top_ref[which])
        low = max(tile - 1, 0) * span
        high = min(tile + 2, tiles) * span
        pieces.append(kv_ref[which, :, low:high, :])
        if tile == tiles - 1:
            pieces.append(bottom_ref[which])
        block = pieces[0] if len(pieces) == 1 else jnp.concatenate(pieces, axis=1)
        return block.reshape(-1, head_size)

    def attend(wide):
        lane = lax.broadcasted_iota(jnp.int32, (frames, span, LANES), 2)
        for tile in range(tiles):
            rows = slice(tile * span, (tile + 1) * span)
            keys = near(0, tile, wide)
            values = near(1, tile, wide)
            bias = None
            if wide and (tile == 0 or tile == tiles - 1):
                place = lax.rem(
                    lax.broadcasted_iota(jnp.int32, (1, keys.shape[0]), 1), 3 * span
                )
                low = jnp.where(edges[0] == 0, span, 0) if tile == 0 else 0
                high = jnp.where(edges[1] == 0, 2 * span, 3 * span) if tile == tiles - 1 else 3 * span
                bias = jnp.where((place >= low) & (place < high), 0.0, -jnp.inf)
            for q_ref, out_ref, stat_ref in zip(q_refs, out_refs, stat_refs):
                query = q_ref[:, rows, :].reshape(-1, head_size)
                scores = (
                    lax.dot_general(
                        query, keys, (((1,), (1,)), ((), ())), preferred_element_type=jnp.float32
                    )
                    * scale
                )
                if bias is not None:
                    scores = scores + bias
                highest = jnp.max(scores, axis=1, keepdims=True)
                expo = jnp.exp(scores - highest)
                total = jnp.sum(expo, axis=1, keepdims=True)
                output = jnp.dot(
                    expo.astype(jnp.bfloat16), values, preferred_element_type=jnp.float32
                ) * (1.0 / total)
                out_ref[:, rows, :] = output.astype(jnp.bfloat16).reshape(frames, span, head_size)
                level = (highest + jnp.log(total)).reshape(frames, span, 1)
                stat_ref[:, rows, :] = jnp.where(lane == step, level, stat_ref[:, rows, :])

    active = step < group
    if columns_only:

        @pl.when(active & (radius_col == 0))
        def _():
            for out_ref in out_refs:
                out_ref[...] = jnp.zeros_like(out_ref)

        active = active & (radius_col != 0)

    @pl.when(active & (radius_row == 0))
    def _():
        attend(False)

    @pl.when(active & (radius_row != 0))
    def _():
        attend(True)

    @pl.when(step == group)
    def _():
        for out_ref, stat_ref in zip(out_refs, stat_refs):
            level = stat_ref[...]
            high = level.astype(jnp.bfloat16).astype(jnp.float32)
            middle = (level - high).astype(jnp.bfloat16).astype(jnp.float32)
            low = level - high - middle
            packed = high + pltpu.roll(middle, LEVEL_STEP, 2) + pltpu.roll(low, 2 * LEVEL_STEP, 2)
            out_ref[...] = packed.astype(jnp.bfloat16)


def attention(windows, edges, query_blocks, keys_values, top, bottom, columns_only):
    frames, tokens, features = query_blocks[0].shape
    group = windows.shape[0]
    head_size = features // group
    span = top.shape[2]
    q_count = len(query_blocks)

    def head_of(step):
        return jnp.minimum(step, group - 1)

    q_spec = pl.BlockSpec((frames, tokens, head_size), lambda h, *_: (0, 0, head_of(h)))
    kv_spec = pl.BlockSpec((2, frames, tokens, head_size), lambda h, *_: (0, 0, 0, head_of(h)))
    halo_spec = pl.BlockSpec((2, frames, span, head_size), lambda h, *_: (0, 0, 0, head_of(h)))
    out_spec = pl.BlockSpec((frames, tokens, head_size), lambda h, *_: (0, 0, h))
    return pl.pallas_call(
        partial(attention_kernel, q_count=q_count, columns_only=columns_only, group=group),
        grid_spec=pltpu.PrefetchScalarGridSpec(
            num_scalar_prefetch=2,
            grid=(group + 1,),
            in_specs=[q_spec] * q_count + [kv_spec, halo_spec, halo_spec],
            out_specs=[out_spec] * q_count,
            scratch_shapes=[pltpu.VMEM((frames, tokens, LANES), jnp.float32)] * q_count,
        ),
        out_shape=[jax.ShapeDtypeStruct((frames, tokens, (group + 1) * head_size), jnp.bfloat16)]
        * q_count,
        compiler_params=kernel_params(),
        cost_estimate=SMALL,
        name="attend_neighbours" if columns_only else "attend_own",
    )(windows, edges, *query_blocks, keys_values, top, bottom)


def combine_kernel(windows, edges, own, left, right, own_stat, left_stat, right_stat, out, *, heads):
    first = pl.program_id(0) * heads
    frames, tokens, width = own.shape
    head_size = width // heads

    for index in range(heads):
        head = first + index
        columns = slice(index * head_size, (index + 1) * head_size)
        radius_col = windows[head, 1]

        @pl.when(radius_col == 0)
        def _(columns=columns):
            out[:, :, columns] = own[:, :, columns]

        @pl.when(radius_col != 0)
        def _(columns=columns, head=head):
            lane = lax.broadcasted_iota(jnp.int32, (LANES, head_size), 0)
            pick = jnp.where(
                (lax.rem(lane, LEVEL_STEP) == head) & (lane < 3 * LEVEL_STEP), 1.0, 0.0
            ).astype(jnp.bfloat16)

            def level(ref):
                return jnp.dot(
                    ref[...].reshape(-1, LANES), pick, preferred_element_type=jnp.float32
                ).reshape(frames, tokens, head_size)

            own_level = level(own_stat)
            left_level = jnp.where(edges[2] == 0, -jnp.inf, level(left_stat))
            right_level = jnp.where(edges[3] == 0, -jnp.inf, level(right_stat))
            highest = jnp.maximum(own_level, jnp.maximum(left_level, right_level))
            weights = [jnp.exp(x - highest) for x in (own_level, left_level, right_level)]
            mixed = sum(
                ref[:, :, columns].astype(jnp.float32) * weight
                for ref, weight in zip((own, left, right), weights)
            )
            out[:, :, columns] = (mixed / (weights[0] + weights[1] + weights[2])).astype(
                jnp.bfloat16
            )


def combine(windows, edges, outputs, features, order):
    frames, tokens, _ = outputs[0].shape
    head_count = windows.shape[0]
    heads = head_count // order
    width = features // order
    spec = pl.BlockSpec((frames, tokens, width), lambda h, *_: (0, 0, h))
    stat_spec = pl.BlockSpec(
        (frames, tokens, features // head_count), lambda h, *_: (0, 0, head_count)
    )
    return pl.pallas_call(
        partial(combine_kernel, heads=heads),
        grid_spec=pltpu.PrefetchScalarGridSpec(
            num_scalar_prefetch=2,
            grid=(order,),
            in_specs=[spec] * 3 + [stat_spec] * 3,
            out_specs=pl.BlockSpec(
                (frames, tokens, width), lambda h, windows, edges: (0, 0, h ^ edges[4])
            ),
        ),
        out_shape=jax.ShapeDtypeStruct((frames, tokens, features), jnp.bfloat16),
        compiler_params=kernel_params(),
        cost_estimate=SMALL,
        name="combine",
    )(windows, edges, *outputs, *outputs)


def project_kernel(place, attended, *refs, slots, carried, start, column):
    arrays = 1 + max(piece[0] for slot in slots for piece in slot)
    pieces, refs = refs[:arrays], refs[arrays:]
    if carried:
        carry, refs = refs[0], refs[1:]
    out, rows, weight, rows_sem, weight_sem = refs
    columns = weight.shape[1]
    depth = weight.shape[2]
    rows_copy = pltpu.make_async_copy(
        attended.at[:, start : start + depth], rows, rows_sem.at[0]
    )
    rows_copy.start()
    for index, slot in enumerate(slots):
        for block in range(columns):
            low = 0
            for number, (array, size, share) in enumerate(slot):
                first = 0
                if share is not None:
                    first = pl.multiple_of((place[0] ^ share) * size, size)
                pltpu.make_async_copy(
                    pieces[array].at[pl.ds(first, size), block * column : (block + 1) * column],
                    weight.at[index, block, low : low + size],
                    weight_sem.at[index, block, number],
                ).start()
                low += size
    rows_copy.wait()
    for index, slot in enumerate(slots):

        def body(block, _, index=index, slot=slot):
            low = 0
            for number, (_, size, _) in enumerate(slot):
                piece = weight.at[index, block, low : low + size]
                pltpu.make_async_copy(piece, piece, weight_sem.at[index, block, number]).wait()
                low += size
            total = jnp.dot(rows[...], weight[index, block], preferred_element_type=jnp.float32)
            here = pl.ds(pl.multiple_of(block * column, column), column)
            if carried:
                total = total + carry[:, here]
            out[index, :, here] = total.astype(out.dtype)
            return 0

        lax.fori_loop(0, columns, body, 0)


def project(place, attended, arrays, slots, carry, start, dtype):
    tokens = attended.shape[0]
    width = arrays[0].shape[1]
    column = 256 if width % 256 == 0 else width
    columns = width // column
    depth = sum(size for _, size, _ in slots[0])
    anywhere = pl.BlockSpec(memory_space=pl.ANY)
    inside = pl.BlockSpec(memory_space=pltpu.VMEM)
    return pl.pallas_call(
        partial(
            project_kernel, slots=slots, carried=carry is not None, start=start, column=column
        ),
        in_specs=[pl.BlockSpec(memory_space=pltpu.SMEM), anywhere]
        + [anywhere] * len(arrays)
        + ([] if carry is None else [inside]),
        out_specs=inside,
        out_shape=jax.ShapeDtypeStruct((len(slots), tokens, width), dtype),
        scratch_shapes=[
            pltpu.VMEM((tokens, depth), attended.dtype),
            pltpu.VMEM((len(slots), columns, depth, column), attended.dtype),
            pltpu.SemaphoreType.DMA((1,)),
            pltpu.SemaphoreType.DMA((len(slots), columns, max(len(slot) for slot in slots))),
        ],
        compiler_params=pltpu.CompilerParams(vmem_limit_bytes=VMEM_LIMIT),
        cost_estimate=SMALL,
        name="project",
    )(place, attended, *arrays, *([] if carry is None else [carry]))


def mix_kernel(
    place, own_part, other_part, own_hidden, other_hidden, own_gate, other_gate, mixed_ref, sums_ref
):
    step = pl.program_id(0)
    mine = place[3 * step] != 0
    hidden = jnp.where(
        mine, own_hidden[...].astype(jnp.float32), other_hidden[...].astype(jnp.float32)
    )
    gate = jnp.where(mine, own_gate[...], other_gate[...])
    mixed = hidden + gate * (
        own_part[0].astype(jnp.float32) + other_part[0].astype(jnp.float32)
    )
    mixed_ref[...] = mixed
    lane = lax.broadcasted_iota(jnp.int32, sums_ref.shape, 1)
    first = jnp.sum(mixed, axis=1, keepdims=True)
    second = jnp.sum(mixed * mixed, axis=1, keepdims=True)
    sums = jnp.where(lane == 0, first, jnp.where(lane == 1, second, 0.0))

    @pl.when(step == 0)
    def _():
        sums_ref[...] = sums

    @pl.when(step != 0)
    def _():
        sums_ref[...] = sums_ref[...] + sums


def mix(place, own_part, other_part, own_hidden, other_hidden, own_gate, other_gate):
    count, tokens, width = own_part.shape
    blocks = own_hidden.shape[1] // width
    part = pl.BlockSpec((1, tokens, width), lambda i, place: (i, 0, 0))
    hidden = pl.BlockSpec((tokens, width), lambda i, place: (0, place[3 * i + 1]))
    gate = pl.BlockSpec((1, width), lambda i, place: (0, place[3 * i + 1]))
    sums = pl.BlockSpec((tokens, LANES), lambda i, place: (0, 0))
    mixed = pl.BlockSpec((tokens, width), lambda i, place: (0, place[3 * i + 2]))
    return pl.pallas_call(
        mix_kernel,
        grid_spec=pltpu.PrefetchScalarGridSpec(
            num_scalar_prefetch=1,
            grid=(count,),
            in_specs=[part, part, hidden, hidden, gate, gate],
            out_specs=[mixed, sums],
        ),
        out_shape=[
            jax.ShapeDtypeStruct((tokens, (blocks + 1) * width), jnp.float32),
            jax.ShapeDtypeStruct((tokens, LANES), jnp.float32),
        ],
        compiler_params=kernel_params(),
        cost_estimate=SMALL,
        name="mix",
    )(place, own_part, other_part, own_hidden, other_hidden, own_gate, other_gate)


def finish_kernel(
    place, own_part, other_part, own_hidden, other_hidden, own_gate, other_gate, scale, shift_by,
    sums, mixed_ref, residual, ffn,
):
    mine = place[0] != 0
    width = own_part.shape[2]
    blocks = residual.shape[1] // width
    hidden = jnp.where(
        mine, own_hidden[...].astype(jnp.float32), other_hidden[...].astype(jnp.float32)
    )
    gate = jnp.where(mine, own_gate[...], other_gate[...])
    last = hidden + gate * (
        own_part[0].astype(jnp.float32) + other_part[0].astype(jnp.float32)
    )
    first = sums[:, 0:1] + jnp.sum(last, axis=1, keepdims=True)
    second = sums[:, 1:2] + jnp.sum(last * last, axis=1, keepdims=True)
    average = first / D
    variance = second / D - average * average
    inverse = lax.rsqrt(variance + EPSILON)
    for block in range(blocks):
        columns = slice(block * width, (block + 1) * width)
        here = mine & (place[1] == block)
        mixed = jnp.where(here, last, mixed_ref[:, columns])
        residual[:, columns] = mixed.astype(jnp.bfloat16)
        ffn[:, columns] = (
            (mixed - average) * inverse * (1.0 + scale[:, columns]) + shift_by[:, columns]
        ).astype(jnp.bfloat16)


def finish(place, own_part, other_part, own_hidden, other_hidden, own_gate, other_gate, scale, shift_by, carry):
    _, tokens, width = own_part.shape
    features = own_hidden.shape[1]
    rows = 128 if tokens % 128 == 0 else tokens
    part = pl.BlockSpec((1, rows, width), lambda i, place: (0, i, 0))
    hidden = pl.BlockSpec((rows, width), lambda i, place: (i, place[1]))
    gate = pl.BlockSpec((1, width), lambda i, place: (0, place[1]))
    whole = pl.BlockSpec((1, features), lambda i, place: (0, 0))
    sums = pl.BlockSpec((rows, LANES), lambda i, place: (i, 0))
    row = pl.BlockSpec((rows, features), lambda i, place: (i, 0))
    return pl.pallas_call(
        finish_kernel,
        grid_spec=pltpu.PrefetchScalarGridSpec(
            num_scalar_prefetch=1,
            grid=(tokens // rows,),
            in_specs=[part, part, hidden, hidden, gate, gate, whole, whole, sums, row],
            out_specs=[row, row],
        ),
        out_shape=[jax.ShapeDtypeStruct((tokens, features), jnp.bfloat16)] * 2,
        compiler_params=kernel_params(),
        cost_estimate=SMALL,
        name="finish",
    )(
        place, own_part, other_part, own_hidden, other_hidden, own_gate, other_gate, scale,
        shift_by, carry[1], carry[0],
    )


def shift(block, axis, step):
    count = lax.axis_size(axis)
    pairs = [(i, i + step) for i in range(count) if 0 <= i + step < count]
    return lax.ppermute(block, axis, pairs)


def turn(block, axis, step):
    count = lax.axis_size(axis)
    return lax.ppermute(block, axis, [(i, (i + step) % count) for i in range(count)])


def swap(block, axis, bit):
    count = lax.axis_size(axis)
    return lax.ppermute(block, axis, [(i, i ^ bit) for i in range(count)])


class Tokens:
    def __init__(self, queries, keys_values, windows, order):
        self.features = queries.shape[3]
        n_ha, n_wa = lax.axis_size("ha"), lax.axis_size("wa")
        ha, wa = lax.axis_index("ha"), lax.axis_index("wa")
        turned = ha if order > 1 else 0 * ha
        self.edges = jnp.stack([ha > 0, ha < n_ha - 1, wa > 0, wa < n_wa - 1, turned]).astype(
            jnp.int32
        )
        self.windows = windows
        self.order = order
        self.queries = self.flat(queries)
        self.keys_values = self.flat(keys_values)

    def flat(self, block):
        return block.reshape(block.shape[:-3] + (-1, self.features))

    def attend(self, query_blocks, halos, columns_only):
        return attention(
            self.windows, self.edges, query_blocks, self.keys_values, *halos, columns_only
        )

    def combine(self, near, back):
        attended = combine(
            self.windows, self.edges, [near, *back], self.features, self.order
        )
        return attended.reshape(-1, self.features)


def edge_rows(keys_values):
    rows = keys_values.shape[2]
    return lax.optimization_barrier(
        (keys_values[:, :, rows - TILE :], keys_values[:, :, :TILE])
    )


def together(*blocks):
    return lax.optimization_barrier(blocks)


def paired(hidden, queries, keys_values, windows, out_weight, picked):
    ha, wa, ta = lax.axis_index("ha"), lax.axis_index("wa"), lax.axis_index("ta")
    n_wa = lax.axis_size("wa")
    blocks = n_wa // 2
    depth = out_weight.shape[0] // 4
    width = out_weight.shape[1]
    cuts = [depth * 2 // 5, depth // 2, depth // 2]

    share = lax.optimization_barrier(lax.dynamic_slice_in_dim(out_weight, ha * depth, depth, 0))
    first = turn(share, "wa", 1)
    last_rows, first_rows = edge_rows(keys_values)
    tokens = Tokens(queries, keys_values, windows, 4)
    top = shift(last_rows, "ha", 1)
    bottom = shift(first_rows, "ha", -1)

    from_left = shift(queries, "wa", 1)
    from_right = shift(queries, "wa", -1)

    first, top, bottom = together(first, top, bottom)
    first_x = swap(first, "ha", 1)
    first_y = swap(first, "ha", 2)
    second = turn(first, "wa", 1)
    halos = tokens.flat(top), tokens.flat(bottom)
    (near,) = tokens.attend([tokens.queries], halos, False)

    near, first_x, first_y, second, from_left, from_right = together(
        near, first_x, first_y, second, from_left, from_right
    )
    third = turn(second, "wa", 1)
    first_far_x = swap(first_y[: cuts[0]], "ha", 1)
    first_far_y = swap(first_x[cuts[0] :], "ha", 2)
    second_x = swap(second, "ha", 1)
    second_y = swap(second, "ha", 2)
    for_left, for_right = tokens.attend(
        [tokens.flat(from_left), tokens.flat(from_right)], halos, True
    )

    for_left, for_right, first_far_x, first_far_y = together(
        for_left, for_right, first_far_x, first_far_y
    )
    left = shift(for_right, "wa", 1)
    right = shift(for_left, "wa", -1)

    third, second_x, second_y, first_far_x = together(third, second_x, second_y, first_far_x)
    second_far_x = swap(second_y[: cuts[1]], "ha", 1)
    second_far_y = swap(second_x[cuts[1] :], "ha", 2)
    third_x = swap(third, "ha", 1)

    third, second_far_x, second_far_y, left, right, hidden, gate = together(
        third, second_far_x, second_far_y, left, right, hidden, picked[0:1]
    )
    third_y = swap(third, "ha", 2)
    other_hidden = swap(hidden, "ta", 1)

    attended = tokens.combine(near, [left, right])
    other_gate = swap(gate, "ta", 1)
    place = ha.reshape(1)
    early = [
        out_weight,
        *(first, first_x, first_y, first_far_x, first_far_y),
        *(second, second_x, second_y, second_far_x, second_far_y),
    ]

    def whole(start, cut):
        sizes = [depth, depth, depth, cut, depth - cut]
        return [(start + index, size, None) for index, size in enumerate(sizes)]

    own = [(0, depth, number) for number in range(4)]
    slots = [own, whole(1, cuts[0]), whole(6, cuts[1])]
    sums = project(place, attended, early, slots, None, 0, jnp.bfloat16)
    third_x, third_y, sums = together(third_x, third_y, sums)
    third_far_x = swap(third_y[: cuts[2]], "ha", 1)
    third_far_y = swap(third_x[cuts[2] :], "ha", 2)
    other_sums = swap(sums, "ta", 1)
    near_slot = [(index, depth, None) for index in range(3)]
    last = project(place, attended, [third, third_x, third_y], [near_slot], None, 0, jnp.float32)

    def placed(distance):
        block = lax.rem(wa - distance + n_wa, n_wa)
        mine = block // blocks == ta
        inner = lax.rem(block, blocks)
        return jnp.stack([mine.astype(jnp.int32), inner, jnp.where(mine, inner, blocks)])

    places = jnp.concatenate([placed(distance) for distance in range(n_wa - 1)])
    sides = hidden, other_hidden, gate, other_gate
    carry = mix(places, sums, other_sums, *sides)

    third_far_x, third_far_y, last, *carry = together(third_far_x, third_far_y, last, *carry)
    far_slot = [(0, cuts[2], None), (1, depth - cuts[2], None)]
    last = project(
        place,
        attended,
        [third_far_x, third_far_y],
        [far_slot],
        last.reshape(-1, width),
        3 * depth,
        jnp.bfloat16,
    )
    other_last = swap(last, "ta", 1)
    return finish(
        placed(n_wa - 1), last, other_last, *sides, picked[2:3], picked[1:2], carry
    )


def gathered(hidden, queries, keys_values, windows, out_weight, picked):
    work = Tokens(queries, keys_values, windows, 1)
    last_rows, first_rows = edge_rows(keys_values)
    halos = work.flat(shift(last_rows, "ha", 1)), work.flat(shift(first_rows, "ha", -1))
    visitors = [work.flat(shift(queries, "wa", 1)), work.flat(shift(queries, "wa", -1))]
    (near,) = work.attend([work.queries], halos, False)
    for_left, for_right = work.attend(visitors, halos, True)
    attended = work.combine(near, [shift(for_right, "wa", 1), shift(for_left, "wa", -1)])
    n_ha, n_wa, n_ta = lax.axis_size("ha"), lax.axis_size("wa"), lax.axis_size("ta")
    ha, ta = lax.axis_index("ha"), lax.axis_index("ta")
    tokens, features = attended.shape
    depth = features // n_ha
    width = out_weight.shape[1]
    share = lax.dynamic_slice_in_dim(out_weight, ha * depth, depth, 0)
    weights = lax.all_gather(share, ("ha", "wa"), axis=0, tiled=False).reshape(
        n_ha, n_wa, depth, width
    )
    partial_sums = jnp.einsum(
        "thk,hwkc->wtc",
        attended.reshape(tokens, n_ha, depth),
        weights,
        preferred_element_type=jnp.float32,
    ).astype(jnp.bfloat16)
    blocks = n_wa // n_ta
    summed = None
    for step in range(n_ta):
        target = lax.rem(ta + step, n_ta)
        piece = lax.dynamic_slice_in_dim(partial_sums, target * blocks, blocks, 0)
        if step:
            piece = turn(piece, "ta", step)
        piece = piece.astype(jnp.float32)
        summed = piece if summed is None else summed + piece
    summed = jnp.transpose(summed, (1, 0, 2)).reshape(tokens, -1)
    mixed = hidden.astype(jnp.float32) + picked[0] * summed
    sum_first, sum_second = lax.psum((jnp.sum(mixed, axis=1), jnp.sum(mixed * mixed, axis=1)), "ta")
    average = (sum_first / D)[:, None]
    variance = (sum_second / D)[:, None] - average * average
    normed = (mixed - average) * lax.rsqrt(variance + EPSILON)
    ffn_input = (normed * (1.0 + picked[2]) + picked[1]).astype(jnp.bfloat16)
    return mixed.astype(jnp.bfloat16), ffn_input


def shards(hidden_states, queries, keys_values, out_weight, mod_table, windows, step_index):
    tokens = math.prod(queries.shape[:3])
    width = hidden_states.shape[3]
    picked = lax.dynamic_index_in_dim(mod_table, step_index[0], 0, keepdims=False)
    sizes = lax.axis_size("ha"), lax.axis_size("wa"), lax.axis_size("ta")
    tuned = sizes == (4, 4, 2) and out_weight.shape[0] % (20 * LANES) == 0
    residual_out, ffn_input = (paired if tuned else gathered)(
        hidden_states.reshape(tokens, width), queries, keys_values, windows, out_weight, picked
    )
    return residual_out.reshape(hidden_states.shape), ffn_input.reshape(hidden_states.shape)


def solution(mesh):
    return jax.shard_map(
        shards,
        mesh=mesh,
        in_specs=(
            P(None, "ha", "wa", "ta"),
            P(None, "ha", "wa", "ta"),
            P(None, None, "ha", "wa", "ta"),
            P("ta", "wa"),
            P(None, None, "ta"),
            P("ta", None),
            P(),
        ),
        out_specs=(P(None, "ha", "wa", "ta"), P(None, "ha", "wa", "ta")),
        check_vma=False,
    )
```

```python
from functools import partial
import math

import jax
import jax.numpy as jnp
from jax import lax
from jax.experimental import pallas as pl
from jax.experimental.pallas import tpu as pltpu
from jax.sharding import PartitionSpec as P

D = 5120
HD = 128
TILE = 8
LANES = 128
LEVEL_STEP = 32

EPSILON = 1e-06
VMEM_LIMIT = 32 * 1024 * 1024
MOST_VMEM = 56 * 1024 * 1024
SMALL = pl.CostEstimate(flops=1, bytes_accessed=1, transcendentals=0)


def kernel_params(limit=VMEM_LIMIT):
    return pltpu.CompilerParams(dimension_semantics=("arbitrary",), vmem_limit_bytes=limit)


def attention_kernel(windows, edges, *refs, q_count, columns_only, group):
    q_refs = refs[:q_count]
    kv_ref, top_ref, bottom_ref = refs[q_count : q_count + 3]
    refs = refs[q_count + 3 :]
    out_refs, stat_refs = refs[:q_count], refs[q_count:]
    frames, tokens, head_size = q_refs[0].shape
    span = top_ref.shape[2]
    tiles = tokens // span
    step = pl.program_id(0)
    head = jnp.minimum(step, group - 1)
    radius_row = windows[head, 0]
    radius_col = windows[head, 1]
    scale = 1.0 / math.sqrt(HD)

    @pl.when(step == 0)
    def _():
        for stat_ref in stat_refs:
            stat_ref[...] = jnp.zeros_like(stat_ref)

    def near(which, tile, wide):
        if not wide:
            return kv_ref[which, :, tile * span : (tile + 1) * span, :].reshape(-1, head_size)
        pieces = []
        if tile == 0:
            pieces.append(top_ref[which])
        low = max(tile - 1, 0) * span
        high = min(tile + 2, tiles) * span
        pieces.append(kv_ref[which, :, low:high, :])
        if tile == tiles - 1:
            pieces.append(bottom_ref[which])
        block = pieces[0] if len(pieces) == 1 else jnp.concatenate(pieces, axis=1)
        return block.reshape(-1, head_size)

    def attend(wide):
        lane = lax.broadcasted_iota(jnp.int32, (frames, span, LANES), 2)
        for tile in range(tiles):
            rows = slice(tile * span, (tile + 1) * span)
            keys = near(0, tile, wide)
            values = near(1, tile, wide)
            bias = None
            if wide and (tile == 0 or tile == tiles - 1):
                place = lax.rem(
                    lax.broadcasted_iota(jnp.int32, (1, keys.shape[0]), 1), 3 * span
                )
                low = jnp.where(edges[0] == 0, span, 0) if tile == 0 else 0
                high = jnp.where(edges[1] == 0, 2 * span, 3 * span) if tile == tiles - 1 else 3 * span
                bias = jnp.where((place >= low) & (place < high), 0.0, -jnp.inf)
            for q_ref, out_ref, stat_ref in zip(q_refs, out_refs, stat_refs):
                query = q_ref[:, rows, :].reshape(-1, head_size)
                scores = (
                    lax.dot_general(
                        query, keys, (((1,), (1,)), ((), ())), preferred_element_type=jnp.float32
                    )
                    * scale
                )
                if bias is not None:
                    scores = scores + bias
                highest = jnp.max(scores, axis=1, keepdims=True)
                expo = jnp.exp(scores - highest)
                total = jnp.sum(expo, axis=1, keepdims=True)
                output = jnp.dot(
                    expo.astype(jnp.bfloat16), values, preferred_element_type=jnp.float32
                ) * (1.0 / total)
                out_ref[:, rows, :] = output.astype(jnp.bfloat16).reshape(frames, span, head_size)
                level = (highest + jnp.log(total)).reshape(frames, span, 1)
                stat_ref[:, rows, :] = jnp.where(lane == step, level, stat_ref[:, rows, :])

    active = step < group
    if columns_only:

        @pl.when(active & (radius_col == 0))
        def _():
            for out_ref in out_refs:
                out_ref[...] = jnp.zeros_like(out_ref)

        active = active & (radius_col != 0)

    @pl.when(active & (radius_row == 0))
    def _():
        attend(False)

    @pl.when(active & (radius_row != 0))
    def _():
        attend(True)

    @pl.when(step == group)
    def _():
        for out_ref, stat_ref in zip(out_refs, stat_refs):
            level = stat_ref[...]
            high = level.astype(jnp.bfloat16).astype(jnp.float32)
            middle = (level - high).astype(jnp.bfloat16).astype(jnp.float32)
            low = level - high - middle
            packed = high + pltpu.roll(middle, LEVEL_STEP, 2) + pltpu.roll(low, 2 * LEVEL_STEP, 2)
            out_ref[...] = packed.astype(jnp.bfloat16)


def attention(windows, edges, query_blocks, keys_values, top, bottom, columns_only):
    frames, tokens, features = query_blocks[0].shape
    group = windows.shape[0]
    head_size = features // group
    span = top.shape[2]
    q_count = len(query_blocks)

    def head_of(step):
        return jnp.minimum(step, group - 1)

    q_spec = pl.BlockSpec((frames, tokens, head_size), lambda h, *_: (0, 0, head_of(h)))
    kv_spec = pl.BlockSpec((2, frames, tokens, head_size), lambda h, *_: (0, 0, 0, head_of(h)))
    halo_spec = pl.BlockSpec((2, frames, span, head_size), lambda h, *_: (0, 0, 0, head_of(h)))
    out_spec = pl.BlockSpec((frames, tokens, head_size), lambda h, *_: (0, 0, h))
    return pl.pallas_call(
        partial(attention_kernel, q_count=q_count, columns_only=columns_only, group=group),
        grid_spec=pltpu.PrefetchScalarGridSpec(
            num_scalar_prefetch=2,
            grid=(group + 1,),
            in_specs=[q_spec] * q_count + [kv_spec, halo_spec, halo_spec],
            out_specs=[out_spec] * q_count,
            scratch_shapes=[pltpu.VMEM((frames, tokens, LANES), jnp.float32)] * q_count,
        ),
        out_shape=[jax.ShapeDtypeStruct((frames, tokens, (group + 1) * head_size), jnp.bfloat16)]
        * q_count,
        compiler_params=kernel_params(),
        cost_estimate=SMALL,
        name="attend_neighbours" if columns_only else "attend_own",
    )(windows, edges, *query_blocks, keys_values, top, bottom)


def combine_kernel(windows, edges, own, left, right, own_stat, left_stat, right_stat, out, *, heads):
    first = pl.program_id(0) * heads
    frames, tokens, width = own.shape
    head_size = width // heads

    for index in range(heads):
        head = first + index
        columns = slice(index * head_size, (index + 1) * head_size)
        radius_col = windows[head, 1]

        @pl.when(radius_col == 0)
        def _(columns=columns):
            out[:, :, columns] = own[:, :, columns]

        @pl.when(radius_col != 0)
        def _(columns=columns, head=head):
            lane = lax.broadcasted_iota(jnp.int32, (LANES, head_size), 0)
            pick = jnp.where(
                (lax.rem(lane, LEVEL_STEP) == head) & (lane < 3 * LEVEL_STEP), 1.0, 0.0
            ).astype(jnp.bfloat16)

            def level(ref):
                return jnp.dot(
                    ref[...].reshape(-1, LANES), pick, preferred_element_type=jnp.float32
                ).reshape(frames, tokens, head_size)

            own_level = level(own_stat)
            left_level = jnp.where(edges[2] == 0, -jnp.inf, level(left_stat))
            right_level = jnp.where(edges[3] == 0, -jnp.inf, level(right_stat))
            highest = jnp.maximum(own_level, jnp.maximum(left_level, right_level))
            weights = [jnp.exp(x - highest) for x in (own_level, left_level, right_level)]
            mixed = sum(
                ref[:, :, columns].astype(jnp.float32) * weight
                for ref, weight in zip((own, left, right), weights)
            )
            out[:, :, columns] = (mixed / (weights[0] + weights[1] + weights[2])).astype(
                jnp.bfloat16
            )


def combine(windows, edges, outputs, features, order):
    frames, tokens, _ = outputs[0].shape
    head_count = windows.shape[0]
    heads = head_count // order
    width = features // order
    spec = pl.BlockSpec((frames, tokens, width), lambda h, *_: (0, 0, h))
    stat_spec = pl.BlockSpec(
        (frames, tokens, features // head_count), lambda h, *_: (0, 0, head_count)
    )
    return pl.pallas_call(
        partial(combine_kernel, heads=heads),
        grid_spec=pltpu.PrefetchScalarGridSpec(
            num_scalar_prefetch=2,
            grid=(order,),
            in_specs=[spec] * 3 + [stat_spec] * 3,
            out_specs=pl.BlockSpec(
                (frames, tokens, width), lambda h, windows, edges: (0, 0, h ^ edges[4])
            ),
        ),
        out_shape=jax.ShapeDtypeStruct((frames, tokens, features), jnp.bfloat16),
        compiler_params=kernel_params(),
        cost_estimate=SMALL,
        name="combine",
    )(windows, edges, *outputs, *outputs)


def project_kernel(place, attended, *refs, slots, carried, start, column):
    arrays = 1 + max(piece[0] for slot in slots for piece in slot)
    pieces, refs = refs[:arrays], refs[arrays:]
    if carried:
        carry, refs = refs[0], refs[1:]
    out, rows, weight, rows_sem, weight_sem = refs
    columns = weight.shape[1]
    depth = weight.shape[2]
    rows_copy = pltpu.make_async_copy(
        attended.at[:, start : start + depth], rows, rows_sem.at[0]
    )
    rows_copy.start()
    for index, slot in enumerate(slots):
        for block in range(columns):
            low = 0
            for number, (array, size, share, turned) in enumerate(slot):
                first = pl.multiple_of((place[0] ^ share if turned else share) * size, size)
                pltpu.make_async_copy(
                    pieces[array].at[pl.ds(first, size), block * column : (block + 1) * column],
                    weight.at[index, block, low : low + size],
                    weight_sem.at[index, block, number],
                ).start()
                low += size
    rows_copy.wait()
    for index, slot in enumerate(slots):

        def body(block, _, index=index, slot=slot):
            low = 0
            for number, (_, size, _, _) in enumerate(slot):
                piece = weight.at[index, block, low : low + size]
                pltpu.make_async_copy(piece, piece, weight_sem.at[index, block, number]).wait()
                low += size
            total = jnp.dot(rows[...], weight[index, block], preferred_element_type=jnp.float32)
            here = pl.ds(pl.multiple_of(block * column, column), column)
            if carried:
                total = total + carry[:, here]
            out[index, :, here] = total.astype(out.dtype)
            return 0

        lax.fori_loop(0, columns, body, 0)


def project(place, attended, arrays, slots, carry, start, dtype):
    tokens = attended.shape[0]
    width = arrays[0].shape[1]
    column = 256 if width % 256 == 0 else width
    columns = width // column
    depth = sum(piece[1] for piece in slots[0])
    anywhere = pl.BlockSpec(memory_space=pl.ANY)
    inside = pl.BlockSpec(memory_space=pltpu.VMEM)
    return pl.pallas_call(
        partial(
            project_kernel, slots=slots, carried=carry is not None, start=start, column=column
        ),
        in_specs=[pl.BlockSpec(memory_space=pltpu.SMEM), anywhere]
        + [anywhere] * len(arrays)
        + ([] if carry is None else [inside]),
        out_specs=inside,
        out_shape=jax.ShapeDtypeStruct((len(slots), tokens, width), dtype),
        scratch_shapes=[
            pltpu.VMEM((tokens, depth), attended.dtype),
            pltpu.VMEM((len(slots), columns, depth, column), attended.dtype),
            pltpu.SemaphoreType.DMA((1,)),
            pltpu.SemaphoreType.DMA((len(slots), columns, max(len(slot) for slot in slots))),
        ],
        compiler_params=pltpu.CompilerParams(vmem_limit_bytes=VMEM_LIMIT),
        cost_estimate=SMALL,
        name="project",
    )(place, attended, *arrays, *([] if carry is None else [carry]))


def mix_kernel(
    place, own_part, other_part, own_hidden, other_hidden, own_gate, other_gate, *refs
):
    mixed_ref, sums_ref = refs[-2:]
    step = pl.program_id(0)
    mine = place[3 * step] != 0
    hidden = jnp.where(
        mine, own_hidden[...].astype(jnp.float32), other_hidden[...].astype(jnp.float32)
    )
    gate = jnp.where(mine, own_gate[...], other_gate[...])
    mixed = hidden + gate * (
        own_part[0].astype(jnp.float32) + other_part[0].astype(jnp.float32)
    )
    mixed_ref[...] = mixed
    lane = lax.broadcasted_iota(jnp.int32, sums_ref.shape, 1)
    first = jnp.sum(mixed, axis=1, keepdims=True)
    second = jnp.sum(mixed * mixed, axis=1, keepdims=True)
    sums = jnp.where(lane == 0, first, jnp.where(lane == 1, second, 0.0))

    @pl.when(step == 0)
    def _():
        sums_ref[...] = sums + refs[0][...] if len(refs) == 4 else sums

    @pl.when(step != 0)
    def _():
        sums_ref[...] = sums_ref[...] + sums


def mix(place, own_part, other_part, own_hidden, other_hidden, own_gate, other_gate, carry):
    count, tokens, width = own_part.shape
    blocks = own_hidden.shape[1] // width
    part = pl.BlockSpec((1, tokens, width), lambda i, place: (i, 0, 0))
    hidden = pl.BlockSpec((tokens, width), lambda i, place: (0, place[3 * i + 1]))
    gate = pl.BlockSpec((1, width), lambda i, place: (0, place[3 * i + 1]))
    sums = pl.BlockSpec((tokens, LANES), lambda i, place: (0, 0))
    mixed = pl.BlockSpec((tokens, width), lambda i, place: (0, place[3 * i + 2]))
    return pl.pallas_call(
        mix_kernel,
        grid_spec=pltpu.PrefetchScalarGridSpec(
            num_scalar_prefetch=1,
            grid=(count,),
            in_specs=[part, part, hidden, hidden, gate, gate]
            + ([sums, pl.BlockSpec(memory_space=pl.ANY)] if carry else []),
            out_specs=[mixed, sums],
        ),
        out_shape=[
            jax.ShapeDtypeStruct((tokens, (blocks + 1) * width), jnp.float32),
            jax.ShapeDtypeStruct((tokens, LANES), jnp.float32),
        ],
        input_output_aliases={8: 0} if carry else {},
        compiler_params=kernel_params(MOST_VMEM),
        cost_estimate=SMALL,
        name="mix",
    )(
        *(place, own_part, other_part, own_hidden, other_hidden, own_gate, other_gate),
        *((carry[1], carry[0]) if carry else ()),
    )


def finish_kernel(
    place, own_part, other_part, own_hidden, other_hidden, own_gate, other_gate, scale, shift_by,
    sums, mixed_ref, residual, ffn,
):
    mine = place[0] != 0
    width = own_part.shape[2]
    blocks = residual.shape[1] // width
    hidden = jnp.where(
        mine, own_hidden[...].astype(jnp.float32), other_hidden[...].astype(jnp.float32)
    )
    gate = jnp.where(mine, own_gate[...], other_gate[...])
    last = hidden + gate * (
        own_part[0].astype(jnp.float32) + other_part[0].astype(jnp.float32)
    )
    first = sums[:, 0:1] + jnp.sum(last, axis=1, keepdims=True)
    second = sums[:, 1:2] + jnp.sum(last * last, axis=1, keepdims=True)
    average = first / D
    variance = second / D - average * average
    inverse = lax.rsqrt(variance + EPSILON)
    for block in range(blocks):
        columns = slice(block * width, (block + 1) * width)
        here = mine & (place[1] == block)
        mixed = jnp.where(here, last, mixed_ref[:, columns])
        residual[:, columns] = mixed.astype(jnp.bfloat16)
        ffn[:, columns] = (
            (mixed - average) * inverse * (1.0 + scale[:, columns]) + shift_by[:, columns]
        ).astype(jnp.bfloat16)


def finish(place, own_part, other_part, own_hidden, other_hidden, own_gate, other_gate, scale, shift_by, carry):
    _, tokens, width = own_part.shape
    features = own_hidden.shape[1]
    rows = 128 if tokens % 128 == 0 else tokens
    part = pl.BlockSpec((1, rows, width), lambda i, place: (0, i, 0))
    hidden = pl.BlockSpec((rows, width), lambda i, place: (i, place[1]))
    gate = pl.BlockSpec((1, width), lambda i, place: (0, place[1]))
    whole = pl.BlockSpec((1, features), lambda i, place: (0, 0))
    sums = pl.BlockSpec((rows, LANES), lambda i, place: (i, 0))
    row = pl.BlockSpec((rows, features), lambda i, place: (i, 0))
    return pl.pallas_call(
        finish_kernel,
        grid_spec=pltpu.PrefetchScalarGridSpec(
            num_scalar_prefetch=1,
            grid=(tokens // rows,),
            in_specs=[part, part, hidden, hidden, gate, gate, whole, whole, sums, row],
            out_specs=[row, row],
        ),
        out_shape=[jax.ShapeDtypeStruct((tokens, features), jnp.bfloat16)] * 2,
        compiler_params=kernel_params(MOST_VMEM),
        cost_estimate=SMALL,
        name="finish",
    )(
        place, own_part, other_part, own_hidden, other_hidden, own_gate, other_gate, scale,
        shift_by, carry[1], carry[0],
    )


def shift(block, axis, step):
    count = lax.axis_size(axis)
    pairs = [(i, i + step) for i in range(count) if 0 <= i + step < count]
    return lax.ppermute(block, axis, pairs)


def turn(block, axis, step):
    count = lax.axis_size(axis)
    return lax.ppermute(block, axis, [(i, (i + step) % count) for i in range(count)])


def swap(block, axis, bit):
    count = lax.axis_size(axis)
    return lax.ppermute(block, axis, [(i, i ^ bit) for i in range(count)])


class Tokens:
    def __init__(self, queries, keys_values, windows, order):
        self.features = queries.shape[3]
        n_ha, n_wa = lax.axis_size("ha"), lax.axis_size("wa")
        ha, wa = lax.axis_index("ha"), lax.axis_index("wa")
        turned = ha if order > 1 else 0 * ha
        self.edges = jnp.stack([ha > 0, ha < n_ha - 1, wa > 0, wa < n_wa - 1, turned]).astype(
            jnp.int32
        )
        self.windows = windows
        self.order = order
        self.queries = self.flat(queries)
        self.keys_values = self.flat(keys_values)

    def flat(self, block):
        return block.reshape(block.shape[:-3] + (-1, self.features))

    def attend(self, query_blocks, halos, columns_only):
        return attention(
            self.windows, self.edges, query_blocks, self.keys_values, *halos, columns_only
        )

    def combine(self, near, back):
        attended = combine(
            self.windows, self.edges, [near, *back], self.features, self.order
        )
        return attended.reshape(-1, self.features)


def edge_rows(keys_values):
    rows = keys_values.shape[2]
    return lax.optimization_barrier(
        (keys_values[:, :, rows - TILE :], keys_values[:, :, :TILE])
    )


def together(*blocks):
    return lax.optimization_barrier(blocks)


def paired(hidden, queries, keys_values, windows, out_weight, picked):
    ha, wa, ta = lax.axis_index("ha"), lax.axis_index("wa"), lax.axis_index("ta")
    n_wa = lax.axis_size("wa")
    blocks = n_wa // 2
    depth = out_weight.shape[0] // 4
    width = out_weight.shape[1]
    cut = depth // 2

    share = lax.optimization_barrier(lax.dynamic_slice_in_dim(out_weight, ha * depth, depth, 0))
    first = turn(share, "wa", 1)
    last_rows, first_rows = edge_rows(keys_values)
    tokens = Tokens(queries, keys_values, windows, 4)
    top = shift(last_rows, "ha", 1)

    first, top, first_rows, queries = together(first, top, first_rows, queries)
    bottom = shift(first_rows, "ha", -1)
    first_y = swap(first, "ha", 2)
    second = turn(first, "wa", 1)
    first_x = swap(first, "ha", 1)

    bottom, first_y, second, queries = together(bottom, first_y, second, queries)
    second_y = swap(second, "ha", 2)
    from_left = shift(queries, "wa", 1)
    from_right = shift(queries, "wa", -1)
    halos = tokens.flat(top), tokens.flat(bottom)
    (near,) = tokens.attend([tokens.queries], halos, False)

    near, first_x, first_y, second = together(near, first_x, first_y, second)
    across = swap(jnp.concatenate([second, first_y], 0), "ha", 1)

    from_left, from_right, second_y, second = together(from_left, from_right, second_y, second)
    third = turn(second, "wa", 1)
    for_left, for_right = tokens.attend(
        [tokens.flat(from_left), tokens.flat(from_right)], halos, True
    )

    for_left, for_right, third = together(for_left, for_right, third)
    left = shift(for_right, "wa", 1)
    right = shift(for_left, "wa", -1)
    third_y = swap(third, "ha", 2)

    third, third_y, across = together(third, third_y, across)
    third_x = swap(third, "ha", 1)
    second_far = swap(across[:depth], "ha", 2)

    left, right, third = together(left, right, third)
    attended = tokens.combine(near, [left, right])
    place = ha.reshape(1)
    own = [(0, depth, number, True) for number in range(4)]

    def whole(*pieces):
        return [(array, depth, number, False) for array, number in pieces]

    sums = project(
        place,
        attended,
        [out_weight, first, first_x, first_y, across],
        [own, whole((1, 0), (2, 0), (3, 0), (4, 1))],
        None,
        0,
        jnp.bfloat16,
    )

    third_x, third_y, second_far, sums, hidden, gate = together(
        third_x, third_y, second_far, sums, hidden, picked[0:1]
    )
    third_far_x = swap(third_y[:cut], "ha", 1)
    third_far_y = swap(third_x[cut:], "ha", 2)
    other_sums = swap(sums, "ta", 1)
    other_hidden = swap(hidden, "ta", 1)
    other_gate = swap(gate, "ta", 1)
    more_sums = project(
        place,
        attended,
        [second, across, second_y, second_far],
        [whole((0, 0), (1, 0), (2, 0), (3, 0))],
        None,
        0,
        jnp.bfloat16,
    )
    other_more = swap(more_sums, "ta", 1)
    last = project(
        place,
        attended,
        [third, third_x, third_y],
        [whole((0, 0), (1, 0), (2, 0))],
        None,
        0,
        jnp.float32,
    )

    def placed(distance):
        block = lax.rem(wa - distance + n_wa, n_wa)
        mine = block // blocks == ta
        inner = lax.rem(block, blocks)
        return jnp.stack([mine.astype(jnp.int32), inner, jnp.where(mine, inner, blocks)])

    sides = hidden, other_hidden, gate, other_gate
    places = jnp.concatenate([placed(0), placed(1)])
    carry = mix(places, sums, other_sums, *sides, None)
    carry = mix(placed(2), more_sums, other_more, *sides, carry)

    third_far_x, third_far_y, last, *carry = together(third_far_x, third_far_y, last, *carry)
    far_slot = [(0, cut, 0, False), (1, depth - cut, 0, False)]
    last = project(
        place,
        attended,
        [third_far_x, third_far_y],
        [far_slot],
        last.reshape(-1, width),
        3 * depth,
        jnp.bfloat16,
    )
    other_last = swap(last, "ta", 1)
    return finish(
        placed(n_wa - 1), last, other_last, *sides, picked[2:3], picked[1:2], carry
    )


def gathered(hidden, queries, keys_values, windows, out_weight, picked):
    work = Tokens(queries, keys_values, windows, 1)
    last_rows, first_rows = edge_rows(keys_values)
    halos = work.flat(shift(last_rows, "ha", 1)), work.flat(shift(first_rows, "ha", -1))
    visitors = [work.flat(shift(queries, "wa", 1)), work.flat(shift(queries, "wa", -1))]
    (near,) = work.attend([work.queries], halos, False)
    for_left, for_right = work.attend(visitors, halos, True)
    attended = work.combine(near, [shift(for_right, "wa", 1), shift(for_left, "wa", -1)])
    n_ha, n_wa, n_ta = lax.axis_size("ha"), lax.axis_size("wa"), lax.axis_size("ta")
    ha, ta = lax.axis_index("ha"), lax.axis_index("ta")
    tokens, features = attended.shape
    depth = features // n_ha
    width = out_weight.shape[1]
    share = lax.dynamic_slice_in_dim(out_weight, ha * depth, depth, 0)
    weights = lax.all_gather(share, ("ha", "wa"), axis=0, tiled=False).reshape(
        n_ha, n_wa, depth, width
    )
    partial_sums = jnp.einsum(
        "thk,hwkc->wtc",
        attended.reshape(tokens, n_ha, depth),
        weights,
        preferred_element_type=jnp.float32,
    ).astype(jnp.bfloat16)
    blocks = n_wa // n_ta
    summed = None
    for step in range(n_ta):
        target = lax.rem(ta + step, n_ta)
        piece = lax.dynamic_slice_in_dim(partial_sums, target * blocks, blocks, 0)
        if step:
            piece = turn(piece, "ta", step)
        piece = piece.astype(jnp.float32)
        summed = piece if summed is None else summed + piece
    summed = jnp.transpose(summed, (1, 0, 2)).reshape(tokens, -1)
    mixed = hidden.astype(jnp.float32) + picked[0] * summed
    sum_first, sum_second = lax.psum((jnp.sum(mixed, axis=1), jnp.sum(mixed * mixed, axis=1)), "ta")
    average = (sum_first / D)[:, None]
    variance = (sum_second / D)[:, None] - average * average
    normed = (mixed - average) * lax.rsqrt(variance + EPSILON)
    ffn_input = (normed * (1.0 + picked[2]) + picked[1]).astype(jnp.bfloat16)
    return mixed.astype(jnp.bfloat16), ffn_input


def shards(hidden_states, queries, keys_values, out_weight, mod_table, windows, step_index):
    tokens = math.prod(queries.shape[:3])
    width = hidden_states.shape[3]
    picked = lax.dynamic_index_in_dim(mod_table, step_index[0], 0, keepdims=False)
    sizes = lax.axis_size("ha"), lax.axis_size("wa"), lax.axis_size("ta")
    tuned = sizes == (4, 4, 2) and out_weight.shape[0] % (20 * LANES) == 0
    residual_out, ffn_input = (paired if tuned else gathered)(
        hidden_states.reshape(tokens, width), queries, keys_values, windows, out_weight, picked
    )
    return residual_out.reshape(hidden_states.shape), ffn_input.reshape(hidden_states.shape)


def solution(mesh):
    return jax.shard_map(
        shards,
        mesh=mesh,
        in_specs=(
            P(None, "ha", "wa", "ta"),
            P(None, "ha", "wa", "ta"),
            P(None, None, "ha", "wa", "ta"),
            P("ta", "wa"),
            P(None, None, "ta"),
            P("ta", None),
            P(),
        ),
        out_specs=(P(None, "ha", "wa", "ta"), P(None, "ha", "wa", "ta")),
        check_vma=False,
    )
```

```python
from functools import partial
import math

import jax
import jax.numpy as jnp
from jax import lax
from jax.experimental import pallas as pl
from jax.experimental.pallas import tpu as pltpu
from jax.sharding import PartitionSpec as P

D = 5120
HD = 128
TILE = 8
LANES = 128
LEVEL_STEP = 32

EPSILON = 1e-06
VMEM_LIMIT = 32 * 1024 * 1024
MOST_VMEM = 56 * 1024 * 1024
SMALL = pl.CostEstimate(flops=1, bytes_accessed=1, transcendentals=0)


def kernel_params(limit=VMEM_LIMIT):
    return pltpu.CompilerParams(dimension_semantics=("arbitrary",), vmem_limit_bytes=limit)


def attention_kernel(windows, edges, *refs, q_count, columns_only, group):
    q_refs = refs[:q_count]
    kv_ref, top_ref, bottom_ref = refs[q_count : q_count + 3]
    refs = refs[q_count + 3 :]
    out_refs, stat_refs = refs[:q_count], refs[q_count:]
    frames, tokens, head_size = q_refs[0].shape
    span = top_ref.shape[2]
    tiles = tokens // span
    step = pl.program_id(0)
    head = jnp.minimum(step, group - 1)
    radius_row = windows[head, 0]
    radius_col = windows[head, 1]
    scale = 1.0 / math.sqrt(HD)

    @pl.when(step == 0)
    def _():
        for stat_ref in stat_refs:
            stat_ref[...] = jnp.zeros_like(stat_ref)

    def near(which, tile, wide):
        if not wide:
            return kv_ref[which, :, tile * span : (tile + 1) * span, :].reshape(-1, head_size)
        pieces = []
        if tile == 0:
            pieces.append(top_ref[which])
        low = max(tile - 1, 0) * span
        high = min(tile + 2, tiles) * span
        pieces.append(kv_ref[which, :, low:high, :])
        if tile == tiles - 1:
            pieces.append(bottom_ref[which])
        block = pieces[0] if len(pieces) == 1 else jnp.concatenate(pieces, axis=1)
        return block.reshape(-1, head_size)

    def attend(wide):
        lane = lax.broadcasted_iota(jnp.int32, (frames, span, LANES), 2)
        for tile in range(tiles):
            rows = slice(tile * span, (tile + 1) * span)
            keys = near(0, tile, wide)
            values = near(1, tile, wide)
            bias = None
            if wide and (tile == 0 or tile == tiles - 1):
                place = lax.rem(
                    lax.broadcasted_iota(jnp.int32, (1, keys.shape[0]), 1), 3 * span
                )
                low = jnp.where(edges[0] == 0, span, 0) if tile == 0 else 0
                high = jnp.where(edges[1] == 0, 2 * span, 3 * span) if tile == tiles - 1 else 3 * span
                bias = jnp.where((place >= low) & (place < high), 0.0, -jnp.inf)
            for q_ref, out_ref, stat_ref in zip(q_refs, out_refs, stat_refs):
                query = q_ref[:, rows, :].reshape(-1, head_size)
                scores = (
                    lax.dot_general(
                        query, keys, (((1,), (1,)), ((), ())), preferred_element_type=jnp.float32
                    )
                    * scale
                )
                if bias is not None:
                    scores = scores + bias
                highest = jnp.max(scores, axis=1, keepdims=True)
                expo = jnp.exp(scores - highest)
                total = jnp.sum(expo, axis=1, keepdims=True)
                output = jnp.dot(
                    expo.astype(jnp.bfloat16), values, preferred_element_type=jnp.float32
                ) * (1.0 / total)
                out_ref[:, rows, :] = output.astype(jnp.bfloat16).reshape(frames, span, head_size)
                level = (highest + jnp.log(total)).reshape(frames, span, 1)
                stat_ref[:, rows, :] = jnp.where(lane == step, level, stat_ref[:, rows, :])

    active = step < group
    if columns_only:

        @pl.when(active & (radius_col == 0))
        def _():
            for out_ref in out_refs:
                out_ref[...] = jnp.zeros_like(out_ref)

        active = active & (radius_col != 0)

    @pl.when(active & (radius_row == 0))
    def _():
        attend(False)

    @pl.when(active & (radius_row != 0))
    def _():
        attend(True)

    @pl.when(step == group)
    def _():
        for out_ref, stat_ref in zip(out_refs, stat_refs):
            level = stat_ref[...]
            high = level.astype(jnp.bfloat16).astype(jnp.float32)
            middle = (level - high).astype(jnp.bfloat16).astype(jnp.float32)
            low = level - high - middle
            packed = high + pltpu.roll(middle, LEVEL_STEP, 2) + pltpu.roll(low, 2 * LEVEL_STEP, 2)
            out_ref[...] = packed.astype(jnp.bfloat16)


def attention(windows, edges, query_blocks, keys_values, top, bottom, columns_only):
    frames, tokens, features = query_blocks[0].shape
    group = windows.shape[0]
    head_size = features // group
    span = top.shape[2]
    q_count = len(query_blocks)

    def head_of(step):
        return jnp.minimum(step, group - 1)

    q_spec = pl.BlockSpec((frames, tokens, head_size), lambda h, *_: (0, 0, head_of(h)))
    kv_spec = pl.BlockSpec((2, frames, tokens, head_size), lambda h, *_: (0, 0, 0, head_of(h)))
    halo_spec = pl.BlockSpec((2, frames, span, head_size), lambda h, *_: (0, 0, 0, head_of(h)))
    out_spec = pl.BlockSpec((frames, tokens, head_size), lambda h, *_: (0, 0, h))
    return pl.pallas_call(
        partial(attention_kernel, q_count=q_count, columns_only=columns_only, group=group),
        grid_spec=pltpu.PrefetchScalarGridSpec(
            num_scalar_prefetch=2,
            grid=(group + 1,),
            in_specs=[q_spec] * q_count + [kv_spec, halo_spec, halo_spec],
            out_specs=[out_spec] * q_count,
            scratch_shapes=[pltpu.VMEM((frames, tokens, LANES), jnp.float32)] * q_count,
        ),
        out_shape=[jax.ShapeDtypeStruct((frames, tokens, (group + 1) * head_size), jnp.bfloat16)]
        * q_count,
        compiler_params=kernel_params(),
        cost_estimate=SMALL,
        name="attend_neighbours" if columns_only else "attend_own",
    )(windows, edges, *query_blocks, keys_values, top, bottom)


def combine_kernel(windows, edges, own, left, right, own_stat, left_stat, right_stat, out, *, heads):
    first = pl.program_id(0) * heads
    frames, tokens, width = own.shape
    head_size = width // heads

    for index in range(heads):
        head = first + index
        columns = slice(index * head_size, (index + 1) * head_size)
        radius_col = windows[head, 1]

        @pl.when(radius_col == 0)
        def _(columns=columns):
            out[:, :, columns] = own[:, :, columns]

        @pl.when(radius_col != 0)
        def _(columns=columns, head=head):
            lane = lax.broadcasted_iota(jnp.int32, (LANES, head_size), 0)
            pick = jnp.where(
                (lax.rem(lane, LEVEL_STEP) == head) & (lane < 3 * LEVEL_STEP), 1.0, 0.0
            ).astype(jnp.bfloat16)

            def level(ref):
                return jnp.dot(
                    ref[...].reshape(-1, LANES), pick, preferred_element_type=jnp.float32
                ).reshape(frames, tokens, head_size)

            own_level = level(own_stat)
            left_level = jnp.where(edges[2] == 0, -jnp.inf, level(left_stat))
            right_level = jnp.where(edges[3] == 0, -jnp.inf, level(right_stat))
            highest = jnp.maximum(own_level, jnp.maximum(left_level, right_level))
            weights = [jnp.exp(x - highest) for x in (own_level, left_level, right_level)]
            mixed = sum(
                ref[:, :, columns].astype(jnp.float32) * weight
                for ref, weight in zip((own, left, right), weights)
            )
            out[:, :, columns] = (mixed / (weights[0] + weights[1] + weights[2])).astype(
                jnp.bfloat16
            )


def combine(windows, edges, outputs, features, order):
    frames, tokens, _ = outputs[0].shape
    head_count = windows.shape[0]
    heads = head_count // order
    width = features // order
    spec = pl.BlockSpec((frames, tokens, width), lambda h, *_: (0, 0, h))
    stat_spec = pl.BlockSpec(
        (frames, tokens, features // head_count), lambda h, *_: (0, 0, head_count)
    )
    return pl.pallas_call(
        partial(combine_kernel, heads=heads),
        grid_spec=pltpu.PrefetchScalarGridSpec(
            num_scalar_prefetch=2,
            grid=(order,),
            in_specs=[spec] * 3 + [stat_spec] * 3,
            out_specs=pl.BlockSpec(
                (frames, tokens, width), lambda h, windows, edges: (0, 0, h ^ edges[4])
            ),
        ),
        out_shape=jax.ShapeDtypeStruct((frames, tokens, features), jnp.bfloat16),
        compiler_params=kernel_params(),
        cost_estimate=SMALL,
        name="combine",
    )(windows, edges, *outputs, *outputs)


def project_kernel(place, attended, *refs, slots, carried, start, column):
    arrays = 1 + max(piece[0] for slot in slots for piece in slot)
    pieces, refs = refs[:arrays], refs[arrays:]
    if carried:
        carry, refs = refs[0], refs[1:]
    out, rows, weight, rows_sem, weight_sem = refs
    columns = weight.shape[1]
    depth = weight.shape[2]
    rows_copy = pltpu.make_async_copy(
        attended.at[:, start : start + depth], rows, rows_sem.at[0]
    )
    rows_copy.start()
    for index, slot in enumerate(slots):
        for block in range(columns):
            low = 0
            for number, (array, size, share, turned) in enumerate(slot):
                first = pl.multiple_of((place[0] ^ share if turned else share) * size, size)
                pltpu.make_async_copy(
                    pieces[array].at[pl.ds(first, size), block * column : (block + 1) * column],
                    weight.at[index, block, low : low + size],
                    weight_sem.at[index, block, number],
                ).start()
                low += size
    rows_copy.wait()
    for index, slot in enumerate(slots):

        def body(block, _, index=index, slot=slot):
            low = 0
            for number, (_, size, _, _) in enumerate(slot):
                piece = weight.at[index, block, low : low + size]
                pltpu.make_async_copy(piece, piece, weight_sem.at[index, block, number]).wait()
                low += size
            total = jnp.dot(rows[...], weight[index, block], preferred_element_type=jnp.float32)
            here = pl.ds(pl.multiple_of(block * column, column), column)
            if carried:
                total = total + carry[index, :, here]
            out[index, :, here] = total.astype(out.dtype)
            return 0

        lax.fori_loop(0, columns, body, 0)


def project(place, attended, arrays, slots, carry, start, dtype):
    tokens = attended.shape[0]
    width = arrays[0].shape[1]
    column = 256 if width % 256 == 0 else width
    columns = width // column
    depth = sum(piece[1] for piece in slots[0])
    anywhere = pl.BlockSpec(memory_space=pl.ANY)
    inside = pl.BlockSpec(memory_space=pltpu.VMEM)
    return pl.pallas_call(
        partial(
            project_kernel, slots=slots, carried=carry is not None, start=start, column=column
        ),
        in_specs=[pl.BlockSpec(memory_space=pltpu.SMEM), anywhere]
        + [anywhere] * len(arrays)
        + ([] if carry is None else [inside]),
        out_specs=inside,
        out_shape=jax.ShapeDtypeStruct((len(slots), tokens, width), dtype),
        scratch_shapes=[
            pltpu.VMEM((tokens, depth), attended.dtype),
            pltpu.VMEM((len(slots), columns, depth, column), attended.dtype),
            pltpu.SemaphoreType.DMA((1,)),
            pltpu.SemaphoreType.DMA((len(slots), columns, max(len(slot) for slot in slots))),
        ],
        compiler_params=pltpu.CompilerParams(vmem_limit_bytes=VMEM_LIMIT),
        cost_estimate=SMALL,
        name="project",
    )(place, attended, *arrays, *([] if carry is None else [carry]))


def mix_kernel(
    place, own_part, other_part, own_hidden, other_hidden, own_gate, other_gate, *refs
):
    mixed_ref, sums_ref = refs[-2:]
    step = pl.program_id(0)
    mine = place[3 * step] != 0
    hidden = jnp.where(
        mine, own_hidden[...].astype(jnp.float32), other_hidden[...].astype(jnp.float32)
    )
    gate = jnp.where(mine, own_gate[...], other_gate[...])
    mixed = hidden + gate * (
        own_part[0].astype(jnp.float32) + other_part[0].astype(jnp.float32)
    )
    mixed_ref[...] = mixed
    lane = lax.broadcasted_iota(jnp.int32, sums_ref.shape, 1)
    first = jnp.sum(mixed, axis=1, keepdims=True)
    second = jnp.sum(mixed * mixed, axis=1, keepdims=True)
    sums = jnp.where(lane == 0, first, jnp.where(lane == 1, second, 0.0))

    @pl.when(step == 0)
    def _():
        sums_ref[...] = sums + refs[0][...] if len(refs) == 4 else sums

    @pl.when(step != 0)
    def _():
        sums_ref[...] = sums_ref[...] + sums


def mix(place, own_part, other_part, own_hidden, other_hidden, own_gate, other_gate, carry):
    count, tokens, width = own_part.shape
    blocks = own_hidden.shape[1] // width
    part = pl.BlockSpec((1, tokens, width), lambda i, place: (i, 0, 0))
    hidden = pl.BlockSpec((tokens, width), lambda i, place: (0, place[3 * i + 1]))
    gate = pl.BlockSpec((1, width), lambda i, place: (0, place[3 * i + 1]))
    sums = pl.BlockSpec((tokens, LANES), lambda i, place: (0, 0))
    mixed = pl.BlockSpec((tokens, width), lambda i, place: (0, place[3 * i + 2]))
    return pl.pallas_call(
        mix_kernel,
        grid_spec=pltpu.PrefetchScalarGridSpec(
            num_scalar_prefetch=1,
            grid=(count,),
            in_specs=[part, part, hidden, hidden, gate, gate]
            + ([sums, pl.BlockSpec(memory_space=pl.ANY)] if carry else []),
            out_specs=[mixed, sums],
        ),
        out_shape=[
            jax.ShapeDtypeStruct((tokens, (blocks + 1) * width), jnp.float32),
            jax.ShapeDtypeStruct((tokens, LANES), jnp.float32),
        ],
        input_output_aliases={8: 0} if carry else {},
        compiler_params=kernel_params(MOST_VMEM),
        cost_estimate=SMALL,
        name="mix",
    )(
        *(place, own_part, other_part, own_hidden, other_hidden, own_gate, other_gate),
        *((carry[1], carry[0]) if carry else ()),
    )


def finish_kernel(place, own_part, other_part, *refs):
    count, _, width = own_part.shape
    sides, refs = refs[: 4 * count], refs[4 * count :]
    scale, shift_by, sums, mixed_ref, residual, ffn = refs
    blocks = residual.shape[1] // width
    first = sums[:, 0:1]
    second = sums[:, 1:2]
    late = []
    for index in range(count):
        own_hidden, other_hidden, own_gate, other_gate = sides[4 * index : 4 * index + 4]
        mine = place[3 * index] != 0
        hidden = jnp.where(
            mine, own_hidden[...].astype(jnp.float32), other_hidden[...].astype(jnp.float32)
        )
        gate = jnp.where(mine, own_gate[...], other_gate[...])
        mixed = hidden + gate * (
            own_part[index].astype(jnp.float32) + other_part[index].astype(jnp.float32)
        )
        first = first + jnp.sum(mixed, axis=1, keepdims=True)
        second = second + jnp.sum(mixed * mixed, axis=1, keepdims=True)
        late.append(mixed)
    average = first / D
    variance = second / D - average * average
    inverse = lax.rsqrt(variance + EPSILON)
    for block in range(blocks):
        columns = slice(block * width, (block + 1) * width)
        mixed = mixed_ref[:, columns]
        for index in range(count):
            here = (place[3 * index] != 0) & (place[3 * index + 1] == block)
            mixed = jnp.where(here, late[index], mixed)
        residual[:, columns] = mixed.astype(jnp.bfloat16)
        ffn[:, columns] = (
            (mixed - average) * inverse * (1.0 + scale[:, columns]) + shift_by[:, columns]
        ).astype(jnp.bfloat16)


def finish(place, own_part, other_part, own_hidden, other_hidden, own_gate, other_gate, scale, shift_by, carry):
    count, tokens, width = own_part.shape
    features = own_hidden.shape[1]
    rows = 64 if tokens % 64 == 0 else tokens
    part = pl.BlockSpec((count, rows, width), lambda i, place: (0, i, 0))
    whole = pl.BlockSpec((1, features), lambda i, place: (0, 0))
    sums = pl.BlockSpec((rows, LANES), lambda i, place: (i, 0))
    row = pl.BlockSpec((rows, features), lambda i, place: (i, 0))
    side_specs = []
    for index in range(count):
        hidden = pl.BlockSpec(
            (rows, width), lambda i, place, index=index: (i, place[3 * index + 1])
        )
        gate = pl.BlockSpec((1, width), lambda i, place, index=index: (0, place[3 * index + 1]))
        side_specs += [hidden, hidden, gate, gate]
    return pl.pallas_call(
        finish_kernel,
        grid_spec=pltpu.PrefetchScalarGridSpec(
            num_scalar_prefetch=1,
            grid=(tokens // rows,),
            in_specs=[part, part, *side_specs, whole, whole, sums, row],
            out_specs=[row, row],
        ),
        out_shape=[jax.ShapeDtypeStruct((tokens, features), jnp.bfloat16)] * 2,
        compiler_params=kernel_params(MOST_VMEM),
        cost_estimate=SMALL,
        name="finish",
    )(
        place, own_part, other_part,
        *((own_hidden, other_hidden, own_gate, other_gate) * count),
        scale, shift_by, carry[1], carry[0],
    )


def shift(block, axis, step):
    count = lax.axis_size(axis)
    pairs = [(i, i + step) for i in range(count) if 0 <= i + step < count]
    return lax.ppermute(block, axis, pairs)


def turn(block, axis, step):
    count = lax.axis_size(axis)
    return lax.ppermute(block, axis, [(i, (i + step) % count) for i in range(count)])


def swap(block, axis, bit):
    count = lax.axis_size(axis)
    return lax.ppermute(block, axis, [(i, i ^ bit) for i in range(count)])


class Tokens:
    def __init__(self, queries, keys_values, windows, order):
        self.features = queries.shape[3]
        n_ha, n_wa = lax.axis_size("ha"), lax.axis_size("wa")
        ha, wa = lax.axis_index("ha"), lax.axis_index("wa")
        turned = ha if order > 1 else 0 * ha
        self.edges = jnp.stack([ha > 0, ha < n_ha - 1, wa > 0, wa < n_wa - 1, turned]).astype(
            jnp.int32
        )
        self.windows = windows
        self.order = order
        self.queries = self.flat(queries)
        self.keys_values = self.flat(keys_values)

    def flat(self, block):
        return block.reshape(block.shape[:-3] + (-1, self.features))

    def attend(self, query_blocks, halos, columns_only):
        return attention(
            self.windows, self.edges, query_blocks, self.keys_values, *halos, columns_only
        )

    def combine(self, near, back):
        attended = combine(
            self.windows, self.edges, [near, *back], self.features, self.order
        )
        return attended.reshape(-1, self.features)


def edge_rows(keys_values):
    rows = keys_values.shape[2]
    return lax.optimization_barrier(
        (keys_values[:, :, rows - TILE :], keys_values[:, :, :TILE])
    )


def together(*blocks):
    return lax.optimization_barrier(blocks)


def paired(hidden, queries, keys_values, windows, out_weight, picked):
    ha, wa, ta = lax.axis_index("ha"), lax.axis_index("wa"), lax.axis_index("ta")
    n_wa = lax.axis_size("wa")
    blocks = n_wa // 2
    depth = out_weight.shape[0] // 4
    width = out_weight.shape[1]
    cut = depth // 2

    share = lax.optimization_barrier(lax.dynamic_slice_in_dim(out_weight, ha * depth, depth, 0))
    first = turn(share, "wa", 1)
    last_rows, first_rows = edge_rows(keys_values)
    tokens = Tokens(queries, keys_values, windows, 4)
    top = shift(last_rows, "ha", 1)
    bottom = shift(first_rows, "ha", -1)
    from_left = shift(queries, "wa", 1)
    from_right = shift(queries, "wa", -1)

    first, top, bottom = together(first, top, bottom)
    first_x = swap(first, "ha", 1)
    first_y = swap(first, "ha", 2)
    second = turn(first, "wa", 1)
    halos = tokens.flat(top), tokens.flat(bottom)
    (near,) = tokens.attend([tokens.queries], halos, False)

    near, first_x, first_y, from_left, from_right = together(
        near, first_x, first_y, from_left, from_right
    )
    first_far_x = swap(first_y[:cut], "ha", 1)
    first_far_y = swap(first_x[cut:], "ha", 2)

    first_far_x, first_far_y, second, from_left, from_right = together(
        first_far_x, first_far_y, second, from_left, from_right
    )
    third = turn(second, "wa", 1)
    second_x = swap(second, "ha", 1)
    second_y = swap(second, "ha", 2)
    for_left, for_right = tokens.attend(
        [tokens.flat(from_left), tokens.flat(from_right)], halos, True
    )

    for_left, for_right, first_far_x = together(for_left, for_right, first_far_x)
    left = shift(for_right, "wa", 1)
    right = shift(for_left, "wa", -1)

    third, second_x, second_y, first_far_x, hidden, gate = together(
        third, second_x, second_y, first_far_x, hidden, picked[0:1]
    )
    third_x = swap(third, "ha", 1)
    third_y = swap(third, "ha", 2)
    other_hidden = swap(hidden, "ta", 1)

    third_x, third_y, second_x, other_hidden = together(third_x, third_y, second_x, other_hidden)
    third_far = swap(third_y, "ha", 1)
    second_far = swap(second_x, "ha", 2)

    left, right, third_x, gate = together(left, right, third_x, gate)
    other_gate = swap(gate, "ta", 1)
    attended = tokens.combine(near, [left, right])

    place = ha.reshape(1)
    sums = project(
        place,
        attended,
        [out_weight, first, first_x, first_y, first_far_x, first_far_y],
        [
            [(0, depth, number, True) for number in range(4)],
            [(number, depth, 0, False) for number in range(1, 4)]
            + [(4, cut, 0, False), (5, depth - cut, 0, False)],
        ],
        None,
        0,
        jnp.bfloat16,
    )
    other_sums = [swap(sums[:1], "ta", 1), swap(sums[1:], "ta", 1)]
    late = project(
        place,
        attended,
        [second, second_x, second_y, third, third_x, third_y],
        [[(start + number, depth, 0, False) for number in range(3)] for start in (0, 3)],
        None,
        0,
        jnp.float32,
    )

    def placed(distance):
        block = lax.rem(wa - distance + n_wa, n_wa)
        mine = block // blocks == ta
        inner = lax.rem(block, blocks)
        return jnp.stack([mine.astype(jnp.int32), inner, jnp.where(mine, inner, blocks)])

    sides = hidden, other_hidden, gate, other_gate
    carry = None
    for distance in range(2):
        part = sums[distance : distance + 1]
        carry = mix(placed(distance), part, other_sums[distance], *sides, carry)

    second_far, third_far, late, *carry = together(second_far, third_far, late, *carry)
    late = project(
        place,
        attended,
        [second_far, third_far],
        [[(0, depth, 0, False)], [(1, depth, 0, False)]],
        late,
        3 * depth,
        jnp.bfloat16,
    )
    other_late = swap(late, "ta", 1)
    places = jnp.concatenate([placed(2), placed(3)])
    return finish(places, late, other_late, *sides, picked[2:3], picked[1:2], carry)


def gathered(hidden, queries, keys_values, windows, out_weight, picked):
    work = Tokens(queries, keys_values, windows, 1)
    last_rows, first_rows = edge_rows(keys_values)
    halos = work.flat(shift(last_rows, "ha", 1)), work.flat(shift(first_rows, "ha", -1))
    visitors = [work.flat(shift(queries, "wa", 1)), work.flat(shift(queries, "wa", -1))]
    (near,) = work.attend([work.queries], halos, False)
    for_left, for_right = work.attend(visitors, halos, True)
    attended = work.combine(near, [shift(for_right, "wa", 1), shift(for_left, "wa", -1)])
    n_ha, n_wa, n_ta = lax.axis_size("ha"), lax.axis_size("wa"), lax.axis_size("ta")
    ha, ta = lax.axis_index("ha"), lax.axis_index("ta")
    tokens, features = attended.shape
    depth = features // n_ha
    width = out_weight.shape[1]
    share = lax.dynamic_slice_in_dim(out_weight, ha * depth, depth, 0)
    weights = lax.all_gather(share, ("ha", "wa"), axis=0, tiled=False).reshape(
        n_ha, n_wa, depth, width
    )
    partial_sums = jnp.einsum(
        "thk,hwkc->wtc",
        attended.reshape(tokens, n_ha, depth),
        weights,
        preferred_element_type=jnp.float32,
    ).astype(jnp.bfloat16)
    blocks = n_wa // n_ta
    summed = None
    for step in range(n_ta):
        target = lax.rem(ta + step, n_ta)
        piece = lax.dynamic_slice_in_dim(partial_sums, target * blocks, blocks, 0)
        if step:
            piece = turn(piece, "ta", step)
        piece = piece.astype(jnp.float32)
        summed = piece if summed is None else summed + piece
    summed = jnp.transpose(summed, (1, 0, 2)).reshape(tokens, -1)
    mixed = hidden.astype(jnp.float32) + picked[0] * summed
    sum_first, sum_second = lax.psum((jnp.sum(mixed, axis=1), jnp.sum(mixed * mixed, axis=1)), "ta")
    average = (sum_first / D)[:, None]
    variance = (sum_second / D)[:, None] - average * average
    normed = (mixed - average) * lax.rsqrt(variance + EPSILON)
    ffn_input = (normed * (1.0 + picked[2]) + picked[1]).astype(jnp.bfloat16)
    return mixed.astype(jnp.bfloat16), ffn_input


def shards(hidden_states, queries, keys_values, out_weight, mod_table, windows, step_index):
    tokens = math.prod(queries.shape[:3])
    width = hidden_states.shape[3]
    picked = lax.dynamic_index_in_dim(mod_table, step_index[0], 0, keepdims=False)
    sizes = lax.axis_size("ha"), lax.axis_size("wa"), lax.axis_size("ta")
    tuned = sizes == (4, 4, 2) and out_weight.shape[0] % (20 * LANES) == 0
    residual_out, ffn_input = (paired if tuned else gathered)(
        hidden_states.reshape(tokens, width), queries, keys_values, windows, out_weight, picked
    )
    return residual_out.reshape(hidden_states.shape), ffn_input.reshape(hidden_states.shape)


def solution(mesh):
    return jax.shard_map(
        shards,
        mesh=mesh,
        in_specs=(
            P(None, "ha", "wa", "ta"),
            P(None, "ha", "wa", "ta"),
            P(None, None, "ha", "wa", "ta"),
            P("ta", "wa"),
            P(None, None, "ta"),
            P("ta", None),
            P(),
        ),
        out_specs=(P(None, "ha", "wa", "ta"), P(None, "ha", "wa", "ta")),
        check_vma=False,
    )
```

```python
from functools import partial
import math

import jax
import jax.numpy as jnp
from jax import lax
from jax.experimental import pallas as pl
from jax.experimental.pallas import tpu as pltpu
from jax.sharding import PartitionSpec as P

D = 5120
HD = 128
TILE = 8
LANES = 128
LEVEL_STEP = 32

EPSILON = 1e-06
VMEM_LIMIT = 32 * 1024 * 1024
MOST_VMEM = 56 * 1024 * 1024
SMALL = pl.CostEstimate(flops=1, bytes_accessed=1, transcendentals=0)


def kernel_params(limit=VMEM_LIMIT):
    return pltpu.CompilerParams(dimension_semantics=("arbitrary",), vmem_limit_bytes=limit)


class Plan:
    def __init__(self, windows, order):
        heads = windows.shape[0]
        self.heads = heads
        self.most = max(heads * 7 // 10, 1)
        self.order = order
        n_ha, n_wa = lax.axis_size("ha"), lax.axis_size("wa")
        ha, wa = lax.axis_index("ha"), lax.axis_index("wa")
        number = lax.broadcasted_iota(jnp.int32, (2, heads, heads), 1)
        other = lax.broadcasted_iota(jnp.int32, (2, heads, heads), 2)
        idle = jnp.where(windows.T > 0, 0, 1)
        before = (idle[:, None, :] < idle[:, :, None]) | (
            (idle[:, None, :] == idle[:, :, None]) & (other < number)
        )
        position = jnp.sum(before.astype(jnp.int32), axis=2)
        sorted_heads = jnp.sum(jnp.where(position[:, None, :] == number, other, 0), axis=2)
        turned = ha if order > 1 else 0 * ha
        edges = jnp.stack([ha > 0, ha < n_ha - 1, wa > 0, wa < n_wa - 1, turned]).astype(jnp.int32)
        self.vector = jnp.concatenate(
            [windows.T.reshape(-1), position.reshape(-1), sorted_heads.reshape(-1), edges]
        )
        counts = lax.pmax(jnp.sum(1.0 - idle, axis=1), "ta")
        self.more_rows = counts[0] > self.most
        self.more_cols = counts[1] > self.most

    def row_radius(self, vector, head):
        return vector[head]

    def col_radius(self, vector, head):
        return vector[self.heads + head]

    def row_position(self, vector, head):
        return vector[2 * self.heads + head]

    def col_position(self, vector, head):
        return vector[3 * self.heads + head]

    def row_head(self, vector, position):
        return vector[4 * self.heads + position]

    def col_head(self, vector, position):
        return vector[5 * self.heads + position]

    def edge(self, vector, number):
        return vector[6 * self.heads + number]


def pack_kernel(vector, source, *refs, head_of, first, rows):
    outs, sem = refs[:-1], refs[-1]
    copies = []
    for number, (out, (low, size)) in enumerate(zip(outs, rows)):
        for slot in range(out.shape[-1] // HD):
            start = pl.multiple_of(head_of(vector, first + slot) * HD, HD)
            lead = (slice(None),) * (len(source.shape) - 2)
            copies.append(
                pltpu.make_async_copy(
                    source.at[(*lead, pl.ds(low, size), pl.ds(start, HD))],
                    out.at[(*lead, slice(None), pl.ds(slot * HD, HD))],
                    sem.at[number, slot],
                )
            )
    for copy in copies:
        copy.start()
    for copy in copies:
        copy.wait()


def pack(vector, source, head_of, first, count, rows):
    anywhere = pl.BlockSpec(memory_space=pl.ANY)
    return pl.pallas_call(
        partial(pack_kernel, head_of=head_of, first=first, rows=rows),
        in_specs=[pl.BlockSpec(memory_space=pltpu.SMEM), anywhere],
        out_specs=[anywhere] * len(rows),
        out_shape=[
            jax.ShapeDtypeStruct((*source.shape[:-2], size, count * HD), source.dtype)
            for _, size in rows
        ],
        scratch_shapes=[pltpu.SemaphoreType.DMA((len(rows), count))],
        compiler_params=pltpu.CompilerParams(vmem_limit_bytes=VMEM_LIMIT),
        cost_estimate=SMALL,
        name="pack",
    )(vector, source)


def attention_kernel(vector, *refs, plan, head_of, q_count, visiting, group):
    q_refs = refs[:q_count]
    kv_ref, top_ref, bottom_ref, top_rest, bottom_rest = refs[q_count : q_count + 5]
    refs = refs[q_count + 5 :]
    out_refs, stat_refs, halo = refs[:q_count], refs[q_count : 2 * q_count], refs[2 * q_count]
    frames, tokens, head_size = q_refs[0].shape
    span = top_ref.shape[2]
    tiles = tokens // span
    step = pl.program_id(0)
    head = head_of(vector, step)
    radius_row = plan.row_radius(vector, head)
    radius_col = plan.col_radius(vector, head)
    scale = 1.0 / math.sqrt(HD)

    @pl.when(step == 0)
    def _():
        for stat_ref in stat_refs:
            stat_ref[...] = jnp.zeros_like(stat_ref)

    def near(which, tile, wide):
        if not wide:
            return kv_ref[which, :, tile * span : (tile + 1) * span, :].reshape(-1, head_size)
        pieces = []
        if tile == 0:
            pieces.append(halo[0, which])
        low = max(tile - 1, 0) * span
        high = min(tile + 2, tiles) * span
        pieces.append(kv_ref[which, :, low:high, :])
        if tile == tiles - 1:
            pieces.append(halo[1, which])
        block = pieces[0] if len(pieces) == 1 else jnp.concatenate(pieces, axis=1)
        return block.reshape(-1, head_size)

    def attend(wide):
        lane = lax.broadcasted_iota(jnp.int32, (frames, span, LANES), 2)
        for tile in range(tiles):
            rows = slice(tile * span, (tile + 1) * span)
            keys = near(0, tile, wide)
            values = near(1, tile, wide)
            bias = None
            if wide and (tile == 0 or tile == tiles - 1):
                place = lax.rem(
                    lax.broadcasted_iota(jnp.int32, (1, keys.shape[0]), 1), 3 * span
                )
                low, high = 0, 3 * span
                if tile == 0:
                    low = jnp.where(plan.edge(vector, 0) == 0, span, 0)
                if tile == tiles - 1:
                    high = jnp.where(plan.edge(vector, 1) == 0, 2 * span, 3 * span)
                bias = jnp.where((place >= low) & (place < high), 0.0, -jnp.inf)
            for q_ref, out_ref, stat_ref in zip(q_refs, out_refs, stat_refs):
                query = q_ref[:, rows, :].reshape(-1, head_size)
                scores = (
                    lax.dot_general(
                        query, keys, (((1,), (1,)), ((), ())), preferred_element_type=jnp.float32
                    )
                    * scale
                )
                if bias is not None:
                    scores = scores + bias
                highest = jnp.max(scores, axis=1, keepdims=True)
                expo = jnp.exp(scores - highest)
                total = jnp.sum(expo, axis=1, keepdims=True)
                output = jnp.dot(
                    expo.astype(jnp.bfloat16), values, preferred_element_type=jnp.float32
                ) * (1.0 / total)
                out_ref[:, rows, :] = output.astype(jnp.bfloat16).reshape(frames, span, head_size)
                level = (highest + jnp.log(total)).reshape(frames, span, 1)
                stat_ref[:, rows, :] = jnp.where(lane == step, level, stat_ref[:, rows, :])

    active = step < group
    if visiting:

        @pl.when(active & (radius_col == 0))
        def _():
            for out_ref in out_refs:
                out_ref[...] = jnp.zeros_like(out_ref)

        active = active & (radius_col != 0)

    @pl.when(active & (radius_row == 0))
    def _():
        attend(False)

    always = plan.row_position(vector, head) < plan.most

    @pl.when(active & (radius_row != 0) & always)
    def _():
        halo[0] = top_ref[...]
        halo[1] = bottom_ref[...]

    @pl.when(active & (radius_row != 0) & jnp.logical_not(always))
    def _():
        halo[0] = top_rest[...]
        halo[1] = bottom_rest[...]

    @pl.when(active & (radius_row != 0))
    def _():
        attend(True)

    @pl.when(step == group)
    def _():
        for out_ref, stat_ref in zip(out_refs, stat_refs):
            level = stat_ref[...]
            high = level.astype(jnp.bfloat16).astype(jnp.float32)
            middle = (level - high).astype(jnp.bfloat16).astype(jnp.float32)
            low = level - high - middle
            packed = high + pltpu.roll(middle, LEVEL_STEP, 2) + pltpu.roll(low, 2 * LEVEL_STEP, 2)
            out_ref[...] = packed.astype(jnp.bfloat16)


def attention(plan, vector, query_blocks, keys_values, halos, first=None):
    frames, tokens, features = query_blocks[0].shape
    group = features // HD
    span = halos[0].shape[2]
    q_count = len(query_blocks)
    visiting = first is not None

    def slot_of(step):
        return jnp.minimum(step, group - 1)

    def head_of(vector, step):
        return plan.col_head(vector, first + slot_of(step)) if visiting else slot_of(step)

    def kv_index(step, vector):
        return 0, 0, 0, head_of(vector, step)

    def halo_index(step, vector):
        position = plan.row_position(vector, head_of(vector, step))
        return 0, 0, 0, jnp.minimum(position, plan.most - 1)

    def rest_index(step, vector):
        position = plan.row_position(vector, head_of(vector, step))
        return 0, 0, 0, jnp.maximum(position - plan.most, 0)

    q_spec = pl.BlockSpec((frames, tokens, HD), lambda step, _: (0, 0, slot_of(step)))
    kv_spec = pl.BlockSpec((2, frames, tokens, HD), kv_index)
    halo_spec = pl.BlockSpec((2, frames, span, HD), halo_index)
    rest_spec = pl.BlockSpec((2, frames, span, HD), rest_index)
    out_spec = pl.BlockSpec((frames, tokens, HD), lambda step, _: (0, 0, step))
    return pl.pallas_call(
        partial(
            attention_kernel,
            plan=plan,
            head_of=head_of,
            q_count=q_count,
            visiting=visiting,
            group=group,
        ),
        grid_spec=pltpu.PrefetchScalarGridSpec(
            num_scalar_prefetch=1,
            grid=(group + 1,),
            in_specs=[q_spec] * q_count + [kv_spec] + [halo_spec] * 2 + [rest_spec] * 2,
            out_specs=[out_spec] * q_count,
            scratch_shapes=[pltpu.VMEM((frames, tokens, LANES), jnp.float32)] * q_count
            + [pltpu.VMEM((2, 2, frames, span, HD), jnp.bfloat16)],
        ),
        out_shape=[jax.ShapeDtypeStruct((frames, tokens, (group + 1) * HD), jnp.bfloat16)]
        * q_count,
        compiler_params=kernel_params(),
        cost_estimate=SMALL,
        name="attend_visitors" if visiting else "attend_own",
    )(vector, *query_blocks, keys_values, *halos)


def combine_kernel(vector, own, own_stat, left, right, left_rest, right_rest, out, *, plan, heads):
    first = pl.program_id(0) * heads
    frames, tokens, _ = own.shape

    def level(stat, number):
        lane = lax.broadcasted_iota(jnp.int32, (LANES, HD), 0)
        pick = jnp.where(
            (lax.rem(lane, LEVEL_STEP) == number) & (lane < 3 * LEVEL_STEP), 1.0, 0.0
        ).astype(jnp.bfloat16)
        return jnp.dot(
            stat.reshape(-1, LANES), pick, preferred_element_type=jnp.float32
        ).reshape(frames, tokens, HD)

    for index in range(heads):
        head = first + index
        columns = slice(index * HD, (index + 1) * HD)
        across = plan.col_radius(vector, head) != 0
        position = plan.col_position(vector, head)

        @pl.when(jnp.logical_not(across))
        def _(columns=columns):
            out[:, :, columns] = own[:, :, columns]

        def join(sides, slot, columns, head):
            here = pl.ds(pl.multiple_of(slot * HD, HD), HD)
            levels = [level(own_stat[...], head)]
            values = [own[:, :, columns]]
            for number, side in enumerate(sides):
                value = level(side[:, :, side.shape[2] - LANES :], slot)
                levels.append(jnp.where(plan.edge(vector, 2 + number) == 0, -jnp.inf, value))
                values.append(side[:, :, here])
            highest = jnp.maximum(levels[0], jnp.maximum(levels[1], levels[2]))
            weights = [jnp.exp(x - highest) for x in levels]
            mixed = sum(value.astype(jnp.float32) * weight for value, weight in zip(values, weights))
            out[:, :, columns] = (mixed / (weights[0] + weights[1] + weights[2])).astype(
                jnp.bfloat16
            )

        @pl.when(across & (position < plan.most))
        def _(position=position, columns=columns, head=head):
            join((left, right), position, columns, head)

        @pl.when(across & (position >= plan.most))
        def _(position=position, columns=columns, head=head):
            join((left_rest, right_rest), position - plan.most, columns, head)


def combine(plan, vector, near, sides):
    frames, tokens, _ = near.shape
    heads = plan.heads // plan.order
    spec = pl.BlockSpec((frames, tokens, heads * HD), lambda h, _: (0, 0, h))
    stat_spec = pl.BlockSpec((frames, tokens, HD), lambda h, _: (0, 0, plan.heads))
    return pl.pallas_call(
        partial(combine_kernel, plan=plan, heads=heads),
        grid_spec=pltpu.PrefetchScalarGridSpec(
            num_scalar_prefetch=1,
            grid=(plan.order,),
            in_specs=[spec, stat_spec]
            + [pl.BlockSpec(side.shape, lambda h, _: (0, 0, 0)) for side in sides],
            out_specs=pl.BlockSpec(
                (frames, tokens, heads * HD), lambda h, vector: (0, 0, h ^ plan.edge(vector, 4))
            ),
        ),
        out_shape=jax.ShapeDtypeStruct((frames, tokens, plan.heads * HD), jnp.bfloat16),
        compiler_params=kernel_params(),
        cost_estimate=SMALL,
        name="combine",
    )(vector, near, near, *sides)


def project_kernel(place, attended, *refs, slots, carried, start, column):
    arrays = 1 + max(piece[0] for slot in slots for piece in slot)
    pieces, refs = refs[:arrays], refs[arrays:]
    if carried:
        carry, refs = refs[: len(slots)], refs[len(slots) :]
    outs, (rows, weight, rows_sem, weight_sem) = refs[: len(slots)], refs[len(slots) :]
    columns = weight.shape[1]
    depth = weight.shape[2]
    rows_copy = pltpu.make_async_copy(
        attended.at[:, start : start + depth], rows, rows_sem.at[0]
    )
    rows_copy.start()
    for index, slot in enumerate(slots):
        for block in range(columns):
            low = 0
            for number, (array, size, share, turned) in enumerate(slot):
                first = pl.multiple_of((place[0] ^ share if turned else share) * size, size)
                pltpu.make_async_copy(
                    pieces[array].at[pl.ds(first, size), block * column : (block + 1) * column],
                    weight.at[index, block, low : low + size],
                    weight_sem.at[index, block, number],
                ).start()
                low += size
    rows_copy.wait()
    for index, slot in enumerate(slots):

        def body(block, _, index=index, slot=slot):
            low = 0
            for number, (_, size, _, _) in enumerate(slot):
                piece = weight.at[index, block, low : low + size]
                pltpu.make_async_copy(piece, piece, weight_sem.at[index, block, number]).wait()
                low += size
            total = jnp.dot(rows[...], weight[index, block], preferred_element_type=jnp.float32)
            here = pl.ds(pl.multiple_of(block * column, column), column)
            if carried:
                total = total + carry[index][0, :, here]
            outs[index][0, :, here] = total.astype(outs[index].dtype)
            return 0

        lax.fori_loop(0, columns, body, 0)


def project(place, attended, arrays, slots, carry, start, dtype):
    tokens = attended.shape[0]
    width = arrays[0].shape[1]
    column = 256 if width % 256 == 0 else width
    columns = width // column
    depth = sum(piece[1] for piece in slots[0])
    anywhere = pl.BlockSpec(memory_space=pl.ANY)
    inside = pl.BlockSpec(memory_space=pltpu.VMEM)
    return pl.pallas_call(
        partial(
            project_kernel, slots=slots, carried=carry is not None, start=start, column=column
        ),
        in_specs=[pl.BlockSpec(memory_space=pltpu.SMEM), anywhere]
        + [anywhere] * len(arrays)
        + ([] if carry is None else [inside] * len(slots)),
        out_specs=[inside] * len(slots),
        out_shape=[jax.ShapeDtypeStruct((1, tokens, width), dtype)] * len(slots),
        scratch_shapes=[
            pltpu.VMEM((tokens, depth), attended.dtype),
            pltpu.VMEM((len(slots), columns, depth, column), attended.dtype),
            pltpu.SemaphoreType.DMA((1,)),
            pltpu.SemaphoreType.DMA((len(slots), columns, max(len(slot) for slot in slots))),
        ],
        compiler_params=pltpu.CompilerParams(vmem_limit_bytes=VMEM_LIMIT),
        cost_estimate=SMALL,
        name="project",
    )(place, attended, *arrays, *([] if carry is None else carry))


def mix_kernel(
    place, own_part, other_part, own_hidden, other_hidden, own_gate, other_gate, *refs
):
    mixed_ref, sums_ref = refs[-2:]
    step = pl.program_id(0)
    mine = place[3 * step] != 0
    hidden = jnp.where(
        mine, own_hidden[...].astype(jnp.float32), other_hidden[...].astype(jnp.float32)
    )
    gate = jnp.where(mine, own_gate[...], other_gate[...])
    mixed = hidden + gate * (
        own_part[0].astype(jnp.float32) + other_part[0].astype(jnp.float32)
    )
    mixed_ref[...] = mixed
    lane = lax.broadcasted_iota(jnp.int32, sums_ref.shape, 1)
    first = jnp.sum(mixed, axis=1, keepdims=True)
    second = jnp.sum(mixed * mixed, axis=1, keepdims=True)
    sums = jnp.where(lane == 0, first, jnp.where(lane == 1, second, 0.0))

    @pl.when(step == 0)
    def _():
        sums_ref[...] = sums + refs[0][...] if len(refs) == 4 else sums

    @pl.when(step != 0)
    def _():
        sums_ref[...] = sums_ref[...] + sums


def mix(place, own_part, other_part, own_hidden, other_hidden, own_gate, other_gate, carry):
    count, tokens, width = own_part.shape
    blocks = own_hidden.shape[1] // width
    part = pl.BlockSpec((1, tokens, width), lambda i, place: (i, 0, 0))
    hidden = pl.BlockSpec((tokens, width), lambda i, place: (0, place[3 * i + 1]))
    gate = pl.BlockSpec((1, width), lambda i, place: (0, place[3 * i + 1]))
    sums = pl.BlockSpec((tokens, LANES), lambda i, place: (0, 0))
    mixed = pl.BlockSpec((tokens, width), lambda i, place: (0, place[3 * i + 2]))
    return pl.pallas_call(
        mix_kernel,
        grid_spec=pltpu.PrefetchScalarGridSpec(
            num_scalar_prefetch=1,
            grid=(count,),
            in_specs=[part, part, hidden, hidden, gate, gate]
            + ([sums, pl.BlockSpec(memory_space=pl.ANY)] if carry else []),
            out_specs=[mixed, sums],
        ),
        out_shape=[
            jax.ShapeDtypeStruct((tokens, (blocks + 1) * width), jnp.float32),
            jax.ShapeDtypeStruct((tokens, LANES), jnp.float32),
        ],
        input_output_aliases={8: 0} if carry else {},
        compiler_params=kernel_params(MOST_VMEM),
        cost_estimate=SMALL,
        name="mix",
    )(
        *(place, own_part, other_part, own_hidden, other_hidden, own_gate, other_gate),
        *((carry[1], carry[0]) if carry else ()),
    )


def finish_kernel(place, *refs, count):
    own_part, other_part, refs = refs[:count], refs[count : 2 * count], refs[2 * count :]
    width = own_part[0].shape[2]
    sides, refs = refs[: 4 * count], refs[4 * count :]
    scale, shift_by, sums, mixed_ref, residual, ffn = refs
    blocks = residual.shape[1] // width
    first = sums[:, 0:1]
    second = sums[:, 1:2]
    late = []
    for index in range(count):
        own_hidden, other_hidden, own_gate, other_gate = sides[4 * index : 4 * index + 4]
        mine = place[3 * index] != 0
        hidden = jnp.where(
            mine, own_hidden[...].astype(jnp.float32), other_hidden[...].astype(jnp.float32)
        )
        gate = jnp.where(mine, own_gate[...], other_gate[...])
        mixed = hidden + gate * (
            own_part[index][0].astype(jnp.float32) + other_part[index][0].astype(jnp.float32)
        )
        first = first + jnp.sum(mixed, axis=1, keepdims=True)
        second = second + jnp.sum(mixed * mixed, axis=1, keepdims=True)
        late.append(mixed)
    average = first / D
    variance = second / D - average * average
    inverse = lax.rsqrt(variance + EPSILON)
    for block in range(blocks):
        columns = slice(block * width, (block + 1) * width)
        mixed = mixed_ref[:, columns]
        for index in range(count):
            here = (place[3 * index] != 0) & (place[3 * index + 1] == block)
            mixed = jnp.where(here, late[index], mixed)
        residual[:, columns] = mixed.astype(jnp.bfloat16)
        ffn[:, columns] = (
            (mixed - average) * inverse * (1.0 + scale[:, columns]) + shift_by[:, columns]
        ).astype(jnp.bfloat16)


def finish(place, own_part, other_part, own_hidden, other_hidden, own_gate, other_gate, scale, shift_by, carry):
    count = len(own_part)
    _, tokens, width = own_part[0].shape
    features = own_hidden.shape[1]
    rows = 64 if tokens % 64 == 0 else tokens
    part = pl.BlockSpec((1, rows, width), lambda i, place: (0, i, 0))
    whole = pl.BlockSpec((1, features), lambda i, place: (0, 0))
    sums = pl.BlockSpec((rows, LANES), lambda i, place: (i, 0))
    row = pl.BlockSpec((rows, features), lambda i, place: (i, 0))
    side_specs = []
    for index in range(count):
        hidden = pl.BlockSpec(
            (rows, width), lambda i, place, index=index: (i, place[3 * index + 1])
        )
        gate = pl.BlockSpec((1, width), lambda i, place, index=index: (0, place[3 * index + 1]))
        side_specs += [hidden, hidden, gate, gate]
    return pl.pallas_call(
        partial(finish_kernel, count=count),
        grid_spec=pltpu.PrefetchScalarGridSpec(
            num_scalar_prefetch=1,
            grid=(tokens // rows,),
            in_specs=[part] * (2 * count) + [*side_specs, whole, whole, sums, row],
            out_specs=[row, row],
        ),
        out_shape=[jax.ShapeDtypeStruct((tokens, features), jnp.bfloat16)] * 2,
        compiler_params=kernel_params(MOST_VMEM),
        cost_estimate=SMALL,
        name="finish",
    )(
        place, *own_part, *other_part,
        *((own_hidden, other_hidden, own_gate, other_gate) * count),
        scale, shift_by, carry[1], carry[0],
    )


def shift(block, axis, step):
    count = lax.axis_size(axis)
    pairs = [(i, i + step) for i in range(count) if 0 <= i + step < count]
    return lax.ppermute(block, axis, pairs)


def turn(block, axis, step):
    count = lax.axis_size(axis)
    return lax.ppermute(block, axis, [(i, (i + step) % count) for i in range(count)])


def swap(block, axis, bit):
    count = lax.axis_size(axis)
    return lax.ppermute(block, axis, [(i, i ^ bit) for i in range(count)])


class Tokens:
    def __init__(self, queries, keys_values, windows, order):
        self.plan = Plan(windows, order)
        self.queries = queries.reshape(queries.shape[0], -1, queries.shape[3])
        self.keys_values = keys_values.reshape(*keys_values.shape[:2], -1, keys_values.shape[4])
        self.span = TILE * queries.shape[2]
        self.parts = (0, self.plan.most), (self.plan.most, self.plan.heads - self.plan.most)

    def edge_rows(self, vector, part):
        low = self.queries.shape[1] - self.span
        rows = [(low, self.span), (0, self.span)]
        return pack(vector, self.keys_values, self.plan.row_head, *self.parts[part], rows)

    def leaving(self, vector, part):
        rows = [(0, self.queries.shape[1])]
        return pack(vector, self.queries, self.plan.col_head, *self.parts[part], rows)[0]

    def halos(self, rows):
        return shift(rows[0], "ha", 1), shift(rows[1], "ha", -1)

    def rest_halos(self, vector):
        shape = (*self.keys_values.shape[:2], self.span, self.parts[1][1] * HD)
        return lax.cond(
            self.plan.more_rows,
            lambda vector: self.halos(self.edge_rows(vector, 1)),
            lambda vector: (jnp.zeros(shape, jnp.bfloat16),) * 2,
            vector,
        )

    def stay(self, vector, halos):
        return attention(self.plan, vector, [self.queries], self.keys_values, halos)[0]

    def visit(self, vector, visitors, halos, part=0):
        first = self.parts[part][0]
        return attention(self.plan, vector, visitors, self.keys_values, halos, first)

    def rest_sides(self, vector, halos):
        shape = (*self.queries.shape[:2], (self.parts[1][1] + 1) * HD)

        def send(vector, *halos):
            queries = self.leaving(vector, 1)
            visitors = shift(queries, "wa", 1), shift(queries, "wa", -1)
            for_left, for_right = self.visit(vector, visitors, halos, 1)
            return shift(for_right, "wa", 1), shift(for_left, "wa", -1)

        return lax.cond(
            self.plan.more_cols,
            send,
            lambda vector, *halos: (jnp.zeros(shape, jnp.bfloat16),) * 2,
            vector,
            *halos,
        )

    def combine(self, vector, near, sides):
        attended = combine(self.plan, vector, near, sides)
        return attended.reshape(-1, attended.shape[2])


def together(*blocks):
    return lax.optimization_barrier(blocks)


def paired(hidden, queries, keys_values, windows, out_weight, picked):
    ha, wa, ta = lax.axis_index("ha"), lax.axis_index("wa"), lax.axis_index("ta")
    n_wa = lax.axis_size("wa")
    blocks = n_wa // 2
    depth = out_weight.shape[0] // 4
    width = out_weight.shape[1]
    cut = depth // 2

    share = lax.optimization_barrier(lax.dynamic_slice_in_dim(out_weight, ha * depth, depth, 0))
    first = turn(share, "wa", 1)
    tokens = Tokens(queries, keys_values, windows, 4)
    vector = tokens.plan.vector
    top, bottom = tokens.halos(tokens.edge_rows(vector, 0))
    queries = tokens.leaving(vector, 0)
    from_left = shift(queries, "wa", 1)
    from_right = shift(queries, "wa", -1)

    first, top, bottom, vector = together(first, top, bottom, vector)
    first_x = swap(first, "ha", 1)
    first_y = swap(first, "ha", 2)
    second = turn(first, "wa", 1)
    halos = top, bottom, *tokens.rest_halos(vector)
    near = tokens.stay(vector, halos)

    near, first_x, first_y, from_left, from_right = together(
        near, first_x, first_y, from_left, from_right
    )
    first_far_x = swap(first_y[:cut], "ha", 1)
    first_far_y = swap(first_x[cut:], "ha", 2)

    first_far_x, first_far_y, second, from_left, from_right = together(
        first_far_x, first_far_y, second, from_left, from_right
    )
    third = turn(second, "wa", 1)
    second_x = swap(second, "ha", 1)
    second_y = swap(second, "ha", 2)
    for_left, for_right = tokens.visit(vector, (from_left, from_right), halos)

    for_left, for_right, first_far_x = together(for_left, for_right, first_far_x)
    left = shift(for_right, "wa", 1)
    right = shift(for_left, "wa", -1)

    third, second_x, second_y, first_far_x, hidden, gate, vector = together(
        third, second_x, second_y, first_far_x, hidden, picked[0:1], vector
    )
    third_x = swap(third, "ha", 1)
    third_y = swap(third, "ha", 2)
    other_hidden = swap(hidden, "ta", 1)
    rest_sides = tokens.rest_sides(vector, halos)

    third_x, third_y, second_x, other_hidden = together(third_x, third_y, second_x, other_hidden)
    third_far = swap(third_y, "ha", 1)
    second_far = swap(second_x, "ha", 2)

    left, right, third_x, gate = together(left, right, third_x, gate)
    other_gate = swap(gate, "ta", 1)
    attended = tokens.combine(vector, near, [left, right, *rest_sides])

    place = ha.reshape(1)
    sums = project(
        place,
        attended,
        [out_weight, first, first_x, first_y, first_far_x, first_far_y],
        [
            [(0, depth, number, True) for number in range(4)],
            [(number, depth, 0, False) for number in range(1, 4)]
            + [(4, cut, 0, False), (5, depth - cut, 0, False)],
        ],
        None,
        0,
        jnp.bfloat16,
    )
    other_sums = [swap(part, "ta", 1) for part in sums]
    late = project(
        place,
        attended,
        [second, second_x, second_y, third, third_x, third_y],
        [[(start + number, depth, 0, False) for number in range(3)] for start in (0, 3)],
        None,
        0,
        jnp.float32,
    )

    def placed(distance):
        block = lax.rem(wa - distance + n_wa, n_wa)
        mine = block // blocks == ta
        inner = lax.rem(block, blocks)
        return jnp.stack([mine.astype(jnp.int32), inner, jnp.where(mine, inner, blocks)])

    sides = hidden, other_hidden, gate, other_gate
    carry = None
    for distance in range(2):
        carry = mix(placed(distance), sums[distance], other_sums[distance], *sides, carry)

    second_far, third_far, *rest = together(second_far, third_far, *late, *carry)
    late, carry = rest[:2], rest[2:]
    late = project(
        place,
        attended,
        [second_far, third_far],
        [[(0, depth, 0, False)], [(1, depth, 0, False)]],
        late,
        3 * depth,
        jnp.bfloat16,
    )
    other_late = [swap(part, "ta", 1) for part in late]
    places = jnp.concatenate([placed(2), placed(3)])
    return finish(places, late, other_late, *sides, picked[2:3], picked[1:2], carry)


def gathered(hidden, queries, keys_values, windows, out_weight, picked):
    n_ha, n_wa, n_ta = lax.axis_size("ha"), lax.axis_size("wa"), lax.axis_size("ta")
    ha, ta = lax.axis_index("ha"), lax.axis_index("ta")
    work = Tokens(queries, keys_values, windows, 1)
    vector = work.plan.vector
    halos = *work.halos(work.edge_rows(vector, 0)), *work.rest_halos(vector)
    sent = work.leaving(vector, 0)
    visitors = shift(sent, "wa", 1), shift(sent, "wa", -1)
    near = work.stay(vector, halos)
    for_left, for_right = work.visit(vector, visitors, halos)
    sides = shift(for_right, "wa", 1), shift(for_left, "wa", -1)
    attended = work.combine(vector, near, [*sides, *work.rest_sides(vector, halos)])
    tokens, features = attended.shape
    depth = features // n_ha
    width = out_weight.shape[1]
    share = lax.dynamic_slice_in_dim(out_weight, ha * depth, depth, 0)
    weights = lax.all_gather(share, ("ha", "wa"), axis=0, tiled=False).reshape(
        n_ha, n_wa, depth, width
    )
    partial_sums = jnp.einsum(
        "thk,hwkc->wtc",
        attended.reshape(tokens, n_ha, depth),
        weights,
        preferred_element_type=jnp.float32,
    ).astype(jnp.bfloat16)
    blocks = n_wa // n_ta
    summed = None
    for step in range(n_ta):
        target = lax.rem(ta + step, n_ta)
        piece = lax.dynamic_slice_in_dim(partial_sums, target * blocks, blocks, 0)
        if step:
            piece = turn(piece, "ta", step)
        piece = piece.astype(jnp.float32)
        summed = piece if summed is None else summed + piece
    summed = jnp.transpose(summed, (1, 0, 2)).reshape(tokens, -1)
    mixed = hidden.astype(jnp.float32) + picked[0] * summed
    sum_first, sum_second = lax.psum((jnp.sum(mixed, axis=1), jnp.sum(mixed * mixed, axis=1)), "ta")
    average = (sum_first / D)[:, None]
    variance = (sum_second / D)[:, None] - average * average
    normed = (mixed - average) * lax.rsqrt(variance + EPSILON)
    ffn_input = (normed * (1.0 + picked[2]) + picked[1]).astype(jnp.bfloat16)
    return mixed.astype(jnp.bfloat16), ffn_input


def shards(hidden_states, queries, keys_values, out_weight, mod_table, windows, step_index):
    tokens = math.prod(queries.shape[:3])
    width = hidden_states.shape[3]
    picked = lax.dynamic_index_in_dim(mod_table, step_index[0], 0, keepdims=False)
    sizes = lax.axis_size("ha"), lax.axis_size("wa"), lax.axis_size("ta")
    tuned = sizes == (4, 4, 2) and out_weight.shape[0] % (20 * LANES) == 0
    residual_out, ffn_input = (paired if tuned else gathered)(
        hidden_states.reshape(tokens, width), queries, keys_values, windows, out_weight, picked
    )
    return residual_out.reshape(hidden_states.shape), ffn_input.reshape(hidden_states.shape)


def solution(mesh):
    return jax.shard_map(
        shards,
        mesh=mesh,
        in_specs=(
            P(None, "ha", "wa", "ta"),
            P(None, "ha", "wa", "ta"),
            P(None, None, "ha", "wa", "ta"),
            P("ta", "wa"),
            P(None, None, "ta"),
            P("ta", None),
            P(),
        ),
        out_specs=(P(None, "ha", "wa", "ta"), P(None, "ha", "wa", "ta")),
        check_vma=False,
    )
```

```python
from functools import partial
import math

import jax
import jax.numpy as jnp
from jax import lax
from jax.experimental import pallas as pl
from jax.experimental.pallas import tpu as pltpu
from jax.sharding import PartitionSpec as P

D = 5120
HD = 128
TILE = 8
LANES = 128
LEVEL_STEP = 32

EPSILON = 1e-06
VMEM_LIMIT = 24 * 1024 * 1024
SMALL = pl.CostEstimate(flops=1, bytes_accessed=1, transcendentals=0)
LARGE = pl.CostEstimate(flops=20_000_000_000, bytes_accessed=1, transcendentals=0)


def kernel_params(limit=VMEM_LIMIT):
    return pltpu.CompilerParams(dimension_semantics=("arbitrary",), vmem_limit_bytes=limit)


class Plan:
    def __init__(self, windows, order):
        heads = windows.shape[0]
        self.heads = heads
        self.most = max(heads * 7 // 10, 1)
        self.order = order
        n_ha, n_wa = lax.axis_size("ha"), lax.axis_size("wa")
        ha, wa = lax.axis_index("ha"), lax.axis_index("wa")
        number = lax.broadcasted_iota(jnp.int32, (2, heads, heads), 1)
        other = lax.broadcasted_iota(jnp.int32, (2, heads, heads), 2)
        idle = jnp.where(windows.T > 0, 0, 1)
        before = (idle[:, None, :] < idle[:, :, None]) | (
            (idle[:, None, :] == idle[:, :, None]) & (other < number)
        )
        position = jnp.sum(before.astype(jnp.int32), axis=2)
        sorted_heads = jnp.sum(jnp.where(position[:, None, :] == number, other, 0), axis=2)
        turned = ha if order > 1 else 0 * ha
        edges = jnp.stack([ha > 0, ha < n_ha - 1, wa > 0, wa < n_wa - 1, turned]).astype(jnp.int32)
        self.vector = jnp.concatenate(
            [windows.T.reshape(-1), position.reshape(-1), sorted_heads.reshape(-1), edges]
        )
        counts = lax.pmax(jnp.sum(1.0 - idle, axis=1), "ta")
        self.more_rows = counts[0] > self.most
        self.more_cols = counts[1] > self.most

    def row_radius(self, vector, head):
        return vector[head]

    def col_radius(self, vector, head):
        return vector[self.heads + head]

    def row_position(self, vector, head):
        return vector[2 * self.heads + head]

    def col_position(self, vector, head):
        return vector[3 * self.heads + head]

    def row_head(self, vector, position):
        return vector[4 * self.heads + position]

    def col_head(self, vector, position):
        return vector[5 * self.heads + position]

    def edge(self, vector, number):
        return vector[6 * self.heads + number]


def pack_kernel(vector, source, *refs, head_of, first, rows):
    outs, sem = refs[:-1], refs[-1]
    copies = []
    for number, (out, (low, size)) in enumerate(zip(outs, rows)):
        for slot in range(out.shape[-1] // HD):
            start = pl.multiple_of(head_of(vector, first + slot) * HD, HD)
            lead = (slice(None),) * (len(source.shape) - 2)
            copies.append(
                pltpu.make_async_copy(
                    source.at[(*lead, pl.ds(low, size), pl.ds(start, HD))],
                    out.at[(*lead, slice(None), pl.ds(slot * HD, HD))],
                    sem.at[number, slot],
                )
            )
    for copy in copies:
        copy.start()
    for copy in copies:
        copy.wait()


def pack(vector, source, head_of, first, count, rows):
    anywhere = pl.BlockSpec(memory_space=pl.ANY)
    return pl.pallas_call(
        partial(pack_kernel, head_of=head_of, first=first, rows=rows),
        in_specs=[pl.BlockSpec(memory_space=pltpu.SMEM), anywhere],
        out_specs=[anywhere] * len(rows),
        out_shape=[
            jax.ShapeDtypeStruct((*source.shape[:-2], size, count * HD), source.dtype)
            for _, size in rows
        ],
        scratch_shapes=[pltpu.SemaphoreType.DMA((len(rows), count))],
        compiler_params=pltpu.CompilerParams(vmem_limit_bytes=VMEM_LIMIT),
        cost_estimate=SMALL,
        name="pack",
    )(vector, source)


def attention_kernel(vector, *refs, plan, head_of, q_count, visiting, group):
    q_refs = refs[:q_count]
    kv_ref, top_ref, bottom_ref, top_rest, bottom_rest = refs[q_count : q_count + 5]
    refs = refs[q_count + 5 :]
    out_refs, stat_refs, halo = refs[:q_count], refs[q_count : 2 * q_count], refs[2 * q_count]
    frames, tokens, head_size = q_refs[0].shape
    span = top_ref.shape[2]
    tiles = tokens // span
    step = pl.program_id(0)
    head = head_of(vector, step)
    radius_row = plan.row_radius(vector, head)
    radius_col = plan.col_radius(vector, head)
    scale = 1.0 / math.sqrt(HD)

    @pl.when(step == 0)
    def _():
        for stat_ref in stat_refs:
            stat_ref[...] = jnp.zeros_like(stat_ref)

    def near(which, tile, wide):
        if not wide:
            return kv_ref[which, :, tile * span : (tile + 1) * span, :].reshape(-1, head_size)
        pieces = []
        if tile == 0:
            pieces.append(halo[0, which])
        low = max(tile - 1, 0) * span
        high = min(tile + 2, tiles) * span
        pieces.append(kv_ref[which, :, low:high, :])
        if tile == tiles - 1:
            pieces.append(halo[1, which])
        block = pieces[0] if len(pieces) == 1 else jnp.concatenate(pieces, axis=1)
        return block.reshape(-1, head_size)

    def attend(wide):
        lane = lax.broadcasted_iota(jnp.int32, (frames, span, LANES), 2)
        for tile in range(tiles):
            rows = slice(tile * span, (tile + 1) * span)
            keys = near(0, tile, wide)
            values = near(1, tile, wide)
            bias = None
            if wide and (tile == 0 or tile == tiles - 1):
                place = lax.rem(
                    lax.broadcasted_iota(jnp.int32, (1, keys.shape[0]), 1), 3 * span
                )
                low, high = 0, 3 * span
                if tile == 0:
                    low = jnp.where(plan.edge(vector, 0) == 0, span, 0)
                if tile == tiles - 1:
                    high = jnp.where(plan.edge(vector, 1) == 0, 2 * span, 3 * span)
                bias = jnp.where((place >= low) & (place < high), 0.0, -jnp.inf)
            for q_ref, out_ref, stat_ref in zip(q_refs, out_refs, stat_refs):
                query = q_ref[:, rows, :].reshape(-1, head_size)
                scores = (
                    lax.dot_general(
                        query, keys, (((1,), (1,)), ((), ())), preferred_element_type=jnp.float32
                    )
                    * scale
                )
                if bias is not None:
                    scores = scores + bias
                highest = jnp.max(scores, axis=1, keepdims=True)
                expo = jnp.exp(scores - highest)
                total = jnp.sum(expo, axis=1, keepdims=True)
                output = jnp.dot(
                    expo.astype(jnp.bfloat16), values, preferred_element_type=jnp.float32
                ) * (1.0 / total)
                out_ref[:, rows, :] = output.astype(jnp.bfloat16).reshape(frames, span, head_size)
                level = (highest + jnp.log(total)).reshape(frames, span, 1)
                stat_ref[:, rows, :] = jnp.where(lane == step, level, stat_ref[:, rows, :])

    active = step < group
    if visiting:

        @pl.when(active & (radius_col == 0))
        def _():
            for out_ref in out_refs:
                out_ref[...] = jnp.zeros_like(out_ref)

        active = active & (radius_col != 0)

    @pl.when(active & (radius_row == 0))
    def _():
        attend(False)

    always = plan.row_position(vector, head) < plan.most

    @pl.when(active & (radius_row != 0) & always)
    def _():
        halo[0] = top_ref[...]
        halo[1] = bottom_ref[...]

    @pl.when(active & (radius_row != 0) & jnp.logical_not(always))
    def _():
        halo[0] = top_rest[...]
        halo[1] = bottom_rest[...]

    @pl.when(active & (radius_row != 0))
    def _():
        attend(True)

    @pl.when(step == group)
    def _():
        for out_ref, stat_ref in zip(out_refs, stat_refs):
            level = stat_ref[...]
            high = level.astype(jnp.bfloat16).astype(jnp.float32)
            middle = (level - high).astype(jnp.bfloat16).astype(jnp.float32)
            low = level - high - middle
            packed = high + pltpu.roll(middle, LEVEL_STEP, 2) + pltpu.roll(low, 2 * LEVEL_STEP, 2)
            out_ref[...] = packed.astype(jnp.bfloat16)


def attention(plan, vector, query_blocks, keys_values, halos, first=None):
    frames, tokens, features = query_blocks[0].shape
    group = features // HD
    span = halos[0].shape[2]
    q_count = len(query_blocks)
    visiting = first is not None

    def slot_of(step):
        return jnp.minimum(step, group - 1)

    def head_of(vector, step):
        return plan.col_head(vector, first + slot_of(step)) if visiting else slot_of(step)

    def kv_index(step, vector):
        return 0, 0, 0, head_of(vector, step)

    def halo_index(step, vector):
        position = plan.row_position(vector, head_of(vector, step))
        return 0, 0, 0, jnp.minimum(position, plan.most - 1)

    def rest_index(step, vector):
        position = plan.row_position(vector, head_of(vector, step))
        return 0, 0, 0, jnp.maximum(position - plan.most, 0)

    q_spec = pl.BlockSpec((frames, tokens, HD), lambda step, _: (0, 0, slot_of(step)))
    kv_spec = pl.BlockSpec((2, frames, tokens, HD), kv_index)
    halo_spec = pl.BlockSpec((2, frames, span, HD), halo_index)
    rest_spec = pl.BlockSpec((2, frames, span, HD), rest_index)
    out_spec = pl.BlockSpec((frames, tokens, HD), lambda step, _: (0, 0, step))
    return pl.pallas_call(
        partial(
            attention_kernel,
            plan=plan,
            head_of=head_of,
            q_count=q_count,
            visiting=visiting,
            group=group,
        ),
        grid_spec=pltpu.PrefetchScalarGridSpec(
            num_scalar_prefetch=1,
            grid=(group + 1,),
            in_specs=[q_spec] * q_count + [kv_spec] + [halo_spec] * 2 + [rest_spec] * 2,
            out_specs=[out_spec] * q_count,
            scratch_shapes=[pltpu.VMEM((frames, tokens, LANES), jnp.float32)] * q_count
            + [pltpu.VMEM((2, 2, frames, span, HD), jnp.bfloat16)],
        ),
        out_shape=[jax.ShapeDtypeStruct((frames, tokens, (group + 1) * HD), jnp.bfloat16)]
        * q_count,
        compiler_params=kernel_params(),
        cost_estimate=SMALL if visiting else LARGE,
        name="attend_visitors" if visiting else "attend_own",
    )(vector, *query_blocks, keys_values, *halos)


def combine_kernel(vector, own, own_stat, left, right, left_rest, right_rest, out, *, plan, heads):
    first = pl.program_id(0) * heads
    frames, tokens, _ = own.shape

    def level(stat, number):
        lane = lax.broadcasted_iota(jnp.int32, (LANES, HD), 0)
        pick = jnp.where(
            (lax.rem(lane, LEVEL_STEP) == number) & (lane < 3 * LEVEL_STEP), 1.0, 0.0
        ).astype(jnp.bfloat16)
        return jnp.dot(
            stat.reshape(-1, LANES), pick, preferred_element_type=jnp.float32
        ).reshape(frames, tokens, HD)

    for index in range(heads):
        head = first + index
        columns = slice(index * HD, (index + 1) * HD)
        across = plan.col_radius(vector, head) != 0
        position = plan.col_position(vector, head)

        @pl.when(jnp.logical_not(across))
        def _(columns=columns):
            out[:, :, columns] = own[:, :, columns]

        def join(sides, slot, columns, head):
            here = pl.ds(pl.multiple_of(slot * HD, HD), HD)
            levels = [level(own_stat[...], head)]
            values = [own[:, :, columns]]
            for number, side in enumerate(sides):
                value = level(side[:, :, side.shape[2] - LANES :], slot)
                levels.append(jnp.where(plan.edge(vector, 2 + number) == 0, -jnp.inf, value))
                values.append(side[:, :, here])
            highest = jnp.maximum(levels[0], jnp.maximum(levels[1], levels[2]))
            weights = [jnp.exp(x - highest) for x in levels]
            mixed = sum(value.astype(jnp.float32) * weight for value, weight in zip(values, weights))
            out[:, :, columns] = (mixed / (weights[0] + weights[1] + weights[2])).astype(
                jnp.bfloat16
            )

        @pl.when(across & (position < plan.most))
        def _(position=position, columns=columns, head=head):
            join((left, right), position, columns, head)

        @pl.when(across & (position >= plan.most))
        def _(position=position, columns=columns, head=head):
            join((left_rest, right_rest), position - plan.most, columns, head)


def combine(plan, vector, near, sides):
    frames, tokens, _ = near.shape
    heads = plan.heads // plan.order
    spec = pl.BlockSpec((frames, tokens, heads * HD), lambda h, _: (0, 0, h))
    stat_spec = pl.BlockSpec((frames, tokens, HD), lambda h, _: (0, 0, plan.heads))
    return pl.pallas_call(
        partial(combine_kernel, plan=plan, heads=heads),
        grid_spec=pltpu.PrefetchScalarGridSpec(
            num_scalar_prefetch=1,
            grid=(plan.order,),
            in_specs=[spec, stat_spec]
            + [pl.BlockSpec(side.shape, lambda h, _: (0, 0, 0)) for side in sides],
            out_specs=pl.BlockSpec(
                (frames, tokens, heads * HD), lambda h, vector: (0, 0, h ^ plan.edge(vector, 4))
            ),
        ),
        out_shape=jax.ShapeDtypeStruct((frames, tokens, plan.heads * HD), jnp.bfloat16),
        compiler_params=kernel_params(),
        cost_estimate=SMALL,
        name="combine",
    )(vector, near, near, *sides)


def project_kernel(place, attended, *refs, slots, carried, start, column):
    arrays = 1 + max(piece[0] for slot in slots for piece in slot)
    pieces, refs = refs[:arrays], refs[arrays:]
    if carried:
        carry, refs = refs[: len(slots)], refs[len(slots) :]
    outs, (rows, weight, rows_sem, weight_sem) = refs[: len(slots)], refs[len(slots) :]
    columns = weight.shape[1]
    depth = weight.shape[2]
    rows_copy = pltpu.make_async_copy(
        attended.at[:, start : start + depth], rows, rows_sem.at[0]
    )
    rows_copy.start()
    for index, slot in enumerate(slots):
        for block in range(columns):
            low = 0
            for number, (array, size, share, turned) in enumerate(slot):
                first = pl.multiple_of((place[0] ^ share if turned else share) * size, size)
                pltpu.make_async_copy(
                    pieces[array].at[pl.ds(first, size), block * column : (block + 1) * column],
                    weight.at[index, block, low : low + size],
                    weight_sem.at[index, block, number],
                ).start()
                low += size
    rows_copy.wait()
    for index, slot in enumerate(slots):

        def body(block, _, index=index, slot=slot):
            low = 0
            for number, (_, size, _, _) in enumerate(slot):
                piece = weight.at[index, block, low : low + size]
                pltpu.make_async_copy(piece, piece, weight_sem.at[index, block, number]).wait()
                low += size
            total = jnp.dot(rows[...], weight[index, block], preferred_element_type=jnp.float32)
            here = pl.ds(pl.multiple_of(block * column, column), column)
            if carried:
                total = total + carry[index][0, :, here]
            outs[index][0, :, here] = total.astype(outs[index].dtype)
            return 0

        lax.fori_loop(0, columns, body, 0)


def project(place, attended, arrays, slots, carry, start, dtype):
    tokens = attended.shape[0]
    width = arrays[0].shape[1]
    column = 256 if width % 256 == 0 else width
    columns = width // column
    depth = sum(piece[1] for piece in slots[0])
    anywhere = pl.BlockSpec(memory_space=pl.ANY)
    inside = pl.BlockSpec(memory_space=pltpu.VMEM)
    return pl.pallas_call(
        partial(
            project_kernel, slots=slots, carried=carry is not None, start=start, column=column
        ),
        in_specs=[pl.BlockSpec(memory_space=pltpu.SMEM), anywhere]
        + [anywhere] * len(arrays)
        + ([] if carry is None else [inside] * len(slots)),
        out_specs=[inside] * len(slots),
        out_shape=[jax.ShapeDtypeStruct((1, tokens, width), dtype)] * len(slots),
        scratch_shapes=[
            pltpu.VMEM((tokens, depth), attended.dtype),
            pltpu.VMEM((len(slots), columns, depth, column), attended.dtype),
            pltpu.SemaphoreType.DMA((1,)),
            pltpu.SemaphoreType.DMA((len(slots), columns, max(len(slot) for slot in slots))),
        ],
        compiler_params=pltpu.CompilerParams(vmem_limit_bytes=VMEM_LIMIT),
        cost_estimate=SMALL,
        name="project",
    )(place, attended, *arrays, *([] if carry is None else carry))


def pick_kernel(place, own_hidden, other_hidden, own_gate, other_gate, hidden, gate):
    mine = place[2 * pl.program_id(0)] != 0

    @pl.when(mine)
    def _():
        hidden[0] = own_hidden[...]
        gate[0] = own_gate[...]

    @pl.when(jnp.logical_not(mine))
    def _():
        hidden[0] = other_hidden[...]
        gate[0] = other_gate[...]


def pick(place, own_hidden, other_hidden, own_gate, other_gate, width):
    tokens, features = own_hidden.shape
    count = 2 * features // width
    hidden = pl.BlockSpec((tokens, width), lambda i, place: (0, place[2 * i + 1]))
    gate = pl.BlockSpec((1, width), lambda i, place: (0, place[2 * i + 1]))
    return pl.pallas_call(
        pick_kernel,
        grid_spec=pltpu.PrefetchScalarGridSpec(
            num_scalar_prefetch=1,
            grid=(count,),
            in_specs=[hidden, hidden, gate, gate],
            out_specs=[
                pl.BlockSpec((1, tokens, width), lambda i, place: (i, 0, 0)),
                pl.BlockSpec((1, 1, width), lambda i, place: (i, 0, 0)),
            ],
        ),
        out_shape=[
            jax.ShapeDtypeStruct((count, tokens, width), jnp.bfloat16),
            jax.ShapeDtypeStruct((count, 1, width), jnp.float32),
        ],
        compiler_params=kernel_params(),
        cost_estimate=SMALL,
        name="pick",
    )(place, own_hidden, other_hidden, own_gate, other_gate)


def mixed_blocks(hidden, gate, first, own_parts, other_parts):
    return [
        hidden[index].astype(jnp.float32)
        + gate[first + index]
        * (own_part[0].astype(jnp.float32) + other_part[0].astype(jnp.float32))
        for index, (own_part, other_part) in enumerate(zip(own_parts, other_parts))
    ]


def mix_kernel(hidden, gate, *refs, count):
    own_parts, other_parts, (mixed_ref, sums_ref) = (
        refs[:count],
        refs[count : 2 * count],
        refs[2 * count :],
    )
    first = second = 0.0
    for index, mixed in enumerate(mixed_blocks(hidden, gate, 0, own_parts, other_parts)):
        mixed_ref[index] = mixed.astype(jnp.bfloat16)
        first = first + jnp.sum(mixed, axis=1, keepdims=True)
        second = second + jnp.sum(mixed * mixed, axis=1, keepdims=True)
    lane = lax.broadcasted_iota(jnp.int32, sums_ref.shape, 1)
    sums_ref[...] = jnp.where(lane == 0, first, jnp.where(lane == 1, second, 0.0))


def mix(hidden, gate, own_parts, other_parts):
    count = len(own_parts)
    _, tokens, width = hidden.shape
    rows = 64 if tokens % 64 == 0 else tokens
    part = pl.BlockSpec((1, rows, width), lambda i: (0, i, 0))
    several = pl.BlockSpec((count, rows, width), lambda i: (0, i, 0))
    return pl.pallas_call(
        partial(mix_kernel, count=count),
        grid=(tokens // rows,),
        in_specs=[several, pl.BlockSpec(gate.shape, lambda i: (0, 0, 0))] + [part] * (2 * count),
        out_specs=[several, pl.BlockSpec((rows, LANES), lambda i: (i, 0))],
        out_shape=[
            jax.ShapeDtypeStruct((count, tokens, width), jnp.bfloat16),
            jax.ShapeDtypeStruct((tokens, LANES), jnp.float32),
        ],
        compiler_params=kernel_params(),
        cost_estimate=SMALL,
        name="mix",
    )(hidden, gate, *own_parts, *other_parts)


def finish_kernel(place, hidden, gate, scale, shift_by, sums, *refs, count, blocks):
    early, refs = refs[:blocks], refs[blocks:]
    own_parts, other_parts, (residual, ffn) = (
        refs[:count],
        refs[count : 2 * count],
        refs[2 * count :],
    )
    width = hidden.shape[2]
    others = gate.shape[0] - count
    late = mixed_blocks(hidden, gate, others, own_parts, other_parts)
    first = sums[:, 0:1]
    second = sums[:, 1:2]
    for mixed in late:
        first = first + jnp.sum(mixed, axis=1, keepdims=True)
        second = second + jnp.sum(mixed * mixed, axis=1, keepdims=True)
    average = first / D
    variance = second / D - average * average
    inverse = lax.rsqrt(variance + EPSILON)
    for block in range(blocks):
        columns = slice(block * width, (block + 1) * width)
        mixed = early[block][0].astype(jnp.float32)
        for index in range(count):
            mixed = jnp.where(place[2 * block] == others + index, late[index], mixed)
        residual[:, columns] = mixed.astype(jnp.bfloat16)
        ffn[:, columns] = (
            (mixed - average) * inverse * (1.0 + scale[:, columns]) + shift_by[:, columns]
        ).astype(jnp.bfloat16)


def finish(place, hidden, gate, scale, shift_by, sums, early, own_parts, other_parts):
    count = len(own_parts)
    _, tokens, width = hidden.shape
    blocks = place.shape[0] // 2
    rows = 64 if tokens % 64 == 0 else tokens
    part = pl.BlockSpec((1, rows, width), lambda i, place: (0, i, 0))
    several = pl.BlockSpec((count, rows, width), lambda i, place: (1, i, 0))
    whole = pl.BlockSpec((1, blocks * width), lambda i, place: (0, 0))
    row = pl.BlockSpec((rows, blocks * width), lambda i, place: (i, 0))
    earlier = [
        pl.BlockSpec((1, rows, width), lambda i, place, block=block: (place[2 * block + 1], i, 0))
        for block in range(blocks)
    ]
    return pl.pallas_call(
        partial(finish_kernel, count=count, blocks=blocks),
        grid_spec=pltpu.PrefetchScalarGridSpec(
            num_scalar_prefetch=1,
            grid=(tokens // rows,),
            in_specs=[several, pl.BlockSpec(gate.shape, lambda i, place: (0, 0, 0)), whole, whole]
            + [pl.BlockSpec((rows, LANES), lambda i, place: (i, 0))]
            + earlier
            + [part] * (2 * count),
            out_specs=[row, row],
        ),
        out_shape=[jax.ShapeDtypeStruct((tokens, blocks * width), jnp.bfloat16)] * 2,
        compiler_params=kernel_params(),
        cost_estimate=SMALL,
        name="finish",
    )(place, hidden, gate, scale, shift_by, sums, *[early] * blocks, *own_parts, *other_parts)


def shift(block, axis, step):
    count = lax.axis_size(axis)
    pairs = [(i, i + step) for i in range(count) if 0 <= i + step < count]
    return lax.ppermute(block, axis, pairs)


def turn(block, axis, step):
    count = lax.axis_size(axis)
    return lax.ppermute(block, axis, [(i, (i + step) % count) for i in range(count)])


def swap(block, axis, bit):
    count = lax.axis_size(axis)
    return lax.ppermute(block, axis, [(i, i ^ bit) for i in range(count)])


class Tokens:
    def __init__(self, queries, keys_values, windows, order):
        self.plan = Plan(windows, order)
        self.queries = queries.reshape(queries.shape[0], -1, queries.shape[3])
        self.keys_values = keys_values.reshape(*keys_values.shape[:2], -1, keys_values.shape[4])
        self.span = TILE * queries.shape[2]
        self.parts = (0, self.plan.most), (self.plan.most, self.plan.heads - self.plan.most)

    def edge_rows(self, vector, part):
        low = self.queries.shape[1] - self.span
        rows = [(low, self.span), (0, self.span)]
        return pack(vector, self.keys_values, self.plan.row_head, *self.parts[part], rows)

    def leaving(self, vector, part):
        rows = [(0, self.queries.shape[1])]
        return pack(vector, self.queries, self.plan.col_head, *self.parts[part], rows)[0]

    def halos(self, rows):
        return shift(rows[0], "ha", 1), shift(rows[1], "ha", -1)

    def rest_halos(self, vector):
        shape = (*self.keys_values.shape[:2], self.span, self.parts[1][1] * HD)
        return lax.cond(
            self.plan.more_rows,
            lambda vector: self.halos(self.edge_rows(vector, 1)),
            lambda vector: (jnp.zeros(shape, jnp.bfloat16),) * 2,
            vector,
        )

    def stay(self, vector, halos):
        return attention(self.plan, vector, [self.queries], self.keys_values, halos)[0]

    def visit(self, vector, visitors, halos, part=0):
        first = self.parts[part][0]
        return attention(self.plan, vector, visitors, self.keys_values, halos, first)

    def rest_sides(self, vector, halos):
        shape = (*self.queries.shape[:2], (self.parts[1][1] + 1) * HD)

        def send(vector, *halos):
            queries = self.leaving(vector, 1)
            visitors = shift(queries, "wa", 1), shift(queries, "wa", -1)
            for_left, for_right = self.visit(vector, visitors, halos, 1)
            return shift(for_right, "wa", 1), shift(for_left, "wa", -1)

        return lax.cond(
            self.plan.more_cols,
            send,
            lambda vector, *halos: (jnp.zeros(shape, jnp.bfloat16),) * 2,
            vector,
            *halos,
        )

    def combine(self, vector, near, sides):
        attended = combine(self.plan, vector, near, sides)
        return attended.reshape(-1, attended.shape[2])


def together(*blocks):
    return lax.optimization_barrier(blocks)


def paired(hidden, queries, keys_values, windows, out_weight, picked):
    ha, wa, ta = lax.axis_index("ha"), lax.axis_index("wa"), lax.axis_index("ta")
    n_wa = lax.axis_size("wa")
    blocks = n_wa // 2
    depth = out_weight.shape[0] // 4
    width = out_weight.shape[1]
    cut = depth // 2

    share = lax.optimization_barrier(lax.dynamic_slice_in_dim(out_weight, ha * depth, depth, 0))
    first = turn(share, "wa", 1)
    tokens = Tokens(queries, keys_values, windows, 4)
    vector = tokens.plan.vector
    top, bottom = tokens.halos(tokens.edge_rows(vector, 0))
    queries = tokens.leaving(vector, 0)
    from_left = shift(queries, "wa", 1)
    from_right = shift(queries, "wa", -1)

    first, top, bottom, vector = together(first, top, bottom, vector)
    first_x = swap(first, "ha", 1)
    first_y = swap(first, "ha", 2)
    second = turn(first, "wa", 1)
    halos = top, bottom, *tokens.rest_halos(vector)
    near = tokens.stay(vector, halos)

    near, first_x, first_y, from_left, from_right = together(
        near, first_x, first_y, from_left, from_right
    )
    first_far_x = swap(first_y[:cut], "ha", 1)
    first_far_y = swap(first_x[cut:], "ha", 2)

    first_far_x, first_far_y, second, from_left, from_right, gate = together(
        first_far_x, first_far_y, second, from_left, from_right, picked[0:1]
    )
    third = turn(second, "wa", 1)
    second_x = swap(second, "ha", 1)
    second_y = swap(second, "ha", 2)
    other_gate = swap(gate, "ta", 1)
    for_left, for_right = tokens.visit(vector, (from_left, from_right), halos)

    for_left, for_right, first_far_x = together(for_left, for_right, first_far_x)
    left = shift(for_right, "wa", 1)
    right = shift(for_left, "wa", -1)

    third, second_x, second_y, first_far_x, other_gate, hidden, vector = together(
        third, second_x, second_y, first_far_x, other_gate, hidden, vector
    )
    third_x = swap(third, "ha", 1)
    third_y = swap(third, "ha", 2)
    other_hidden = swap(hidden, "ta", 1)
    rest_sides = tokens.rest_sides(vector, halos)

    def block_of(distance):
        return lax.rem(wa - distance + n_wa, n_wa)

    owners = jnp.stack([block_of(distance) // blocks == ta for distance in range(n_wa)])
    inner = jnp.stack([lax.rem(block_of(distance), blocks) for distance in range(n_wa)])
    place = jnp.stack([owners.astype(jnp.int32), inner], axis=1).reshape(-1)
    base, gates = pick(place, hidden, other_hidden, gate, other_gate, width)
    left, right, base, gates = together(left, right, base, gates)
    attended = tokens.combine(vector, near, [left, right, *rest_sides])

    third_x, third_y, second_x, attended = together(third_x, third_y, second_x, attended)
    third_far = swap(third_y, "ha", 1)
    second_far = swap(second_x, "ha", 2)

    turned = ha.reshape(1)
    sums = project(
        turned,
        attended,
        [out_weight, first, first_x, first_y, first_far_x, first_far_y],
        [
            [(0, depth, number, True) for number in range(4)],
            [(number, depth, 0, False) for number in range(1, 4)]
            + [(4, cut, 0, False), (5, depth - cut, 0, False)],
        ],
        None,
        0,
        jnp.bfloat16,
    )
    other_sums = [swap(part, "ta", 1) for part in sums]
    late = project(
        turned,
        attended,
        [second, second_x, second_y, third, third_x, third_y],
        [[(start + number, depth, 0, False) for number in range(3)] for start in (0, 3)],
        None,
        0,
        jnp.float32,
    )
    early, totals = mix(base, gates, sums, other_sums)

    second_far, third_far, early, totals, *late = together(
        second_far, third_far, early, totals, *late
    )
    late = project(
        turned,
        attended,
        [second_far, third_far],
        [[(0, depth, 0, False)], [(1, depth, 0, False)]],
        late,
        3 * depth,
        jnp.bfloat16,
    )
    other_late = [swap(part, "ta", 1) for part in late]
    mine = [lax.rem(wa - ta * blocks - block + 2 * n_wa, n_wa) for block in range(blocks)]
    place = jnp.stack([value for slot in mine for value in (slot, jnp.minimum(slot, 1))])
    return finish(
        place, base, gates, picked[2:3], picked[1:2], totals, early, late, other_late
    )


def gathered(hidden, queries, keys_values, windows, out_weight, picked):
    n_ha, n_wa, n_ta = lax.axis_size("ha"), lax.axis_size("wa"), lax.axis_size("ta")
    ha, ta = lax.axis_index("ha"), lax.axis_index("ta")
    work = Tokens(queries, keys_values, windows, 1)
    vector = work.plan.vector
    halos = *work.halos(work.edge_rows(vector, 0)), *work.rest_halos(vector)
    sent = work.leaving(vector, 0)
    visitors = shift(sent, "wa", 1), shift(sent, "wa", -1)
    near = work.stay(vector, halos)
    for_left, for_right = work.visit(vector, visitors, halos)
    sides = shift(for_right, "wa", 1), shift(for_left, "wa", -1)
    attended = work.combine(vector, near, [*sides, *work.rest_sides(vector, halos)])
    tokens, features = attended.shape
    depth = features // n_ha
    width = out_weight.shape[1]
    share = lax.dynamic_slice_in_dim(out_weight, ha * depth, depth, 0)
    weights = lax.all_gather(share, ("ha", "wa"), axis=0, tiled=False).reshape(
        n_ha, n_wa, depth, width
    )
    partial_sums = jnp.einsum(
        "thk,hwkc->wtc",
        attended.reshape(tokens, n_ha, depth),
        weights,
        preferred_element_type=jnp.float32,
    ).astype(jnp.bfloat16)
    blocks = n_wa // n_ta
    summed = None
    for step in range(n_ta):
        target = lax.rem(ta + step, n_ta)
        piece = lax.dynamic_slice_in_dim(partial_sums, target * blocks, blocks, 0)
        if step:
            piece = turn(piece, "ta", step)
        piece = piece.astype(jnp.float32)
        summed = piece if summed is None else summed + piece
    summed = jnp.transpose(summed, (1, 0, 2)).reshape(tokens, -1)
    mixed = hidden.astype(jnp.float32) + picked[0] * summed
    sum_first, sum_second = lax.psum((jnp.sum(mixed, axis=1), jnp.sum(mixed * mixed, axis=1)), "ta")
    average = (sum_first / D)[:, None]
    variance = (sum_second / D)[:, None] - average * average
    normed = (mixed - average) * lax.rsqrt(variance + EPSILON)
    ffn_input = (normed * (1.0 + picked[2]) + picked[1]).astype(jnp.bfloat16)
    return mixed.astype(jnp.bfloat16), ffn_input


def shards(hidden_states, queries, keys_values, out_weight, mod_table, windows, step_index):
    tokens = math.prod(queries.shape[:3])
    width = hidden_states.shape[3]
    picked = lax.dynamic_index_in_dim(mod_table, step_index[0], 0, keepdims=False)
    sizes = lax.axis_size("ha"), lax.axis_size("wa"), lax.axis_size("ta")
    tuned = sizes == (4, 4, 2) and out_weight.shape[0] % (20 * LANES) == 0
    residual_out, ffn_input = (paired if tuned else gathered)(
        hidden_states.reshape(tokens, width), queries, keys_values, windows, out_weight, picked
    )
    return residual_out.reshape(hidden_states.shape), ffn_input.reshape(hidden_states.shape)


def solution(mesh):
    return jax.shard_map(
        shards,
        mesh=mesh,
        in_specs=(
            P(None, "ha", "wa", "ta"),
            P(None, "ha", "wa", "ta"),
            P(None, None, "ha", "wa", "ta"),
            P("ta", "wa"),
            P(None, None, "ta"),
            P("ta", None),
            P(),
        ),
        out_specs=(P(None, "ha", "wa", "ta"), P(None, "ha", "wa", "ta")),
        check_vma=False,
    )
```

```python
from functools import partial
import math

import jax
import jax.numpy as jnp
from jax import lax
from jax.experimental import pallas as pl
from jax.experimental.pallas import tpu as pltpu
from jax.sharding import PartitionSpec as P

D = 5120
HD = 128
TILE = 8
LANES = 128
LEVEL_STEP = 32

EPSILON = 1e-06
VMEM_LIMIT = 28 * 1024 * 1024
SMALL = pl.CostEstimate(flops=1, bytes_accessed=1, transcendentals=0)
LARGE = pl.CostEstimate(flops=20_000_000_000, bytes_accessed=1, transcendentals=0)


def kernel_params(limit=VMEM_LIMIT):
    return pltpu.CompilerParams(dimension_semantics=("arbitrary",), vmem_limit_bytes=limit)


class Plan:
    def __init__(self, windows, order):
        heads = windows.shape[0]
        self.heads = heads
        self.most = max(heads * 7 // 10, 1)
        self.order = order
        n_ha, n_wa = lax.axis_size("ha"), lax.axis_size("wa")
        ha, wa = lax.axis_index("ha"), lax.axis_index("wa")
        number = lax.broadcasted_iota(jnp.int32, (2, heads, heads), 1)
        other = lax.broadcasted_iota(jnp.int32, (2, heads, heads), 2)
        idle = jnp.where(windows.T > 0, 0, 1)
        before = (idle[:, None, :] < idle[:, :, None]) | (
            (idle[:, None, :] == idle[:, :, None]) & (other < number)
        )
        position = jnp.sum(before.astype(jnp.int32), axis=2)
        sorted_heads = jnp.sum(jnp.where(position[:, None, :] == number, other, 0), axis=2)
        turned = ha if order > 1 else 0 * ha
        edges = jnp.stack([ha > 0, ha < n_ha - 1, wa > 0, wa < n_wa - 1, turned]).astype(jnp.int32)
        self.vector = jnp.concatenate(
            [windows.T.reshape(-1), position.reshape(-1), sorted_heads.reshape(-1), edges]
        )
        counts = lax.pmax(jnp.sum(1.0 - idle, axis=1), "ta")
        self.more_rows = counts[0] > self.most
        self.more_cols = counts[1] > self.most

    def row_radius(self, vector, head):
        return vector[head]

    def col_radius(self, vector, head):
        return vector[self.heads + head]

    def row_position(self, vector, head):
        return vector[2 * self.heads + head]

    def col_position(self, vector, head):
        return vector[3 * self.heads + head]

    def row_head(self, vector, position):
        return vector[4 * self.heads + position]

    def col_head(self, vector, position):
        return vector[5 * self.heads + position]

    def edge(self, vector, number):
        return vector[6 * self.heads + number]


def pack_kernel(vector, source, *refs, head_of, first, rows):
    outs, sem = refs[:-1], refs[-1]
    copies = []
    for number, (out, (low, size)) in enumerate(zip(outs, rows)):
        for slot in range(out.shape[-1] // HD):
            start = pl.multiple_of(head_of(vector, first + slot) * HD, HD)
            lead = (slice(None),) * (len(source.shape) - 2)
            copies.append(
                pltpu.make_async_copy(
                    source.at[(*lead, pl.ds(low, size), pl.ds(start, HD))],
                    out.at[(*lead, slice(None), pl.ds(slot * HD, HD))],
                    sem.at[number, slot],
                )
            )
    for copy in copies:
        copy.start()
    for copy in copies:
        copy.wait()


def pack(vector, source, head_of, first, count, rows):
    anywhere = pl.BlockSpec(memory_space=pl.ANY)
    return pl.pallas_call(
        partial(pack_kernel, head_of=head_of, first=first, rows=rows),
        in_specs=[pl.BlockSpec(memory_space=pltpu.SMEM), anywhere],
        out_specs=[pl.BlockSpec(memory_space=pltpu.VMEM)] * len(rows),
        out_shape=[
            jax.ShapeDtypeStruct((*source.shape[:-2], size, count * HD), source.dtype)
            for _, size in rows
        ],
        scratch_shapes=[pltpu.SemaphoreType.DMA((len(rows), count))],
        compiler_params=pltpu.CompilerParams(vmem_limit_bytes=VMEM_LIMIT),
        cost_estimate=SMALL,
        name="pack",
    )(vector, source)


def attention_kernel(vector, *refs, plan, head_of, q_count, visiting, group):
    q_refs = refs[:q_count]
    kv_ref, top_ref, bottom_ref, top_rest, bottom_rest = refs[q_count : q_count + 5]
    refs = refs[q_count + 5 :]
    out_refs, stat_refs, halo = refs[:q_count], refs[q_count : 2 * q_count], refs[2 * q_count]
    frames, tokens, head_size = q_refs[0].shape
    span = top_ref.shape[2]
    tiles = tokens // span
    step = pl.program_id(0)
    head = head_of(vector, step)
    radius_row = plan.row_radius(vector, head)
    radius_col = plan.col_radius(vector, head)
    scale = 1.0 / math.sqrt(HD)

    @pl.when(step == 0)
    def _():
        for stat_ref in stat_refs:
            stat_ref[...] = jnp.zeros_like(stat_ref)

    def near(which, tile, wide):
        if not wide:
            return kv_ref[which, :, tile * span : (tile + 1) * span, :].reshape(-1, head_size)
        pieces = []
        if tile == 0:
            pieces.append(halo[0, which])
        low = max(tile - 1, 0) * span
        high = min(tile + 2, tiles) * span
        pieces.append(kv_ref[which, :, low:high, :])
        if tile == tiles - 1:
            pieces.append(halo[1, which])
        block = pieces[0] if len(pieces) == 1 else jnp.concatenate(pieces, axis=1)
        return block.reshape(-1, head_size)

    def attend(wide):
        lane = lax.broadcasted_iota(jnp.int32, (frames, span, LANES), 2)
        for tile in range(tiles):
            rows = slice(tile * span, (tile + 1) * span)
            keys = near(0, tile, wide)
            values = near(1, tile, wide)
            bias = None
            if wide and (tile == 0 or tile == tiles - 1):
                place = lax.rem(
                    lax.broadcasted_iota(jnp.int32, (1, keys.shape[0]), 1), 3 * span
                )
                low, high = 0, 3 * span
                if tile == 0:
                    low = jnp.where(plan.edge(vector, 0) == 0, span, 0)
                if tile == tiles - 1:
                    high = jnp.where(plan.edge(vector, 1) == 0, 2 * span, 3 * span)
                bias = jnp.where((place >= low) & (place < high), 0.0, -jnp.inf)
            for q_ref, out_ref, stat_ref in zip(q_refs, out_refs, stat_refs):
                query = q_ref[:, rows, :].reshape(-1, head_size)
                scores = (
                    lax.dot_general(
                        query, keys, (((1,), (1,)), ((), ())), preferred_element_type=jnp.float32
                    )
                    * scale
                )
                if bias is not None:
                    scores = scores + bias
                highest = jnp.max(scores, axis=1, keepdims=True)
                expo = jnp.exp(scores - highest)
                total = jnp.sum(expo, axis=1, keepdims=True)
                output = jnp.dot(
                    expo.astype(jnp.bfloat16), values, preferred_element_type=jnp.float32
                ) * (1.0 / total)
                out_ref[:, rows, :] = output.astype(jnp.bfloat16).reshape(frames, span, head_size)
                level = (highest + jnp.log(total)).reshape(frames, span, 1)
                stat_ref[:, rows, :] = jnp.where(lane == step, level, stat_ref[:, rows, :])

    active = step < group
    if visiting:

        @pl.when(active & (radius_col == 0))
        def _():
            for out_ref in out_refs:
                out_ref[...] = jnp.zeros_like(out_ref)

        active = active & (radius_col != 0)

    @pl.when(active & (radius_row == 0))
    def _():
        attend(False)

    always = plan.row_position(vector, head) < plan.most

    @pl.when(active & (radius_row != 0) & always)
    def _():
        halo[0] = top_ref[...]
        halo[1] = bottom_ref[...]

    @pl.when(active & (radius_row != 0) & jnp.logical_not(always))
    def _():
        halo[0] = top_rest[...]
        halo[1] = bottom_rest[...]

    @pl.when(active & (radius_row != 0))
    def _():
        attend(True)

    @pl.when(step == group)
    def _():
        for out_ref, stat_ref in zip(out_refs, stat_refs):
            level = stat_ref[...]
            high = level.astype(jnp.bfloat16).astype(jnp.float32)
            middle = (level - high).astype(jnp.bfloat16).astype(jnp.float32)
            low = level - high - middle
            packed = high + pltpu.roll(middle, LEVEL_STEP, 2) + pltpu.roll(low, 2 * LEVEL_STEP, 2)
            out_ref[...] = packed.astype(jnp.bfloat16)


def attention(plan, vector, query_blocks, keys_values, halos, first=None):
    frames, tokens, features = query_blocks[0].shape
    group = features // HD
    span = halos[0].shape[2]
    q_count = len(query_blocks)
    visiting = first is not None

    def slot_of(step):
        return jnp.minimum(step, group - 1)

    def head_of(vector, step):
        return plan.col_head(vector, first + slot_of(step)) if visiting else slot_of(step)

    def kv_index(step, vector):
        return 0, 0, 0, head_of(vector, step)

    def halo_index(step, vector):
        position = plan.row_position(vector, head_of(vector, step))
        return 0, 0, 0, jnp.minimum(position, plan.most - 1)

    def rest_index(step, vector):
        position = plan.row_position(vector, head_of(vector, step))
        return 0, 0, 0, jnp.maximum(position - plan.most, 0)

    q_spec = pl.BlockSpec((frames, tokens, HD), lambda step, _: (0, 0, slot_of(step)))
    kv_spec = pl.BlockSpec((2, frames, tokens, HD), kv_index)
    halo_spec = pl.BlockSpec((2, frames, span, HD), halo_index)
    rest_spec = pl.BlockSpec((2, frames, span, HD), rest_index)
    out_spec = pl.BlockSpec((frames, tokens, HD), lambda step, _: (0, 0, step))
    return pl.pallas_call(
        partial(
            attention_kernel,
            plan=plan,
            head_of=head_of,
            q_count=q_count,
            visiting=visiting,
            group=group,
        ),
        grid_spec=pltpu.PrefetchScalarGridSpec(
            num_scalar_prefetch=1,
            grid=(group + 1,),
            in_specs=[q_spec] * q_count + [kv_spec] + [halo_spec] * 2 + [rest_spec] * 2,
            out_specs=[out_spec] * q_count,
            scratch_shapes=[pltpu.VMEM((frames, tokens, LANES), jnp.float32)] * q_count
            + [pltpu.VMEM((2, 2, frames, span, HD), jnp.bfloat16)],
        ),
        out_shape=[jax.ShapeDtypeStruct((frames, tokens, (group + 1) * HD), jnp.bfloat16)]
        * q_count,
        compiler_params=kernel_params(),
        cost_estimate=SMALL if visiting else LARGE,
        name="attend_visitors" if visiting else "attend_own",
    )(vector, *query_blocks, keys_values, *halos)


def combine_kernel(vector, own, own_stat, left, right, left_rest, right_rest, out, *, plan, heads):
    first = pl.program_id(0) * heads
    frames, tokens, _ = own.shape

    def level(stat, number):
        lane = lax.broadcasted_iota(jnp.int32, (LANES, HD), 0)
        pick = jnp.where(
            (lax.rem(lane, LEVEL_STEP) == number) & (lane < 3 * LEVEL_STEP), 1.0, 0.0
        ).astype(jnp.bfloat16)
        return jnp.dot(
            stat.reshape(-1, LANES), pick, preferred_element_type=jnp.float32
        ).reshape(frames, tokens, HD)

    for index in range(heads):
        head = first + index
        columns = slice(index * HD, (index + 1) * HD)
        across = plan.col_radius(vector, head) != 0
        position = plan.col_position(vector, head)

        @pl.when(jnp.logical_not(across))
        def _(columns=columns):
            out[:, :, columns] = own[:, :, columns]

        def join(sides, slot, columns, head):
            here = pl.ds(pl.multiple_of(slot * HD, HD), HD)
            levels = [level(own_stat[...], head)]
            values = [own[:, :, columns]]
            for number, side in enumerate(sides):
                value = level(side[:, :, side.shape[2] - LANES :], slot)
                levels.append(jnp.where(plan.edge(vector, 2 + number) == 0, -jnp.inf, value))
                values.append(side[:, :, here])
            highest = jnp.maximum(levels[0], jnp.maximum(levels[1], levels[2]))
            weights = [jnp.exp(x - highest) for x in levels]
            mixed = sum(value.astype(jnp.float32) * weight for value, weight in zip(values, weights))
            out[:, :, columns] = (mixed / (weights[0] + weights[1] + weights[2])).astype(
                jnp.bfloat16
            )

        @pl.when(across & (position < plan.most))
        def _(position=position, columns=columns, head=head):
            join((left, right), position, columns, head)

        @pl.when(across & (position >= plan.most))
        def _(position=position, columns=columns, head=head):
            join((left_rest, right_rest), position - plan.most, columns, head)


def combine(plan, vector, near, sides):
    frames, tokens, _ = near.shape
    heads = plan.heads // plan.order
    spec = pl.BlockSpec((frames, tokens, heads * HD), lambda h, _: (0, 0, h))
    stat_spec = pl.BlockSpec((frames, tokens, HD), lambda h, _: (0, 0, plan.heads))
    return pl.pallas_call(
        partial(combine_kernel, plan=plan, heads=heads),
        grid_spec=pltpu.PrefetchScalarGridSpec(
            num_scalar_prefetch=1,
            grid=(plan.order,),
            in_specs=[spec, stat_spec]
            + [pl.BlockSpec(side.shape, lambda h, _: (0, 0, 0)) for side in sides],
            out_specs=pl.BlockSpec(
                (frames, tokens, heads * HD), lambda h, vector: (0, 0, h ^ plan.edge(vector, 4))
            ),
        ),
        out_shape=jax.ShapeDtypeStruct((frames, tokens, plan.heads * HD), jnp.bfloat16),
        compiler_params=kernel_params(),
        cost_estimate=LARGE,
        name="combine",
    )(vector, near, near, *sides)


def project_kernel(place, attended, *refs, slots, carried, start, column):
    arrays = 1 + max(piece[0] for slot in slots for piece in slot)
    pieces, refs = refs[:arrays], refs[arrays:]
    if carried:
        carry, refs = refs[: len(slots)], refs[len(slots) :]
    outs, (rows, weight, rows_sem, weight_sem) = refs[: len(slots)], refs[len(slots) :]
    columns = weight.shape[1]
    depth = weight.shape[2]
    rows_copy = pltpu.make_async_copy(
        attended.at[:, start : start + depth], rows, rows_sem.at[0]
    )
    rows_copy.start()
    for index, slot in enumerate(slots):
        for block in range(columns):
            low = 0
            for number, (array, size, share, turned) in enumerate(slot):
                first = pl.multiple_of((place[0] ^ share if turned else share) * size, size)
                pltpu.make_async_copy(
                    pieces[array].at[pl.ds(first, size), block * column : (block + 1) * column],
                    weight.at[index, block, low : low + size],
                    weight_sem.at[index, block, number],
                ).start()
                low += size
    rows_copy.wait()
    for index, slot in enumerate(slots):

        def body(block, _, index=index, slot=slot):
            low = 0
            for number, (_, size, _, _) in enumerate(slot):
                piece = weight.at[index, block, low : low + size]
                pltpu.make_async_copy(piece, piece, weight_sem.at[index, block, number]).wait()
                low += size
            total = jnp.dot(rows[...], weight[index, block], preferred_element_type=jnp.float32)
            here = pl.ds(pl.multiple_of(block * column, column), column)
            if carried:
                total = total + carry[index][0, :, here]
            outs[index][0, :, here] = total.astype(outs[index].dtype)
            return 0

        lax.fori_loop(0, columns, body, 0)


def project(place, attended, arrays, slots, carry, start, dtype):
    tokens = attended.shape[0]
    width = arrays[0].shape[1]
    column = 256 if width % 256 == 0 else width
    columns = width // column
    depth = sum(piece[1] for piece in slots[0])
    anywhere = pl.BlockSpec(memory_space=pl.ANY)
    inside = pl.BlockSpec(memory_space=pltpu.VMEM)
    return pl.pallas_call(
        partial(
            project_kernel, slots=slots, carried=carry is not None, start=start, column=column
        ),
        in_specs=[pl.BlockSpec(memory_space=pltpu.SMEM), anywhere]
        + [anywhere] * len(arrays)
        + ([] if carry is None else [inside] * len(slots)),
        out_specs=[inside] * len(slots),
        out_shape=[jax.ShapeDtypeStruct((1, tokens, width), dtype)] * len(slots),
        scratch_shapes=[
            pltpu.VMEM((tokens, depth), attended.dtype),
            pltpu.VMEM((len(slots), columns, depth, column), attended.dtype),
            pltpu.SemaphoreType.DMA((1,)),
            pltpu.SemaphoreType.DMA((len(slots), columns, max(len(slot) for slot in slots))),
        ],
        compiler_params=pltpu.CompilerParams(vmem_limit_bytes=VMEM_LIMIT),
        cost_estimate=SMALL,
        name="project",
    )(place, attended, *arrays, *([] if carry is None else carry))


def pick_kernel(place, own_hidden, other_hidden, own_gate, other_gate, hidden, gate):
    mine = place[2 * pl.program_id(0)] != 0

    @pl.when(mine)
    def _():
        hidden[0] = own_hidden[...]
        gate[0] = own_gate[...]

    @pl.when(jnp.logical_not(mine))
    def _():
        hidden[0] = other_hidden[...]
        gate[0] = other_gate[...]


def pick(place, own_hidden, other_hidden, own_gate, other_gate, width):
    tokens, features = own_hidden.shape
    count = 2 * features // width
    hidden = pl.BlockSpec((tokens, width), lambda i, place: (0, place[2 * i + 1]))
    gate = pl.BlockSpec((1, width), lambda i, place: (0, place[2 * i + 1]))
    return pl.pallas_call(
        pick_kernel,
        grid_spec=pltpu.PrefetchScalarGridSpec(
            num_scalar_prefetch=1,
            grid=(count,),
            in_specs=[hidden, hidden, gate, gate],
            out_specs=[
                pl.BlockSpec((1, tokens, width), lambda i, place: (i, 0, 0)),
                pl.BlockSpec((1, 1, width), lambda i, place: (i, 0, 0)),
            ],
        ),
        out_shape=[
            jax.ShapeDtypeStruct((count, tokens, width), jnp.bfloat16),
            jax.ShapeDtypeStruct((count, 1, width), jnp.float32),
        ],
        compiler_params=kernel_params(),
        cost_estimate=SMALL,
        name="pick",
    )(place, own_hidden, other_hidden, own_gate, other_gate)


def mixed_blocks(hidden, gate, first, own_parts, other_parts):
    return [
        hidden[index].astype(jnp.float32)
        + gate[first + index]
        * (own_part[0].astype(jnp.float32) + other_part[0].astype(jnp.float32))
        for index, (own_part, other_part) in enumerate(zip(own_parts, other_parts))
    ]


def mix_kernel(hidden, gate, *refs, count):
    own_parts, other_parts, (mixed_ref, sums_ref) = (
        refs[:count],
        refs[count : 2 * count],
        refs[2 * count :],
    )
    first = second = 0.0
    for index, mixed in enumerate(mixed_blocks(hidden, gate, 0, own_parts, other_parts)):
        mixed_ref[index] = mixed.astype(jnp.bfloat16)
        first = first + jnp.sum(mixed, axis=1, keepdims=True)
        second = second + jnp.sum(mixed * mixed, axis=1, keepdims=True)
    lane = lax.broadcasted_iota(jnp.int32, sums_ref.shape, 1)
    sums_ref[...] = jnp.where(lane == 0, first, jnp.where(lane == 1, second, 0.0))


def mix(hidden, gate, own_parts, other_parts):
    count = len(own_parts)
    _, tokens, width = hidden.shape
    rows = 64 if tokens % 64 == 0 else tokens
    part = pl.BlockSpec((1, rows, width), lambda i: (0, i, 0))
    several = pl.BlockSpec((count, rows, width), lambda i: (0, i, 0))
    return pl.pallas_call(
        partial(mix_kernel, count=count),
        grid=(tokens // rows,),
        in_specs=[several, pl.BlockSpec(gate.shape, lambda i: (0, 0, 0))] + [part] * (2 * count),
        out_specs=[several, pl.BlockSpec((rows, LANES), lambda i: (i, 0))],
        out_shape=[
            jax.ShapeDtypeStruct((count, tokens, width), jnp.bfloat16),
            jax.ShapeDtypeStruct((tokens, LANES), jnp.float32),
        ],
        compiler_params=kernel_params(),
        cost_estimate=SMALL,
        name="mix",
    )(hidden, gate, *own_parts, *other_parts)


def finish_kernel(place, gate, scale, shift_by, sums, early, *refs, count, blocks):
    hidden, own_parts, other_parts = (refs[count * k : count * (k + 1)] for k in range(3))
    residual, ffn = refs[3 * count :]
    width = early.shape[2]
    late = [
        block
        for index in range(count)
        for block in mixed_blocks(
            hidden[index], gate, 1 + index, own_parts[index : index + 1], other_parts[index : index + 1]
        )
    ]
    first = sums[:, 0:1]
    second = sums[:, 1:2]
    for mixed in late:
        first = first + jnp.sum(mixed, axis=1, keepdims=True)
        second = second + jnp.sum(mixed * mixed, axis=1, keepdims=True)
    average = first / D
    variance = second / D - average * average
    inverse = lax.rsqrt(variance + EPSILON)
    for block in range(blocks):
        columns = slice(block * width, (block + 1) * width)
        mixed = early[0].astype(jnp.float32)
        for index in range(count):
            mixed = jnp.where(place[block] == 1 + index, late[index], mixed)
        residual[:, columns] = mixed.astype(jnp.bfloat16)
        ffn[:, columns] = (
            (mixed - average) * inverse * (1.0 + scale[:, columns]) + shift_by[:, columns]
        ).astype(jnp.bfloat16)


def finish(place, hidden, gate, scale, shift_by, sums, early, own_parts, other_parts):
    count = len(own_parts)
    _, tokens, width = hidden.shape
    blocks = place.shape[0]
    rows = 64 if tokens % 64 == 0 else tokens
    part = pl.BlockSpec((1, rows, width), lambda i, place: (0, i, 0))
    whole = pl.BlockSpec((1, blocks * width), lambda i, place: (0, 0))
    row = pl.BlockSpec((rows, blocks * width), lambda i, place: (i, 0))
    later = [
        pl.BlockSpec((1, rows, width), lambda i, place, index=index: (1 + index, i, 0))
        for index in range(count)
    ]
    return pl.pallas_call(
        partial(finish_kernel, count=count, blocks=blocks),
        grid_spec=pltpu.PrefetchScalarGridSpec(
            num_scalar_prefetch=1,
            grid=(tokens // rows,),
            in_specs=[pl.BlockSpec(gate.shape, lambda i, place: (0, 0, 0)), whole, whole]
            + [pl.BlockSpec((rows, LANES), lambda i, place: (i, 0)), part]
            + later
            + [part] * (2 * count),
            out_specs=[row, row],
        ),
        out_shape=[jax.ShapeDtypeStruct((tokens, blocks * width), jnp.bfloat16)] * 2,
        compiler_params=kernel_params(),
        cost_estimate=SMALL,
        name="finish",
    )(place, gate, scale, shift_by, sums, early, *[hidden] * count, *own_parts, *other_parts)


def shift(block, axis, step):
    count = lax.axis_size(axis)
    pairs = [(i, i + step) for i in range(count) if 0 <= i + step < count]
    return lax.ppermute(block, axis, pairs)


def turn(block, axis, step):
    count = lax.axis_size(axis)
    return lax.ppermute(block, axis, [(i, (i + step) % count) for i in range(count)])


def swap(block, axis, bit):
    count = lax.axis_size(axis)
    return lax.ppermute(block, axis, [(i, i ^ bit) for i in range(count)])


class Tokens:
    def __init__(self, queries, keys_values, windows, order):
        self.plan = Plan(windows, order)
        self.queries = queries.reshape(queries.shape[0], -1, queries.shape[3])
        self.keys_values = keys_values.reshape(*keys_values.shape[:2], -1, keys_values.shape[4])
        self.span = TILE * queries.shape[2]
        self.parts = (0, self.plan.most), (self.plan.most, self.plan.heads - self.plan.most)

    def edge_rows(self, vector, part):
        low = self.queries.shape[1] - self.span
        rows = [(low, self.span), (0, self.span)]
        return pack(vector, self.keys_values, self.plan.row_head, *self.parts[part], rows)

    def leaving(self, vector, part):
        rows = [(0, self.queries.shape[1])]
        return pack(vector, self.queries, self.plan.col_head, *self.parts[part], rows)[0]

    def halos(self, rows):
        return shift(rows[0], "ha", 1), shift(rows[1], "ha", -1)

    def rest_halos(self, vector):
        shape = (*self.keys_values.shape[:2], self.span, self.parts[1][1] * HD)
        return lax.cond(
            self.plan.more_rows,
            lambda vector: self.halos(self.edge_rows(vector, 1)),
            lambda vector: (jnp.zeros(shape, jnp.bfloat16),) * 2,
            vector,
        )

    def stay(self, vector, halos):
        return attention(self.plan, vector, [self.queries], self.keys_values, halos)[0]

    def visit(self, vector, visitors, halos, part=0):
        first = self.parts[part][0]
        return attention(self.plan, vector, visitors, self.keys_values, halos, first)

    def rest_sides(self, vector, halos):
        shape = (*self.queries.shape[:2], (self.parts[1][1] + 1) * HD)

        def send(vector, *halos):
            queries = self.leaving(vector, 1)
            visitors = shift(queries, "wa", 1), shift(queries, "wa", -1)
            for_left, for_right = self.visit(vector, visitors, halos, 1)
            return shift(for_right, "wa", 1), shift(for_left, "wa", -1)

        return lax.cond(
            self.plan.more_cols,
            send,
            lambda vector, *halos: (jnp.zeros(shape, jnp.bfloat16),) * 2,
            vector,
            *halos,
        )

    def combine(self, vector, near, sides):
        attended = combine(self.plan, vector, near, sides)
        return attended.reshape(-1, attended.shape[2])


def together(*blocks):
    return lax.optimization_barrier(blocks)


def paired(hidden, queries, keys_values, windows, out_weight, picked):
    ha, wa, ta = lax.axis_index("ha"), lax.axis_index("wa"), lax.axis_index("ta")
    n_wa = lax.axis_size("wa")
    blocks = n_wa // 2
    depth = out_weight.shape[0] // 4
    width = out_weight.shape[1]

    def share(number):
        return lax.dynamic_slice_in_dim(out_weight, number * depth, depth, 0)

    mine = lax.optimization_barrier(share(ha))
    first = turn(mine, "wa", 1)
    tokens = Tokens(queries, keys_values, windows, 4)
    vector = tokens.plan.vector
    top, bottom = tokens.halos(tokens.edge_rows(vector, 0))
    queries = tokens.leaving(vector, 0)
    from_left = shift(queries, "wa", 1)
    from_right = shift(queries, "wa", -1)

    first, top, bottom, vector, mine = together(first, top, bottom, vector, mine)
    first_x = swap(first, "ha", 1)
    first_y = swap(first, "ha", 2)
    third = turn(mine, "wa", -1)
    halos = top, bottom, *tokens.rest_halos(vector)
    near = tokens.stay(vector, halos)

    near, first_x, first_y, third, from_left, from_right, first, gate, hidden = together(
        near, first_x, first_y, third, from_left, from_right, first, picked[0:1], hidden
    )
    third_x = swap(third, "ha", 1)
    third_y = swap(third, "ha", 2)
    second = turn(first, "wa", 1)
    other_gate = swap(gate, "ta", 1)
    other_hidden = swap(hidden, "ta", 1)
    for_left, for_right = tokens.visit(vector, (from_left, from_right), halos)

    for_left, for_right, other_gate, other_hidden = together(
        for_left, for_right, other_gate, other_hidden
    )
    left = shift(for_right, "wa", 1)
    right = shift(for_left, "wa", -1)

    third_x, third_y, second, other_gate, vector = together(
        third_x, third_y, second, other_gate, vector
    )
    second_x = swap(second, "ha", 1)
    second_y = swap(second, "ha", 2)
    rest_sides = tokens.rest_sides(vector, halos)

    def block_of(distance):
        return lax.rem(wa - distance + n_wa, n_wa)

    owners = jnp.stack([block_of(distance) // blocks == ta for distance in range(n_wa)])
    inner = jnp.stack([lax.rem(block_of(distance), blocks) for distance in range(n_wa)])
    place = jnp.stack([owners.astype(jnp.int32), inner], axis=1).reshape(-1)
    base, gates = pick(place, hidden, other_hidden, gate, other_gate, width)
    left, right, base, gates = together(left, right, base, gates)
    attended = tokens.combine(vector, near, [left, right, *rest_sides])

    second_x, second_y, first_y, attended = together(second_x, second_y, first_y, attended)
    first_far = swap(first_y, "ha", 1)
    second_far = swap(second_x, "ha", 2)
    third_far = turn(share(ha ^ 3), "wa", -1)

    turned = ha.reshape(1)
    sums = project(
        turned,
        attended,
        [out_weight],
        [[(0, depth, number, True) for number in range(4)]],
        None,
        0,
        jnp.bfloat16,
    )
    other_sums = [swap(part, "ta", 1) for part in sums]
    late = project(
        turned,
        attended,
        [first, first_x, first_y, second, second_x, second_y, third, third_x, third_y],
        [[(start + number, depth, 0, False) for number in range(3)] for start in (0, 3, 6)],
        None,
        0,
        jnp.float32,
    )
    early, totals = mix(base, gates, sums, other_sums)

    first_far, second_far, third_far, early, totals, *late = together(
        first_far, second_far, third_far, early, totals, *late
    )
    late = project(
        turned,
        attended,
        [first_far, second_far, third_far],
        [[(number, depth, 0, False)] for number in range(3)],
        late,
        3 * depth,
        jnp.bfloat16,
    )
    other_late = [swap(part, "ta", 1) for part in late]
    place = jnp.stack(
        [lax.rem(wa - ta * blocks - block + 2 * n_wa, n_wa) for block in range(blocks)]
    )
    return finish(
        place, base, gates, picked[2:3], picked[1:2], totals, early, late, other_late
    )


def gathered(hidden, queries, keys_values, windows, out_weight, picked):
    n_ha, n_wa, n_ta = lax.axis_size("ha"), lax.axis_size("wa"), lax.axis_size("ta")
    ha, ta = lax.axis_index("ha"), lax.axis_index("ta")
    work = Tokens(queries, keys_values, windows, 1)
    vector = work.plan.vector
    halos = *work.halos(work.edge_rows(vector, 0)), *work.rest_halos(vector)
    sent = work.leaving(vector, 0)
    visitors = shift(sent, "wa", 1), shift(sent, "wa", -1)
    near = work.stay(vector, halos)
    for_left, for_right = work.visit(vector, visitors, halos)
    sides = shift(for_right, "wa", 1), shift(for_left, "wa", -1)
    attended = work.combine(vector, near, [*sides, *work.rest_sides(vector, halos)])
    tokens, features = attended.shape
    depth = features // n_ha
    width = out_weight.shape[1]
    share = lax.dynamic_slice_in_dim(out_weight, ha * depth, depth, 0)
    weights = lax.all_gather(share, ("ha", "wa"), axis=0, tiled=False).reshape(
        n_ha, n_wa, depth, width
    )
    partial_sums = jnp.einsum(
        "thk,hwkc->wtc",
        attended.reshape(tokens, n_ha, depth),
        weights,
        preferred_element_type=jnp.float32,
    ).astype(jnp.bfloat16)
    blocks = n_wa // n_ta
    summed = None
    for step in range(n_ta):
        target = lax.rem(ta + step, n_ta)
        piece = lax.dynamic_slice_in_dim(partial_sums, target * blocks, blocks, 0)
        if step:
            piece = turn(piece, "ta", step)
        piece = piece.astype(jnp.float32)
        summed = piece if summed is None else summed + piece
    summed = jnp.transpose(summed, (1, 0, 2)).reshape(tokens, -1)
    mixed = hidden.astype(jnp.float32) + picked[0] * summed
    sum_first, sum_second = lax.psum((jnp.sum(mixed, axis=1), jnp.sum(mixed * mixed, axis=1)), "ta")
    average = (sum_first / D)[:, None]
    variance = (sum_second / D)[:, None] - average * average
    normed = (mixed - average) * lax.rsqrt(variance + EPSILON)
    ffn_input = (normed * (1.0 + picked[2]) + picked[1]).astype(jnp.bfloat16)
    return mixed.astype(jnp.bfloat16), ffn_input


def shards(hidden_states, queries, keys_values, out_weight, mod_table, windows, step_index):
    tokens = math.prod(queries.shape[:3])
    width = hidden_states.shape[3]
    picked = lax.dynamic_index_in_dim(mod_table, step_index[0], 0, keepdims=False)
    sizes = lax.axis_size("ha"), lax.axis_size("wa"), lax.axis_size("ta")
    tuned = sizes == (4, 4, 2) and out_weight.shape[0] % (20 * LANES) == 0
    residual_out, ffn_input = (paired if tuned else gathered)(
        hidden_states.reshape(tokens, width), queries, keys_values, windows, out_weight, picked
    )
    return residual_out.reshape(hidden_states.shape), ffn_input.reshape(hidden_states.shape)


def solution(mesh):
    return jax.shard_map(
        shards,
        mesh=mesh,
        in_specs=(
            P(None, "ha", "wa", "ta"),
            P(None, "ha", "wa", "ta"),
            P(None, None, "ha", "wa", "ta"),
            P("ta", "wa"),
            P(None, None, "ta"),
            P("ta", None),
            P(),
        ),
        out_specs=(P(None, "ha", "wa", "ta"), P(None, "ha", "wa", "ta")),
        check_vma=False,
    )
```

```python
from functools import partial
import math

import jax
import jax.numpy as jnp
from jax import lax
from jax.experimental import pallas as pl
from jax.experimental.pallas import tpu as pltpu
from jax.sharding import PartitionSpec as P

D = 5120
HD = 128
TILE = 8
LANES = 128
LEVEL_STEP = 32

EPSILON = 1e-06
VMEM_LIMIT = 24 * 1024 * 1024
SMALL = pl.CostEstimate(flops=1, bytes_accessed=1, transcendentals=0)
LARGE = pl.CostEstimate(flops=20_000_000_000, bytes_accessed=1, transcendentals=0)


def kernel_params(limit=VMEM_LIMIT):
    return pltpu.CompilerParams(dimension_semantics=("arbitrary",), vmem_limit_bytes=limit)


class Plan:
    def __init__(self, windows, order):
        heads = windows.shape[0]
        self.heads = heads
        self.most = max(heads * 7 // 10, 1)
        self.order = order
        n_ha, n_wa = lax.axis_size("ha"), lax.axis_size("wa")
        ha, wa = lax.axis_index("ha"), lax.axis_index("wa")
        number = lax.broadcasted_iota(jnp.int32, (2, heads, heads), 1)
        other = lax.broadcasted_iota(jnp.int32, (2, heads, heads), 2)
        idle = jnp.where(windows.T > 0, 0, 1)
        before = (idle[:, None, :] < idle[:, :, None]) | (
            (idle[:, None, :] == idle[:, :, None]) & (other < number)
        )
        position = jnp.sum(before.astype(jnp.int32), axis=2)
        sorted_heads = jnp.sum(jnp.where(position[:, None, :] == number, other, 0), axis=2)
        turned = ha if order > 1 else 0 * ha
        edges = jnp.stack([ha > 0, ha < n_ha - 1, wa > 0, wa < n_wa - 1, turned]).astype(jnp.int32)
        self.vector = jnp.concatenate(
            [windows.T.reshape(-1), position.reshape(-1), sorted_heads.reshape(-1), edges]
        )
        counts = lax.pmax(jnp.sum(1.0 - idle, axis=1), "ta")
        self.more_rows = counts[0] > self.most
        self.more_cols = counts[1] > self.most

    def row_radius(self, vector, head):
        return vector[head]

    def col_radius(self, vector, head):
        return vector[self.heads + head]

    def row_position(self, vector, head):
        return vector[2 * self.heads + head]

    def col_position(self, vector, head):
        return vector[3 * self.heads + head]

    def row_head(self, vector, position):
        return vector[4 * self.heads + position]

    def col_head(self, vector, position):
        return vector[5 * self.heads + position]

    def edge(self, vector, number):
        return vector[6 * self.heads + number]


def pack_kernel(vector, source, *refs, head_of, first, rows):
    outs, sem = refs[:-1], refs[-1]
    copies = []
    for number, (out, (low, size)) in enumerate(zip(outs, rows)):
        for slot in range(out.shape[-1] // HD):
            start = pl.multiple_of(head_of(vector, first + slot) * HD, HD)
            lead = (slice(None),) * (len(source.shape) - 2)
            copies.append(
                pltpu.make_async_copy(
                    source.at[(*lead, pl.ds(low, size), pl.ds(start, HD))],
                    out.at[(*lead, slice(None), pl.ds(slot * HD, HD))],
                    sem.at[number, slot],
                )
            )
    for copy in copies:
        copy.start()
    for copy in copies:
        copy.wait()


def pack(vector, source, head_of, first, count, rows):
    anywhere = pl.BlockSpec(memory_space=pl.ANY)
    return pl.pallas_call(
        partial(pack_kernel, head_of=head_of, first=first, rows=rows),
        in_specs=[pl.BlockSpec(memory_space=pltpu.SMEM), anywhere],
        out_specs=[pl.BlockSpec(memory_space=pltpu.VMEM)] * len(rows),
        out_shape=[
            jax.ShapeDtypeStruct((*source.shape[:-2], size, count * HD), source.dtype)
            for _, size in rows
        ],
        scratch_shapes=[pltpu.SemaphoreType.DMA((len(rows), count))],
        compiler_params=pltpu.CompilerParams(vmem_limit_bytes=VMEM_LIMIT),
        cost_estimate=SMALL,
        name="pack",
    )(vector, source)


def attention_kernel(vector, *refs, plan, head_of, q_count, visiting, group):
    q_refs = refs[:q_count]
    kv_ref, top_ref, bottom_ref, top_rest, bottom_rest = refs[q_count : q_count + 5]
    refs = refs[q_count + 5 :]
    out_refs, stat_refs, halo = refs[:q_count], refs[q_count : 2 * q_count], refs[2 * q_count]
    frames, tokens, head_size = q_refs[0].shape
    span = top_ref.shape[2]
    tiles = tokens // span
    step = pl.program_id(0)
    head = head_of(vector, step)
    radius_row = plan.row_radius(vector, head)
    radius_col = plan.col_radius(vector, head)
    scale = 1.0 / math.sqrt(HD)

    @pl.when(step == 0)
    def _():
        for stat_ref in stat_refs:
            stat_ref[...] = jnp.zeros_like(stat_ref)

    def near(which, tile, wide):
        if not wide:
            return kv_ref[which, :, tile * span : (tile + 1) * span, :].reshape(-1, head_size)
        pieces = []
        if tile == 0:
            pieces.append(halo[0, which])
        low = max(tile - 1, 0) * span
        high = min(tile + 2, tiles) * span
        pieces.append(kv_ref[which, :, low:high, :])
        if tile == tiles - 1:
            pieces.append(halo[1, which])
        block = pieces[0] if len(pieces) == 1 else jnp.concatenate(pieces, axis=1)
        return block.reshape(-1, head_size)

    def attend(wide):
        lane = lax.broadcasted_iota(jnp.int32, (frames, span, LANES), 2)
        for tile in range(tiles):
            rows = slice(tile * span, (tile + 1) * span)
            keys = near(0, tile, wide)
            values = near(1, tile, wide)
            bias = None
            if wide and (tile == 0 or tile == tiles - 1):
                place = lax.rem(
                    lax.broadcasted_iota(jnp.int32, (1, keys.shape[0]), 1), 3 * span
                )
                low, high = 0, 3 * span
                if tile == 0:
                    low = jnp.where(plan.edge(vector, 0) == 0, span, 0)
                if tile == tiles - 1:
                    high = jnp.where(plan.edge(vector, 1) == 0, 2 * span, 3 * span)
                bias = jnp.where((place >= low) & (place < high), 0.0, -jnp.inf)
            for q_ref, out_ref, stat_ref in zip(q_refs, out_refs, stat_refs):
                query = q_ref[:, rows, :].reshape(-1, head_size)
                scores = (
                    lax.dot_general(
                        query, keys, (((1,), (1,)), ((), ())), preferred_element_type=jnp.float32
                    )
                    * scale
                )
                if bias is not None:
                    scores = scores + bias
                highest = jnp.max(scores, axis=1, keepdims=True)
                expo = jnp.exp(scores - highest)
                total = jnp.sum(expo, axis=1, keepdims=True)
                output = jnp.dot(
                    expo.astype(jnp.bfloat16), values, preferred_element_type=jnp.float32
                ) * (1.0 / total)
                out_ref[:, rows, :] = output.astype(jnp.bfloat16).reshape(frames, span, head_size)
                level = (highest + jnp.log(total)).reshape(frames, span, 1)
                stat_ref[:, rows, :] = jnp.where(lane == step, level, stat_ref[:, rows, :])

    active = step < group
    if visiting:

        @pl.when(active & (radius_col == 0))
        def _():
            for out_ref in out_refs:
                out_ref[...] = jnp.zeros_like(out_ref)

        active = active & (radius_col != 0)

    @pl.when(active & (radius_row == 0))
    def _():
        attend(False)

    always = plan.row_position(vector, head) < plan.most

    @pl.when(active & (radius_row != 0) & always)
    def _():
        halo[0] = top_ref[...]
        halo[1] = bottom_ref[...]

    @pl.when(active & (radius_row != 0) & jnp.logical_not(always))
    def _():
        halo[0] = top_rest[...]
        halo[1] = bottom_rest[...]

    @pl.when(active & (radius_row != 0))
    def _():
        attend(True)

    @pl.when(step == group)
    def _():
        for out_ref, stat_ref in zip(out_refs, stat_refs):
            level = stat_ref[...]
            high = level.astype(jnp.bfloat16).astype(jnp.float32)
            middle = (level - high).astype(jnp.bfloat16).astype(jnp.float32)
            low = level - high - middle
            packed = high + pltpu.roll(middle, LEVEL_STEP, 2) + pltpu.roll(low, 2 * LEVEL_STEP, 2)
            out_ref[...] = packed.astype(jnp.bfloat16)


def attention(plan, vector, query_blocks, keys_values, halos, first=None):
    frames, tokens, features = query_blocks[0].shape
    group = features // HD
    span = halos[0].shape[2]
    q_count = len(query_blocks)
    visiting = first is not None

    def slot_of(step):
        return jnp.minimum(step, group - 1)

    def head_of(vector, step):
        return plan.col_head(vector, first + slot_of(step)) if visiting else slot_of(step)

    def kv_index(step, vector):
        return 0, 0, 0, head_of(vector, step)

    def halo_index(step, vector):
        position = plan.row_position(vector, head_of(vector, step))
        return 0, 0, 0, jnp.minimum(position, plan.most - 1)

    def rest_index(step, vector):
        position = plan.row_position(vector, head_of(vector, step))
        return 0, 0, 0, jnp.maximum(position - plan.most, 0)

    q_spec = pl.BlockSpec((frames, tokens, HD), lambda step, _: (0, 0, slot_of(step)))
    kv_spec = pl.BlockSpec((2, frames, tokens, HD), kv_index)
    halo_spec = pl.BlockSpec((2, frames, span, HD), halo_index)
    rest_spec = pl.BlockSpec((2, frames, span, HD), rest_index)
    out_spec = pl.BlockSpec((frames, tokens, HD), lambda step, _: (0, 0, step))
    return pl.pallas_call(
        partial(
            attention_kernel,
            plan=plan,
            head_of=head_of,
            q_count=q_count,
            visiting=visiting,
            group=group,
        ),
        grid_spec=pltpu.PrefetchScalarGridSpec(
            num_scalar_prefetch=1,
            grid=(group + 1,),
            in_specs=[q_spec] * q_count + [kv_spec] + [halo_spec] * 2 + [rest_spec] * 2,
            out_specs=[out_spec] * q_count,
            scratch_shapes=[pltpu.VMEM((frames, tokens, LANES), jnp.float32)] * q_count
            + [pltpu.VMEM((2, 2, frames, span, HD), jnp.bfloat16)],
        ),
        out_shape=[jax.ShapeDtypeStruct((frames, tokens, (group + 1) * HD), jnp.bfloat16)]
        * q_count,
        compiler_params=kernel_params(),
        cost_estimate=SMALL if visiting else LARGE,
        name="attend_visitors" if visiting else "attend_own",
    )(vector, *query_blocks, keys_values, *halos)


def combine_kernel(vector, own, own_stat, left, right, left_rest, right_rest, out, *, plan, heads):
    first = pl.program_id(0) * heads
    frames, tokens, _ = own.shape

    def level(stat, number):
        lane = lax.broadcasted_iota(jnp.int32, (LANES, HD), 0)
        pick = jnp.where(
            (lax.rem(lane, LEVEL_STEP) == number) & (lane < 3 * LEVEL_STEP), 1.0, 0.0
        ).astype(jnp.bfloat16)
        return jnp.dot(
            stat.reshape(-1, LANES), pick, preferred_element_type=jnp.float32
        ).reshape(frames, tokens, HD)

    for index in range(heads):
        head = first + index
        columns = slice(index * HD, (index + 1) * HD)
        across = plan.col_radius(vector, head) != 0
        position = plan.col_position(vector, head)

        @pl.when(jnp.logical_not(across))
        def _(columns=columns):
            out[:, :, columns] = own[:, :, columns]

        def join(sides, slot, columns, head):
            here = pl.ds(pl.multiple_of(slot * HD, HD), HD)
            levels = [level(own_stat[...], head)]
            values = [own[:, :, columns]]
            for number, side in enumerate(sides):
                value = level(side[:, :, side.shape[2] - LANES :], slot)
                levels.append(jnp.where(plan.edge(vector, 2 + number) == 0, -jnp.inf, value))
                values.append(side[:, :, here])
            highest = jnp.maximum(levels[0], jnp.maximum(levels[1], levels[2]))
            weights = [jnp.exp(x - highest) for x in levels]
            mixed = sum(value.astype(jnp.float32) * weight for value, weight in zip(values, weights))
            out[:, :, columns] = (mixed / (weights[0] + weights[1] + weights[2])).astype(
                jnp.bfloat16
            )

        @pl.when(across & (position < plan.most))
        def _(position=position, columns=columns, head=head):
            join((left, right), position, columns, head)

        @pl.when(across & (position >= plan.most))
        def _(position=position, columns=columns, head=head):
            join((left_rest, right_rest), position - plan.most, columns, head)


def combine(plan, vector, near, sides):
    frames, tokens, _ = near.shape
    heads = plan.heads // plan.order
    spec = pl.BlockSpec((frames, tokens, heads * HD), lambda h, _: (0, 0, h))
    stat_spec = pl.BlockSpec((frames, tokens, HD), lambda h, _: (0, 0, plan.heads))
    return pl.pallas_call(
        partial(combine_kernel, plan=plan, heads=heads),
        grid_spec=pltpu.PrefetchScalarGridSpec(
            num_scalar_prefetch=1,
            grid=(plan.order,),
            in_specs=[spec, stat_spec]
            + [pl.BlockSpec(side.shape, lambda h, _: (0, 0, 0)) for side in sides],
            out_specs=pl.BlockSpec(
                (frames, tokens, heads * HD), lambda h, vector: (0, 0, h ^ plan.edge(vector, 4))
            ),
        ),
        out_shape=jax.ShapeDtypeStruct((frames, tokens, plan.heads * HD), jnp.bfloat16),
        compiler_params=kernel_params(),
        cost_estimate=LARGE,
        name="combine",
    )(vector, near, near, *sides)


def project_kernel(place, attended, *refs, slots, carried, start, column):
    arrays = 1 + max(piece[0] for slot in slots for piece in slot)
    pieces, refs = refs[:arrays], refs[arrays:]
    if carried:
        carry, refs = refs[0], refs[1:]
    out, rows, weight, rows_sem, weight_sem = refs
    columns = weight.shape[1]
    depth = weight.shape[2]
    rows_copy = pltpu.make_async_copy(
        attended.at[:, start : start + depth], rows, rows_sem.at[0]
    )
    rows_copy.start()
    for index, slot in enumerate(slots):
        for block in range(columns):
            low = 0
            for number, (array, size, share, turned) in enumerate(slot):
                first = pl.multiple_of((place[0] ^ share if turned else share) * size, size)
                pltpu.make_async_copy(
                    pieces[array].at[pl.ds(first, size), block * column : (block + 1) * column],
                    weight.at[index, block, low : low + size],
                    weight_sem.at[index, block, number],
                ).start()
                low += size
    rows_copy.wait()
    for index, slot in enumerate(slots):

        def body(block, _, index=index, slot=slot):
            low = 0
            for number, (_, size, _, _) in enumerate(slot):
                piece = weight.at[index, block, low : low + size]
                pltpu.make_async_copy(piece, piece, weight_sem.at[index, block, number]).wait()
                low += size
            total = jnp.dot(rows[...], weight[index, block], preferred_element_type=jnp.float32)
            here = pl.ds(pl.multiple_of(block * column, column), column)
            if carried:
                total = total + carry[index, :, here]
            out[index, :, here] = total.astype(out.dtype)
            return 0

        lax.fori_loop(0, columns, body, 0)


def project(place, attended, arrays, slots, carry, start, dtype):
    tokens = attended.shape[0]
    width = arrays[0].shape[1]
    column = 256 if width % 256 == 0 else width
    columns = width // column
    depth = sum(piece[1] for piece in slots[0])
    anywhere = pl.BlockSpec(memory_space=pl.ANY)
    inside = pl.BlockSpec(memory_space=pltpu.VMEM)
    return pl.pallas_call(
        partial(
            project_kernel, slots=slots, carried=carry is not None, start=start, column=column
        ),
        in_specs=[pl.BlockSpec(memory_space=pltpu.SMEM), anywhere]
        + [anywhere] * len(arrays)
        + ([] if carry is None else [inside]),
        out_specs=inside,
        out_shape=jax.ShapeDtypeStruct((len(slots), tokens, width), dtype),
        scratch_shapes=[
            pltpu.VMEM((tokens, depth), attended.dtype),
            pltpu.VMEM((len(slots), columns, depth, column), attended.dtype),
            pltpu.SemaphoreType.DMA((1,)),
            pltpu.SemaphoreType.DMA((len(slots), columns, max(len(slot) for slot in slots))),
        ],
        compiler_params=pltpu.CompilerParams(vmem_limit_bytes=VMEM_LIMIT),
        cost_estimate=SMALL,
        name="project",
    )(place, attended, *arrays, *([] if carry is None else [carry]))


def pick_kernel(place, own_hidden, other_hidden, own_gate, other_gate, hidden, gate):
    mine = place[2 * pl.program_id(0)] != 0

    @pl.when(mine)
    def _():
        hidden[0] = own_hidden[...]
        gate[0] = own_gate[...]

    @pl.when(jnp.logical_not(mine))
    def _():
        hidden[0] = other_hidden[...]
        gate[0] = other_gate[...]


def pick(place, own_hidden, other_hidden, own_gate, other_gate, width):
    tokens, features = own_hidden.shape
    count = 2 * features // width
    hidden = pl.BlockSpec((tokens, width), lambda i, place: (0, place[2 * i + 1]))
    gate = pl.BlockSpec((1, width), lambda i, place: (0, place[2 * i + 1]))
    return pl.pallas_call(
        pick_kernel,
        grid_spec=pltpu.PrefetchScalarGridSpec(
            num_scalar_prefetch=1,
            grid=(count,),
            in_specs=[hidden, hidden, gate, gate],
            out_specs=[
                pl.BlockSpec((1, tokens, width), lambda i, place: (i, 0, 0)),
                pl.BlockSpec((1, 1, width), lambda i, place: (i, 0, 0)),
            ],
        ),
        out_shape=[
            jax.ShapeDtypeStruct((count, tokens, width), jnp.bfloat16),
            jax.ShapeDtypeStruct((count, 1, width), jnp.float32),
        ],
        compiler_params=kernel_params(),
        cost_estimate=SMALL,
        name="pick",
    )(place, own_hidden, other_hidden, own_gate, other_gate)


def mixed_block(hidden, gate, own_part, other_part):
    parts = own_part[0].astype(jnp.float32) + other_part[0].astype(jnp.float32)
    return hidden[0].astype(jnp.float32) + gate * parts


def mix_kernel(hidden, gate, own_part, other_part, mixed_ref, sums_ref):
    mixed = mixed_block(hidden, gate[0], own_part, other_part)
    mixed_ref[0] = mixed.astype(jnp.bfloat16)
    first = jnp.sum(mixed, axis=1, keepdims=True)
    second = jnp.sum(mixed * mixed, axis=1, keepdims=True)
    lane = lax.broadcasted_iota(jnp.int32, sums_ref.shape, 1)
    sums_ref[...] = jnp.where(lane == 0, first, jnp.where(lane == 1, second, 0.0))


def mix(hidden, gate, own_part, other_part):
    _, tokens, width = hidden.shape
    rows = 64 if tokens % 64 == 0 else tokens
    part = pl.BlockSpec((1, rows, width), lambda i: (0, i, 0))
    return pl.pallas_call(
        mix_kernel,
        grid=(tokens // rows,),
        in_specs=[part, pl.BlockSpec(gate.shape, lambda i: (0, 0, 0)), part, part],
        out_specs=[part, pl.BlockSpec((rows, LANES), lambda i: (i, 0))],
        out_shape=[
            jax.ShapeDtypeStruct((1, tokens, width), jnp.bfloat16),
            jax.ShapeDtypeStruct((tokens, LANES), jnp.float32),
        ],
        compiler_params=kernel_params(),
        cost_estimate=SMALL,
        name="mix",
    )(hidden, gate, own_part, other_part)


def finish_kernel(place, gate, scale, shift_by, sums, early, *refs, count, blocks):
    hidden, own_parts, other_parts = (refs[count * k : count * (k + 1)] for k in range(3))
    residual, ffn = refs[3 * count :]
    width = early.shape[2]
    late = [
        mixed_block(hidden[index], gate[1 + index], own_parts[index], other_parts[index])
        for index in range(count)
    ]
    first = sums[:, 0:1]
    second = sums[:, 1:2]
    for mixed in late:
        first = first + jnp.sum(mixed, axis=1, keepdims=True)
        second = second + jnp.sum(mixed * mixed, axis=1, keepdims=True)
    average = first / D
    variance = second / D - average * average
    inverse = lax.rsqrt(variance + EPSILON)
    for block in range(blocks):
        columns = slice(block * width, (block + 1) * width)
        mixed = early[0].astype(jnp.float32)
        for index in range(count):
            mixed = jnp.where(place[block] == 1 + index, late[index], mixed)
        residual[:, columns] = mixed.astype(jnp.bfloat16)
        ffn[:, columns] = (
            (mixed - average) * inverse * (1.0 + scale[:, columns]) + shift_by[:, columns]
        ).astype(jnp.bfloat16)


def finish(place, hidden, gate, scale, shift_by, sums, early, own_parts, other_parts):
    count = own_parts.shape[0]
    _, tokens, width = hidden.shape
    blocks = place.shape[0]
    rows = 64 if tokens % 64 == 0 else tokens
    part = pl.BlockSpec((1, rows, width), lambda i, place: (0, i, 0))
    whole = pl.BlockSpec((1, blocks * width), lambda i, place: (0, 0))
    row = pl.BlockSpec((rows, blocks * width), lambda i, place: (i, 0))
    parts = [
        pl.BlockSpec((1, rows, width), lambda i, place, index=index: (index, i, 0))
        for index in range(count + 1)
    ]
    return pl.pallas_call(
        partial(finish_kernel, count=count, blocks=blocks),
        grid_spec=pltpu.PrefetchScalarGridSpec(
            num_scalar_prefetch=1,
            grid=(tokens // rows,),
            in_specs=[pl.BlockSpec(gate.shape, lambda i, place: (0, 0, 0)), whole, whole]
            + [pl.BlockSpec((rows, LANES), lambda i, place: (i, 0)), part]
            + parts[1:]
            + parts[:-1] * 2,
            out_specs=[row, row],
        ),
        out_shape=[jax.ShapeDtypeStruct((tokens, blocks * width), jnp.bfloat16)] * 2,
        compiler_params=kernel_params(),
        cost_estimate=SMALL,
        name="finish",
    )(
        *(place, gate, scale, shift_by, sums, early),
        *([hidden] * count + [own_parts] * count + [other_parts] * count),
    )


def shift(block, axis, step):
    count = lax.axis_size(axis)
    pairs = [(i, i + step) for i in range(count) if 0 <= i + step < count]
    return lax.ppermute(block, axis, pairs)


def turn(block, axis, step):
    count = lax.axis_size(axis)
    return lax.ppermute(block, axis, [(i, (i + step) % count) for i in range(count)])


def swap(block, axis, bit):
    count = lax.axis_size(axis)
    return lax.ppermute(block, axis, [(i, i ^ bit) for i in range(count)])


class Tokens:
    def __init__(self, queries, keys_values, windows, order):
        self.plan = Plan(windows, order)
        self.queries = queries.reshape(queries.shape[0], -1, queries.shape[3])
        self.keys_values = keys_values.reshape(*keys_values.shape[:2], -1, keys_values.shape[4])
        self.span = TILE * queries.shape[2]
        self.parts = (0, self.plan.most), (self.plan.most, self.plan.heads - self.plan.most)

    def edge_rows(self, vector, part):
        low = self.queries.shape[1] - self.span
        rows = [(low, self.span), (0, self.span)]
        return pack(vector, self.keys_values, self.plan.row_head, *self.parts[part], rows)

    def leaving(self, vector, part):
        rows = [(0, self.queries.shape[1])]
        return pack(vector, self.queries, self.plan.col_head, *self.parts[part], rows)[0]

    def halos(self, rows):
        return shift(rows[0], "ha", 1), shift(rows[1], "ha", -1)

    def rest_halos(self, vector):
        shape = (*self.keys_values.shape[:2], self.span, self.parts[1][1] * HD)
        return lax.cond(
            self.plan.more_rows,
            lambda vector: self.halos(self.edge_rows(vector, 1)),
            lambda vector: (jnp.zeros(shape, jnp.bfloat16),) * 2,
            vector,
        )

    def stay(self, vector, halos):
        return attention(self.plan, vector, [self.queries], self.keys_values, halos)[0]

    def visit(self, vector, visitors, halos, part=0):
        first = self.parts[part][0]
        return attention(self.plan, vector, visitors, self.keys_values, halos, first)

    def rest_sides(self, vector, halos):
        shape = (*self.queries.shape[:2], (self.parts[1][1] + 1) * HD)

        def send(vector, *halos):
            queries = self.leaving(vector, 1)
            visitors = shift(queries, "wa", 1), shift(queries, "wa", -1)
            for_left, for_right = self.visit(vector, visitors, halos, 1)
            return shift(for_right, "wa", 1), shift(for_left, "wa", -1)

        return lax.cond(
            self.plan.more_cols,
            send,
            lambda vector, *halos: (jnp.zeros(shape, jnp.bfloat16),) * 2,
            vector,
            *halos,
        )

    def combine(self, vector, near, sides):
        attended = combine(self.plan, vector, near, sides)
        return attended.reshape(-1, attended.shape[2])


def together(*blocks):
    return lax.optimization_barrier(blocks)


def paired(hidden, queries, keys_values, windows, out_weight, picked):
    ha, wa, ta = lax.axis_index("ha"), lax.axis_index("wa"), lax.axis_index("ta")
    n_wa = lax.axis_size("wa")
    blocks = n_wa // 2
    depth = out_weight.shape[0] // 4
    width = out_weight.shape[1]

    def share(number):
        return lax.dynamic_slice_in_dim(out_weight, number * depth, depth, 0)

    mine = lax.optimization_barrier(share(ha))
    first = turn(mine, "wa", 1)
    third = turn(mine, "wa", -1)
    tokens = Tokens(queries, keys_values, windows, 4)
    vector = tokens.plan.vector
    top, bottom = tokens.halos(tokens.edge_rows(vector, 0))
    queries = tokens.leaving(vector, 0)

    first, top, bottom, vector, queries = together(first, top, bottom, vector, queries)
    first_x = swap(first, "ha", 1)
    first_y = swap(first, "ha", 2)
    from_left = shift(queries, "wa", 1)
    from_right = shift(queries, "wa", -1)
    halos = top, bottom, *tokens.rest_halos(vector)
    near = tokens.stay(vector, halos)

    near, first_x, first_y, third, first, gate, hidden = together(
        near, first_x, first_y, third, first, picked[0:1], hidden
    )
    third_x = swap(third, "ha", 1)
    third_y = swap(third, "ha", 2)
    second = turn(first, "wa", 1)
    from_left, from_right, gate, hidden = together(from_left, from_right, gate, hidden)
    other_gate = swap(gate, "ta", 1)
    other_hidden = swap(hidden, "ta", 1)
    for_left, for_right = tokens.visit(vector, (from_left, from_right), halos)

    for_left, for_right, other_gate, other_hidden = together(
        for_left, for_right, other_gate, other_hidden
    )
    left = shift(for_right, "wa", 1)
    right = shift(for_left, "wa", -1)

    third_x, third_y, second, other_gate, vector = together(
        third_x, third_y, second, other_gate, vector
    )
    second_x = swap(second, "ha", 1)
    second_y = swap(second, "ha", 2)
    rest_sides = tokens.rest_sides(vector, halos)

    def block_of(distance):
        return lax.rem(wa - distance + n_wa, n_wa)

    owners = jnp.stack([block_of(distance) // blocks == ta for distance in range(n_wa)])
    inner = jnp.stack([lax.rem(block_of(distance), blocks) for distance in range(n_wa)])
    place = jnp.stack([owners.astype(jnp.int32), inner], axis=1).reshape(-1)
    base, gates = pick(place, hidden, other_hidden, gate, other_gate, width)
    left, right, base, gates = together(left, right, base, gates)
    attended = tokens.combine(vector, near, [left, right, *rest_sides])

    far = lax.optimization_barrier(share(ha ^ 3))
    second_x, second_y, first_y, far, attended = together(
        second_x, second_y, first_y, far, attended
    )
    first_far = swap(first_y, "ha", 1)
    second_far = swap(second_x, "ha", 2)
    third_far = turn(far, "wa", -1)

    turned = ha.reshape(1)
    sums = project(
        turned,
        attended,
        [out_weight],
        [[(0, depth, number, True) for number in range(4)]],
        None,
        0,
        jnp.bfloat16,
    )
    other_sums = swap(sums, "ta", 1)
    late = project(
        turned,
        attended,
        [first, first_x, first_y, second, second_x, second_y, third, third_x, third_y],
        [[(start + number, depth, 0, False) for number in range(3)] for start in (0, 3, 6)],
        None,
        0,
        jnp.float32,
    )
    early, totals = mix(base, gates, sums, other_sums)

    first_far, second_far, third_far, early, totals, late = together(
        first_far, second_far, third_far, early, totals, late
    )
    late = project(
        turned,
        attended,
        [first_far, second_far, third_far],
        [[(number, depth, 0, False)] for number in range(3)],
        late,
        3 * depth,
        jnp.bfloat16,
    )
    other_late = swap(late, "ta", 1)
    place = jnp.stack(
        [lax.rem(wa - ta * blocks - block + 2 * n_wa, n_wa) for block in range(blocks)]
    )
    return finish(
        place, base, gates, picked[2:3], picked[1:2], totals, early, late, other_late
    )


def gathered(hidden, queries, keys_values, windows, out_weight, picked):
    n_ha, n_wa, n_ta = lax.axis_size("ha"), lax.axis_size("wa"), lax.axis_size("ta")
    ha, ta = lax.axis_index("ha"), lax.axis_index("ta")
    work = Tokens(queries, keys_values, windows, 1)
    vector = work.plan.vector
    halos = *work.halos(work.edge_rows(vector, 0)), *work.rest_halos(vector)
    sent = work.leaving(vector, 0)
    visitors = shift(sent, "wa", 1), shift(sent, "wa", -1)
    near = work.stay(vector, halos)
    for_left, for_right = work.visit(vector, visitors, halos)
    sides = shift(for_right, "wa", 1), shift(for_left, "wa", -1)
    attended = work.combine(vector, near, [*sides, *work.rest_sides(vector, halos)])
    tokens, features = attended.shape
    depth = features // n_ha
    width = out_weight.shape[1]
    share = lax.dynamic_slice_in_dim(out_weight, ha * depth, depth, 0)
    weights = lax.all_gather(share, ("ha", "wa"), axis=0, tiled=False).reshape(
        n_ha, n_wa, depth, width
    )
    partial_sums = jnp.einsum(
        "thk,hwkc->wtc",
        attended.reshape(tokens, n_ha, depth),
        weights,
        preferred_element_type=jnp.float32,
    ).astype(jnp.bfloat16)
    blocks = n_wa // n_ta
    summed = None
    for step in range(n_ta):
        target = lax.rem(ta + step, n_ta)
        piece = lax.dynamic_slice_in_dim(partial_sums, target * blocks, blocks, 0)
        if step:
            piece = turn(piece, "ta", step)
        piece = piece.astype(jnp.float32)
        summed = piece if summed is None else summed + piece
    summed = jnp.transpose(summed, (1, 0, 2)).reshape(tokens, -1)
    mixed = hidden.astype(jnp.float32) + picked[0] * summed
    sum_first, sum_second = lax.psum((jnp.sum(mixed, axis=1), jnp.sum(mixed * mixed, axis=1)), "ta")
    average = (sum_first / D)[:, None]
    variance = (sum_second / D)[:, None] - average * average
    normed = (mixed - average) * lax.rsqrt(variance + EPSILON)
    ffn_input = (normed * (1.0 + picked[2]) + picked[1]).astype(jnp.bfloat16)
    return mixed.astype(jnp.bfloat16), ffn_input


def shards(hidden_states, queries, keys_values, out_weight, mod_table, windows, step_index):
    tokens = math.prod(queries.shape[:3])
    width = hidden_states.shape[3]
    picked = lax.dynamic_index_in_dim(mod_table, step_index[0], 0, keepdims=False)
    sizes = lax.axis_size("ha"), lax.axis_size("wa"), lax.axis_size("ta")
    tuned = sizes == (4, 4, 2) and out_weight.shape[0] % (20 * LANES) == 0
    residual_out, ffn_input = (paired if tuned else gathered)(
        hidden_states.reshape(tokens, width), queries, keys_values, windows, out_weight, picked
    )
    return residual_out.reshape(hidden_states.shape), ffn_input.reshape(hidden_states.shape)


def solution(mesh):
    return jax.shard_map(
        shards,
        mesh=mesh,
        in_specs=(
            P(None, "ha", "wa", "ta"),
            P(None, "ha", "wa", "ta"),
            P(None, None, "ha", "wa", "ta"),
            P("ta", "wa"),
            P(None, None, "ta"),
            P("ta", None),
            P(),
        ),
        out_specs=(P(None, "ha", "wa", "ta"), P(None, "ha", "wa", "ta")),
        check_vma=False,
    )
```

```python
from functools import partial
import math

import jax
import jax.numpy as jnp
from jax import lax
from jax.experimental import pallas as pl
from jax.experimental.pallas import tpu as pltpu
from jax.sharding import PartitionSpec as P

D = 5120
HD = 128
TILE = 8
LANES = 128
LEVEL_STEP = 32

EPSILON = 1e-06
VMEM_LIMIT = 24 * 1024 * 1024
SMALL = pl.CostEstimate(flops=1, bytes_accessed=1, transcendentals=0)
LARGE = pl.CostEstimate(flops=20_000_000_000, bytes_accessed=1, transcendentals=0)


def kernel_params(limit=VMEM_LIMIT):
    return pltpu.CompilerParams(dimension_semantics=("arbitrary",), vmem_limit_bytes=limit)


class Plan:
    def __init__(self, windows, order):
        heads = windows.shape[0]
        self.heads = heads
        self.most = max(heads * 7 // 10, 1)
        self.order = order
        n_ha, n_wa = lax.axis_size("ha"), lax.axis_size("wa")
        ha, wa = lax.axis_index("ha"), lax.axis_index("wa")
        number = lax.broadcasted_iota(jnp.int32, (2, heads, heads), 1)
        other = lax.broadcasted_iota(jnp.int32, (2, heads, heads), 2)
        idle = jnp.where(windows.T > 0, 0, 1)
        before = (idle[:, None, :] < idle[:, :, None]) | (
            (idle[:, None, :] == idle[:, :, None]) & (other < number)
        )
        position = jnp.sum(before.astype(jnp.int32), axis=2)
        sorted_heads = jnp.sum(jnp.where(position[:, None, :] == number, other, 0), axis=2)
        turned = ha if order > 1 else 0 * ha
        edges = jnp.stack([ha > 0, ha < n_ha - 1, wa > 0, wa < n_wa - 1, turned]).astype(jnp.int32)
        self.vector = jnp.concatenate(
            [windows.T.reshape(-1), position.reshape(-1), sorted_heads.reshape(-1), edges]
        )
        counts = lax.pmax(jnp.sum(1.0 - idle, axis=1), "ta")
        self.more_rows = counts[0] > self.most
        self.more_cols = counts[1] > self.most

    def row_radius(self, vector, head):
        return vector[head]

    def col_radius(self, vector, head):
        return vector[self.heads + head]

    def row_position(self, vector, head):
        return vector[2 * self.heads + head]

    def col_position(self, vector, head):
        return vector[3 * self.heads + head]

    def row_head(self, vector, position):
        return vector[4 * self.heads + position]

    def col_head(self, vector, position):
        return vector[5 * self.heads + position]

    def edge(self, vector, number):
        return vector[6 * self.heads + number]


def pack_kernel(vector, source, *refs, head_of, first, rows):
    outs, sem = refs[:-1], refs[-1]
    copies = []
    for number, (out, (low, size)) in enumerate(zip(outs, rows)):
        for slot in range(out.shape[-1] // HD):
            start = pl.multiple_of(head_of(vector, first + slot) * HD, HD)
            lead = (slice(None),) * (len(source.shape) - 2)
            copies.append(
                pltpu.make_async_copy(
                    source.at[(*lead, pl.ds(low, size), pl.ds(start, HD))],
                    out.at[(*lead, slice(None), pl.ds(slot * HD, HD))],
                    sem.at[number, slot],
                )
            )
    for copy in copies:
        copy.start()
    for copy in copies:
        copy.wait()


def pack(vector, source, head_of, first, count, rows):
    anywhere = pl.BlockSpec(memory_space=pl.ANY)
    return pl.pallas_call(
        partial(pack_kernel, head_of=head_of, first=first, rows=rows),
        in_specs=[pl.BlockSpec(memory_space=pltpu.SMEM), anywhere],
        out_specs=[pl.BlockSpec(memory_space=pltpu.VMEM)] * len(rows),
        out_shape=[
            jax.ShapeDtypeStruct((*source.shape[:-2], size, count * HD), source.dtype)
            for _, size in rows
        ],
        scratch_shapes=[pltpu.SemaphoreType.DMA((len(rows), count))],
        compiler_params=pltpu.CompilerParams(vmem_limit_bytes=VMEM_LIMIT),
        cost_estimate=SMALL,
        name="pack",
    )(vector, source)


def attention_kernel(vector, *refs, plan, head_of, q_count, visiting, group):
    q_refs = refs[:q_count]
    kv_ref, top_ref, bottom_ref, top_rest, bottom_rest = refs[q_count : q_count + 5]
    refs = refs[q_count + 5 :]
    out_refs, stat_refs, halo = refs[:q_count], refs[q_count : 2 * q_count], refs[2 * q_count]
    frames, tokens, head_size = q_refs[0].shape
    span = top_ref.shape[2]
    tiles = tokens // span
    step = pl.program_id(0)
    head = head_of(vector, step)
    radius_row = plan.row_radius(vector, head)
    radius_col = plan.col_radius(vector, head)
    scale = 1.0 / math.sqrt(HD)

    @pl.when(step == 0)
    def _():
        for stat_ref in stat_refs:
            stat_ref[...] = jnp.zeros_like(stat_ref)

    def near(which, tile, wide):
        if not wide:
            return kv_ref[which, :, tile * span : (tile + 1) * span, :].reshape(-1, head_size)
        pieces = []
        if tile == 0:
            pieces.append(halo[0, which])
        low = max(tile - 1, 0) * span
        high = min(tile + 2, tiles) * span
        pieces.append(kv_ref[which, :, low:high, :])
        if tile == tiles - 1:
            pieces.append(halo[1, which])
        block = pieces[0] if len(pieces) == 1 else jnp.concatenate(pieces, axis=1)
        return block.reshape(-1, head_size)

    def attend(wide):
        lane = lax.broadcasted_iota(jnp.int32, (frames, span, LANES), 2)
        for tile in range(tiles):
            rows = slice(tile * span, (tile + 1) * span)
            keys = near(0, tile, wide)
            values = near(1, tile, wide)
            bias = None
            if wide and (tile == 0 or tile == tiles - 1):
                place = lax.rem(
                    lax.broadcasted_iota(jnp.int32, (1, keys.shape[0]), 1), 3 * span
                )
                low, high = 0, 3 * span
                if tile == 0:
                    low = jnp.where(plan.edge(vector, 0) == 0, span, 0)
                if tile == tiles - 1:
                    high = jnp.where(plan.edge(vector, 1) == 0, 2 * span, 3 * span)
                bias = jnp.where((place >= low) & (place < high), 0.0, -jnp.inf)
            for q_ref, out_ref, stat_ref in zip(q_refs, out_refs, stat_refs):
                query = q_ref[:, rows, :].reshape(-1, head_size)
                scores = (
                    lax.dot_general(
                        query, keys, (((1,), (1,)), ((), ())), preferred_element_type=jnp.float32
                    )
                    * scale
                )
                if bias is not None:
                    scores = scores + bias
                highest = jnp.max(scores, axis=1, keepdims=True)
                expo = jnp.exp(scores - highest)
                total = jnp.sum(expo, axis=1, keepdims=True)
                output = jnp.dot(
                    expo.astype(jnp.bfloat16), values, preferred_element_type=jnp.float32
                ) * (1.0 / total)
                out_ref[:, rows, :] = output.astype(jnp.bfloat16).reshape(frames, span, head_size)
                level = (highest + jnp.log(total)).reshape(frames, span, 1)
                stat_ref[:, rows, :] = jnp.where(lane == step, level, stat_ref[:, rows, :])

    active = step < group
    if visiting:

        @pl.when(active & (radius_col == 0))
        def _():
            for out_ref in out_refs:
                out_ref[...] = jnp.zeros_like(out_ref)

        active = active & (radius_col != 0)

    @pl.when(active & (radius_row == 0))
    def _():
        attend(False)

    always = plan.row_position(vector, head) < plan.most

    @pl.when(active & (radius_row != 0) & always)
    def _():
        halo[0] = top_ref[...]
        halo[1] = bottom_ref[...]

    @pl.when(active & (radius_row != 0) & jnp.logical_not(always))
    def _():
        halo[0] = top_rest[...]
        halo[1] = bottom_rest[...]

    @pl.when(active & (radius_row != 0))
    def _():
        attend(True)

    @pl.when(step == group)
    def _():
        for out_ref, stat_ref in zip(out_refs, stat_refs):
            level = stat_ref[...]
            high = level.astype(jnp.bfloat16).astype(jnp.float32)
            middle = (level - high).astype(jnp.bfloat16).astype(jnp.float32)
            low = level - high - middle
            packed = high + pltpu.roll(middle, LEVEL_STEP, 2) + pltpu.roll(low, 2 * LEVEL_STEP, 2)
            out_ref[...] = packed.astype(jnp.bfloat16)


def attention(plan, vector, query_blocks, keys_values, halos, first=None):
    frames, tokens, features = query_blocks[0].shape
    group = features // HD
    span = halos[0].shape[2]
    q_count = len(query_blocks)
    visiting = first is not None

    def slot_of(step):
        return jnp.minimum(step, group - 1)

    def head_of(vector, step):
        return plan.col_head(vector, first + slot_of(step)) if visiting else slot_of(step)

    def kv_index(step, vector):
        return 0, 0, 0, head_of(vector, step)

    def halo_index(step, vector):
        position = plan.row_position(vector, head_of(vector, step))
        return 0, 0, 0, jnp.minimum(position, plan.most - 1)

    def rest_index(step, vector):
        position = plan.row_position(vector, head_of(vector, step))
        return 0, 0, 0, jnp.maximum(position - plan.most, 0)

    q_spec = pl.BlockSpec((frames, tokens, HD), lambda step, _: (0, 0, slot_of(step)))
    kv_spec = pl.BlockSpec((2, frames, tokens, HD), kv_index)
    halo_spec = pl.BlockSpec((2, frames, span, HD), halo_index)
    rest_spec = pl.BlockSpec((2, frames, span, HD), rest_index)
    out_spec = pl.BlockSpec((frames, tokens, HD), lambda step, _: (0, 0, step))
    return pl.pallas_call(
        partial(
            attention_kernel,
            plan=plan,
            head_of=head_of,
            q_count=q_count,
            visiting=visiting,
            group=group,
        ),
        grid_spec=pltpu.PrefetchScalarGridSpec(
            num_scalar_prefetch=1,
            grid=(group + 1,),
            in_specs=[q_spec] * q_count + [kv_spec] + [halo_spec] * 2 + [rest_spec] * 2,
            out_specs=[out_spec] * q_count,
            scratch_shapes=[pltpu.VMEM((frames, tokens, LANES), jnp.float32)] * q_count
            + [pltpu.VMEM((2, 2, frames, span, HD), jnp.bfloat16)],
        ),
        out_shape=[jax.ShapeDtypeStruct((frames, tokens, (group + 1) * HD), jnp.bfloat16)]
        * q_count,
        compiler_params=kernel_params(),
        cost_estimate=SMALL if visiting else LARGE,
        name="attend_visitors" if visiting else "attend_own",
    )(vector, *query_blocks, keys_values, *halos)


def combine_kernel(vector, own, own_stat, left, right, left_rest, right_rest, out, *, plan, heads):
    first = pl.program_id(0) * heads
    frames, tokens, _ = own.shape

    def level(stat, number):
        lane = lax.broadcasted_iota(jnp.int32, (LANES, HD), 0)
        pick = jnp.where(
            (lax.rem(lane, LEVEL_STEP) == number) & (lane < 3 * LEVEL_STEP), 1.0, 0.0
        ).astype(jnp.bfloat16)
        return jnp.dot(
            stat.reshape(-1, LANES), pick, preferred_element_type=jnp.float32
        ).reshape(frames, tokens, HD)

    for index in range(heads):
        head = first + index
        columns = slice(index * HD, (index + 1) * HD)
        across = plan.col_radius(vector, head) != 0
        position = plan.col_position(vector, head)

        @pl.when(jnp.logical_not(across))
        def _(columns=columns):
            out[:, :, columns] = own[:, :, columns]

        def join(sides, slot, columns, head):
            here = pl.ds(pl.multiple_of(slot * HD, HD), HD)
            levels = [level(own_stat[...], head)]
            values = [own[:, :, columns]]
            for number, side in enumerate(sides):
                value = level(side[:, :, side.shape[2] - LANES :], slot)
                levels.append(jnp.where(plan.edge(vector, 2 + number) == 0, -jnp.inf, value))
                values.append(side[:, :, here])
            highest = jnp.maximum(levels[0], jnp.maximum(levels[1], levels[2]))
            weights = [jnp.exp(x - highest) for x in levels]
            mixed = sum(value.astype(jnp.float32) * weight for value, weight in zip(values, weights))
            out[:, :, columns] = (mixed / (weights[0] + weights[1] + weights[2])).astype(
                jnp.bfloat16
            )

        @pl.when(across & (position < plan.most))
        def _(position=position, columns=columns, head=head):
            join((left, right), position, columns, head)

        @pl.when(across & (position >= plan.most))
        def _(position=position, columns=columns, head=head):
            join((left_rest, right_rest), position - plan.most, columns, head)


def combine(plan, vector, near, sides):
    frames, tokens, _ = near.shape
    heads = plan.heads // plan.order
    spec = pl.BlockSpec((frames, tokens, heads * HD), lambda h, _: (0, 0, h))
    stat_spec = pl.BlockSpec((frames, tokens, HD), lambda h, _: (0, 0, plan.heads))
    return pl.pallas_call(
        partial(combine_kernel, plan=plan, heads=heads),
        grid_spec=pltpu.PrefetchScalarGridSpec(
            num_scalar_prefetch=1,
            grid=(plan.order,),
            in_specs=[spec, stat_spec]
            + [pl.BlockSpec(side.shape, lambda h, _: (0, 0, 0)) for side in sides],
            out_specs=pl.BlockSpec(
                (frames, tokens, heads * HD), lambda h, vector: (0, 0, h ^ plan.edge(vector, 4))
            ),
        ),
        out_shape=jax.ShapeDtypeStruct((frames, tokens, plan.heads * HD), jnp.bfloat16),
        compiler_params=kernel_params(),
        cost_estimate=LARGE,
        name="combine",
    )(vector, near, near, *sides)


def project_kernel(place, attended, *refs, slots, carried, start, column):
    arrays = 1 + max(piece[0] for slot in slots for piece in slot)
    pieces, refs = refs[:arrays], refs[arrays:]
    if carried:
        carry, refs = refs[0], refs[1:]
    out, rows, weight, rows_sem, weight_sem = refs
    columns = weight.shape[1]
    depth = weight.shape[2]
    rows_copy = pltpu.make_async_copy(
        attended.at[:, start : start + depth], rows, rows_sem.at[0]
    )
    rows_copy.start()
    for index, slot in enumerate(slots):
        for block in range(columns):
            low = 0
            for number, (array, size, share, turned) in enumerate(slot):
                first = pl.multiple_of((place[0] ^ share if turned else share) * size, size)
                pltpu.make_async_copy(
                    pieces[array].at[pl.ds(first, size), block * column : (block + 1) * column],
                    weight.at[index, block, low : low + size],
                    weight_sem.at[index, block, number],
                ).start()
                low += size
    rows_copy.wait()
    for index, slot in enumerate(slots):

        def body(block, _, index=index, slot=slot):
            low = 0
            for number, (_, size, _, _) in enumerate(slot):
                piece = weight.at[index, block, low : low + size]
                pltpu.make_async_copy(piece, piece, weight_sem.at[index, block, number]).wait()
                low += size
            total = jnp.dot(rows[...], weight[index, block], preferred_element_type=jnp.float32)
            here = pl.ds(pl.multiple_of(block * column, column), column)
            if carried:
                total = total + carry[index, :, here]
            out[index, :, here] = total.astype(out.dtype)
            return 0

        lax.fori_loop(0, columns, body, 0)


def project(place, attended, arrays, slots, carry, start, dtype):
    tokens = attended.shape[0]
    width = arrays[0].shape[1]
    column = 256 if width % 256 == 0 else width
    columns = width // column
    depth = sum(piece[1] for piece in slots[0])
    anywhere = pl.BlockSpec(memory_space=pl.ANY)
    inside = pl.BlockSpec(memory_space=pltpu.VMEM)
    return pl.pallas_call(
        partial(
            project_kernel, slots=slots, carried=carry is not None, start=start, column=column
        ),
        in_specs=[pl.BlockSpec(memory_space=pltpu.SMEM), anywhere]
        + [anywhere] * len(arrays)
        + ([] if carry is None else [inside]),
        out_specs=inside,
        out_shape=jax.ShapeDtypeStruct((len(slots), tokens, width), dtype),
        scratch_shapes=[
            pltpu.VMEM((tokens, depth), attended.dtype),
            pltpu.VMEM((len(slots), columns, depth, column), attended.dtype),
            pltpu.SemaphoreType.DMA((1,)),
            pltpu.SemaphoreType.DMA((len(slots), columns, max(len(slot) for slot in slots))),
        ],
        compiler_params=pltpu.CompilerParams(vmem_limit_bytes=VMEM_LIMIT),
        cost_estimate=SMALL,
        name="project",
    )(place, attended, *arrays, *([] if carry is None else [carry]))


def pick_kernel(place, own_hidden, other_hidden, own_gate, other_gate, hidden, gate):
    mine = place[2 * pl.program_id(0)] != 0

    @pl.when(mine)
    def _():
        hidden[0] = own_hidden[...]
        gate[0] = own_gate[...]

    @pl.when(jnp.logical_not(mine))
    def _():
        hidden[0] = other_hidden[...]
        gate[0] = other_gate[...]


def pick(place, own_hidden, other_hidden, own_gate, other_gate, width):
    tokens, features = own_hidden.shape
    count = 2 * features // width
    hidden = pl.BlockSpec((tokens, width), lambda i, place: (0, place[2 * i + 1]))
    gate = pl.BlockSpec((1, width), lambda i, place: (0, place[2 * i + 1]))
    return pl.pallas_call(
        pick_kernel,
        grid_spec=pltpu.PrefetchScalarGridSpec(
            num_scalar_prefetch=1,
            grid=(count,),
            in_specs=[hidden, hidden, gate, gate],
            out_specs=[
                pl.BlockSpec((1, tokens, width), lambda i, place: (i, 0, 0)),
                pl.BlockSpec((1, 1, width), lambda i, place: (i, 0, 0)),
            ],
        ),
        out_shape=[
            jax.ShapeDtypeStruct((count, tokens, width), jnp.bfloat16),
            jax.ShapeDtypeStruct((count, 1, width), jnp.float32),
        ],
        compiler_params=kernel_params(),
        cost_estimate=SMALL,
        name="pick",
    )(place, own_hidden, other_hidden, own_gate, other_gate)


def mixed_block(hidden, gate, own_part, other_part):
    parts = own_part[0].astype(jnp.float32) + other_part[0].astype(jnp.float32)
    return hidden[0].astype(jnp.float32) + gate * parts


def mix_kernel(hidden, gate, own_part, other_part, mixed_ref, sums_ref):
    mixed = mixed_block(hidden, gate[0], own_part, other_part)
    mixed_ref[0] = mixed.astype(jnp.bfloat16)
    first = jnp.sum(mixed, axis=1, keepdims=True)
    second = jnp.sum(mixed * mixed, axis=1, keepdims=True)
    lane = lax.broadcasted_iota(jnp.int32, sums_ref.shape, 1)
    sums_ref[...] = jnp.where(lane == 0, first, jnp.where(lane == 1, second, 0.0))


def mix(hidden, gate, own_part, other_part):
    _, tokens, width = hidden.shape
    rows = 64 if tokens % 64 == 0 else tokens
    part = pl.BlockSpec((1, rows, width), lambda i: (0, i, 0))
    return pl.pallas_call(
        mix_kernel,
        grid=(tokens // rows,),
        in_specs=[part, pl.BlockSpec(gate.shape, lambda i: (0, 0, 0)), part, part],
        out_specs=[part, pl.BlockSpec((rows, LANES), lambda i: (i, 0))],
        out_shape=[
            jax.ShapeDtypeStruct((1, tokens, width), jnp.bfloat16),
            jax.ShapeDtypeStruct((tokens, LANES), jnp.float32),
        ],
        compiler_params=kernel_params(),
        cost_estimate=SMALL,
        name="mix",
    )(hidden, gate, own_part, other_part)


def finish_kernel(place, gate, scale, shift_by, sums, early, *refs, count, blocks):
    hidden, own_parts, other_parts = (refs[count * k : count * (k + 1)] for k in range(3))
    residual, ffn = refs[3 * count :]
    width = early.shape[2]
    late = [
        mixed_block(hidden[index], gate[1 + index], own_parts[index], other_parts[index])
        for index in range(count)
    ]
    first = sums[:, 0:1]
    second = sums[:, 1:2]
    for mixed in late:
        first = first + jnp.sum(mixed, axis=1, keepdims=True)
        second = second + jnp.sum(mixed * mixed, axis=1, keepdims=True)
    average = first / D
    variance = second / D - average * average
    inverse = lax.rsqrt(variance + EPSILON)
    for block in range(blocks):
        columns = slice(block * width, (block + 1) * width)
        mixed = early[0].astype(jnp.float32)
        for index in range(count):
            mixed = jnp.where(place[block] == 1 + index, late[index], mixed)
        residual[:, columns] = mixed.astype(jnp.bfloat16)
        ffn[:, columns] = (
            (mixed - average) * inverse * (1.0 + scale[:, columns]) + shift_by[:, columns]
        ).astype(jnp.bfloat16)


def finish(place, hidden, gate, scale, shift_by, sums, early, own_parts, other_parts):
    count = own_parts.shape[0]
    _, tokens, width = hidden.shape
    blocks = place.shape[0]
    rows = 64 if tokens % 64 == 0 else tokens
    part = pl.BlockSpec((1, rows, width), lambda i, place: (0, i, 0))
    whole = pl.BlockSpec((1, blocks * width), lambda i, place: (0, 0))
    row = pl.BlockSpec((rows, blocks * width), lambda i, place: (i, 0))
    parts = [
        pl.BlockSpec((1, rows, width), lambda i, place, index=index: (index, i, 0))
        for index in range(count + 1)
    ]
    return pl.pallas_call(
        partial(finish_kernel, count=count, blocks=blocks),
        grid_spec=pltpu.PrefetchScalarGridSpec(
            num_scalar_prefetch=1,
            grid=(tokens // rows,),
            in_specs=[pl.BlockSpec(gate.shape, lambda i, place: (0, 0, 0)), whole, whole]
            + [pl.BlockSpec((rows, LANES), lambda i, place: (i, 0)), part]
            + parts[1:]
            + parts[:-1] * 2,
            out_specs=[row, row],
        ),
        out_shape=[jax.ShapeDtypeStruct((tokens, blocks * width), jnp.bfloat16)] * 2,
        compiler_params=kernel_params(),
        cost_estimate=SMALL,
        name="finish",
    )(
        *(place, gate, scale, shift_by, sums, early),
        *([hidden] * count + [own_parts] * count + [other_parts] * count),
    )


def shift(block, axis, step):
    count = lax.axis_size(axis)
    pairs = [(i, i + step) for i in range(count) if 0 <= i + step < count]
    return lax.ppermute(block, axis, pairs)


def turn(block, axis, step):
    count = lax.axis_size(axis)
    return lax.ppermute(block, axis, [(i, (i + step) % count) for i in range(count)])


def swap(block, axis, bit):
    count = lax.axis_size(axis)
    return lax.ppermute(block, axis, [(i, i ^ bit) for i in range(count)])


class Tokens:
    def __init__(self, queries, keys_values, windows, order):
        self.plan = Plan(windows, order)
        self.queries = queries.reshape(queries.shape[0], -1, queries.shape[3])
        self.keys_values = keys_values.reshape(*keys_values.shape[:2], -1, keys_values.shape[4])
        self.span = TILE * queries.shape[2]
        self.parts = (0, self.plan.most), (self.plan.most, self.plan.heads - self.plan.most)

    def edge_rows(self, vector, part):
        low = self.queries.shape[1] - self.span
        rows = [(low, self.span), (0, self.span)]
        return pack(vector, self.keys_values, self.plan.row_head, *self.parts[part], rows)

    def leaving(self, vector, part):
        rows = [(0, self.queries.shape[1])]
        return pack(vector, self.queries, self.plan.col_head, *self.parts[part], rows)[0]

    def halos(self, rows):
        return shift(rows[0], "ha", 1), shift(rows[1], "ha", -1)

    def rest_halos(self, vector):
        shape = (*self.keys_values.shape[:2], self.span, self.parts[1][1] * HD)
        return lax.cond(
            self.plan.more_rows,
            lambda vector: self.halos(self.edge_rows(vector, 1)),
            lambda vector: (jnp.zeros(shape, jnp.bfloat16),) * 2,
            vector,
        )

    def stay(self, vector, halos):
        return attention(self.plan, vector, [self.queries], self.keys_values, halos)[0]

    def visit(self, vector, visitors, halos, part=0):
        first = self.parts[part][0]
        return attention(self.plan, vector, visitors, self.keys_values, halos, first)

    def rest_sides(self, vector, halos):
        shape = (*self.queries.shape[:2], (self.parts[1][1] + 1) * HD)

        def send(vector, *halos):
            queries = self.leaving(vector, 1)
            visitors = shift(queries, "wa", 1), shift(queries, "wa", -1)
            for_left, for_right = self.visit(vector, visitors, halos, 1)
            return shift(for_right, "wa", 1), shift(for_left, "wa", -1)

        return lax.cond(
            self.plan.more_cols,
            send,
            lambda vector, *halos: (jnp.zeros(shape, jnp.bfloat16),) * 2,
            vector,
            *halos,
        )

    def combine(self, vector, near, sides):
        attended = combine(self.plan, vector, near, sides)
        return attended.reshape(-1, attended.shape[2])


def together(*blocks):
    return lax.optimization_barrier(blocks)


def paired(hidden, queries, keys_values, windows, out_weight, picked):
    ha, wa, ta = lax.axis_index("ha"), lax.axis_index("wa"), lax.axis_index("ta")
    n_wa = lax.axis_size("wa")
    blocks = n_wa // 2
    depth = out_weight.shape[0] // 4
    width = out_weight.shape[1]

    def share(number):
        return lax.dynamic_slice_in_dim(out_weight, number * depth, depth, 0)

    mine = lax.optimization_barrier(share(ha))
    first = turn(mine, "wa", 1)
    gate = picked[0:1]
    other_gate = swap(gate, "ta", 1)
    tokens = Tokens(queries, keys_values, windows, 4)
    vector = tokens.plan.vector
    top, bottom = tokens.halos(tokens.edge_rows(vector, 0))
    queries = tokens.leaving(vector, 0)

    top, mine = together(top, mine)
    third = turn(mine, "wa", -1)

    first, top, bottom, other_gate, vector, queries = together(
        first, top, bottom, other_gate, vector, queries
    )
    first_x = swap(first, "ha", 1)
    first_y = swap(first, "ha", 2)
    from_left = shift(queries, "wa", 1)
    from_right = shift(queries, "wa", -1)
    halos = top, bottom, *tokens.rest_halos(vector)
    near = tokens.stay(vector, halos)

    near, first_x, first_y, third, first = together(near, first_x, first_y, third, first)
    third_x = swap(third, "ha", 1)
    third_y = swap(third, "ha", 2)
    second = turn(first, "wa", 1)
    for_left, for_right = tokens.visit(vector, (from_left, from_right), halos)

    left = shift(for_right, "wa", 1)
    right = shift(for_left, "wa", -1)

    third_x, third_y, second, vector, hidden = together(third_x, third_y, second, vector, hidden)
    second_x = swap(second, "ha", 1)
    second_y = swap(second, "ha", 2)
    other_hidden = swap(hidden, "ta", 1)
    rest_sides = tokens.rest_sides(vector, halos)

    attended = tokens.combine(vector, near, [left, right, *rest_sides])

    far = lax.optimization_barrier(share(ha ^ 3))
    second_x, second_y, first_y, far, attended = together(
        second_x, second_y, first_y, far, attended
    )
    first_far = swap(first_y, "ha", 1)
    second_far = swap(second_x, "ha", 2)
    third_far = turn(far, "wa", -1)

    turned = ha.reshape(1)
    sums = project(
        turned,
        attended,
        [out_weight],
        [[(0, depth, number, True) for number in range(4)]],
        None,
        0,
        jnp.bfloat16,
    )
    other_sums = swap(sums, "ta", 1)
    late = project(
        turned,
        attended,
        [first, first_x, first_y, second, second_x, second_y, third, third_x, third_y],
        [[(start + number, depth, 0, False) for number in range(3)] for start in (0, 3, 6)],
        None,
        0,
        jnp.float32,
    )
    def block_of(distance):
        return lax.rem(wa - distance + n_wa, n_wa)

    owners = jnp.stack([block_of(distance) // blocks == ta for distance in range(n_wa)])
    inner = jnp.stack([lax.rem(block_of(distance), blocks) for distance in range(n_wa)])
    place = jnp.stack([owners.astype(jnp.int32), inner], axis=1).reshape(-1)
    late, place, other_hidden = together(late, place, other_hidden)
    base, gates = pick(place, hidden, other_hidden, gate, other_gate, width)
    early, totals = mix(base, gates, sums, other_sums)

    first_far, second_far, third_far, early, totals, late = together(
        first_far, second_far, third_far, early, totals, late
    )
    late = project(
        turned,
        attended,
        [first_far, second_far, third_far],
        [[(number, depth, 0, False)] for number in range(3)],
        late,
        3 * depth,
        jnp.bfloat16,
    )
    other_late = swap(late, "ta", 1)
    place = jnp.stack(
        [lax.rem(wa - ta * blocks - block + 2 * n_wa, n_wa) for block in range(blocks)]
    )
    return finish(
        place, base, gates, picked[2:3], picked[1:2], totals, early, late, other_late
    )


def gathered(hidden, queries, keys_values, windows, out_weight, picked):
    n_ha, n_wa, n_ta = lax.axis_size("ha"), lax.axis_size("wa"), lax.axis_size("ta")
    ha, ta = lax.axis_index("ha"), lax.axis_index("ta")
    work = Tokens(queries, keys_values, windows, 1)
    vector = work.plan.vector
    halos = *work.halos(work.edge_rows(vector, 0)), *work.rest_halos(vector)
    sent = work.leaving(vector, 0)
    visitors = shift(sent, "wa", 1), shift(sent, "wa", -1)
    near = work.stay(vector, halos)
    for_left, for_right = work.visit(vector, visitors, halos)
    sides = shift(for_right, "wa", 1), shift(for_left, "wa", -1)
    attended = work.combine(vector, near, [*sides, *work.rest_sides(vector, halos)])
    tokens, features = attended.shape
    depth = features // n_ha
    width = out_weight.shape[1]
    share = lax.dynamic_slice_in_dim(out_weight, ha * depth, depth, 0)
    weights = lax.all_gather(share, ("ha", "wa"), axis=0, tiled=False).reshape(
        n_ha, n_wa, depth, width
    )
    partial_sums = jnp.einsum(
        "thk,hwkc->wtc",
        attended.reshape(tokens, n_ha, depth),
        weights,
        preferred_element_type=jnp.float32,
    ).astype(jnp.bfloat16)
    blocks = n_wa // n_ta
    summed = None
    for step in range(n_ta):
        target = lax.rem(ta + step, n_ta)
        piece = lax.dynamic_slice_in_dim(partial_sums, target * blocks, blocks, 0)
        if step:
            piece = turn(piece, "ta", step)
        piece = piece.astype(jnp.float32)
        summed = piece if summed is None else summed + piece
    summed = jnp.transpose(summed, (1, 0, 2)).reshape(tokens, -1)
    mixed = hidden.astype(jnp.float32) + picked[0] * summed
    sum_first, sum_second = lax.psum((jnp.sum(mixed, axis=1), jnp.sum(mixed * mixed, axis=1)), "ta")
    average = (sum_first / D)[:, None]
    variance = (sum_second / D)[:, None] - average * average
    normed = (mixed - average) * lax.rsqrt(variance + EPSILON)
    ffn_input = (normed * (1.0 + picked[2]) + picked[1]).astype(jnp.bfloat16)
    return mixed.astype(jnp.bfloat16), ffn_input


def shards(hidden_states, queries, keys_values, out_weight, mod_table, windows, step_index):
    tokens = math.prod(queries.shape[:3])
    width = hidden_states.shape[3]
    picked = lax.dynamic_index_in_dim(mod_table, step_index[0], 0, keepdims=False)
    sizes = lax.axis_size("ha"), lax.axis_size("wa"), lax.axis_size("ta")
    tuned = sizes == (4, 4, 2) and out_weight.shape[0] % (20 * LANES) == 0
    residual_out, ffn_input = (paired if tuned else gathered)(
        hidden_states.reshape(tokens, width), queries, keys_values, windows, out_weight, picked
    )
    return residual_out.reshape(hidden_states.shape), ffn_input.reshape(hidden_states.shape)


def solution(mesh):
    return jax.shard_map(
        shards,
        mesh=mesh,
        in_specs=(
            P(None, "ha", "wa", "ta"),
            P(None, "ha", "wa", "ta"),
            P(None, None, "ha", "wa", "ta"),
            P("ta", "wa"),
            P(None, None, "ta"),
            P("ta", None),
            P(),
        ),
        out_specs=(P(None, "ha", "wa", "ta"), P(None, "ha", "wa", "ta")),
        check_vma=False,
    )
```

```python
from functools import partial
import math

import jax
import jax.numpy as jnp
from jax import lax
from jax.experimental import pallas as pl
from jax.experimental.pallas import tpu as pltpu
from jax.sharding import PartitionSpec as P

D = 5120
HD = 128
TILE = 8
LANES = 128
LEVEL_STEP = 32

EPSILON = 1e-06
MEBI = 1024 * 1024
SMALL = pl.CostEstimate(flops=1, bytes_accessed=1, transcendentals=0)
LARGE = pl.CostEstimate(flops=20_000_000_000, bytes_accessed=1, transcendentals=0)


def kernel_params(limit):
    return pltpu.CompilerParams(vmem_limit_bytes=limit * MEBI)


class Plan:
    def __init__(self, windows, order):
        heads = windows.shape[0]
        self.heads = heads
        self.most = max(heads * 7 // 10, 1)
        self.order = order
        n_ha, n_wa = lax.axis_size("ha"), lax.axis_size("wa")
        ha, wa = lax.axis_index("ha"), lax.axis_index("wa")
        number = lax.broadcasted_iota(jnp.int32, (2, heads, heads), 1)
        other = lax.broadcasted_iota(jnp.int32, (2, heads, heads), 2)
        idle = jnp.where(windows.T > 0, 0, 1)
        before = (idle[:, None, :] < idle[:, :, None]) | (
            (idle[:, None, :] == idle[:, :, None]) & (other < number)
        )
        position = jnp.sum(before.astype(jnp.int32), axis=2)
        sorted_heads = jnp.sum(jnp.where(position[:, None, :] == number, other, 0), axis=2)
        turned = ha if order > 1 else 0 * ha
        edges = jnp.stack([ha > 0, ha < n_ha - 1, wa > 0, wa < n_wa - 1, turned]).astype(jnp.int32)
        self.vector = jnp.concatenate(
            [windows.T.reshape(-1), position.reshape(-1), sorted_heads.reshape(-1), edges]
        )
        counts = lax.pmax(jnp.sum(1.0 - idle, axis=1), "ta")
        self.more_rows = counts[0] > self.most
        self.more_cols = counts[1] > self.most

    def row_radius(self, vector, head):
        return vector[head]

    def col_radius(self, vector, head):
        return vector[self.heads + head]

    def row_position(self, vector, head):
        return vector[2 * self.heads + head]

    def col_position(self, vector, head):
        return vector[3 * self.heads + head]

    def row_head(self, vector, position):
        return vector[4 * self.heads + position]

    def col_head(self, vector, position):
        return vector[5 * self.heads + position]

    def edge(self, vector, number):
        return vector[6 * self.heads + number]


def pack_kernel(vector, source, *refs, head_of, first, rows):
    outs, sem = refs[:-1], refs[-1]
    copies = []
    for number, (out, (low, size)) in enumerate(zip(outs, rows)):
        for slot in range(out.shape[-1] // HD):
            start = pl.multiple_of(head_of(vector, first + slot) * HD, HD)
            lead = (slice(None),) * (len(source.shape) - 2)
            copies.append(
                pltpu.make_async_copy(
                    source.at[(*lead, pl.ds(low, size), pl.ds(start, HD))],
                    out.at[(*lead, slice(None), pl.ds(slot * HD, HD))],
                    sem.at[number, slot],
                )
            )
    for copy in copies:
        copy.start()
    for copy in copies:
        copy.wait()


def pack(vector, source, head_of, first, count, rows):
    anywhere = pl.BlockSpec(memory_space=pl.ANY)
    return pl.pallas_call(
        partial(pack_kernel, head_of=head_of, first=first, rows=rows),
        in_specs=[pl.BlockSpec(memory_space=pltpu.SMEM), anywhere],
        out_specs=[pl.BlockSpec(memory_space=pltpu.VMEM)] * len(rows),
        out_shape=[
            jax.ShapeDtypeStruct((*source.shape[:-2], size, count * HD), source.dtype)
            for _, size in rows
        ],
        scratch_shapes=[pltpu.SemaphoreType.DMA((len(rows), count))],
        compiler_params=kernel_params(8),
        cost_estimate=SMALL,
        name="pack",
    )(vector, source)


def attention_kernel(vector, *refs, plan, head_of, q_count, visiting, group):
    q_refs = refs[:q_count]
    kv_ref, top_ref, bottom_ref, top_rest, bottom_rest = refs[q_count : q_count + 5]
    refs = refs[q_count + 5 :]
    out_refs, stat_refs, halo = refs[:q_count], refs[q_count : 2 * q_count], refs[2 * q_count]
    frames, tokens, head_size = q_refs[0].shape
    span = top_ref.shape[2]
    tiles = tokens // span
    step = pl.program_id(0)
    head = head_of(vector, step)
    radius_row = plan.row_radius(vector, head)
    radius_col = plan.col_radius(vector, head)
    scale = 1.0 / math.sqrt(HD)

    @pl.when(step == 0)
    def _():
        for stat_ref in stat_refs:
            stat_ref[...] = jnp.zeros_like(stat_ref)

    def near(which, tile, wide):
        if not wide:
            return kv_ref[which, :, tile * span : (tile + 1) * span, :].reshape(-1, head_size)
        pieces = []
        if tile == 0:
            pieces.append(halo[0, which])
        low = max(tile - 1, 0) * span
        high = min(tile + 2, tiles) * span
        pieces.append(kv_ref[which, :, low:high, :])
        if tile == tiles - 1:
            pieces.append(halo[1, which])
        block = pieces[0] if len(pieces) == 1 else jnp.concatenate(pieces, axis=1)
        return block.reshape(-1, head_size)

    def attend(wide):
        lane = lax.broadcasted_iota(jnp.int32, (frames, span, LANES), 2)
        for tile in range(tiles):
            rows = slice(tile * span, (tile + 1) * span)
            keys = near(0, tile, wide)
            values = near(1, tile, wide)
            bias = None
            if wide and (tile == 0 or tile == tiles - 1):
                place = lax.rem(
                    lax.broadcasted_iota(jnp.int32, (1, keys.shape[0]), 1), 3 * span
                )
                low, high = 0, 3 * span
                if tile == 0:
                    low = jnp.where(plan.edge(vector, 0) == 0, span, 0)
                if tile == tiles - 1:
                    high = jnp.where(plan.edge(vector, 1) == 0, 2 * span, 3 * span)
                bias = jnp.where((place >= low) & (place < high), 0.0, -jnp.inf)
            for q_ref, out_ref, stat_ref in zip(q_refs, out_refs, stat_refs):
                query = q_ref[:, rows, :].reshape(-1, head_size)
                scores = (
                    lax.dot_general(
                        query, keys, (((1,), (1,)), ((), ())), preferred_element_type=jnp.float32
                    )
                    * scale
                )
                if bias is not None:
                    scores = scores + bias
                highest = jnp.max(scores, axis=1, keepdims=True)
                expo = jnp.exp(scores - highest)
                total = jnp.sum(expo, axis=1, keepdims=True)
                output = jnp.dot(
                    expo.astype(jnp.bfloat16), values, preferred_element_type=jnp.float32
                ) * (1.0 / total)
                out_ref[:, rows, :] = output.astype(jnp.bfloat16).reshape(frames, span, head_size)
                level = (highest + jnp.log(total)).reshape(frames, span, 1)
                stat_ref[:, rows, :] = jnp.where(lane == step, level, stat_ref[:, rows, :])

    active = step < group
    if visiting:

        @pl.when(active & (radius_col == 0))
        def _():
            for out_ref in out_refs:
                out_ref[...] = jnp.zeros_like(out_ref)

        active = active & (radius_col != 0)

    @pl.when(active & (radius_row == 0))
    def _():
        attend(False)

    always = plan.row_position(vector, head) < plan.most

    @pl.when(active & (radius_row != 0) & always)
    def _():
        halo[0] = top_ref[...]
        halo[1] = bottom_ref[...]

    @pl.when(active & (radius_row != 0) & jnp.logical_not(always))
    def _():
        halo[0] = top_rest[...]
        halo[1] = bottom_rest[...]

    @pl.when(active & (radius_row != 0))
    def _():
        attend(True)

    @pl.when(step == group)
    def _():
        for out_ref, stat_ref in zip(out_refs, stat_refs):
            level = stat_ref[...]
            high = level.astype(jnp.bfloat16).astype(jnp.float32)
            middle = (level - high).astype(jnp.bfloat16).astype(jnp.float32)
            low = level - high - middle
            packed = high + pltpu.roll(middle, LEVEL_STEP, 2) + pltpu.roll(low, 2 * LEVEL_STEP, 2)
            out_ref[...] = packed.astype(jnp.bfloat16)


def attention(plan, vector, query_blocks, keys_values, halos, first=None):
    frames, tokens, features = query_blocks[0].shape
    group = features // HD
    span = halos[0].shape[2]
    q_count = len(query_blocks)
    visiting = first is not None

    def slot_of(step):
        return jnp.minimum(step, group - 1)

    def head_of(vector, step):
        return plan.col_head(vector, first + slot_of(step)) if visiting else slot_of(step)

    def kv_index(step, vector):
        return 0, 0, 0, head_of(vector, step)

    def halo_index(step, vector):
        position = plan.row_position(vector, head_of(vector, step))
        return 0, 0, 0, jnp.minimum(position, plan.most - 1)

    def rest_index(step, vector):
        position = plan.row_position(vector, head_of(vector, step))
        return 0, 0, 0, jnp.maximum(position - plan.most, 0)

    q_spec = pl.BlockSpec((frames, tokens, HD), lambda step, _: (0, 0, slot_of(step)))
    kv_spec = pl.BlockSpec((2, frames, tokens, HD), kv_index)
    halo_spec = pl.BlockSpec((2, frames, span, HD), halo_index)
    rest_spec = pl.BlockSpec((2, frames, span, HD), rest_index)
    out_spec = pl.BlockSpec((frames, tokens, HD), lambda step, _: (0, 0, step))
    return pl.pallas_call(
        partial(
            attention_kernel,
            plan=plan,
            head_of=head_of,
            q_count=q_count,
            visiting=visiting,
            group=group,
        ),
        grid_spec=pltpu.PrefetchScalarGridSpec(
            num_scalar_prefetch=1,
            grid=(group + 1,),
            in_specs=[q_spec] * q_count + [kv_spec] + [halo_spec] * 2 + [rest_spec] * 2,
            out_specs=[out_spec] * q_count,
            scratch_shapes=[pltpu.VMEM((frames, tokens, LANES), jnp.float32)] * q_count
            + [pltpu.VMEM((2, 2, frames, span, HD), jnp.bfloat16)],
        ),
        out_shape=[jax.ShapeDtypeStruct((frames, tokens, (group + 1) * HD), jnp.bfloat16)]
        * q_count,
        compiler_params=kernel_params(12),
        cost_estimate=SMALL if visiting else LARGE,
        name="attend_visitors" if visiting else "attend_own",
    )(vector, *query_blocks, keys_values, *halos)


def combine_kernel(vector, own, own_stat, left, right, left_rest, right_rest, out, *, plan, heads):
    first = pl.program_id(0) * heads
    frames, tokens, _ = own.shape

    def level(stat, number):
        lane = lax.broadcasted_iota(jnp.int32, (LANES, HD), 0)
        pick = jnp.where(
            (lax.rem(lane, LEVEL_STEP) == number) & (lane < 3 * LEVEL_STEP), 1.0, 0.0
        ).astype(jnp.bfloat16)
        return jnp.dot(
            stat.reshape(-1, LANES), pick, preferred_element_type=jnp.float32
        ).reshape(frames, tokens, HD)

    for index in range(heads):
        head = first + index
        columns = slice(index * HD, (index + 1) * HD)
        across = plan.col_radius(vector, head) != 0
        position = plan.col_position(vector, head)

        @pl.when(jnp.logical_not(across))
        def _(columns=columns):
            out[:, :, columns] = own[:, :, columns]

        def join(sides, slot, columns, head):
            here = pl.ds(pl.multiple_of(slot * HD, HD), HD)
            levels = [level(own_stat[...], head)]
            values = [own[:, :, columns]]
            for number, side in enumerate(sides):
                value = level(side[:, :, side.shape[2] - LANES :], slot)
                levels.append(jnp.where(plan.edge(vector, 2 + number) == 0, -jnp.inf, value))
                values.append(side[:, :, here])
            highest = jnp.maximum(levels[0], jnp.maximum(levels[1], levels[2]))
            weights = [jnp.exp(x - highest) for x in levels]
            mixed = sum(value.astype(jnp.float32) * weight for value, weight in zip(values, weights))
            out[:, :, columns] = (mixed / (weights[0] + weights[1] + weights[2])).astype(
                jnp.bfloat16
            )

        @pl.when(across & (position < plan.most))
        def _(position=position, columns=columns, head=head):
            join((left, right), position, columns, head)

        @pl.when(across & (position >= plan.most))
        def _(position=position, columns=columns, head=head):
            join((left_rest, right_rest), position - plan.most, columns, head)


def combine(plan, vector, near, sides):
    frames, tokens, _ = near.shape
    heads = plan.heads // plan.order
    spec = pl.BlockSpec((frames, tokens, heads * HD), lambda h, _: (0, 0, h))
    stat_spec = pl.BlockSpec((frames, tokens, HD), lambda h, _: (0, 0, plan.heads))
    return pl.pallas_call(
        partial(combine_kernel, plan=plan, heads=heads),
        grid_spec=pltpu.PrefetchScalarGridSpec(
            num_scalar_prefetch=1,
            grid=(plan.order,),
            in_specs=[spec, stat_spec]
            + [pl.BlockSpec(side.shape, lambda h, _: (0, 0, 0)) for side in sides],
            out_specs=pl.BlockSpec(
                (frames, tokens, heads * HD), lambda h, vector: (0, 0, h ^ plan.edge(vector, 4))
            ),
        ),
        out_shape=jax.ShapeDtypeStruct((frames, tokens, plan.heads * HD), jnp.bfloat16),
        compiler_params=kernel_params(18),
        cost_estimate=LARGE,
        name="combine",
    )(vector, near, near, *sides)


def project_kernel(place, attended, *refs, slots, carried, start, column):
    arrays = 1 + max(piece[0] for slot in slots for piece in slot)
    pieces, refs = refs[:arrays], refs[arrays:]
    if carried:
        carry, refs = refs[0], refs[1:]
    out, rows, weight, rows_sem, weight_sem = refs
    columns = weight.shape[1]
    depth = weight.shape[2]
    rows_copy = pltpu.make_async_copy(
        attended.at[:, start : start + depth], rows, rows_sem.at[0]
    )
    rows_copy.start()
    for index, slot in enumerate(slots):
        for block in range(columns):
            low = 0
            for number, (array, size, share, turned) in enumerate(slot):
                first = pl.multiple_of((place[0] ^ share if turned else share) * size, size)
                pltpu.make_async_copy(
                    pieces[array].at[pl.ds(first, size), block * column : (block + 1) * column],
                    weight.at[index, block, low : low + size],
                    weight_sem.at[index, block, number],
                ).start()
                low += size
    rows_copy.wait()
    for index, slot in enumerate(slots):

        def body(block, _, index=index, slot=slot):
            low = 0
            for number, (_, size, _, _) in enumerate(slot):
                piece = weight.at[index, block, low : low + size]
                pltpu.make_async_copy(piece, piece, weight_sem.at[index, block, number]).wait()
                low += size
            total = jnp.dot(rows[...], weight[index, block], preferred_element_type=jnp.float32)
            here = pl.ds(pl.multiple_of(block * column, column), column)
            if carried:
                total = total + carry[index, :, here]
            out[index, :, here] = total.astype(out.dtype)
            return 0

        lax.fori_loop(0, columns, body, 0)


def project(place, attended, arrays, slots, carry, start, dtype):
    tokens = attended.shape[0]
    width = arrays[0].shape[1]
    column = 256 if width % 256 == 0 else width
    columns = width // column
    depth = sum(piece[1] for piece in slots[0])
    held = len(slots) * width * (2 * depth + tokens * jnp.dtype(dtype).itemsize)
    held += tokens * (2 * depth + (0 if carry is None else 4 * len(slots) * width))
    anywhere = pl.BlockSpec(memory_space=pl.ANY)
    inside = pl.BlockSpec(memory_space=pltpu.VMEM)
    return pl.pallas_call(
        partial(
            project_kernel, slots=slots, carried=carry is not None, start=start, column=column
        ),
        in_specs=[pl.BlockSpec(memory_space=pltpu.SMEM), anywhere]
        + [anywhere] * len(arrays)
        + ([] if carry is None else [inside]),
        out_specs=inside,
        out_shape=jax.ShapeDtypeStruct((len(slots), tokens, width), dtype),
        scratch_shapes=[
            pltpu.VMEM((tokens, depth), attended.dtype),
            pltpu.VMEM((len(slots), columns, depth, column), attended.dtype),
            pltpu.SemaphoreType.DMA((1,)),
            pltpu.SemaphoreType.DMA((len(slots), columns, max(len(slot) for slot in slots))),
        ],
        compiler_params=kernel_params(held // MEBI + 3),
        cost_estimate=SMALL,
        name="project",
    )(place, attended, *arrays, *([] if carry is None else [carry]))


def pick_kernel(place, own_hidden, other_hidden, own_gate, other_gate, hidden, gate):
    mine = place[2 * pl.program_id(0)] != 0

    @pl.when(mine)
    def _():
        hidden[0] = own_hidden[...]
        gate[0] = own_gate[...]

    @pl.when(jnp.logical_not(mine))
    def _():
        hidden[0] = other_hidden[...]
        gate[0] = other_gate[...]


def pick(place, own_hidden, other_hidden, own_gate, other_gate, width):
    tokens, features = own_hidden.shape
    count = 2 * features // width
    hidden = pl.BlockSpec((tokens, width), lambda i, place: (0, place[2 * i + 1]))
    gate = pl.BlockSpec((1, width), lambda i, place: (0, place[2 * i + 1]))
    return pl.pallas_call(
        pick_kernel,
        grid_spec=pltpu.PrefetchScalarGridSpec(
            num_scalar_prefetch=1,
            grid=(count,),
            in_specs=[hidden, hidden, gate, gate],
            out_specs=[
                pl.BlockSpec((1, tokens, width), lambda i, place: (i, 0, 0)),
                pl.BlockSpec((1, 1, width), lambda i, place: (i, 0, 0)),
            ],
        ),
        out_shape=[
            jax.ShapeDtypeStruct((count, tokens, width), jnp.bfloat16),
            jax.ShapeDtypeStruct((count, 1, width), jnp.float32),
        ],
        compiler_params=kernel_params(14),
        cost_estimate=SMALL,
        name="pick",
    )(place, own_hidden, other_hidden, own_gate, other_gate)


def mixed_block(hidden, gate, own_part, other_part):
    parts = own_part[0].astype(jnp.float32) + other_part[0].astype(jnp.float32)
    return hidden[0].astype(jnp.float32) + gate * parts


def mix_kernel(hidden, gate, own_part, other_part, mixed_ref, sums_ref):
    mixed = mixed_block(hidden, gate[0], own_part, other_part)
    mixed_ref[0] = mixed.astype(jnp.bfloat16)
    first = jnp.sum(mixed, axis=1, keepdims=True)
    second = jnp.sum(mixed * mixed, axis=1, keepdims=True)
    lane = lax.broadcasted_iota(jnp.int32, sums_ref.shape, 1)
    sums_ref[...] = jnp.where(lane == 0, first, jnp.where(lane == 1, second, 0.0))


def mix(hidden, gate, own_part, other_part):
    _, tokens, width = hidden.shape
    rows = 64 if tokens % 64 == 0 else tokens
    part = pl.BlockSpec((1, rows, width), lambda i: (0, i, 0))
    return pl.pallas_call(
        mix_kernel,
        grid=(tokens // rows,),
        in_specs=[part, pl.BlockSpec(gate.shape, lambda i: (0, 0, 0)), part, part],
        out_specs=[part, pl.BlockSpec((rows, LANES), lambda i: (i, 0))],
        out_shape=[
            jax.ShapeDtypeStruct((1, tokens, width), jnp.bfloat16),
            jax.ShapeDtypeStruct((tokens, LANES), jnp.float32),
        ],
        compiler_params=kernel_params(14),
        cost_estimate=SMALL,
        name="mix",
    )(hidden, gate, own_part, other_part)


def finish_kernel(place, gate, scale, shift_by, sums, early, *refs, count, blocks):
    hidden, own_parts, other_parts = (refs[count * k : count * (k + 1)] for k in range(3))
    residual, ffn = refs[3 * count :]
    width = early.shape[2]
    late = [
        mixed_block(hidden[index], gate[1 + index], own_parts[index], other_parts[index])
        for index in range(count)
    ]
    first = sums[:, 0:1]
    second = sums[:, 1:2]
    for mixed in late:
        first = first + jnp.sum(mixed, axis=1, keepdims=True)
        second = second + jnp.sum(mixed * mixed, axis=1, keepdims=True)
    average = first / D
    variance = second / D - average * average
    inverse = lax.rsqrt(variance + EPSILON)
    for block in range(blocks):
        columns = slice(block * width, (block + 1) * width)
        mixed = early[0].astype(jnp.float32)
        for index in range(count):
            mixed = jnp.where(place[block] == 1 + index, late[index], mixed)
        residual[:, columns] = mixed.astype(jnp.bfloat16)
        ffn[:, columns] = (
            (mixed - average) * inverse * (1.0 + scale[:, columns]) + shift_by[:, columns]
        ).astype(jnp.bfloat16)


def finish(place, hidden, gate, scale, shift_by, sums, early, own_parts, other_parts):
    count = own_parts.shape[0]
    _, tokens, width = hidden.shape
    blocks = place.shape[0]
    rows = 64 if tokens % 64 == 0 else tokens
    part = pl.BlockSpec((1, rows, width), lambda i, place: (0, i, 0))
    whole = pl.BlockSpec((1, blocks * width), lambda i, place: (0, 0))
    row = pl.BlockSpec((rows, blocks * width), lambda i, place: (i, 0))
    parts = [
        pl.BlockSpec((1, rows, width), lambda i, place, index=index: (index, i, 0))
        for index in range(count + 1)
    ]
    return pl.pallas_call(
        partial(finish_kernel, count=count, blocks=blocks),
        grid_spec=pltpu.PrefetchScalarGridSpec(
            num_scalar_prefetch=1,
            grid=(tokens // rows,),
            in_specs=[pl.BlockSpec(gate.shape, lambda i, place: (0, 0, 0)), whole, whole]
            + [pl.BlockSpec((rows, LANES), lambda i, place: (i, 0)), part]
            + parts[1:]
            + parts[:-1] * 2,
            out_specs=[row, row],
        ),
        out_shape=[jax.ShapeDtypeStruct((tokens, blocks * width), jnp.bfloat16)] * 2,
        compiler_params=kernel_params(14),
        cost_estimate=SMALL,
        name="finish",
    )(
        *(place, gate, scale, shift_by, sums, early),
        *([hidden] * count + [own_parts] * count + [other_parts] * count),
    )


def shift(block, axis, step):
    count = lax.axis_size(axis)
    pairs = [(i, i + step) for i in range(count) if 0 <= i + step < count]
    return lax.ppermute(block, axis, pairs)


def turn(block, axis, step):
    count = lax.axis_size(axis)
    return lax.ppermute(block, axis, [(i, (i + step) % count) for i in range(count)])


def swap(block, axis, bit):
    count = lax.axis_size(axis)
    return lax.ppermute(block, axis, [(i, i ^ bit) for i in range(count)])


class Tokens:
    def __init__(self, queries, keys_values, windows, order):
        self.plan = Plan(windows, order)
        self.queries = queries.reshape(queries.shape[0], -1, queries.shape[3])
        self.keys_values = keys_values.reshape(*keys_values.shape[:2], -1, keys_values.shape[4])
        self.span = TILE * queries.shape[2]
        self.parts = (0, self.plan.most), (self.plan.most, self.plan.heads - self.plan.most)

    def edge_rows(self, vector, part):
        low = self.queries.shape[1] - self.span
        rows = [(low, self.span), (0, self.span)]
        return pack(vector, self.keys_values, self.plan.row_head, *self.parts[part], rows)

    def leaving(self, vector, part):
        rows = [(0, self.queries.shape[1])]
        return pack(vector, self.queries, self.plan.col_head, *self.parts[part], rows)[0]

    def halos(self, rows):
        return shift(rows[0], "ha", 1), shift(rows[1], "ha", -1)

    def rest_halos(self, vector):
        shape = (*self.keys_values.shape[:2], self.span, self.parts[1][1] * HD)
        return lax.cond(
            self.plan.more_rows,
            lambda vector: self.halos(self.edge_rows(vector, 1)),
            lambda vector: (jnp.zeros(shape, jnp.bfloat16),) * 2,
            vector,
        )

    def stay(self, vector, halos):
        return attention(self.plan, vector, [self.queries], self.keys_values, halos)[0]

    def visit(self, vector, visitors, halos, part=0):
        first = self.parts[part][0]
        return attention(self.plan, vector, visitors, self.keys_values, halos, first)

    def rest_sides(self, vector, halos):
        shape = (*self.queries.shape[:2], (self.parts[1][1] + 1) * HD)

        def send(vector, *halos):
            queries = self.leaving(vector, 1)
            visitors = shift(queries, "wa", 1), shift(queries, "wa", -1)
            for_left, for_right = self.visit(vector, visitors, halos, 1)
            return shift(for_right, "wa", 1), shift(for_left, "wa", -1)

        return lax.cond(
            self.plan.more_cols,
            send,
            lambda vector, *halos: (jnp.zeros(shape, jnp.bfloat16),) * 2,
            vector,
            *halos,
        )

    def combine(self, vector, near, sides):
        attended = combine(self.plan, vector, near, sides)
        return attended.reshape(-1, attended.shape[2])


def together(*blocks):
    return lax.optimization_barrier(blocks)


def paired(hidden, queries, keys_values, windows, out_weight, picked):
    ha, wa, ta = lax.axis_index("ha"), lax.axis_index("wa"), lax.axis_index("ta")
    n_wa = lax.axis_size("wa")
    blocks = n_wa // 2
    depth = out_weight.shape[0] // 4
    width = out_weight.shape[1]

    def share(shares, number):
        return lax.dynamic_slice_in_dim(shares, number * depth, depth, 0)

    mine = lax.optimization_barrier(share(out_weight, ha))
    first = turn(mine, "wa", 1)
    tokens = Tokens(queries, keys_values, windows, 4)
    vector = tokens.plan.vector
    top, bottom = tokens.halos(tokens.edge_rows(vector, 0))
    queries = tokens.leaving(vector, 0)

    top, gate = together(top, picked[0:1])
    other_gate = swap(gate, "ta", 1)
    other_gate, mine = together(other_gate, mine)
    third = turn(mine, "wa", -1)

    first, top, bottom, other_gate, vector, queries = together(
        first, top, bottom, other_gate, vector, queries
    )
    first_x = swap(first, "ha", 1)
    first_y = swap(first, "ha", 2)
    from_left = shift(queries, "wa", 1)
    from_right = shift(queries, "wa", -1)
    halos = top, bottom, *tokens.rest_halos(vector)
    near = tokens.stay(vector, halos)

    near, first_x, first_y, third, first = together(near, first_x, first_y, third, first)
    third_x = swap(third, "ha", 1)
    third_y = swap(third, "ha", 2)
    second = turn(first, "wa", 1)
    for_left, for_right = tokens.visit(vector, (from_left, from_right), halos)

    left = shift(for_right, "wa", 1)
    right = shift(for_left, "wa", -1)

    third_x, third_y, second, vector, hidden, all_shares = together(
        third_x, third_y, second, vector, hidden, out_weight
    )
    second_x = swap(second, "ha", 1)
    second_y = swap(second, "ha", 2)
    other_hidden = swap(hidden, "ta", 1)
    rest_sides = tokens.rest_sides(vector, halos)

    attended = tokens.combine(vector, near, [left, right, *rest_sides])

    far = lax.optimization_barrier(share(all_shares, ha ^ 3))
    second_x, second_y, first_y, far, attended = together(
        second_x, second_y, first_y, far, attended
    )
    first_far = swap(first_y, "ha", 1)
    second_far = swap(second_x, "ha", 2)
    third_far = turn(far, "wa", -1)

    turned = ha.reshape(1)
    sums = project(
        turned,
        attended,
        [out_weight],
        [[(0, depth, number, True) for number in range(4)]],
        None,
        0,
        jnp.bfloat16,
    )
    other_sums = swap(sums, "ta", 1)
    late = project(
        turned,
        attended,
        [first, first_x, first_y, second, second_x, second_y, third, third_x, third_y],
        [[(start + number, depth, 0, False) for number in range(3)] for start in (0, 3, 6)],
        None,
        0,
        jnp.float32,
    )
    def block_of(distance):
        return lax.rem(wa - distance + n_wa, n_wa)

    owners = jnp.stack([block_of(distance) // blocks == ta for distance in range(n_wa)])
    inner = jnp.stack([lax.rem(block_of(distance), blocks) for distance in range(n_wa)])
    place = jnp.stack([owners.astype(jnp.int32), inner], axis=1).reshape(-1)
    late, place, other_hidden = together(late, place, other_hidden)
    base, gates = pick(place, hidden, other_hidden, gate, other_gate, width)
    early, totals = mix(base, gates, sums, other_sums)

    first_far, second_far, third_far, early, totals, late = together(
        first_far, second_far, third_far, early, totals, late
    )
    late = project(
        turned,
        attended,
        [first_far, second_far, third_far],
        [[(number, depth, 0, False)] for number in range(3)],
        late,
        3 * depth,
        jnp.bfloat16,
    )
    other_late = swap(late, "ta", 1)
    place = jnp.stack(
        [lax.rem(wa - ta * blocks - block + 2 * n_wa, n_wa) for block in range(blocks)]
    )
    return finish(
        place, base, gates, picked[2:3], picked[1:2], totals, early, late, other_late
    )


def gathered(hidden, queries, keys_values, windows, out_weight, picked):
    n_ha, n_wa, n_ta = lax.axis_size("ha"), lax.axis_size("wa"), lax.axis_size("ta")
    ha, ta = lax.axis_index("ha"), lax.axis_index("ta")
    work = Tokens(queries, keys_values, windows, 1)
    vector = work.plan.vector
    halos = *work.halos(work.edge_rows(vector, 0)), *work.rest_halos(vector)
    sent = work.leaving(vector, 0)
    visitors = shift(sent, "wa", 1), shift(sent, "wa", -1)
    near = work.stay(vector, halos)
    for_left, for_right = work.visit(vector, visitors, halos)
    sides = shift(for_right, "wa", 1), shift(for_left, "wa", -1)
    attended = work.combine(vector, near, [*sides, *work.rest_sides(vector, halos)])
    tokens, features = attended.shape
    depth = features // n_ha
    width = out_weight.shape[1]
    share = lax.dynamic_slice_in_dim(out_weight, ha * depth, depth, 0)
    weights = lax.all_gather(share, ("ha", "wa"), axis=0, tiled=False).reshape(
        n_ha, n_wa, depth, width
    )
    partial_sums = jnp.einsum(
        "thk,hwkc->wtc",
        attended.reshape(tokens, n_ha, depth),
        weights,
        preferred_element_type=jnp.float32,
    ).astype(jnp.bfloat16)
    blocks = n_wa // n_ta
    summed = None
    for step in range(n_ta):
        target = lax.rem(ta + step, n_ta)
        piece = lax.dynamic_slice_in_dim(partial_sums, target * blocks, blocks, 0)
        if step:
            piece = turn(piece, "ta", step)
        piece = piece.astype(jnp.float32)
        summed = piece if summed is None else summed + piece
    summed = jnp.transpose(summed, (1, 0, 2)).reshape(tokens, -1)
    mixed = hidden.astype(jnp.float32) + picked[0] * summed
    sum_first, sum_second = lax.psum((jnp.sum(mixed, axis=1), jnp.sum(mixed * mixed, axis=1)), "ta")
    average = (sum_first / D)[:, None]
    variance = (sum_second / D)[:, None] - average * average
    normed = (mixed - average) * lax.rsqrt(variance + EPSILON)
    ffn_input = (normed * (1.0 + picked[2]) + picked[1]).astype(jnp.bfloat16)
    return mixed.astype(jnp.bfloat16), ffn_input


def shards(hidden_states, queries, keys_values, out_weight, mod_table, windows, step_index):
    tokens = math.prod(queries.shape[:3])
    width = hidden_states.shape[3]
    picked = lax.dynamic_index_in_dim(mod_table, step_index[0], 0, keepdims=False)
    sizes = lax.axis_size("ha"), lax.axis_size("wa"), lax.axis_size("ta")
    tuned = sizes == (4, 4, 2) and out_weight.shape[0] % (20 * LANES) == 0
    residual_out, ffn_input = (paired if tuned else gathered)(
        hidden_states.reshape(tokens, width), queries, keys_values, windows, out_weight, picked
    )
    return residual_out.reshape(hidden_states.shape), ffn_input.reshape(hidden_states.shape)


def solution(mesh):
    return jax.shard_map(
        shards,
        mesh=mesh,
        in_specs=(
            P(None, "ha", "wa", "ta"),
            P(None, "ha", "wa", "ta"),
            P(None, None, "ha", "wa", "ta"),
            P("ta", "wa"),
            P(None, None, "ta"),
            P("ta", None),
            P(),
        ),
        out_specs=(P(None, "ha", "wa", "ta"), P(None, "ha", "wa", "ta")),
        check_vma=False,
    )
```

```python
from functools import partial
import math

import jax
import jax.numpy as jnp
from jax import lax
from jax.experimental import pallas as pl
from jax.experimental.pallas import tpu as pltpu
from jax.sharding import PartitionSpec as P

D = 5120
HD = 128
TILE = 8
LANES = 128
LEVEL_STEP = 32

EPSILON = 1e-06
MEBI = 1024 * 1024
SMALL = pl.CostEstimate(flops=1, bytes_accessed=1, transcendentals=0)
LARGE = pl.CostEstimate(flops=20_000_000_000, bytes_accessed=1, transcendentals=0)


def kernel_params(limit):
    return pltpu.CompilerParams(vmem_limit_bytes=limit * MEBI)


class Plan:
    def __init__(self, windows, order):
        heads = windows.shape[0]
        self.heads = heads
        self.most = max(heads * 7 // 10, 1)
        self.order = order
        n_ha, n_wa = lax.axis_size("ha"), lax.axis_size("wa")
        ha, wa = lax.axis_index("ha"), lax.axis_index("wa")
        number = lax.broadcasted_iota(jnp.int32, (2, heads, heads), 1)
        other = lax.broadcasted_iota(jnp.int32, (2, heads, heads), 2)
        idle = jnp.where(windows.T > 0, 0, 1)
        before = (idle[:, None, :] < idle[:, :, None]) | (
            (idle[:, None, :] == idle[:, :, None]) & (other < number)
        )
        position = jnp.sum(before.astype(jnp.int32), axis=2)
        sorted_heads = jnp.sum(jnp.where(position[:, None, :] == number, other, 0), axis=2)
        turned = ha if order > 1 else 0 * ha
        edges = jnp.stack([ha > 0, ha < n_ha - 1, wa > 0, wa < n_wa - 1, turned]).astype(jnp.int32)
        self.vector = jnp.concatenate(
            [windows.T.reshape(-1), position.reshape(-1), sorted_heads.reshape(-1), edges]
        )
        self.counts = jnp.sum(1.0 - idle, axis=1)

    def agree(self, counts):
        counts = lax.pmax(counts, "ta")
        self.more_rows = counts[0] > self.most
        self.more_cols = counts[1] > self.most
        return counts

    def row_radius(self, vector, head):
        return vector[head]

    def col_radius(self, vector, head):
        return vector[self.heads + head]

    def row_position(self, vector, head):
        return vector[2 * self.heads + head]

    def col_position(self, vector, head):
        return vector[3 * self.heads + head]

    def row_head(self, vector, position):
        return vector[4 * self.heads + position]

    def col_head(self, vector, position):
        return vector[5 * self.heads + position]

    def edge(self, vector, number):
        return vector[6 * self.heads + number]


def pack_kernel(vector, source, *refs, head_of, first, rows):
    outs, sem = refs[:-1], refs[-1]
    copies = []
    for number, (out, (low, size)) in enumerate(zip(outs, rows)):
        for slot in range(out.shape[-1] // HD):
            start = pl.multiple_of(head_of(vector, first + slot) * HD, HD)
            lead = (slice(None),) * (len(source.shape) - 2)
            copies.append(
                pltpu.make_async_copy(
                    source.at[(*lead, pl.ds(low, size), pl.ds(start, HD))],
                    out.at[(*lead, slice(None), pl.ds(slot * HD, HD))],
                    sem.at[number, slot],
                )
            )
    for copy in copies:
        copy.start()
    for copy in copies:
        copy.wait()


def pack(vector, source, head_of, first, count, rows):
    anywhere = pl.BlockSpec(memory_space=pl.ANY)
    return pl.pallas_call(
        partial(pack_kernel, head_of=head_of, first=first, rows=rows),
        in_specs=[pl.BlockSpec(memory_space=pltpu.SMEM), anywhere],
        out_specs=[pl.BlockSpec(memory_space=pltpu.VMEM)] * len(rows),
        out_shape=[
            jax.ShapeDtypeStruct((*source.shape[:-2], size, count * HD), source.dtype)
            for _, size in rows
        ],
        scratch_shapes=[pltpu.SemaphoreType.DMA((len(rows), count))],
        compiler_params=kernel_params(8),
        cost_estimate=SMALL,
        name="pack",
    )(vector, source)


def attention_kernel(vector, *refs, plan, head_of, q_count, visiting, group):
    q_refs = refs[:q_count]
    kv_ref, top_ref, bottom_ref, top_rest, bottom_rest = refs[q_count : q_count + 5]
    refs = refs[q_count + 5 :]
    out_refs, stat_refs, halo = refs[:q_count], refs[q_count : 2 * q_count], refs[2 * q_count]
    frames, tokens, head_size = q_refs[0].shape
    span = top_ref.shape[2]
    tiles = tokens // span
    step = pl.program_id(0)
    head = head_of(vector, step)
    radius_row = plan.row_radius(vector, head)
    radius_col = plan.col_radius(vector, head)
    scale = 1.0 / math.sqrt(HD)

    @pl.when(step == 0)
    def _():
        for stat_ref in stat_refs:
            stat_ref[...] = jnp.zeros_like(stat_ref)

    def near(which, tile, wide):
        if not wide:
            return kv_ref[which, :, tile * span : (tile + 1) * span, :].reshape(-1, head_size)
        pieces = []
        if tile == 0:
            pieces.append(halo[0, which])
        low = max(tile - 1, 0) * span
        high = min(tile + 2, tiles) * span
        pieces.append(kv_ref[which, :, low:high, :])
        if tile == tiles - 1:
            pieces.append(halo[1, which])
        block = pieces[0] if len(pieces) == 1 else jnp.concatenate(pieces, axis=1)
        return block.reshape(-1, head_size)

    def attend(wide):
        lane = lax.broadcasted_iota(jnp.int32, (frames, span, LANES), 2)
        for tile in range(tiles):
            rows = slice(tile * span, (tile + 1) * span)
            keys = near(0, tile, wide)
            values = near(1, tile, wide)
            bias = None
            if wide and (tile == 0 or tile == tiles - 1):
                place = lax.rem(
                    lax.broadcasted_iota(jnp.int32, (1, keys.shape[0]), 1), 3 * span
                )
                low, high = 0, 3 * span
                if tile == 0:
                    low = jnp.where(plan.edge(vector, 0) == 0, span, 0)
                if tile == tiles - 1:
                    high = jnp.where(plan.edge(vector, 1) == 0, 2 * span, 3 * span)
                bias = jnp.where((place >= low) & (place < high), 0.0, -jnp.inf)
            for q_ref, out_ref, stat_ref in zip(q_refs, out_refs, stat_refs):
                query = q_ref[:, rows, :].reshape(-1, head_size)
                scores = (
                    lax.dot_general(
                        query, keys, (((1,), (1,)), ((), ())), preferred_element_type=jnp.float32
                    )
                    * scale
                )
                if bias is not None:
                    scores = scores + bias
                highest = jnp.max(scores, axis=1, keepdims=True)
                expo = jnp.exp(scores - highest)
                total = jnp.sum(expo, axis=1, keepdims=True)
                output = jnp.dot(
                    expo.astype(jnp.bfloat16), values, preferred_element_type=jnp.float32
                ) * (1.0 / total)
                out_ref[:, rows, :] = output.astype(jnp.bfloat16).reshape(frames, span, head_size)
                level = (highest + jnp.log(total)).reshape(frames, span, 1)
                stat_ref[:, rows, :] = jnp.where(lane == step, level, stat_ref[:, rows, :])

    active = step < group
    if visiting:

        @pl.when(active & (radius_col == 0))
        def _():
            for out_ref in out_refs:
                out_ref[...] = jnp.zeros_like(out_ref)

        active = active & (radius_col != 0)

    @pl.when(active & (radius_row == 0))
    def _():
        attend(False)

    always = plan.row_position(vector, head) < plan.most

    @pl.when(active & (radius_row != 0) & always)
    def _():
        halo[0] = top_ref[...]
        halo[1] = bottom_ref[...]

    @pl.when(active & (radius_row != 0) & jnp.logical_not(always))
    def _():
        halo[0] = top_rest[...]
        halo[1] = bottom_rest[...]

    @pl.when(active & (radius_row != 0))
    def _():
        attend(True)

    @pl.when(step == group)
    def _():
        for out_ref, stat_ref in zip(out_refs, stat_refs):
            level = stat_ref[...]
            high = level.astype(jnp.bfloat16).astype(jnp.float32)
            middle = (level - high).astype(jnp.bfloat16).astype(jnp.float32)
            low = level - high - middle
            packed = high + pltpu.roll(middle, LEVEL_STEP, 2) + pltpu.roll(low, 2 * LEVEL_STEP, 2)
            out_ref[...] = packed.astype(jnp.bfloat16)


def attention(plan, vector, query_blocks, keys_values, halos, first=None):
    frames, tokens, features = query_blocks[0].shape
    group = features // HD
    span = halos[0].shape[2]
    q_count = len(query_blocks)
    visiting = first is not None

    def slot_of(step):
        return jnp.minimum(step, group - 1)

    def head_of(vector, step):
        return plan.col_head(vector, first + slot_of(step)) if visiting else slot_of(step)

    def kv_index(step, vector):
        return 0, 0, 0, head_of(vector, step)

    def halo_index(step, vector):
        position = plan.row_position(vector, head_of(vector, step))
        return 0, 0, 0, jnp.minimum(position, plan.most - 1)

    def rest_index(step, vector):
        position = plan.row_position(vector, head_of(vector, step))
        return 0, 0, 0, jnp.maximum(position - plan.most, 0)

    q_spec = pl.BlockSpec((frames, tokens, HD), lambda step, _: (0, 0, slot_of(step)))
    kv_spec = pl.BlockSpec((2, frames, tokens, HD), kv_index)
    halo_spec = pl.BlockSpec((2, frames, span, HD), halo_index)
    rest_spec = pl.BlockSpec((2, frames, span, HD), rest_index)
    out_spec = pl.BlockSpec((frames, tokens, HD), lambda step, _: (0, 0, step))
    return pl.pallas_call(
        partial(
            attention_kernel,
            plan=plan,
            head_of=head_of,
            q_count=q_count,
            visiting=visiting,
            group=group,
        ),
        grid_spec=pltpu.PrefetchScalarGridSpec(
            num_scalar_prefetch=1,
            grid=(group + 1,),
            in_specs=[q_spec] * q_count + [kv_spec] + [halo_spec] * 2 + [rest_spec] * 2,
            out_specs=[out_spec] * q_count,
            scratch_shapes=[pltpu.VMEM((frames, tokens, LANES), jnp.float32)] * q_count
            + [pltpu.VMEM((2, 2, frames, span, HD), jnp.bfloat16)],
        ),
        out_shape=[jax.ShapeDtypeStruct((frames, tokens, (group + 1) * HD), jnp.bfloat16)]
        * q_count,
        compiler_params=kernel_params(12),
        cost_estimate=SMALL if visiting else LARGE,
        name="attend_visitors" if visiting else "attend_own",
    )(vector, *query_blocks, keys_values, *halos)


def combine_kernel(vector, own, own_stat, left, right, left_rest, right_rest, out, *, plan, heads):
    first = pl.program_id(0) * heads
    frames, tokens, _ = own.shape

    def level(stat, number):
        lane = lax.broadcasted_iota(jnp.int32, (LANES, HD), 0)
        pick = jnp.where(
            (lax.rem(lane, LEVEL_STEP) == number) & (lane < 3 * LEVEL_STEP), 1.0, 0.0
        ).astype(jnp.bfloat16)
        return jnp.dot(
            stat.reshape(-1, LANES), pick, preferred_element_type=jnp.float32
        ).reshape(frames, tokens, HD)

    for index in range(heads):
        head = first + index
        columns = slice(index * HD, (index + 1) * HD)
        across = plan.col_radius(vector, head) != 0
        position = plan.col_position(vector, head)

        @pl.when(jnp.logical_not(across))
        def _(columns=columns):
            out[:, :, columns] = own[:, :, columns]

        def join(sides, slot, columns, head):
            here = pl.ds(pl.multiple_of(slot * HD, HD), HD)
            levels = [level(own_stat[...], head)]
            values = [own[:, :, columns]]
            for number, side in enumerate(sides):
                value = level(side[:, :, side.shape[2] - LANES :], slot)
                levels.append(jnp.where(plan.edge(vector, 2 + number) == 0, -jnp.inf, value))
                values.append(side[:, :, here])
            highest = jnp.maximum(levels[0], jnp.maximum(levels[1], levels[2]))
            weights = [jnp.exp(x - highest) for x in levels]
            mixed = sum(value.astype(jnp.float32) * weight for value, weight in zip(values, weights))
            out[:, :, columns] = (mixed / (weights[0] + weights[1] + weights[2])).astype(
                jnp.bfloat16
            )

        @pl.when(across & (position < plan.most))
        def _(position=position, columns=columns, head=head):
            join((left, right), position, columns, head)

        @pl.when(across & (position >= plan.most))
        def _(position=position, columns=columns, head=head):
            join((left_rest, right_rest), position - plan.most, columns, head)


def combine(plan, vector, near, sides):
    frames, tokens, _ = near.shape
    heads = plan.heads // plan.order
    spec = pl.BlockSpec((frames, tokens, heads * HD), lambda h, _: (0, 0, h))
    stat_spec = pl.BlockSpec((frames, tokens, HD), lambda h, _: (0, 0, plan.heads))
    return pl.pallas_call(
        partial(combine_kernel, plan=plan, heads=heads),
        grid_spec=pltpu.PrefetchScalarGridSpec(
            num_scalar_prefetch=1,
            grid=(plan.order,),
            in_specs=[spec, stat_spec]
            + [pl.BlockSpec(side.shape, lambda h, _: (0, 0, 0)) for side in sides],
            out_specs=pl.BlockSpec(
                (frames, tokens, heads * HD), lambda h, vector: (0, 0, h ^ plan.edge(vector, 4))
            ),
        ),
        out_shape=jax.ShapeDtypeStruct((frames, tokens, plan.heads * HD), jnp.bfloat16),
        compiler_params=kernel_params(18),
        cost_estimate=LARGE,
        name="combine",
    )(vector, near, near, *sides)


def project_kernel(place, attended, *refs, slots, carried, start, column):
    arrays = 1 + max(piece[0] for slot in slots for piece in slot)
    pieces, refs = refs[:arrays], refs[arrays:]
    if carried:
        carry, refs = refs[0], refs[1:]
    out, rows, weight, rows_sem, weight_sem = refs
    columns = weight.shape[1]
    depth = weight.shape[2]
    rows_copy = pltpu.make_async_copy(
        attended.at[:, start : start + depth], rows, rows_sem.at[0]
    )
    rows_copy.start()
    for index, slot in enumerate(slots):
        for block in range(columns):
            low = 0
            for number, (array, size, share, turned) in enumerate(slot):
                first = pl.multiple_of((place[0] ^ share if turned else share) * size, size)
                pltpu.make_async_copy(
                    pieces[array].at[pl.ds(first, size), block * column : (block + 1) * column],
                    weight.at[index, block, low : low + size],
                    weight_sem.at[index, block, number],
                ).start()
                low += size
    rows_copy.wait()
    for index, slot in enumerate(slots):

        def body(block, _, index=index, slot=slot):
            low = 0
            for number, (_, size, _, _) in enumerate(slot):
                piece = weight.at[index, block, low : low + size]
                pltpu.make_async_copy(piece, piece, weight_sem.at[index, block, number]).wait()
                low += size
            total = jnp.dot(rows[...], weight[index, block], preferred_element_type=jnp.float32)
            here = pl.ds(pl.multiple_of(block * column, column), column)
            if carried:
                total = total + carry[index, :, here]
            out[index, :, here] = total.astype(out.dtype)
            return 0

        lax.fori_loop(0, columns, body, 0)


def project(place, attended, arrays, slots, carry, start, dtype):
    tokens = attended.shape[0]
    width = arrays[0].shape[1]
    column = 256 if width % 256 == 0 else width
    columns = width // column
    depth = sum(piece[1] for piece in slots[0])
    held = len(slots) * width * (2 * depth + tokens * jnp.dtype(dtype).itemsize)
    held += tokens * (2 * depth + (0 if carry is None else 4 * len(slots) * width))
    anywhere = pl.BlockSpec(memory_space=pl.ANY)
    inside = pl.BlockSpec(memory_space=pltpu.VMEM)
    return pl.pallas_call(
        partial(
            project_kernel, slots=slots, carried=carry is not None, start=start, column=column
        ),
        in_specs=[pl.BlockSpec(memory_space=pltpu.SMEM), anywhere]
        + [anywhere] * len(arrays)
        + ([] if carry is None else [inside]),
        out_specs=inside,
        out_shape=jax.ShapeDtypeStruct((len(slots), tokens, width), dtype),
        scratch_shapes=[
            pltpu.VMEM((tokens, depth), attended.dtype),
            pltpu.VMEM((len(slots), columns, depth, column), attended.dtype),
            pltpu.SemaphoreType.DMA((1,)),
            pltpu.SemaphoreType.DMA((len(slots), columns, max(len(slot) for slot in slots))),
        ],
        compiler_params=kernel_params(held // MEBI + 3),
        cost_estimate=SMALL,
        name="project",
    )(place, attended, *arrays, *([] if carry is None else [carry]))


def pick_kernel(place, own_hidden, other_hidden, own_gate, other_gate, hidden, gate):
    mine = place[2 * pl.program_id(0)] != 0

    @pl.when(mine)
    def _():
        hidden[0] = own_hidden[...]
        gate[0] = own_gate[...]

    @pl.when(jnp.logical_not(mine))
    def _():
        hidden[0] = other_hidden[...]
        gate[0] = other_gate[...]


def pick(place, own_hidden, other_hidden, own_gate, other_gate, width):
    tokens, features = own_hidden.shape
    count = 2 * features // width
    hidden = pl.BlockSpec((tokens, width), lambda i, place: (0, place[2 * i + 1]))
    gate = pl.BlockSpec((1, width), lambda i, place: (0, place[2 * i + 1]))
    return pl.pallas_call(
        pick_kernel,
        grid_spec=pltpu.PrefetchScalarGridSpec(
            num_scalar_prefetch=1,
            grid=(count,),
            in_specs=[hidden, hidden, gate, gate],
            out_specs=[
                pl.BlockSpec((1, tokens, width), lambda i, place: (i, 0, 0)),
                pl.BlockSpec((1, 1, width), lambda i, place: (i, 0, 0)),
            ],
        ),
        out_shape=[
            jax.ShapeDtypeStruct((count, tokens, width), jnp.bfloat16),
            jax.ShapeDtypeStruct((count, 1, width), jnp.float32),
        ],
        compiler_params=kernel_params(14),
        cost_estimate=SMALL,
        name="pick",
    )(place, own_hidden, other_hidden, own_gate, other_gate)


def mixed_block(hidden, gate, own_part, other_part):
    parts = own_part[0].astype(jnp.float32) + other_part[0].astype(jnp.float32)
    return hidden[0].astype(jnp.float32) + gate * parts


def mix_kernel(hidden, gate, own_part, other_part, mixed_ref, sums_ref):
    mixed = mixed_block(hidden, gate[0], own_part, other_part)
    mixed_ref[0] = mixed.astype(jnp.bfloat16)
    first = jnp.sum(mixed, axis=1, keepdims=True)
    second = jnp.sum(mixed * mixed, axis=1, keepdims=True)
    lane = lax.broadcasted_iota(jnp.int32, sums_ref.shape, 1)
    sums_ref[...] = jnp.where(lane == 0, first, jnp.where(lane == 1, second, 0.0))


def mix(hidden, gate, own_part, other_part):
    _, tokens, width = hidden.shape
    rows = 64 if tokens % 64 == 0 else tokens
    part = pl.BlockSpec((1, rows, width), lambda i: (0, i, 0))
    return pl.pallas_call(
        mix_kernel,
        grid=(tokens // rows,),
        in_specs=[part, pl.BlockSpec(gate.shape, lambda i: (0, 0, 0)), part, part],
        out_specs=[part, pl.BlockSpec((rows, LANES), lambda i: (i, 0))],
        out_shape=[
            jax.ShapeDtypeStruct((1, tokens, width), jnp.bfloat16),
            jax.ShapeDtypeStruct((tokens, LANES), jnp.float32),
        ],
        compiler_params=kernel_params(14),
        cost_estimate=SMALL,
        name="mix",
    )(hidden, gate, own_part, other_part)


def finish_kernel(place, gate, scale, shift_by, sums, early, *refs, count, blocks):
    hidden, own_parts, other_parts = (refs[count * k : count * (k + 1)] for k in range(3))
    residual, ffn = refs[3 * count :]
    width = early.shape[2]
    late = [
        mixed_block(hidden[index], gate[1 + index], own_parts[index], other_parts[index])
        for index in range(count)
    ]
    first = sums[:, 0:1]
    second = sums[:, 1:2]
    for mixed in late:
        first = first + jnp.sum(mixed, axis=1, keepdims=True)
        second = second + jnp.sum(mixed * mixed, axis=1, keepdims=True)
    average = first / D
    variance = second / D - average * average
    inverse = lax.rsqrt(variance + EPSILON)
    for block in range(blocks):
        columns = slice(block * width, (block + 1) * width)
        mixed = early[0].astype(jnp.float32)
        for index in range(count):
            mixed = jnp.where(place[block] == 1 + index, late[index], mixed)
        residual[:, columns] = mixed.astype(jnp.bfloat16)
        ffn[:, columns] = (
            (mixed - average) * inverse * (1.0 + scale[:, columns]) + shift_by[:, columns]
        ).astype(jnp.bfloat16)


def finish(place, hidden, gate, scale, shift_by, sums, early, own_parts, other_parts):
    count = own_parts.shape[0]
    _, tokens, width = hidden.shape
    blocks = place.shape[0]
    rows = 64 if tokens % 64 == 0 else tokens
    part = pl.BlockSpec((1, rows, width), lambda i, place: (0, i, 0))
    whole = pl.BlockSpec((1, blocks * width), lambda i, place: (0, 0))
    row = pl.BlockSpec((rows, blocks * width), lambda i, place: (i, 0))
    parts = [
        pl.BlockSpec((1, rows, width), lambda i, place, index=index: (index, i, 0))
        for index in range(count + 1)
    ]
    return pl.pallas_call(
        partial(finish_kernel, count=count, blocks=blocks),
        grid_spec=pltpu.PrefetchScalarGridSpec(
            num_scalar_prefetch=1,
            grid=(tokens // rows,),
            in_specs=[pl.BlockSpec(gate.shape, lambda i, place: (0, 0, 0)), whole, whole]
            + [pl.BlockSpec((rows, LANES), lambda i, place: (i, 0)), part]
            + parts[1:]
            + parts[:-1] * 2,
            out_specs=[row, row],
        ),
        out_shape=[jax.ShapeDtypeStruct((tokens, blocks * width), jnp.bfloat16)] * 2,
        compiler_params=kernel_params(14),
        cost_estimate=SMALL,
        name="finish",
    )(
        *(place, gate, scale, shift_by, sums, early),
        *([hidden] * count + [own_parts] * count + [other_parts] * count),
    )


def shift(block, axis, step):
    count = lax.axis_size(axis)
    pairs = [(i, i + step) for i in range(count) if 0 <= i + step < count]
    return lax.ppermute(block, axis, pairs)


def turn(block, axis, step):
    count = lax.axis_size(axis)
    return lax.ppermute(block, axis, [(i, (i + step) % count) for i in range(count)])


def swap(block, axis, bit):
    count = lax.axis_size(axis)
    return lax.ppermute(block, axis, [(i, i ^ bit) for i in range(count)])


class Tokens:
    def __init__(self, queries, keys_values, windows, order):
        self.plan = Plan(windows, order)
        self.queries = queries.reshape(queries.shape[0], -1, queries.shape[3])
        self.keys_values = keys_values.reshape(*keys_values.shape[:2], -1, keys_values.shape[4])
        self.span = TILE * queries.shape[2]
        self.parts = (0, self.plan.most), (self.plan.most, self.plan.heads - self.plan.most)

    def edge_rows(self, vector, part):
        low = self.queries.shape[1] - self.span
        rows = [(low, self.span), (0, self.span)]
        return pack(vector, self.keys_values, self.plan.row_head, *self.parts[part], rows)

    def leaving(self, vector, part):
        rows = [(0, self.queries.shape[1])]
        return pack(vector, self.queries, self.plan.col_head, *self.parts[part], rows)[0]

    def halos(self, rows):
        return shift(rows[0], "ha", 1), shift(rows[1], "ha", -1)

    def rest_halos(self, vector):
        shape = (*self.keys_values.shape[:2], self.span, self.parts[1][1] * HD)
        return lax.cond(
            self.plan.more_rows,
            lambda vector: self.halos(self.edge_rows(vector, 1)),
            lambda vector: (jnp.zeros(shape, jnp.bfloat16),) * 2,
            vector,
        )

    def stay(self, vector, halos):
        return attention(self.plan, vector, [self.queries], self.keys_values, halos)[0]

    def visit(self, vector, visitors, halos, part=0):
        first = self.parts[part][0]
        return attention(self.plan, vector, visitors, self.keys_values, halos, first)

    def rest_sides(self, vector, halos):
        shape = (*self.queries.shape[:2], (self.parts[1][1] + 1) * HD)

        def send(vector, *halos):
            queries = self.leaving(vector, 1)
            visitors = shift(queries, "wa", 1), shift(queries, "wa", -1)
            for_left, for_right = self.visit(vector, visitors, halos, 1)
            return shift(for_right, "wa", 1), shift(for_left, "wa", -1)

        return lax.cond(
            self.plan.more_cols,
            send,
            lambda vector, *halos: (jnp.zeros(shape, jnp.bfloat16),) * 2,
            vector,
            *halos,
        )

    def combine(self, vector, near, sides):
        attended = combine(self.plan, vector, near, sides)
        return attended.reshape(-1, attended.shape[2])


def together(*blocks):
    return lax.optimization_barrier(blocks)


def paired(hidden, queries, keys_values, windows, out_weight, picked):
    ha, wa, ta = lax.axis_index("ha"), lax.axis_index("wa"), lax.axis_index("ta")
    n_wa = lax.axis_size("wa")
    blocks = n_wa // 2
    depth = out_weight.shape[0] // 4
    width = out_weight.shape[1]

    def share(shares, number):
        return lax.dynamic_slice_in_dim(shares, number * depth, depth, 0)

    mine = lax.optimization_barrier(share(out_weight, ha))
    first = turn(mine, "wa", 1)
    tokens = Tokens(queries, keys_values, windows, 4)
    vector = tokens.plan.vector
    top, bottom = tokens.halos(tokens.edge_rows(vector, 0))

    top, gate = together(top, picked[0:1])
    other_gate = swap(gate, "ta", 1)
    other_gate, counts = together(other_gate, tokens.plan.counts)
    counts, vector = together(tokens.plan.agree(counts), vector)
    queries, mine = together(tokens.leaving(vector, 0), mine)
    third = turn(mine, "wa", -1)

    first, top, bottom, other_gate, vector, queries = together(
        first, top, bottom, other_gate, vector, queries
    )
    first_x = swap(first, "ha", 1)
    first_y = swap(first, "ha", 2)
    from_left = shift(queries, "wa", 1)
    from_right = shift(queries, "wa", -1)
    halos = top, bottom, *tokens.rest_halos(vector)
    near = tokens.stay(vector, halos)

    near, first_x, first_y, third, first = together(near, first_x, first_y, third, first)
    third_x = swap(third, "ha", 1)
    third_y = swap(third, "ha", 2)
    second = turn(first, "wa", 1)
    for_left, for_right = tokens.visit(vector, (from_left, from_right), halos)

    left = shift(for_right, "wa", 1)
    right = shift(for_left, "wa", -1)

    third_x, third_y, second, vector, hidden, all_shares = together(
        third_x, third_y, second, vector, hidden, out_weight
    )
    second_x = swap(second, "ha", 1)
    second_y = swap(second, "ha", 2)
    other_hidden = swap(hidden, "ta", 1)
    rest_sides = tokens.rest_sides(vector, halos)

    far = lax.optimization_barrier(share(all_shares, ha ^ 3))
    left, right, far = together(left, right, far)
    attended = tokens.combine(vector, near, [left, right, *rest_sides])

    second_x, second_y, first_y, far, attended = together(
        second_x, second_y, first_y, far, attended
    )
    first_far = swap(first_y, "ha", 1)
    second_far = swap(second_x, "ha", 2)
    third_far = turn(far, "wa", -1)

    turned = ha.reshape(1)
    sums = project(
        turned,
        attended,
        [out_weight],
        [[(0, depth, number, True) for number in range(4)]],
        None,
        0,
        jnp.bfloat16,
    )
    other_sums = swap(sums, "ta", 1)
    late = project(
        turned,
        attended,
        [first, first_x, first_y, second, second_x, second_y, third, third_x, third_y],
        [[(start + number, depth, 0, False) for number in range(3)] for start in (0, 3, 6)],
        None,
        0,
        jnp.float32,
    )
    def block_of(distance):
        return lax.rem(wa - distance + n_wa, n_wa)

    owners = jnp.stack([block_of(distance) // blocks == ta for distance in range(n_wa)])
    inner = jnp.stack([lax.rem(block_of(distance), blocks) for distance in range(n_wa)])
    place = jnp.stack([owners.astype(jnp.int32), inner], axis=1).reshape(-1)
    late, place, other_hidden = together(late, place, other_hidden)
    base, gates = pick(place, hidden, other_hidden, gate, other_gate, width)
    early, totals = mix(base, gates, sums, other_sums)

    first_far, second_far, third_far, early, totals, late = together(
        first_far, second_far, third_far, early, totals, late
    )
    late = project(
        turned,
        attended,
        [first_far, second_far, third_far],
        [[(number, depth, 0, False)] for number in range(3)],
        late,
        3 * depth,
        jnp.bfloat16,
    )
    other_late = swap(late, "ta", 1)
    place = jnp.stack(
        [lax.rem(wa - ta * blocks - block + 2 * n_wa, n_wa) for block in range(blocks)]
    )
    return finish(
        place, base, gates, picked[2:3], picked[1:2], totals, early, late, other_late
    )


def gathered(hidden, queries, keys_values, windows, out_weight, picked):
    n_ha, n_wa, n_ta = lax.axis_size("ha"), lax.axis_size("wa"), lax.axis_size("ta")
    ha, ta = lax.axis_index("ha"), lax.axis_index("ta")
    work = Tokens(queries, keys_values, windows, 1)
    vector = work.plan.vector
    work.plan.agree(work.plan.counts)
    halos = *work.halos(work.edge_rows(vector, 0)), *work.rest_halos(vector)
    sent = work.leaving(vector, 0)
    visitors = shift(sent, "wa", 1), shift(sent, "wa", -1)
    near = work.stay(vector, halos)
    for_left, for_right = work.visit(vector, visitors, halos)
    sides = shift(for_right, "wa", 1), shift(for_left, "wa", -1)
    attended = work.combine(vector, near, [*sides, *work.rest_sides(vector, halos)])
    tokens, features = attended.shape
    depth = features // n_ha
    width = out_weight.shape[1]
    share = lax.dynamic_slice_in_dim(out_weight, ha * depth, depth, 0)
    weights = lax.all_gather(share, ("ha", "wa"), axis=0, tiled=False).reshape(
        n_ha, n_wa, depth, width
    )
    partial_sums = jnp.einsum(
        "thk,hwkc->wtc",
        attended.reshape(tokens, n_ha, depth),
        weights,
        preferred_element_type=jnp.float32,
    ).astype(jnp.bfloat16)
    blocks = n_wa // n_ta
    summed = None
    for step in range(n_ta):
        target = lax.rem(ta + step, n_ta)
        piece = lax.dynamic_slice_in_dim(partial_sums, target * blocks, blocks, 0)
        if step:
            piece = turn(piece, "ta", step)
        piece = piece.astype(jnp.float32)
        summed = piece if summed is None else summed + piece
    summed = jnp.transpose(summed, (1, 0, 2)).reshape(tokens, -1)
    mixed = hidden.astype(jnp.float32) + picked[0] * summed
    sum_first, sum_second = lax.psum((jnp.sum(mixed, axis=1), jnp.sum(mixed * mixed, axis=1)), "ta")
    average = (sum_first / D)[:, None]
    variance = (sum_second / D)[:, None] - average * average
    normed = (mixed - average) * lax.rsqrt(variance + EPSILON)
    ffn_input = (normed * (1.0 + picked[2]) + picked[1]).astype(jnp.bfloat16)
    return mixed.astype(jnp.bfloat16), ffn_input


def shards(hidden_states, queries, keys_values, out_weight, mod_table, windows, step_index):
    tokens = math.prod(queries.shape[:3])
    width = hidden_states.shape[3]
    picked = lax.dynamic_index_in_dim(mod_table, step_index[0], 0, keepdims=False)
    sizes = lax.axis_size("ha"), lax.axis_size("wa"), lax.axis_size("ta")
    tuned = sizes == (4, 4, 2) and out_weight.shape[0] % (20 * LANES) == 0
    residual_out, ffn_input = (paired if tuned else gathered)(
        hidden_states.reshape(tokens, width), queries, keys_values, windows, out_weight, picked
    )
    return residual_out.reshape(hidden_states.shape), ffn_input.reshape(hidden_states.shape)


def solution(mesh):
    return jax.shard_map(
        shards,
        mesh=mesh,
        in_specs=(
            P(None, "ha", "wa", "ta"),
            P(None, "ha", "wa", "ta"),
            P(None, None, "ha", "wa", "ta"),
            P("ta", "wa"),
            P(None, None, "ta"),
            P("ta", None),
            P(),
        ),
        out_specs=(P(None, "ha", "wa", "ta"), P(None, "ha", "wa", "ta")),
        check_vma=False,
    )
```

```python
from functools import partial
import math

import jax
import jax.numpy as jnp
from jax import lax
from jax.experimental import pallas as pl
from jax.experimental.pallas import tpu as pltpu
from jax.sharding import PartitionSpec as P

D = 5120
HD = 128
TILE = 8
LANES = 128
LEVEL_STEP = 32

EPSILON = 1e-06
MEBI = 1024 * 1024
SMALL = pl.CostEstimate(flops=1, bytes_accessed=1, transcendentals=0)
LARGE = pl.CostEstimate(flops=20_000_000_000, bytes_accessed=1, transcendentals=0)


def kernel_params(limit):
    return pltpu.CompilerParams(vmem_limit_bytes=limit * MEBI)


class Plan:
    def __init__(self, windows, order):
        heads = windows.shape[0]
        self.heads = heads
        self.most = max(heads * 7 // 10, 1)
        self.order = order
        n_ha, n_wa = lax.axis_size("ha"), lax.axis_size("wa")
        ha, wa = lax.axis_index("ha"), lax.axis_index("wa")
        number = lax.broadcasted_iota(jnp.int32, (2, heads, heads), 1)
        other = lax.broadcasted_iota(jnp.int32, (2, heads, heads), 2)
        idle = jnp.where(windows.T > 0, 0, 1)
        before = (idle[:, None, :] < idle[:, :, None]) | (
            (idle[:, None, :] == idle[:, :, None]) & (other < number)
        )
        position = jnp.sum(before.astype(jnp.int32), axis=2)
        sorted_heads = jnp.sum(jnp.where(position[:, None, :] == number, other, 0), axis=2)
        turned = ha if order > 1 else 0 * ha
        edges = jnp.stack([ha > 0, ha < n_ha - 1, wa > 0, wa < n_wa - 1, turned]).astype(jnp.int32)
        self.vector = jnp.concatenate(
            [windows.T.reshape(-1), position.reshape(-1), sorted_heads.reshape(-1), edges]
        )
        self.counts = jnp.sum(1.0 - idle, axis=1)

    def agree(self, counts):
        counts = lax.pmax(counts, "ta")
        self.more_rows = counts[0] > self.most
        self.more_cols = counts[1] > self.most
        return counts

    def row_radius(self, vector, head):
        return vector[head]

    def col_radius(self, vector, head):
        return vector[self.heads + head]

    def row_position(self, vector, head):
        return vector[2 * self.heads + head]

    def col_position(self, vector, head):
        return vector[3 * self.heads + head]

    def row_head(self, vector, position):
        return vector[4 * self.heads + position]

    def col_head(self, vector, position):
        return vector[5 * self.heads + position]

    def edge(self, vector, number):
        return vector[6 * self.heads + number]


def pack_kernel(vector, source, *refs, head_of, first, rows):
    outs, sem = refs[:-1], refs[-1]
    copies = []
    for number, (out, (low, size)) in enumerate(zip(outs, rows)):
        for slot in range(out.shape[-1] // HD):
            start = pl.multiple_of(head_of(vector, first + slot) * HD, HD)
            lead = (slice(None),) * (len(source.shape) - 2)
            copies.append(
                pltpu.make_async_copy(
                    source.at[(*lead, pl.ds(low, size), pl.ds(start, HD))],
                    out.at[(*lead, slice(None), pl.ds(slot * HD, HD))],
                    sem.at[number, slot],
                )
            )
    for copy in copies:
        copy.start()
    for copy in copies:
        copy.wait()


def pack(vector, source, head_of, first, count, rows):
    anywhere = pl.BlockSpec(memory_space=pl.ANY)
    return pl.pallas_call(
        partial(pack_kernel, head_of=head_of, first=first, rows=rows),
        in_specs=[pl.BlockSpec(memory_space=pltpu.SMEM), anywhere],
        out_specs=[pl.BlockSpec(memory_space=pltpu.VMEM)] * len(rows),
        out_shape=[
            jax.ShapeDtypeStruct((*source.shape[:-2], size, count * HD), source.dtype)
            for _, size in rows
        ],
        scratch_shapes=[pltpu.SemaphoreType.DMA((len(rows), count))],
        compiler_params=kernel_params(8),
        cost_estimate=SMALL,
        name="pack",
    )(vector, source)


def attention_kernel(vector, *refs, plan, head_of, q_count, visiting, group):
    q_refs = refs[:q_count]
    kv_ref, top_ref, bottom_ref, top_rest, bottom_rest = refs[q_count : q_count + 5]
    refs = refs[q_count + 5 :]
    out_refs, stat_refs, halo = refs[:q_count], refs[q_count : 2 * q_count], refs[2 * q_count]
    frames, tokens, head_size = q_refs[0].shape
    span = top_ref.shape[2]
    tiles = tokens // span
    step = pl.program_id(0)
    head = head_of(vector, step)
    radius_row = plan.row_radius(vector, head)
    radius_col = plan.col_radius(vector, head)
    scale = 1.0 / math.sqrt(HD)

    @pl.when(step == 0)
    def _():
        for stat_ref in stat_refs:
            stat_ref[...] = jnp.zeros_like(stat_ref)

    def near(which, tile, wide):
        if not wide:
            return kv_ref[which, :, tile * span : (tile + 1) * span, :].reshape(-1, head_size)
        pieces = []
        if tile == 0:
            pieces.append(halo[0, which])
        low = max(tile - 1, 0) * span
        high = min(tile + 2, tiles) * span
        pieces.append(kv_ref[which, :, low:high, :])
        if tile == tiles - 1:
            pieces.append(halo[1, which])
        block = pieces[0] if len(pieces) == 1 else jnp.concatenate(pieces, axis=1)
        return block.reshape(-1, head_size)

    def attend(wide):
        lane = lax.broadcasted_iota(jnp.int32, (frames, span, LANES), 2)
        for tile in range(tiles):
            rows = slice(tile * span, (tile + 1) * span)
            keys = near(0, tile, wide)
            values = near(1, tile, wide)
            bias = None
            if wide and (tile == 0 or tile == tiles - 1):
                place = lax.rem(
                    lax.broadcasted_iota(jnp.int32, (1, keys.shape[0]), 1), 3 * span
                )
                low, high = 0, 3 * span
                if tile == 0:
                    low = jnp.where(plan.edge(vector, 0) == 0, span, 0)
                if tile == tiles - 1:
                    high = jnp.where(plan.edge(vector, 1) == 0, 2 * span, 3 * span)
                bias = jnp.where((place >= low) & (place < high), 0.0, -jnp.inf)
            for q_ref, out_ref, stat_ref in zip(q_refs, out_refs, stat_refs):
                query = q_ref[:, rows, :].reshape(-1, head_size)
                scores = (
                    lax.dot_general(
                        query, keys, (((1,), (1,)), ((), ())), preferred_element_type=jnp.float32
                    )
                    * scale
                )
                if bias is not None:
                    scores = scores + bias
                highest = jnp.max(scores, axis=1, keepdims=True)
                expo = jnp.exp(scores - highest)
                total = jnp.sum(expo, axis=1, keepdims=True)
                output = jnp.dot(
                    expo.astype(jnp.bfloat16), values, preferred_element_type=jnp.float32
                ) * (1.0 / total)
                out_ref[:, rows, :] = output.astype(jnp.bfloat16).reshape(frames, span, head_size)
                level = (highest + jnp.log(total)).reshape(frames, span, 1)
                stat_ref[:, rows, :] = jnp.where(lane == step, level, stat_ref[:, rows, :])

    active = step < group
    if visiting:

        @pl.when(active & (radius_col == 0))
        def _():
            for out_ref in out_refs:
                out_ref[...] = jnp.zeros_like(out_ref)

        active = active & (radius_col != 0)

    @pl.when(active & (radius_row == 0))
    def _():
        attend(False)

    always = plan.row_position(vector, head) < plan.most

    @pl.when(active & (radius_row != 0) & always)
    def _():
        halo[0] = top_ref[...]
        halo[1] = bottom_ref[...]

    @pl.when(active & (radius_row != 0) & jnp.logical_not(always))
    def _():
        halo[0] = top_rest[...]
        halo[1] = bottom_rest[...]

    @pl.when(active & (radius_row != 0))
    def _():
        attend(True)

    @pl.when(step == group)
    def _():
        for out_ref, stat_ref in zip(out_refs, stat_refs):
            level = stat_ref[...]
            high = level.astype(jnp.bfloat16).astype(jnp.float32)
            middle = (level - high).astype(jnp.bfloat16).astype(jnp.float32)
            low = level - high - middle
            packed = high + pltpu.roll(middle, LEVEL_STEP, 2) + pltpu.roll(low, 2 * LEVEL_STEP, 2)
            out_ref[...] = packed.astype(jnp.bfloat16)


def attention(plan, vector, query_blocks, keys_values, halos, first=None):
    frames, tokens, features = query_blocks[0].shape
    group = features // HD
    span = halos[0].shape[2]
    q_count = len(query_blocks)
    visiting = first is not None

    def slot_of(step):
        return jnp.minimum(step, group - 1)

    def head_of(vector, step):
        return plan.col_head(vector, first + slot_of(step)) if visiting else slot_of(step)

    def kv_index(step, vector):
        return 0, 0, 0, head_of(vector, step)

    def halo_index(step, vector):
        position = plan.row_position(vector, head_of(vector, step))
        return 0, 0, 0, jnp.minimum(position, plan.most - 1)

    def rest_index(step, vector):
        position = plan.row_position(vector, head_of(vector, step))
        return 0, 0, 0, jnp.maximum(position - plan.most, 0)

    q_spec = pl.BlockSpec((frames, tokens, HD), lambda step, _: (0, 0, slot_of(step)))
    kv_spec = pl.BlockSpec((2, frames, tokens, HD), kv_index)
    halo_spec = pl.BlockSpec((2, frames, span, HD), halo_index)
    rest_spec = pl.BlockSpec((2, frames, span, HD), rest_index)
    out_spec = pl.BlockSpec((frames, tokens, HD), lambda step, _: (0, 0, step))
    return pl.pallas_call(
        partial(
            attention_kernel,
            plan=plan,
            head_of=head_of,
            q_count=q_count,
            visiting=visiting,
            group=group,
        ),
        grid_spec=pltpu.PrefetchScalarGridSpec(
            num_scalar_prefetch=1,
            grid=(group + 1,),
            in_specs=[q_spec] * q_count + [kv_spec] + [halo_spec] * 2 + [rest_spec] * 2,
            out_specs=[out_spec] * q_count,
            scratch_shapes=[pltpu.VMEM((frames, tokens, LANES), jnp.float32)] * q_count
            + [pltpu.VMEM((2, 2, frames, span, HD), jnp.bfloat16)],
        ),
        out_shape=[jax.ShapeDtypeStruct((frames, tokens, (group + 1) * HD), jnp.bfloat16)]
        * q_count,
        compiler_params=kernel_params(12),
        cost_estimate=SMALL if visiting else LARGE,
        name="attend_visitors" if visiting else "attend_own",
    )(vector, *query_blocks, keys_values, *halos)


def combine_kernel(vector, own, own_stat, left, right, left_rest, right_rest, out, *, plan, heads):
    first = pl.program_id(0) * heads
    frames, tokens, _ = own.shape

    def level(stat, number):
        lane = lax.broadcasted_iota(jnp.int32, (LANES, HD), 0)
        pick = jnp.where(
            (lax.rem(lane, LEVEL_STEP) == number) & (lane < 3 * LEVEL_STEP), 1.0, 0.0
        ).astype(jnp.bfloat16)
        return jnp.dot(
            stat.reshape(-1, LANES), pick, preferred_element_type=jnp.float32
        ).reshape(frames, tokens, HD)

    for index in range(heads):
        head = first + index
        columns = slice(index * HD, (index + 1) * HD)
        across = plan.col_radius(vector, head) != 0
        position = plan.col_position(vector, head)

        @pl.when(jnp.logical_not(across))
        def _(columns=columns):
            out[:, :, columns] = own[:, :, columns]

        def join(sides, slot, columns, head):
            here = pl.ds(pl.multiple_of(slot * HD, HD), HD)
            levels = [level(own_stat[...], head)]
            values = [own[:, :, columns]]
            for number, side in enumerate(sides):
                value = level(side[:, :, side.shape[2] - LANES :], slot)
                levels.append(jnp.where(plan.edge(vector, 2 + number) == 0, -jnp.inf, value))
                values.append(side[:, :, here])
            highest = jnp.maximum(levels[0], jnp.maximum(levels[1], levels[2]))
            weights = [jnp.exp(x - highest) for x in levels]
            mixed = sum(value.astype(jnp.float32) * weight for value, weight in zip(values, weights))
            out[:, :, columns] = (mixed / (weights[0] + weights[1] + weights[2])).astype(
                jnp.bfloat16
            )

        @pl.when(across & (position < plan.most))
        def _(position=position, columns=columns, head=head):
            join((left, right), position, columns, head)

        @pl.when(across & (position >= plan.most))
        def _(position=position, columns=columns, head=head):
            join((left_rest, right_rest), position - plan.most, columns, head)


def combine(plan, vector, near, sides):
    frames, tokens, _ = near.shape
    heads = plan.heads // plan.order
    spec = pl.BlockSpec((frames, tokens, heads * HD), lambda h, _: (0, 0, h))
    stat_spec = pl.BlockSpec((frames, tokens, HD), lambda h, _: (0, 0, plan.heads))
    return pl.pallas_call(
        partial(combine_kernel, plan=plan, heads=heads),
        grid_spec=pltpu.PrefetchScalarGridSpec(
            num_scalar_prefetch=1,
            grid=(plan.order,),
            in_specs=[spec, stat_spec]
            + [pl.BlockSpec(side.shape, lambda h, _: (0, 0, 0)) for side in sides],
            out_specs=pl.BlockSpec(
                (frames, tokens, heads * HD), lambda h, vector: (0, 0, h ^ plan.edge(vector, 4))
            ),
        ),
        out_shape=jax.ShapeDtypeStruct((frames, tokens, plan.heads * HD), jnp.bfloat16),
        compiler_params=kernel_params(18),
        cost_estimate=LARGE,
        name="combine",
    )(vector, near, near, *sides)


def project_kernel(place, attended, *refs, slots, carried, start, column):
    arrays = 1 + max(piece[0] for slot in slots for piece in slot)
    pieces, refs = refs[:arrays], refs[arrays:]
    if carried:
        carry, refs = refs[0], refs[1:]
    out, rows, weight, rows_sem, weight_sem = refs
    columns = weight.shape[1]
    depth = weight.shape[2]
    rows_copy = pltpu.make_async_copy(
        attended.at[:, start : start + depth], rows, rows_sem.at[0]
    )
    rows_copy.start()
    for index, slot in enumerate(slots):
        for block in range(columns):
            low = 0
            for number, (array, size, share, turned) in enumerate(slot):
                first = pl.multiple_of((place[0] ^ share if turned else share) * size, size)
                pltpu.make_async_copy(
                    pieces[array].at[pl.ds(first, size), block * column : (block + 1) * column],
                    weight.at[index, block, low : low + size],
                    weight_sem.at[index, block, number],
                ).start()
                low += size
    rows_copy.wait()
    for index, slot in enumerate(slots):

        def body(block, _, index=index, slot=slot):
            low = 0
            for number, (_, size, _, _) in enumerate(slot):
                piece = weight.at[index, block, low : low + size]
                pltpu.make_async_copy(piece, piece, weight_sem.at[index, block, number]).wait()
                low += size
            total = jnp.dot(rows[...], weight[index, block], preferred_element_type=jnp.float32)
            here = pl.ds(pl.multiple_of(block * column, column), column)
            if carried:
                total = total + carry[index, :, here]
            out[index, :, here] = total.astype(out.dtype)
            return 0

        lax.fori_loop(0, columns, body, 0)


def project(place, attended, arrays, slots, carry, start, dtype):
    tokens = attended.shape[0]
    width = arrays[0].shape[1]
    column = 256 if width % 256 == 0 else width
    columns = width // column
    depth = sum(piece[1] for piece in slots[0])
    held = len(slots) * width * (2 * depth + tokens * jnp.dtype(dtype).itemsize)
    held += tokens * (2 * depth + (0 if carry is None else 4 * len(slots) * width))
    anywhere = pl.BlockSpec(memory_space=pl.ANY)
    inside = pl.BlockSpec(memory_space=pltpu.VMEM)
    return pl.pallas_call(
        partial(
            project_kernel, slots=slots, carried=carry is not None, start=start, column=column
        ),
        in_specs=[pl.BlockSpec(memory_space=pltpu.SMEM), anywhere]
        + [anywhere] * len(arrays)
        + ([] if carry is None else [inside]),
        out_specs=inside,
        out_shape=jax.ShapeDtypeStruct((len(slots), tokens, width), dtype),
        scratch_shapes=[
            pltpu.VMEM((tokens, depth), attended.dtype),
            pltpu.VMEM((len(slots), columns, depth, column), attended.dtype),
            pltpu.SemaphoreType.DMA((1,)),
            pltpu.SemaphoreType.DMA((len(slots), columns, max(len(slot) for slot in slots))),
        ],
        compiler_params=kernel_params(held // MEBI + 3),
        cost_estimate=SMALL,
        name="project",
    )(place, attended, *arrays, *([] if carry is None else [carry]))


def pick_kernel(place, own_hidden, other_hidden, own_gate, other_gate, hidden, gate):
    mine = place[2 * pl.program_id(0)] != 0

    @pl.when(mine)
    def _():
        hidden[0] = own_hidden[...]
        gate[0] = own_gate[...]

    @pl.when(jnp.logical_not(mine))
    def _():
        hidden[0] = other_hidden[...]
        gate[0] = other_gate[...]


def pick(place, own_hidden, other_hidden, own_gate, other_gate, width):
    tokens, features = own_hidden.shape
    count = 2 * features // width
    hidden = pl.BlockSpec((tokens, width), lambda i, place: (0, place[2 * i + 1]))
    gate = pl.BlockSpec((1, width), lambda i, place: (0, place[2 * i + 1]))
    return pl.pallas_call(
        pick_kernel,
        grid_spec=pltpu.PrefetchScalarGridSpec(
            num_scalar_prefetch=1,
            grid=(count,),
            in_specs=[hidden, hidden, gate, gate],
            out_specs=[
                pl.BlockSpec((1, tokens, width), lambda i, place: (i, 0, 0)),
                pl.BlockSpec((1, 1, width), lambda i, place: (i, 0, 0)),
            ],
        ),
        out_shape=[
            jax.ShapeDtypeStruct((count, tokens, width), jnp.bfloat16),
            jax.ShapeDtypeStruct((count, 1, width), jnp.float32),
        ],
        compiler_params=kernel_params(14),
        cost_estimate=SMALL,
        name="pick",
    )(place, own_hidden, other_hidden, own_gate, other_gate)


def mixed_block(hidden, gate, own_part, other_part):
    parts = own_part[0].astype(jnp.float32) + other_part[0].astype(jnp.float32)
    return hidden[0].astype(jnp.float32) + gate * parts


def mix_kernel(hidden, gate, own_part, other_part, mixed_ref, sums_ref):
    mixed = mixed_block(hidden, gate[0], own_part, other_part)
    mixed_ref[0] = mixed.astype(jnp.bfloat16)
    first = jnp.sum(mixed, axis=1, keepdims=True)
    second = jnp.sum(mixed * mixed, axis=1, keepdims=True)
    lane = lax.broadcasted_iota(jnp.int32, sums_ref.shape, 1)
    sums_ref[...] = jnp.where(lane == 0, first, jnp.where(lane == 1, second, 0.0))


def mix(hidden, gate, own_part, other_part):
    _, tokens, width = hidden.shape
    rows = 64 if tokens % 64 == 0 else tokens
    part = pl.BlockSpec((1, rows, width), lambda i: (0, i, 0))
    return pl.pallas_call(
        mix_kernel,
        grid=(tokens // rows,),
        in_specs=[part, pl.BlockSpec(gate.shape, lambda i: (0, 0, 0)), part, part],
        out_specs=[part, pl.BlockSpec((rows, LANES), lambda i: (i, 0))],
        out_shape=[
            jax.ShapeDtypeStruct((1, tokens, width), jnp.bfloat16),
            jax.ShapeDtypeStruct((tokens, LANES), jnp.float32),
        ],
        compiler_params=kernel_params(14),
        cost_estimate=SMALL,
        name="mix",
    )(hidden, gate, own_part, other_part)


def finish_kernel(place, gate, scale, shift_by, sums, early, *refs, count, blocks):
    hidden, own_parts, other_parts = (refs[count * k : count * (k + 1)] for k in range(3))
    residual, ffn = refs[3 * count :]
    width = early.shape[2]
    late = [
        mixed_block(hidden[index], gate[1 + index], own_parts[index], other_parts[index])
        for index in range(count)
    ]
    first = sums[:, 0:1]
    second = sums[:, 1:2]
    for mixed in late:
        first = first + jnp.sum(mixed, axis=1, keepdims=True)
        second = second + jnp.sum(mixed * mixed, axis=1, keepdims=True)
    average = first / D
    variance = second / D - average * average
    inverse = lax.rsqrt(variance + EPSILON)
    for block in range(blocks):
        columns = slice(block * width, (block + 1) * width)
        mixed = early[0].astype(jnp.float32)
        for index in range(count):
            mixed = jnp.where(place[block] == 1 + index, late[index], mixed)
        residual[:, columns] = mixed.astype(jnp.bfloat16)
        ffn[:, columns] = (
            (mixed - average) * inverse * (1.0 + scale[:, columns]) + shift_by[:, columns]
        ).astype(jnp.bfloat16)


def finish(place, hidden, gate, scale, shift_by, sums, early, own_parts, other_parts):
    count = own_parts.shape[0]
    _, tokens, width = hidden.shape
    blocks = place.shape[0]
    rows = 64 if tokens % 64 == 0 else tokens
    part = pl.BlockSpec((1, rows, width), lambda i, place: (0, i, 0))
    whole = pl.BlockSpec((1, blocks * width), lambda i, place: (0, 0))
    row = pl.BlockSpec((rows, blocks * width), lambda i, place: (i, 0))
    parts = [
        pl.BlockSpec((1, rows, width), lambda i, place, index=index: (index, i, 0))
        for index in range(count + 1)
    ]
    return pl.pallas_call(
        partial(finish_kernel, count=count, blocks=blocks),
        grid_spec=pltpu.PrefetchScalarGridSpec(
            num_scalar_prefetch=1,
            grid=(tokens // rows,),
            in_specs=[pl.BlockSpec(gate.shape, lambda i, place: (0, 0, 0)), whole, whole]
            + [pl.BlockSpec((rows, LANES), lambda i, place: (i, 0)), part]
            + parts[1:]
            + parts[:-1] * 2,
            out_specs=[row, row],
        ),
        out_shape=[jax.ShapeDtypeStruct((tokens, blocks * width), jnp.bfloat16)] * 2,
        compiler_params=kernel_params(14),
        cost_estimate=SMALL,
        name="finish",
    )(
        *(place, gate, scale, shift_by, sums, early),
        *([hidden] * count + [own_parts] * count + [other_parts] * count),
    )


def shift(block, axis, step):
    count = lax.axis_size(axis)
    pairs = [(i, i + step) for i in range(count) if 0 <= i + step < count]
    return lax.ppermute(block, axis, pairs)


def turn(block, axis, step):
    count = lax.axis_size(axis)
    return lax.ppermute(block, axis, [(i, (i + step) % count) for i in range(count)])


def swap(block, axis, bit):
    count = lax.axis_size(axis)
    return lax.ppermute(block, axis, [(i, i ^ bit) for i in range(count)])


class Tokens:
    def __init__(self, queries, keys_values, windows, order):
        self.plan = Plan(windows, order)
        self.queries = queries.reshape(queries.shape[0], -1, queries.shape[3])
        self.keys_values = keys_values.reshape(*keys_values.shape[:2], -1, keys_values.shape[4])
        self.span = TILE * queries.shape[2]
        self.parts = (0, self.plan.most), (self.plan.most, self.plan.heads - self.plan.most)

    def edge_rows(self, vector, part):
        low = self.queries.shape[1] - self.span
        rows = [(low, self.span), (0, self.span)]
        return pack(vector, self.keys_values, self.plan.row_head, *self.parts[part], rows)

    def leaving(self, vector, part):
        rows = [(0, self.queries.shape[1])]
        return pack(vector, self.queries, self.plan.col_head, *self.parts[part], rows)[0]

    def halos(self, rows):
        return shift(rows[0], "ha", 1), shift(rows[1], "ha", -1)

    def rest_halos(self, vector):
        shape = (*self.keys_values.shape[:2], self.span, self.parts[1][1] * HD)
        return lax.cond(
            self.plan.more_rows,
            lambda vector: self.halos(self.edge_rows(vector, 1)),
            lambda vector: (jnp.zeros(shape, jnp.bfloat16),) * 2,
            vector,
        )

    def stay(self, vector, halos):
        return attention(self.plan, vector, [self.queries], self.keys_values, halos)[0]

    def visit(self, vector, visitors, halos, part=0):
        first = self.parts[part][0]
        return attention(self.plan, vector, visitors, self.keys_values, halos, first)

    def rest_sides(self, vector, halos):
        shape = (*self.queries.shape[:2], (self.parts[1][1] + 1) * HD)

        def send(vector, *halos):
            queries = self.leaving(vector, 1)
            visitors = shift(queries, "wa", 1), shift(queries, "wa", -1)
            for_left, for_right = self.visit(vector, visitors, halos, 1)
            return shift(for_right, "wa", 1), shift(for_left, "wa", -1)

        return lax.cond(
            self.plan.more_cols,
            send,
            lambda vector, *halos: (jnp.zeros(shape, jnp.bfloat16),) * 2,
            vector,
            *halos,
        )

    def combine(self, vector, near, sides):
        attended = combine(self.plan, vector, near, sides)
        return attended.reshape(-1, attended.shape[2])


def together(*blocks):
    return lax.optimization_barrier(blocks)


def paired(hidden, queries, keys_values, windows, out_weight, picked):
    ha, wa, ta = lax.axis_index("ha"), lax.axis_index("wa"), lax.axis_index("ta")
    n_wa = lax.axis_size("wa")
    blocks = n_wa // 2
    depth = out_weight.shape[0] // 4
    width = out_weight.shape[1]

    def share(shares, number):
        return lax.dynamic_slice_in_dim(shares, number * depth, depth, 0)

    mine = lax.optimization_barrier(share(out_weight, ha))
    first = turn(mine, "wa", 1)
    tokens = Tokens(queries, keys_values, windows, 4)
    vector = tokens.plan.vector
    top, bottom = tokens.halos(tokens.edge_rows(vector, 0))

    top, gate = together(top, picked[0:1])
    other_gate = swap(gate, "ta", 1)
    other_gate, counts = together(other_gate, tokens.plan.counts)
    counts, vector = together(tokens.plan.agree(counts), vector)
    queries, mine = together(tokens.leaving(vector, 0), mine)
    third = turn(mine, "wa", -1)

    first, top, bottom, other_gate, vector, queries = together(
        first, top, bottom, other_gate, vector, queries
    )
    first_x = swap(first, "ha", 1)
    first_y = swap(first, "ha", 2)
    from_left = shift(queries, "wa", 1)
    from_right = shift(queries, "wa", -1)
    halos = top, bottom, *tokens.rest_halos(vector)
    near = tokens.stay(vector, halos)

    near, first_x, first_y, third, first = together(near, first_x, first_y, third, first)
    third_x = swap(third, "ha", 1)
    third_y = swap(third, "ha", 2)
    second = turn(first, "wa", 1)
    for_left, for_right = tokens.visit(vector, (from_left, from_right), halos)

    left = shift(for_right, "wa", 1)
    right = shift(for_left, "wa", -1)

    third_x, third_y, second, vector, hidden, all_shares = together(
        third_x, third_y, second, vector, hidden, out_weight
    )
    second_x = swap(second, "ha", 1)
    second_y = swap(second, "ha", 2)
    other_hidden = swap(hidden, "ta", 1)
    rest_sides = tokens.rest_sides(vector, halos)

    far = lax.optimization_barrier(share(all_shares, ha ^ 3))
    left, right, far, *rest_sides = together(left, right, far, *rest_sides)
    attended = tokens.combine(vector, near, [left, right, *rest_sides])

    second_x, second_y, first_y, far, attended = together(
        second_x, second_y, first_y, far, attended
    )
    first_far = swap(first_y, "ha", 1)
    second_far = swap(second_x, "ha", 2)
    third_far = turn(far, "wa", -1)

    turned = ha.reshape(1)
    sums = project(
        turned,
        attended,
        [out_weight],
        [[(0, depth, number, True) for number in range(4)]],
        None,
        0,
        jnp.bfloat16,
    )
    other_sums = swap(sums, "ta", 1)
    late = project(
        turned,
        attended,
        [first, first_x, first_y, second, second_x, second_y, third, third_x, third_y],
        [[(start + number, depth, 0, False) for number in range(3)] for start in (0, 3, 6)],
        None,
        0,
        jnp.float32,
    )
    def block_of(distance):
        return lax.rem(wa - distance + n_wa, n_wa)

    owners = jnp.stack([block_of(distance) // blocks == ta for distance in range(n_wa)])
    inner = jnp.stack([lax.rem(block_of(distance), blocks) for distance in range(n_wa)])
    place = jnp.stack([owners.astype(jnp.int32), inner], axis=1).reshape(-1)
    late, place, other_hidden = together(late, place, other_hidden)
    base, gates = pick(place, hidden, other_hidden, gate, other_gate, width)
    early, totals = mix(base, gates, sums, other_sums)

    first_far, second_far, third_far, early, totals, late = together(
        first_far, second_far, third_far, early, totals, late
    )
    late = project(
        turned,
        attended,
        [first_far, second_far, third_far],
        [[(number, depth, 0, False)] for number in range(3)],
        late,
        3 * depth,
        jnp.bfloat16,
    )
    other_late = swap(late, "ta", 1)
    place = jnp.stack(
        [lax.rem(wa - ta * blocks - block + 2 * n_wa, n_wa) for block in range(blocks)]
    )
    return finish(
        place, base, gates, picked[2:3], picked[1:2], totals, early, late, other_late
    )


def gathered(hidden, queries, keys_values, windows, out_weight, picked):
    n_ha, n_wa, n_ta = lax.axis_size("ha"), lax.axis_size("wa"), lax.axis_size("ta")
    ha, ta = lax.axis_index("ha"), lax.axis_index("ta")
    work = Tokens(queries, keys_values, windows, 1)
    vector = work.plan.vector
    work.plan.agree(work.plan.counts)
    halos = *work.halos(work.edge_rows(vector, 0)), *work.rest_halos(vector)
    sent = work.leaving(vector, 0)
    visitors = shift(sent, "wa", 1), shift(sent, "wa", -1)
    near = work.stay(vector, halos)
    for_left, for_right = work.visit(vector, visitors, halos)
    sides = shift(for_right, "wa", 1), shift(for_left, "wa", -1)
    attended = work.combine(vector, near, [*sides, *work.rest_sides(vector, halos)])
    tokens, features = attended.shape
    depth = features // n_ha
    width = out_weight.shape[1]
    share = lax.dynamic_slice_in_dim(out_weight, ha * depth, depth, 0)
    weights = lax.all_gather(share, ("ha", "wa"), axis=0, tiled=False).reshape(
        n_ha, n_wa, depth, width
    )
    partial_sums = jnp.einsum(
        "thk,hwkc->wtc",
        attended.reshape(tokens, n_ha, depth),
        weights,
        preferred_element_type=jnp.float32,
    ).astype(jnp.bfloat16)
    blocks = n_wa // n_ta
    summed = None
    for step in range(n_ta):
        target = lax.rem(ta + step, n_ta)
        piece = lax.dynamic_slice_in_dim(partial_sums, target * blocks, blocks, 0)
        if step:
            piece = turn(piece, "ta", step)
        piece = piece.astype(jnp.float32)
        summed = piece if summed is None else summed + piece
    summed = jnp.transpose(summed, (1, 0, 2)).reshape(tokens, -1)
    mixed = hidden.astype(jnp.float32) + picked[0] * summed
    sum_first, sum_second = lax.psum((jnp.sum(mixed, axis=1), jnp.sum(mixed * mixed, axis=1)), "ta")
    average = (sum_first / D)[:, None]
    variance = (sum_second / D)[:, None] - average * average
    normed = (mixed - average) * lax.rsqrt(variance + EPSILON)
    ffn_input = (normed * (1.0 + picked[2]) + picked[1]).astype(jnp.bfloat16)
    return mixed.astype(jnp.bfloat16), ffn_input


def shards(hidden_states, queries, keys_values, out_weight, mod_table, windows, step_index):
    tokens = math.prod(queries.shape[:3])
    width = hidden_states.shape[3]
    picked = lax.dynamic_index_in_dim(mod_table, step_index[0], 0, keepdims=False)
    sizes = lax.axis_size("ha"), lax.axis_size("wa"), lax.axis_size("ta")
    tuned = sizes == (4, 4, 2) and out_weight.shape[0] % (20 * LANES) == 0
    residual_out, ffn_input = (paired if tuned else gathered)(
        hidden_states.reshape(tokens, width), queries, keys_values, windows, out_weight, picked
    )
    return residual_out.reshape(hidden_states.shape), ffn_input.reshape(hidden_states.shape)


def solution(mesh):
    return jax.shard_map(
        shards,
        mesh=mesh,
        in_specs=(
            P(None, "ha", "wa", "ta"),
            P(None, "ha", "wa", "ta"),
            P(None, None, "ha", "wa", "ta"),
            P("ta", "wa"),
            P(None, None, "ta"),
            P("ta", None),
            P(),
        ),
        out_specs=(P(None, "ha", "wa", "ta"), P(None, "ha", "wa", "ta")),
        check_vma=False,
    )
```

```python
from functools import partial
import math

import jax
import jax.numpy as jnp
from jax import lax
from jax.experimental import pallas as pl
from jax.experimental.pallas import tpu as pltpu
from jax.sharding import PartitionSpec as P

D = 5120
HD = 128
TILE = 8
LANES = 128
LEVEL_STEP = 32

EPSILON = 1e-06
MEBI = 1024 * 1024
SMALL = pl.CostEstimate(flops=1, bytes_accessed=1, transcendentals=0)
LARGE = pl.CostEstimate(flops=20_000_000_000, bytes_accessed=1, transcendentals=0)


def kernel_params(limit):
    return pltpu.CompilerParams(vmem_limit_bytes=limit * MEBI)


class Plan:
    def __init__(self, windows, order):
        heads = windows.shape[0]
        self.heads = heads
        self.most = max(heads * 7 // 10, 1)
        self.order = order
        n_ha, n_wa = lax.axis_size("ha"), lax.axis_size("wa")
        ha, wa = lax.axis_index("ha"), lax.axis_index("wa")
        number = lax.broadcasted_iota(jnp.int32, (2, heads, heads), 1)
        other = lax.broadcasted_iota(jnp.int32, (2, heads, heads), 2)
        idle = jnp.where(windows.T > 0, 0, 1)
        before = (idle[:, None, :] < idle[:, :, None]) | (
            (idle[:, None, :] == idle[:, :, None]) & (other < number)
        )
        position = jnp.sum(before.astype(jnp.int32), axis=2)
        sorted_heads = jnp.sum(jnp.where(position[:, None, :] == number, other, 0), axis=2)
        turned = ha if order > 1 else 0 * ha
        edges = jnp.stack([ha > 0, ha < n_ha - 1, wa > 0, wa < n_wa - 1, turned]).astype(jnp.int32)
        self.vector = jnp.concatenate(
            [windows.T.reshape(-1), position.reshape(-1), sorted_heads.reshape(-1), edges]
        )
        self.counts = jnp.sum(1.0 - idle, axis=1)

    def agree(self, counts):
        counts = lax.pmax(counts, "ta")
        self.more_rows = counts[0] > self.most
        self.more_cols = counts[1] > self.most
        return counts

    def row_radius(self, vector, head):
        return vector[head]

    def col_radius(self, vector, head):
        return vector[self.heads + head]

    def row_position(self, vector, head):
        return vector[2 * self.heads + head]

    def col_position(self, vector, head):
        return vector[3 * self.heads + head]

    def row_head(self, vector, position):
        return vector[4 * self.heads + position]

    def col_head(self, vector, position):
        return vector[5 * self.heads + position]

    def edge(self, vector, number):
        return vector[6 * self.heads + number]


def pack_kernel(vector, source, *refs, head_of, first, rows):
    outs, sem = refs[:-1], refs[-1]
    copies = []
    for number, (out, (low, size)) in enumerate(zip(outs, rows)):
        for slot in range(out.shape[-1] // HD):
            start = pl.multiple_of(head_of(vector, first + slot) * HD, HD)
            lead = (slice(None),) * (len(source.shape) - 2)
            copies.append(
                pltpu.make_async_copy(
                    source.at[(*lead, pl.ds(low, size), pl.ds(start, HD))],
                    out.at[(*lead, slice(None), pl.ds(slot * HD, HD))],
                    sem.at[number, slot],
                )
            )
    for copy in copies:
        copy.start()
    for copy in copies:
        copy.wait()


def pack(vector, source, head_of, first, count, rows):
    anywhere = pl.BlockSpec(memory_space=pl.ANY)
    return pl.pallas_call(
        partial(pack_kernel, head_of=head_of, first=first, rows=rows),
        in_specs=[pl.BlockSpec(memory_space=pltpu.SMEM), anywhere],
        out_specs=[pl.BlockSpec(memory_space=pltpu.VMEM)] * len(rows),
        out_shape=[
            jax.ShapeDtypeStruct((*source.shape[:-2], size, count * HD), source.dtype)
            for _, size in rows
        ],
        scratch_shapes=[pltpu.SemaphoreType.DMA((len(rows), count))],
        compiler_params=kernel_params(8),
        cost_estimate=SMALL,
        name="pack",
    )(vector, source)


def attention_kernel(vector, *refs, plan, head_of, q_count, visiting, group):
    q_refs = refs[:q_count]
    kv_ref, top_ref, bottom_ref, top_rest, bottom_rest = refs[q_count : q_count + 5]
    refs = refs[q_count + 5 :]
    out_refs, stat_refs, halo = refs[:q_count], refs[q_count : 2 * q_count], refs[2 * q_count]
    frames, tokens, head_size = q_refs[0].shape
    span = top_ref.shape[2]
    tiles = tokens // span
    step = pl.program_id(0)
    head = head_of(vector, step)
    radius_row = plan.row_radius(vector, head)
    radius_col = plan.col_radius(vector, head)
    scale = 1.0 / math.sqrt(HD)

    @pl.when(step == 0)
    def _():
        for stat_ref in stat_refs:
            stat_ref[...] = jnp.zeros_like(stat_ref)

    def near(which, tile, wide):
        if not wide:
            return kv_ref[which, :, tile * span : (tile + 1) * span, :].reshape(-1, head_size)
        pieces = []
        if tile == 0:
            pieces.append(halo[0, which])
        low = max(tile - 1, 0) * span
        high = min(tile + 2, tiles) * span
        pieces.append(kv_ref[which, :, low:high, :])
        if tile == tiles - 1:
            pieces.append(halo[1, which])
        block = pieces[0] if len(pieces) == 1 else jnp.concatenate(pieces, axis=1)
        return block.reshape(-1, head_size)

    def attend(wide):
        lane = lax.broadcasted_iota(jnp.int32, (frames, span, LANES), 2)
        for tile in range(tiles):
            rows = slice(tile * span, (tile + 1) * span)
            keys = near(0, tile, wide)
            values = near(1, tile, wide)
            bias = None
            if wide and (tile == 0 or tile == tiles - 1):
                place = lax.rem(
                    lax.broadcasted_iota(jnp.int32, (1, keys.shape[0]), 1), 3 * span
                )
                low, high = 0, 3 * span
                if tile == 0:
                    low = jnp.where(plan.edge(vector, 0) == 0, span, 0)
                if tile == tiles - 1:
                    high = jnp.where(plan.edge(vector, 1) == 0, 2 * span, 3 * span)
                bias = jnp.where((place >= low) & (place < high), 0.0, -jnp.inf)
            for q_ref, out_ref, stat_ref in zip(q_refs, out_refs, stat_refs):
                query = q_ref[:, rows, :].reshape(-1, head_size)
                scores = (
                    lax.dot_general(
                        query, keys, (((1,), (1,)), ((), ())), preferred_element_type=jnp.float32
                    )
                    * scale
                )
                if bias is not None:
                    scores = scores + bias
                highest = jnp.max(scores, axis=1, keepdims=True)
                expo = jnp.exp(scores - highest)
                total = jnp.sum(expo, axis=1, keepdims=True)
                output = jnp.dot(
                    expo.astype(jnp.bfloat16), values, preferred_element_type=jnp.float32
                ) * (1.0 / total)
                out_ref[:, rows, :] = output.astype(jnp.bfloat16).reshape(frames, span, head_size)
                level = (highest + jnp.log(total)).reshape(frames, span, 1)
                stat_ref[:, rows, :] = jnp.where(lane == step, level, stat_ref[:, rows, :])

    active = step < group
    if visiting:

        @pl.when(active & (radius_col == 0))
        def _():
            for out_ref in out_refs:
                out_ref[...] = jnp.zeros_like(out_ref)

        active = active & (radius_col != 0)

    @pl.when(active & (radius_row == 0))
    def _():
        attend(False)

    always = plan.row_position(vector, head) < plan.most

    @pl.when(active & (radius_row != 0) & always)
    def _():
        halo[0] = top_ref[...]
        halo[1] = bottom_ref[...]

    @pl.when(active & (radius_row != 0) & jnp.logical_not(always))
    def _():
        halo[0] = top_rest[...]
        halo[1] = bottom_rest[...]

    @pl.when(active & (radius_row != 0))
    def _():
        attend(True)

    @pl.when(step == group)
    def _():
        for out_ref, stat_ref in zip(out_refs, stat_refs):
            level = stat_ref[...]
            high = level.astype(jnp.bfloat16).astype(jnp.float32)
            middle = (level - high).astype(jnp.bfloat16).astype(jnp.float32)
            low = level - high - middle
            packed = high + pltpu.roll(middle, LEVEL_STEP, 2) + pltpu.roll(low, 2 * LEVEL_STEP, 2)
            out_ref[...] = packed.astype(jnp.bfloat16)


def attention(plan, vector, query_blocks, keys_values, halos, first=None):
    frames, tokens, features = query_blocks[0].shape
    group = features // HD
    span = halos[0].shape[2]
    q_count = len(query_blocks)
    visiting = first is not None

    def slot_of(step):
        return jnp.minimum(step, group - 1)

    def head_of(vector, step):
        return plan.col_head(vector, first + slot_of(step)) if visiting else slot_of(step)

    def kv_index(step, vector):
        return 0, 0, 0, head_of(vector, step)

    def halo_index(step, vector):
        position = plan.row_position(vector, head_of(vector, step))
        return 0, 0, 0, jnp.minimum(position, plan.most - 1)

    def rest_index(step, vector):
        position = plan.row_position(vector, head_of(vector, step))
        return 0, 0, 0, jnp.maximum(position - plan.most, 0)

    q_spec = pl.BlockSpec((frames, tokens, HD), lambda step, _: (0, 0, slot_of(step)))
    kv_spec = pl.BlockSpec((2, frames, tokens, HD), kv_index)
    halo_spec = pl.BlockSpec((2, frames, span, HD), halo_index)
    rest_spec = pl.BlockSpec((2, frames, span, HD), rest_index)
    out_spec = pl.BlockSpec((frames, tokens, HD), lambda step, _: (0, 0, step))
    return pl.pallas_call(
        partial(
            attention_kernel,
            plan=plan,
            head_of=head_of,
            q_count=q_count,
            visiting=visiting,
            group=group,
        ),
        grid_spec=pltpu.PrefetchScalarGridSpec(
            num_scalar_prefetch=1,
            grid=(group + 1,),
            in_specs=[q_spec] * q_count + [kv_spec] + [halo_spec] * 2 + [rest_spec] * 2,
            out_specs=[out_spec] * q_count,
            scratch_shapes=[pltpu.VMEM((frames, tokens, LANES), jnp.float32)] * q_count
            + [pltpu.VMEM((2, 2, frames, span, HD), jnp.bfloat16)],
        ),
        out_shape=[jax.ShapeDtypeStruct((frames, tokens, (group + 1) * HD), jnp.bfloat16)]
        * q_count,
        compiler_params=kernel_params(12),
        cost_estimate=SMALL if visiting else LARGE,
        name="attend_visitors" if visiting else "attend_own",
    )(vector, *query_blocks, keys_values, *halos)


def combine_kernel(vector, own, own_stat, left, right, left_rest, right_rest, out, *, plan, heads):
    first = pl.program_id(0) * heads
    frames, tokens, _ = own.shape

    def level(stat, number):
        lane = lax.broadcasted_iota(jnp.int32, (LANES, HD), 0)
        pick = jnp.where(
            (lax.rem(lane, LEVEL_STEP) == number) & (lane < 3 * LEVEL_STEP), 1.0, 0.0
        ).astype(jnp.bfloat16)
        return jnp.dot(
            stat.reshape(-1, LANES), pick, preferred_element_type=jnp.float32
        ).reshape(frames, tokens, HD)

    for index in range(heads):
        head = first + index
        columns = slice(index * HD, (index + 1) * HD)
        across = plan.col_radius(vector, head) != 0
        position = plan.col_position(vector, head)

        @pl.when(jnp.logical_not(across))
        def _(columns=columns):
            out[:, :, columns] = own[:, :, columns]

        def join(sides, slot, columns, head):
            here = pl.ds(pl.multiple_of(slot * HD, HD), HD)
            levels = [level(own_stat[...], head)]
            values = [own[:, :, columns]]
            for number, side in enumerate(sides):
                value = level(side[:, :, side.shape[2] - LANES :], slot)
                levels.append(jnp.where(plan.edge(vector, 2 + number) == 0, -jnp.inf, value))
                values.append(side[:, :, here])
            highest = jnp.maximum(levels[0], jnp.maximum(levels[1], levels[2]))
            weights = [jnp.exp(x - highest) for x in levels]
            mixed = sum(value.astype(jnp.float32) * weight for value, weight in zip(values, weights))
            out[:, :, columns] = (mixed / (weights[0] + weights[1] + weights[2])).astype(
                jnp.bfloat16
            )

        @pl.when(across & (position < plan.most))
        def _(position=position, columns=columns, head=head):
            join((left, right), position, columns, head)

        @pl.when(across & (position >= plan.most))
        def _(position=position, columns=columns, head=head):
            join((left_rest, right_rest), position - plan.most, columns, head)


def combine(plan, vector, near, sides):
    frames, tokens, _ = near.shape
    heads = plan.heads // plan.order
    spec = pl.BlockSpec((frames, tokens, heads * HD), lambda h, _: (0, 0, h))
    stat_spec = pl.BlockSpec((frames, tokens, HD), lambda h, _: (0, 0, plan.heads))
    return pl.pallas_call(
        partial(combine_kernel, plan=plan, heads=heads),
        grid_spec=pltpu.PrefetchScalarGridSpec(
            num_scalar_prefetch=1,
            grid=(plan.order,),
            in_specs=[spec, stat_spec]
            + [pl.BlockSpec(side.shape, lambda h, _: (0, 0, 0)) for side in sides],
            out_specs=pl.BlockSpec(
                (frames, tokens, heads * HD), lambda h, vector: (0, 0, h ^ plan.edge(vector, 4))
            ),
        ),
        out_shape=jax.ShapeDtypeStruct((frames, tokens, plan.heads * HD), jnp.bfloat16),
        compiler_params=kernel_params(18),
        cost_estimate=LARGE,
        name="combine",
    )(vector, near, near, *sides)


def project_kernel(place, attended, *refs, slots, carried, start, column):
    arrays = 1 + max(piece[0] for slot in slots for piece in slot)
    pieces, refs = refs[:arrays], refs[arrays:]
    if carried:
        carry, refs = refs[0], refs[1:]
    out, rows, weight, rows_sem, weight_sem = refs
    columns = weight.shape[1]
    depth = weight.shape[2]
    rows_copy = pltpu.make_async_copy(
        attended.at[:, start : start + depth], rows, rows_sem.at[0]
    )
    rows_copy.start()
    for index, slot in enumerate(slots):
        for block in range(columns):
            low = 0
            for number, (array, size, share, turned) in enumerate(slot):
                first = pl.multiple_of((place[0] ^ share if turned else share) * size, size)
                pltpu.make_async_copy(
                    pieces[array].at[pl.ds(first, size), block * column : (block + 1) * column],
                    weight.at[index, block, low : low + size],
                    weight_sem.at[index, block, number],
                ).start()
                low += size
    rows_copy.wait()
    for index, slot in enumerate(slots):

        def body(block, _, index=index, slot=slot):
            low = 0
            for number, (_, size, _, _) in enumerate(slot):
                piece = weight.at[index, block, low : low + size]
                pltpu.make_async_copy(piece, piece, weight_sem.at[index, block, number]).wait()
                low += size
            total = jnp.dot(rows[...], weight[index, block], preferred_element_type=jnp.float32)
            here = pl.ds(pl.multiple_of(block * column, column), column)
            if carried:
                total = total + carry[index, :, here]
            out[index, :, here] = total.astype(out.dtype)
            return 0

        lax.fori_loop(0, columns, body, 0)


def project(place, attended, arrays, slots, carry, start, dtype):
    tokens = attended.shape[0]
    width = arrays[0].shape[1]
    column = 256 if width % 256 == 0 else width
    columns = width // column
    depth = sum(piece[1] for piece in slots[0])
    held = len(slots) * width * (2 * depth + tokens * jnp.dtype(dtype).itemsize)
    held += tokens * (2 * depth + (0 if carry is None else 4 * len(slots) * width))
    anywhere = pl.BlockSpec(memory_space=pl.ANY)
    inside = pl.BlockSpec(memory_space=pltpu.VMEM)
    return pl.pallas_call(
        partial(
            project_kernel, slots=slots, carried=carry is not None, start=start, column=column
        ),
        in_specs=[pl.BlockSpec(memory_space=pltpu.SMEM), anywhere]
        + [anywhere] * len(arrays)
        + ([] if carry is None else [inside]),
        out_specs=inside,
        out_shape=jax.ShapeDtypeStruct((len(slots), tokens, width), dtype),
        scratch_shapes=[
            pltpu.VMEM((tokens, depth), attended.dtype),
            pltpu.VMEM((len(slots), columns, depth, column), attended.dtype),
            pltpu.SemaphoreType.DMA((1,)),
            pltpu.SemaphoreType.DMA((len(slots), columns, max(len(slot) for slot in slots))),
        ],
        compiler_params=kernel_params(held // MEBI + 3),
        cost_estimate=SMALL,
        name="project",
    )(place, attended, *arrays, *([] if carry is None else [carry]))


def pick_kernel(place, own_hidden, other_hidden, own_gate, other_gate, hidden, gate):
    mine = place[2 * pl.program_id(0)] != 0

    @pl.when(mine)
    def _():
        hidden[0] = own_hidden[...]
        gate[0] = own_gate[...]

    @pl.when(jnp.logical_not(mine))
    def _():
        hidden[0] = other_hidden[...]
        gate[0] = other_gate[...]


def pick(place, own_hidden, other_hidden, own_gate, other_gate, width):
    tokens, features = own_hidden.shape
    count = 2 * features // width
    hidden = pl.BlockSpec((tokens, width), lambda i, place: (0, place[2 * i + 1]))
    gate = pl.BlockSpec((1, width), lambda i, place: (0, place[2 * i + 1]))
    return pl.pallas_call(
        pick_kernel,
        grid_spec=pltpu.PrefetchScalarGridSpec(
            num_scalar_prefetch=1,
            grid=(count,),
            in_specs=[hidden, hidden, gate, gate],
            out_specs=[
                pl.BlockSpec((1, tokens, width), lambda i, place: (i, 0, 0)),
                pl.BlockSpec((1, 1, width), lambda i, place: (i, 0, 0)),
            ],
        ),
        out_shape=[
            jax.ShapeDtypeStruct((count, tokens, width), jnp.bfloat16),
            jax.ShapeDtypeStruct((count, 1, width), jnp.float32),
        ],
        compiler_params=kernel_params(14),
        cost_estimate=SMALL,
        name="pick",
    )(place, own_hidden, other_hidden, own_gate, other_gate)


def mixed_block(hidden, gate, own_part, other_part):
    parts = own_part[0].astype(jnp.float32) + other_part[0].astype(jnp.float32)
    return hidden[0].astype(jnp.float32) + gate * parts


def mix_kernel(hidden, gate, own_part, other_part, mixed_ref, sums_ref):
    mixed = mixed_block(hidden, gate[0], own_part, other_part)
    mixed_ref[0] = mixed.astype(jnp.bfloat16)
    first = jnp.sum(mixed, axis=1, keepdims=True)
    second = jnp.sum(mixed * mixed, axis=1, keepdims=True)
    lane = lax.broadcasted_iota(jnp.int32, sums_ref.shape, 1)
    sums_ref[...] = jnp.where(lane == 0, first, jnp.where(lane == 1, second, 0.0))


def mix(hidden, gate, own_part, other_part):
    _, tokens, width = hidden.shape
    rows = 64 if tokens % 64 == 0 else tokens
    part = pl.BlockSpec((1, rows, width), lambda i: (0, i, 0))
    return pl.pallas_call(
        mix_kernel,
        grid=(tokens // rows,),
        in_specs=[part, pl.BlockSpec(gate.shape, lambda i: (0, 0, 0)), part, part],
        out_specs=[part, pl.BlockSpec((rows, LANES), lambda i: (i, 0))],
        out_shape=[
            jax.ShapeDtypeStruct((1, tokens, width), jnp.bfloat16),
            jax.ShapeDtypeStruct((tokens, LANES), jnp.float32),
        ],
        compiler_params=kernel_params(14),
        cost_estimate=SMALL,
        name="mix",
    )(hidden, gate, own_part, other_part)


def finish_kernel(place, gate, scale, shift_by, sums, early, *refs, count, blocks):
    hidden, own_parts, other_parts = (refs[count * k : count * (k + 1)] for k in range(3))
    residual, ffn = refs[3 * count :]
    width = early.shape[2]
    late = [
        mixed_block(hidden[index], gate[1 + index], own_parts[index], other_parts[index])
        for index in range(count)
    ]
    first = sums[:, 0:1]
    second = sums[:, 1:2]
    for mixed in late:
        first = first + jnp.sum(mixed, axis=1, keepdims=True)
        second = second + jnp.sum(mixed * mixed, axis=1, keepdims=True)
    average = first / D
    variance = second / D - average * average
    inverse = lax.rsqrt(variance + EPSILON)
    for block in range(blocks):
        columns = slice(block * width, (block + 1) * width)
        mixed = early[0].astype(jnp.float32)
        for index in range(count):
            mixed = jnp.where(place[block] == 1 + index, late[index], mixed)
        residual[:, columns] = mixed.astype(jnp.bfloat16)
        ffn[:, columns] = (
            (mixed - average) * inverse * (1.0 + scale[:, columns]) + shift_by[:, columns]
        ).astype(jnp.bfloat16)


def finish(place, hidden, gate, scale, shift_by, sums, early, own_parts, other_parts):
    count = own_parts.shape[0]
    _, tokens, width = hidden.shape
    blocks = place.shape[0]
    rows = 64 if tokens % 64 == 0 else tokens
    part = pl.BlockSpec((1, rows, width), lambda i, place: (0, i, 0))
    whole = pl.BlockSpec((1, blocks * width), lambda i, place: (0, 0))
    row = pl.BlockSpec((rows, blocks * width), lambda i, place: (i, 0))
    parts = [
        pl.BlockSpec((1, rows, width), lambda i, place, index=index: (index, i, 0))
        for index in range(count + 1)
    ]
    return pl.pallas_call(
        partial(finish_kernel, count=count, blocks=blocks),
        grid_spec=pltpu.PrefetchScalarGridSpec(
            num_scalar_prefetch=1,
            grid=(tokens // rows,),
            in_specs=[pl.BlockSpec(gate.shape, lambda i, place: (0, 0, 0)), whole, whole]
            + [pl.BlockSpec((rows, LANES), lambda i, place: (i, 0)), part]
            + parts[1:]
            + parts[:-1] * 2,
            out_specs=[row, row],
        ),
        out_shape=[jax.ShapeDtypeStruct((tokens, blocks * width), jnp.bfloat16)] * 2,
        compiler_params=kernel_params(14),
        cost_estimate=SMALL,
        name="finish",
    )(
        *(place, gate, scale, shift_by, sums, early),
        *([hidden] * count + [own_parts] * count + [other_parts] * count),
    )


def shift(block, axis, step):
    count = lax.axis_size(axis)
    pairs = [(i, i + step) for i in range(count) if 0 <= i + step < count]
    return lax.ppermute(block, axis, pairs)


def turn(block, axis, step):
    count = lax.axis_size(axis)
    return lax.ppermute(block, axis, [(i, (i + step) % count) for i in range(count)])


def swap(block, axis, bit):
    count = lax.axis_size(axis)
    return lax.ppermute(block, axis, [(i, i ^ bit) for i in range(count)])


class Tokens:
    def __init__(self, queries, keys_values, windows, order):
        self.plan = Plan(windows, order)
        self.queries = queries.reshape(queries.shape[0], -1, queries.shape[3])
        self.keys_values = keys_values.reshape(*keys_values.shape[:2], -1, keys_values.shape[4])
        self.span = TILE * queries.shape[2]
        self.parts = (0, self.plan.most), (self.plan.most, self.plan.heads - self.plan.most)

    def edge_rows(self, vector, part):
        low = self.queries.shape[1] - self.span
        rows = [(low, self.span), (0, self.span)]
        return pack(vector, self.keys_values, self.plan.row_head, *self.parts[part], rows)

    def leaving(self, vector, part):
        rows = [(0, self.queries.shape[1])]
        return pack(vector, self.queries, self.plan.col_head, *self.parts[part], rows)[0]

    def halos(self, rows):
        return shift(rows[0], "ha", 1), shift(rows[1], "ha", -1)

    def rest_halos(self, vector):
        shape = (*self.keys_values.shape[:2], self.span, self.parts[1][1] * HD)
        return lax.cond(
            self.plan.more_rows,
            lambda vector: self.halos(self.edge_rows(vector, 1)),
            lambda vector: (jnp.zeros(shape, jnp.bfloat16),) * 2,
            vector,
        )

    def stay(self, vector, halos):
        return attention(self.plan, vector, [self.queries], self.keys_values, halos)[0]

    def visit(self, vector, visitors, halos, part=0):
        first = self.parts[part][0]
        return attention(self.plan, vector, visitors, self.keys_values, halos, first)

    def rest_sides(self, vector, halos):
        shape = (*self.queries.shape[:2], (self.parts[1][1] + 1) * HD)

        def send(vector, *halos):
            queries = self.leaving(vector, 1)
            visitors = shift(queries, "wa", 1), shift(queries, "wa", -1)
            for_left, for_right = self.visit(vector, visitors, halos, 1)
            return shift(for_right, "wa", 1), shift(for_left, "wa", -1)

        return lax.cond(
            self.plan.more_cols,
            send,
            lambda vector, *halos: (jnp.zeros(shape, jnp.bfloat16),) * 2,
            vector,
            *halos,
        )

    def combine(self, vector, near, sides):
        attended = combine(self.plan, vector, near, sides)
        return attended.reshape(-1, attended.shape[2])


def together(*blocks):
    return lax.optimization_barrier(blocks)


def paired(hidden, queries, keys_values, windows, out_weight, picked):
    ha, wa, ta = lax.axis_index("ha"), lax.axis_index("wa"), lax.axis_index("ta")
    n_wa = lax.axis_size("wa")
    blocks = n_wa // 2
    depth = out_weight.shape[0] // 4
    width = out_weight.shape[1]

    def share(shares, number):
        return lax.dynamic_slice_in_dim(shares, number * depth, depth, 0)

    mine = lax.optimization_barrier(share(out_weight, ha))
    first = turn(mine, "wa", 1)
    tokens = Tokens(queries, keys_values, windows, 4)
    vector = tokens.plan.vector
    top, bottom = tokens.halos(tokens.edge_rows(vector, 0))

    top, gate = together(top, picked[0:1])
    other_gate = swap(gate, "ta", 1)
    other_gate, counts = together(other_gate, tokens.plan.counts)
    counts, vector = together(tokens.plan.agree(counts), vector)
    queries, mine = together(tokens.leaving(vector, 0), mine)
    third = turn(mine, "wa", -1)

    first, top, bottom, other_gate, vector, queries = together(
        first, top, bottom, other_gate, vector, queries
    )
    first_x = swap(first, "ha", 1)
    first_y = swap(first, "ha", 2)
    from_left = shift(queries, "wa", 1)
    from_right = shift(queries, "wa", -1)
    halos = top, bottom, *tokens.rest_halos(vector)
    near = tokens.stay(vector, halos)

    rest_sides = tokens.rest_sides(vector, halos)

    near, first_x, first_y, third, first, *rest_sides = together(
        near, first_x, first_y, third, first, *rest_sides
    )
    third_x = swap(third, "ha", 1)
    third_y = swap(third, "ha", 2)
    second = turn(first, "wa", 1)
    for_left, for_right = tokens.visit(vector, (from_left, from_right), halos)

    left = shift(for_right, "wa", 1)
    right = shift(for_left, "wa", -1)

    third_x, third_y, second, vector, hidden, all_shares = together(
        third_x, third_y, second, vector, hidden, out_weight
    )
    second_x = swap(second, "ha", 1)
    second_y = swap(second, "ha", 2)
    other_hidden = swap(hidden, "ta", 1)

    far = lax.optimization_barrier(share(all_shares, ha ^ 3))
    left, right, far = together(left, right, far)
    attended = tokens.combine(vector, near, [left, right, *rest_sides])

    second_x, second_y, first_y, far, attended = together(
        second_x, second_y, first_y, far, attended
    )
    first_far = swap(first_y, "ha", 1)
    second_far = swap(second_x, "ha", 2)
    third_far = turn(far, "wa", -1)

    turned = ha.reshape(1)
    sums = project(
        turned,
        attended,
        [out_weight],
        [[(0, depth, number, True) for number in range(4)]],
        None,
        0,
        jnp.bfloat16,
    )
    other_sums = swap(sums, "ta", 1)
    late = project(
        turned,
        attended,
        [first, first_x, first_y, second, second_x, second_y, third, third_x, third_y],
        [[(start + number, depth, 0, False) for number in range(3)] for start in (0, 3, 6)],
        None,
        0,
        jnp.float32,
    )
    def block_of(distance):
        return lax.rem(wa - distance + n_wa, n_wa)

    owners = jnp.stack([block_of(distance) // blocks == ta for distance in range(n_wa)])
    inner = jnp.stack([lax.rem(block_of(distance), blocks) for distance in range(n_wa)])
    place = jnp.stack([owners.astype(jnp.int32), inner], axis=1).reshape(-1)
    late, place, other_hidden = together(late, place, other_hidden)
    base, gates = pick(place, hidden, other_hidden, gate, other_gate, width)
    early, totals = mix(base, gates, sums, other_sums)

    first_far, second_far, third_far, early, totals, late = together(
        first_far, second_far, third_far, early, totals, late
    )
    late = project(
        turned,
        attended,
        [first_far, second_far, third_far],
        [[(number, depth, 0, False)] for number in range(3)],
        late,
        3 * depth,
        jnp.bfloat16,
    )
    other_late = swap(late, "ta", 1)
    place = jnp.stack(
        [lax.rem(wa - ta * blocks - block + 2 * n_wa, n_wa) for block in range(blocks)]
    )
    return finish(
        place, base, gates, picked[2:3], picked[1:2], totals, early, late, other_late
    )


def gathered(hidden, queries, keys_values, windows, out_weight, picked):
    n_ha, n_wa, n_ta = lax.axis_size("ha"), lax.axis_size("wa"), lax.axis_size("ta")
    ha, ta = lax.axis_index("ha"), lax.axis_index("ta")
    work = Tokens(queries, keys_values, windows, 1)
    vector = work.plan.vector
    work.plan.agree(work.plan.counts)
    halos = *work.halos(work.edge_rows(vector, 0)), *work.rest_halos(vector)
    sent = work.leaving(vector, 0)
    visitors = shift(sent, "wa", 1), shift(sent, "wa", -1)
    near = work.stay(vector, halos)
    for_left, for_right = work.visit(vector, visitors, halos)
    sides = shift(for_right, "wa", 1), shift(for_left, "wa", -1)
    attended = work.combine(vector, near, [*sides, *work.rest_sides(vector, halos)])
    tokens, features = attended.shape
    depth = features // n_ha
    width = out_weight.shape[1]
    share = lax.dynamic_slice_in_dim(out_weight, ha * depth, depth, 0)
    weights = lax.all_gather(share, ("ha", "wa"), axis=0, tiled=False).reshape(
        n_ha, n_wa, depth, width
    )
    partial_sums = jnp.einsum(
        "thk,hwkc->wtc",
        attended.reshape(tokens, n_ha, depth),
        weights,
        preferred_element_type=jnp.float32,
    ).astype(jnp.bfloat16)
    blocks = n_wa // n_ta
    summed = None
    for step in range(n_ta):
        target = lax.rem(ta + step, n_ta)
        piece = lax.dynamic_slice_in_dim(partial_sums, target * blocks, blocks, 0)
        if step:
            piece = turn(piece, "ta", step)
        piece = piece.astype(jnp.float32)
        summed = piece if summed is None else summed + piece
    summed = jnp.transpose(summed, (1, 0, 2)).reshape(tokens, -1)
    mixed = hidden.astype(jnp.float32) + picked[0] * summed
    sum_first, sum_second = lax.psum((jnp.sum(mixed, axis=1), jnp.sum(mixed * mixed, axis=1)), "ta")
    average = (sum_first / D)[:, None]
    variance = (sum_second / D)[:, None] - average * average
    normed = (mixed - average) * lax.rsqrt(variance + EPSILON)
    ffn_input = (normed * (1.0 + picked[2]) + picked[1]).astype(jnp.bfloat16)
    return mixed.astype(jnp.bfloat16), ffn_input


def shards(hidden_states, queries, keys_values, out_weight, mod_table, windows, step_index):
    tokens = math.prod(queries.shape[:3])
    width = hidden_states.shape[3]
    picked = lax.dynamic_index_in_dim(mod_table, step_index[0], 0, keepdims=False)
    sizes = lax.axis_size("ha"), lax.axis_size("wa"), lax.axis_size("ta")
    tuned = sizes == (4, 4, 2) and out_weight.shape[0] % (20 * LANES) == 0
    residual_out, ffn_input = (paired if tuned else gathered)(
        hidden_states.reshape(tokens, width), queries, keys_values, windows, out_weight, picked
    )
    return residual_out.reshape(hidden_states.shape), ffn_input.reshape(hidden_states.shape)


def solution(mesh):
    return jax.shard_map(
        shards,
        mesh=mesh,
        in_specs=(
            P(None, "ha", "wa", "ta"),
            P(None, "ha", "wa", "ta"),
            P(None, None, "ha", "wa", "ta"),
            P("ta", "wa"),
            P(None, None, "ta"),
            P("ta", None),
            P(),
        ),
        out_specs=(P(None, "ha", "wa", "ta"), P(None, "ha", "wa", "ta")),
        check_vma=False,
    )
```

```python
from functools import partial
import math

import jax
import jax.numpy as jnp
from jax import lax
from jax.experimental import pallas as pl
from jax.experimental.pallas import tpu as pltpu
from jax.sharding import PartitionSpec as P

D = 5120
HD = 128
TILE = 8
LANES = 128
LEVEL_STEP = 32

EPSILON = 1e-06
MEBI = 1024 * 1024
SMALL = pl.CostEstimate(flops=1, bytes_accessed=1, transcendentals=0)
LARGE = pl.CostEstimate(flops=20_000_000_000, bytes_accessed=1, transcendentals=0)


def kernel_params(limit):
    return pltpu.CompilerParams(vmem_limit_bytes=limit * MEBI)


class Plan:
    def __init__(self, windows, order):
        heads = windows.shape[0]
        self.heads = heads
        self.most = max(heads * 3 // 4, 1)
        self.order = order
        n_ha, n_wa = lax.axis_size("ha"), lax.axis_size("wa")
        ha, wa = lax.axis_index("ha"), lax.axis_index("wa")
        number = lax.broadcasted_iota(jnp.int32, (2, heads, heads), 1)
        other = lax.broadcasted_iota(jnp.int32, (2, heads, heads), 2)
        idle = jnp.where(windows.T > 0, 0, 1)
        before = (idle[:, None, :] < idle[:, :, None]) | (
            (idle[:, None, :] == idle[:, :, None]) & (other < number)
        )
        position = jnp.sum(before.astype(jnp.int32), axis=2)
        sorted_heads = jnp.sum(jnp.where(position[:, None, :] == number, other, 0), axis=2)
        turned = ha if order > 1 else 0 * ha
        edges = jnp.stack([ha > 0, ha < n_ha - 1, wa > 0, wa < n_wa - 1, turned]).astype(jnp.int32)
        self.vector = jnp.concatenate(
            [windows.T.reshape(-1), position.reshape(-1), sorted_heads.reshape(-1), edges]
        )
        self.counts = jnp.sum(1.0 - idle, axis=1)

    def agree(self, counts):
        counts = lax.pmax(counts, "ta")
        self.more_rows = counts[0] > self.most
        self.more_cols = counts[1] > self.most
        return counts

    def row_radius(self, vector, head):
        return vector[head]

    def col_radius(self, vector, head):
        return vector[self.heads + head]

    def row_position(self, vector, head):
        return vector[2 * self.heads + head]

    def col_position(self, vector, head):
        return vector[3 * self.heads + head]

    def row_head(self, vector, position):
        return vector[4 * self.heads + position]

    def col_head(self, vector, position):
        return vector[5 * self.heads + position]

    def edge(self, vector, number):
        return vector[6 * self.heads + number]


def pack_kernel(vector, source, *refs, head_of, first, rows):
    outs, sem = refs[:-1], refs[-1]
    copies = []
    for number, (out, (low, size)) in enumerate(zip(outs, rows)):
        for slot in range(out.shape[-1] // HD):
            start = pl.multiple_of(head_of(vector, first + slot) * HD, HD)
            lead = (slice(None),) * (len(source.shape) - 2)
            copies.append(
                pltpu.make_async_copy(
                    source.at[(*lead, pl.ds(low, size), pl.ds(start, HD))],
                    out.at[(*lead, slice(None), pl.ds(slot * HD, HD))],
                    sem.at[number, slot],
                )
            )
    for copy in copies:
        copy.start()
    for copy in copies:
        copy.wait()


def pack(vector, source, head_of, first, count, rows):
    anywhere = pl.BlockSpec(memory_space=pl.ANY)
    return pl.pallas_call(
        partial(pack_kernel, head_of=head_of, first=first, rows=rows),
        in_specs=[pl.BlockSpec(memory_space=pltpu.SMEM), anywhere],
        out_specs=[pl.BlockSpec(memory_space=pltpu.VMEM)] * len(rows),
        out_shape=[
            jax.ShapeDtypeStruct((*source.shape[:-2], size, count * HD), source.dtype)
            for _, size in rows
        ],
        scratch_shapes=[pltpu.SemaphoreType.DMA((len(rows), count))],
        compiler_params=kernel_params(8),
        cost_estimate=SMALL,
        name="pack",
    )(vector, source)


def attention_kernel(vector, *refs, plan, head_of, q_count, visiting, group):
    q_refs = refs[:q_count]
    kv_ref, top_ref, bottom_ref, top_rest, bottom_rest = refs[q_count : q_count + 5]
    refs = refs[q_count + 5 :]
    out_refs, stat_refs, halo = refs[:q_count], refs[q_count : 2 * q_count], refs[2 * q_count]
    frames, tokens, head_size = q_refs[0].shape
    span = top_ref.shape[2]
    tiles = tokens // span
    step = pl.program_id(0)
    head = head_of(vector, step)
    radius_row = plan.row_radius(vector, head)
    radius_col = plan.col_radius(vector, head)
    scale = 1.0 / math.sqrt(HD)

    @pl.when(step == 0)
    def _():
        for stat_ref in stat_refs:
            stat_ref[...] = jnp.zeros_like(stat_ref)

    def near(which, tile, wide):
        if not wide:
            return kv_ref[which, :, tile * span : (tile + 1) * span, :].reshape(-1, head_size)
        pieces = []
        if tile == 0:
            pieces.append(halo[0, which])
        low = max(tile - 1, 0) * span
        high = min(tile + 2, tiles) * span
        pieces.append(kv_ref[which, :, low:high, :])
        if tile == tiles - 1:
            pieces.append(halo[1, which])
        block = pieces[0] if len(pieces) == 1 else jnp.concatenate(pieces, axis=1)
        return block.reshape(-1, head_size)

    def attend(wide):
        lane = lax.broadcasted_iota(jnp.int32, (frames, span, LANES), 2)
        for tile in range(tiles):
            rows = slice(tile * span, (tile + 1) * span)
            keys = near(0, tile, wide)
            values = near(1, tile, wide)
            bias = None
            if wide and (tile == 0 or tile == tiles - 1):
                place = lax.rem(
                    lax.broadcasted_iota(jnp.int32, (1, keys.shape[0]), 1), 3 * span
                )
                low, high = 0, 3 * span
                if tile == 0:
                    low = jnp.where(plan.edge(vector, 0) == 0, span, 0)
                if tile == tiles - 1:
                    high = jnp.where(plan.edge(vector, 1) == 0, 2 * span, 3 * span)
                bias = jnp.where((place >= low) & (place < high), 0.0, -jnp.inf)
            for q_ref, out_ref, stat_ref in zip(q_refs, out_refs, stat_refs):
                query = q_ref[:, rows, :].reshape(-1, head_size)
                scores = (
                    lax.dot_general(
                        query, keys, (((1,), (1,)), ((), ())), preferred_element_type=jnp.float32
                    )
                    * scale
                )
                if bias is not None:
                    scores = scores + bias
                highest = jnp.max(scores, axis=1, keepdims=True)
                expo = jnp.exp(scores - highest)
                total = jnp.sum(expo, axis=1, keepdims=True)
                output = jnp.dot(
                    expo.astype(jnp.bfloat16), values, preferred_element_type=jnp.float32
                ) * (1.0 / total)
                out_ref[:, rows, :] = output.astype(jnp.bfloat16).reshape(frames, span, head_size)
                level = (highest + jnp.log(total)).reshape(frames, span, 1)
                stat_ref[:, rows, :] = jnp.where(lane == step, level, stat_ref[:, rows, :])

    active = step < group
    if visiting:

        @pl.when(active & (radius_col == 0))
        def _():
            for out_ref in out_refs:
                out_ref[...] = jnp.zeros_like(out_ref)

        active = active & (radius_col != 0)

    @pl.when(active & (radius_row == 0))
    def _():
        attend(False)

    always = plan.row_position(vector, head) < plan.most

    @pl.when(active & (radius_row != 0) & always)
    def _():
        halo[0] = top_ref[...]
        halo[1] = bottom_ref[...]

    @pl.when(active & (radius_row != 0) & jnp.logical_not(always))
    def _():
        halo[0] = top_rest[...]
        halo[1] = bottom_rest[...]

    @pl.when(active & (radius_row != 0))
    def _():
        attend(True)

    @pl.when(step == group)
    def _():
        for out_ref, stat_ref in zip(out_refs, stat_refs):
            level = stat_ref[...]
            high = level.astype(jnp.bfloat16).astype(jnp.float32)
            middle = (level - high).astype(jnp.bfloat16).astype(jnp.float32)
            low = level - high - middle
            packed = high + pltpu.roll(middle, LEVEL_STEP, 2) + pltpu.roll(low, 2 * LEVEL_STEP, 2)
            out_ref[...] = packed.astype(jnp.bfloat16)


def attention(plan, vector, query_blocks, keys_values, halos, first=None):
    frames, tokens, features = query_blocks[0].shape
    group = features // HD
    span = halos[0].shape[2]
    q_count = len(query_blocks)
    visiting = first is not None

    def slot_of(step):
        return jnp.minimum(step, group - 1)

    def head_of(vector, step):
        return plan.col_head(vector, first + slot_of(step)) if visiting else slot_of(step)

    def kv_index(step, vector):
        return 0, 0, 0, head_of(vector, step)

    def halo_index(step, vector):
        position = plan.row_position(vector, head_of(vector, step))
        return 0, 0, 0, jnp.minimum(position, plan.most - 1)

    def rest_index(step, vector):
        position = plan.row_position(vector, head_of(vector, step))
        return 0, 0, 0, jnp.maximum(position - plan.most, 0)

    q_spec = pl.BlockSpec((frames, tokens, HD), lambda step, _: (0, 0, slot_of(step)))
    kv_spec = pl.BlockSpec((2, frames, tokens, HD), kv_index)
    halo_spec = pl.BlockSpec((2, frames, span, HD), halo_index)
    rest_spec = pl.BlockSpec((2, frames, span, HD), rest_index)
    out_spec = pl.BlockSpec((frames, tokens, HD), lambda step, _: (0, 0, step))
    return pl.pallas_call(
        partial(
            attention_kernel,
            plan=plan,
            head_of=head_of,
            q_count=q_count,
            visiting=visiting,
            group=group,
        ),
        grid_spec=pltpu.PrefetchScalarGridSpec(
            num_scalar_prefetch=1,
            grid=(group + 1,),
            in_specs=[q_spec] * q_count + [kv_spec] + [halo_spec] * 2 + [rest_spec] * 2,
            out_specs=[out_spec] * q_count,
            scratch_shapes=[pltpu.VMEM((frames, tokens, LANES), jnp.float32)] * q_count
            + [pltpu.VMEM((2, 2, frames, span, HD), jnp.bfloat16)],
        ),
        out_shape=[jax.ShapeDtypeStruct((frames, tokens, (group + 1) * HD), jnp.bfloat16)]
        * q_count,
        compiler_params=kernel_params(12),
        cost_estimate=SMALL if visiting else LARGE,
        name="attend_visitors" if visiting else "attend_own",
    )(vector, *query_blocks, keys_values, *halos)


def combine_kernel(vector, own, own_stat, left, right, left_rest, right_rest, out, *, plan, heads):
    first = pl.program_id(0) * heads
    frames, tokens, _ = own.shape

    def level(stat, number):
        lane = lax.broadcasted_iota(jnp.int32, (LANES, HD), 0)
        pick = jnp.where(
            (lax.rem(lane, LEVEL_STEP) == number) & (lane < 3 * LEVEL_STEP), 1.0, 0.0
        ).astype(jnp.bfloat16)
        return jnp.dot(
            stat.reshape(-1, LANES), pick, preferred_element_type=jnp.float32
        ).reshape(frames, tokens, HD)

    for index in range(heads):
        head = first + index
        columns = slice(index * HD, (index + 1) * HD)
        across = plan.col_radius(vector, head) != 0
        position = plan.col_position(vector, head)

        @pl.when(jnp.logical_not(across))
        def _(columns=columns):
            out[:, :, columns] = own[:, :, columns]

        def join(sides, slot, columns, head):
            here = pl.ds(pl.multiple_of(slot * HD, HD), HD)
            levels = [level(own_stat[...], head)]
            values = [own[:, :, columns]]
            for number, side in enumerate(sides):
                value = level(side[:, :, side.shape[2] - LANES :], slot)
                levels.append(jnp.where(plan.edge(vector, 2 + number) == 0, -jnp.inf, value))
                values.append(side[:, :, here])
            highest = jnp.maximum(levels[0], jnp.maximum(levels[1], levels[2]))
            weights = [jnp.exp(x - highest) for x in levels]
            mixed = sum(value.astype(jnp.float32) * weight for value, weight in zip(values, weights))
            out[:, :, columns] = (mixed / (weights[0] + weights[1] + weights[2])).astype(
                jnp.bfloat16
            )

        @pl.when(across & (position < plan.most))
        def _(position=position, columns=columns, head=head):
            join((left, right), position, columns, head)

        @pl.when(across & (position >= plan.most))
        def _(position=position, columns=columns, head=head):
            join((left_rest, right_rest), position - plan.most, columns, head)


def combine(plan, vector, near, sides):
    frames, tokens, _ = near.shape
    heads = plan.heads // plan.order
    spec = pl.BlockSpec((frames, tokens, heads * HD), lambda h, _: (0, 0, h))
    stat_spec = pl.BlockSpec((frames, tokens, HD), lambda h, _: (0, 0, plan.heads))
    return pl.pallas_call(
        partial(combine_kernel, plan=plan, heads=heads),
        grid_spec=pltpu.PrefetchScalarGridSpec(
            num_scalar_prefetch=1,
            grid=(plan.order,),
            in_specs=[spec, stat_spec]
            + [pl.BlockSpec(side.shape, lambda h, _: (0, 0, 0)) for side in sides],
            out_specs=pl.BlockSpec(
                (frames, tokens, heads * HD), lambda h, vector: (0, 0, h ^ plan.edge(vector, 4))
            ),
        ),
        out_shape=jax.ShapeDtypeStruct((frames, tokens, plan.heads * HD), jnp.bfloat16),
        compiler_params=kernel_params(18),
        cost_estimate=LARGE,
        name="combine",
    )(vector, near, near, *sides)


def project_kernel(place, attended, *refs, slots, carried, start, column):
    arrays = 1 + max(piece[0] for slot in slots for piece in slot)
    pieces, refs = refs[:arrays], refs[arrays:]
    if carried:
        carry, refs = refs[0], refs[1:]
    out, rows, weight, rows_sem, weight_sem = refs
    columns = weight.shape[1]
    depth = weight.shape[2]
    rows_copy = pltpu.make_async_copy(
        attended.at[:, start : start + depth], rows, rows_sem.at[0]
    )
    rows_copy.start()
    for index, slot in enumerate(slots):
        for block in range(columns):
            low = 0
            for number, (array, size, share, turned) in enumerate(slot):
                first = pl.multiple_of((place[0] ^ share if turned else share) * size, size)
                pltpu.make_async_copy(
                    pieces[array].at[pl.ds(first, size), block * column : (block + 1) * column],
                    weight.at[index, block, low : low + size],
                    weight_sem.at[index, block, number],
                ).start()
                low += size
    rows_copy.wait()
    for index, slot in enumerate(slots):

        def body(block, _, index=index, slot=slot):
            low = 0
            for number, (_, size, _, _) in enumerate(slot):
                piece = weight.at[index, block, low : low + size]
                pltpu.make_async_copy(piece, piece, weight_sem.at[index, block, number]).wait()
                low += size
            total = jnp.dot(rows[...], weight[index, block], preferred_element_type=jnp.float32)
            here = pl.ds(pl.multiple_of(block * column, column), column)
            if carried:
                total = total + carry[index, :, here]
            out[index, :, here] = total.astype(out.dtype)
            return 0

        lax.fori_loop(0, columns, body, 0)


def project(place, attended, arrays, slots, carry, start, dtype):
    tokens = attended.shape[0]
    width = arrays[0].shape[1]
    column = 256 if width % 256 == 0 else width
    columns = width // column
    depth = sum(piece[1] for piece in slots[0])
    held = len(slots) * width * (2 * depth + tokens * jnp.dtype(dtype).itemsize)
    held += tokens * (2 * depth + (0 if carry is None else 4 * len(slots) * width))
    anywhere = pl.BlockSpec(memory_space=pl.ANY)
    inside = pl.BlockSpec(memory_space=pltpu.VMEM)
    return pl.pallas_call(
        partial(
            project_kernel, slots=slots, carried=carry is not None, start=start, column=column
        ),
        in_specs=[pl.BlockSpec(memory_space=pltpu.SMEM), anywhere]
        + [anywhere] * len(arrays)
        + ([] if carry is None else [inside]),
        out_specs=inside,
        out_shape=jax.ShapeDtypeStruct((len(slots), tokens, width), dtype),
        scratch_shapes=[
            pltpu.VMEM((tokens, depth), attended.dtype),
            pltpu.VMEM((len(slots), columns, depth, column), attended.dtype),
            pltpu.SemaphoreType.DMA((1,)),
            pltpu.SemaphoreType.DMA((len(slots), columns, max(len(slot) for slot in slots))),
        ],
        compiler_params=kernel_params(held // MEBI + 3),
        cost_estimate=SMALL,
        name="project",
    )(place, attended, *arrays, *([] if carry is None else [carry]))


def pick_kernel(place, own_hidden, other_hidden, own_gate, other_gate, hidden, gate):
    mine = place[2 * pl.program_id(0)] != 0

    @pl.when(mine)
    def _():
        hidden[0] = own_hidden[...]
        gate[0] = own_gate[...]

    @pl.when(jnp.logical_not(mine))
    def _():
        hidden[0] = other_hidden[...]
        gate[0] = other_gate[...]


def pick(place, own_hidden, other_hidden, own_gate, other_gate, width):
    tokens, features = own_hidden.shape
    count = 2 * features // width
    hidden = pl.BlockSpec((tokens, width), lambda i, place: (0, place[2 * i + 1]))
    gate = pl.BlockSpec((1, width), lambda i, place: (0, place[2 * i + 1]))
    return pl.pallas_call(
        pick_kernel,
        grid_spec=pltpu.PrefetchScalarGridSpec(
            num_scalar_prefetch=1,
            grid=(count,),
            in_specs=[hidden, hidden, gate, gate],
            out_specs=[
                pl.BlockSpec((1, tokens, width), lambda i, place: (i, 0, 0)),
                pl.BlockSpec((1, 1, width), lambda i, place: (i, 0, 0)),
            ],
        ),
        out_shape=[
            jax.ShapeDtypeStruct((count, tokens, width), jnp.bfloat16),
            jax.ShapeDtypeStruct((count, 1, width), jnp.float32),
        ],
        compiler_params=kernel_params(14),
        cost_estimate=SMALL,
        name="pick",
    )(place, own_hidden, other_hidden, own_gate, other_gate)


def mixed_block(hidden, gate, own_part, other_part):
    parts = own_part[0].astype(jnp.float32) + other_part[0].astype(jnp.float32)
    return hidden[0].astype(jnp.float32) + gate * parts


def mix_kernel(hidden, gate, own_part, other_part, mixed_ref, sums_ref):
    mixed = mixed_block(hidden, gate[0], own_part, other_part)
    mixed_ref[0] = mixed.astype(jnp.bfloat16)
    first = jnp.sum(mixed, axis=1, keepdims=True)
    second = jnp.sum(mixed * mixed, axis=1, keepdims=True)
    lane = lax.broadcasted_iota(jnp.int32, sums_ref.shape, 1)
    sums_ref[...] = jnp.where(lane == 0, first, jnp.where(lane == 1, second, 0.0))


def mix(hidden, gate, own_part, other_part):
    _, tokens, width = hidden.shape
    rows = 64 if tokens % 64 == 0 else tokens
    part = pl.BlockSpec((1, rows, width), lambda i: (0, i, 0))
    return pl.pallas_call(
        mix_kernel,
        grid=(tokens // rows,),
        in_specs=[part, pl.BlockSpec(gate.shape, lambda i: (0, 0, 0)), part, part],
        out_specs=[part, pl.BlockSpec((rows, LANES), lambda i: (i, 0))],
        out_shape=[
            jax.ShapeDtypeStruct((1, tokens, width), jnp.bfloat16),
            jax.ShapeDtypeStruct((tokens, LANES), jnp.float32),
        ],
        compiler_params=kernel_params(14),
        cost_estimate=SMALL,
        name="mix",
    )(hidden, gate, own_part, other_part)


def finish_kernel(place, gate, scale, shift_by, sums, early, *refs, count, blocks):
    hidden, own_parts, other_parts = (refs[count * k : count * (k + 1)] for k in range(3))
    residual, ffn = refs[3 * count :]
    width = early.shape[2]
    late = [
        mixed_block(hidden[index], gate[1 + index], own_parts[index], other_parts[index])
        for index in range(count)
    ]
    first = sums[:, 0:1]
    second = sums[:, 1:2]
    for mixed in late:
        first = first + jnp.sum(mixed, axis=1, keepdims=True)
        second = second + jnp.sum(mixed * mixed, axis=1, keepdims=True)
    average = first / D
    variance = second / D - average * average
    inverse = lax.rsqrt(variance + EPSILON)
    for block in range(blocks):
        columns = slice(block * width, (block + 1) * width)
        mixed = early[0].astype(jnp.float32)
        for index in range(count):
            mixed = jnp.where(place[block] == 1 + index, late[index], mixed)
        residual[:, columns] = mixed.astype(jnp.bfloat16)
        ffn[:, columns] = (
            (mixed - average) * inverse * (1.0 + scale[:, columns]) + shift_by[:, columns]
        ).astype(jnp.bfloat16)


def finish(place, hidden, gate, scale, shift_by, sums, early, own_parts, other_parts):
    count = own_parts.shape[0]
    _, tokens, width = hidden.shape
    blocks = place.shape[0]
    rows = 64 if tokens % 64 == 0 else tokens
    part = pl.BlockSpec((1, rows, width), lambda i, place: (0, i, 0))
    whole = pl.BlockSpec((1, blocks * width), lambda i, place: (0, 0))
    row = pl.BlockSpec((rows, blocks * width), lambda i, place: (i, 0))
    parts = [
        pl.BlockSpec((1, rows, width), lambda i, place, index=index: (index, i, 0))
        for index in range(count + 1)
    ]
    return pl.pallas_call(
        partial(finish_kernel, count=count, blocks=blocks),
        grid_spec=pltpu.PrefetchScalarGridSpec(
            num_scalar_prefetch=1,
            grid=(tokens // rows,),
            in_specs=[pl.BlockSpec(gate.shape, lambda i, place: (0, 0, 0)), whole, whole]
            + [pl.BlockSpec((rows, LANES), lambda i, place: (i, 0)), part]
            + parts[1:]
            + parts[:-1] * 2,
            out_specs=[row, row],
        ),
        out_shape=[jax.ShapeDtypeStruct((tokens, blocks * width), jnp.bfloat16)] * 2,
        compiler_params=kernel_params(14),
        cost_estimate=SMALL,
        name="finish",
    )(
        *(place, gate, scale, shift_by, sums, early),
        *([hidden] * count + [own_parts] * count + [other_parts] * count),
    )


def shift(block, axis, step):
    count = lax.axis_size(axis)
    pairs = [(i, i + step) for i in range(count) if 0 <= i + step < count]
    return lax.ppermute(block, axis, pairs)


def turn(block, axis, step):
    count = lax.axis_size(axis)
    return lax.ppermute(block, axis, [(i, (i + step) % count) for i in range(count)])


def swap(block, axis, bit):
    count = lax.axis_size(axis)
    return lax.ppermute(block, axis, [(i, i ^ bit) for i in range(count)])


class Tokens:
    def __init__(self, queries, keys_values, windows, order):
        self.plan = Plan(windows, order)
        self.queries = queries.reshape(queries.shape[0], -1, queries.shape[3])
        self.keys_values = keys_values.reshape(*keys_values.shape[:2], -1, keys_values.shape[4])
        self.span = TILE * queries.shape[2]
        self.parts = (0, self.plan.most), (self.plan.most, self.plan.heads - self.plan.most)

    def edge_rows(self, vector, part):
        low = self.queries.shape[1] - self.span
        rows = [(low, self.span), (0, self.span)]
        return pack(vector, self.keys_values, self.plan.row_head, *self.parts[part], rows)

    def leaving(self, vector, part):
        rows = [(0, self.queries.shape[1])]
        return pack(vector, self.queries, self.plan.col_head, *self.parts[part], rows)[0]

    def halos(self, rows):
        return shift(rows[0], "ha", 1), shift(rows[1], "ha", -1)

    def rest_halos(self, vector):
        shape = (*self.keys_values.shape[:2], self.span, self.parts[1][1] * HD)
        return lax.cond(
            self.plan.more_rows,
            lambda vector: self.halos(self.edge_rows(vector, 1)),
            lambda vector: (jnp.zeros(shape, jnp.bfloat16),) * 2,
            vector,
        )

    def stay(self, vector, halos):
        return attention(self.plan, vector, [self.queries], self.keys_values, halos)[0]

    def visit(self, vector, visitors, halos, part=0):
        first = self.parts[part][0]
        return attention(self.plan, vector, visitors, self.keys_values, halos, first)

    def rest_sides(self, vector, halos):
        shape = (*self.queries.shape[:2], (self.parts[1][1] + 1) * HD)

        def send(vector, *halos):
            queries = self.leaving(vector, 1)
            visitors = shift(queries, "wa", 1), shift(queries, "wa", -1)
            for_left, for_right = self.visit(vector, visitors, halos, 1)
            return shift(for_right, "wa", 1), shift(for_left, "wa", -1)

        return lax.cond(
            self.plan.more_cols,
            send,
            lambda vector, *halos: (jnp.zeros(shape, jnp.bfloat16),) * 2,
            vector,
            *halos,
        )

    def combine(self, vector, near, sides):
        attended = combine(self.plan, vector, near, sides)
        return attended.reshape(-1, attended.shape[2])


def together(*blocks):
    return lax.optimization_barrier(blocks)


def paired(hidden, queries, keys_values, windows, out_weight, picked):
    ha, wa, ta = lax.axis_index("ha"), lax.axis_index("wa"), lax.axis_index("ta")
    n_wa = lax.axis_size("wa")
    blocks = n_wa // 2
    depth = out_weight.shape[0] // 4
    width = out_weight.shape[1]

    def share(shares, number):
        return lax.dynamic_slice_in_dim(shares, number * depth, depth, 0)

    mine = lax.optimization_barrier(share(out_weight, ha))
    first = turn(mine, "wa", 1)
    tokens = Tokens(queries, keys_values, windows, 4)
    vector = tokens.plan.vector
    top, bottom = tokens.halos(tokens.edge_rows(vector, 0))

    top, gate = together(top, picked[0:1])
    other_gate = swap(gate, "ta", 1)
    other_gate, counts = together(other_gate, tokens.plan.counts)
    counts, vector = together(tokens.plan.agree(counts), vector)
    queries, mine = together(tokens.leaving(vector, 0), mine)
    third = turn(mine, "wa", -1)

    first, top, bottom, other_gate, vector, queries = together(
        first, top, bottom, other_gate, vector, queries
    )
    first_x = swap(first, "ha", 1)
    first_y = swap(first, "ha", 2)
    from_left = shift(queries, "wa", 1)
    from_right = shift(queries, "wa", -1)
    halos = top, bottom, *tokens.rest_halos(vector)
    near = tokens.stay(vector, halos)

    rest_sides = tokens.rest_sides(vector, halos)

    near, first_x, first_y, third, first, *rest_sides = together(
        near, first_x, first_y, third, first, *rest_sides
    )
    third_x = swap(third, "ha", 1)
    third_y = swap(third, "ha", 2)
    second = turn(first, "wa", 1)
    for_left, for_right = tokens.visit(vector, (from_left, from_right), halos)

    left = shift(for_right, "wa", 1)
    right = shift(for_left, "wa", -1)

    third_x, third_y, second, vector, hidden, all_shares = together(
        third_x, third_y, second, vector, hidden, out_weight
    )
    second_x = swap(second, "ha", 1)
    second_y = swap(second, "ha", 2)
    other_hidden = swap(hidden, "ta", 1)

    far = lax.optimization_barrier(share(all_shares, ha ^ 3))
    left, right, far = together(left, right, far)
    attended = tokens.combine(vector, near, [left, right, *rest_sides])

    second_x, second_y, first_y, far, attended = together(
        second_x, second_y, first_y, far, attended
    )
    first_far = swap(first_y, "ha", 1)
    second_far = swap(second_x, "ha", 2)
    third_far = turn(far, "wa", -1)

    turned = ha.reshape(1)
    sums = project(
        turned,
        attended,
        [out_weight],
        [[(0, depth, number, True) for number in range(4)]],
        None,
        0,
        jnp.bfloat16,
    )
    other_sums = swap(sums, "ta", 1)
    late = project(
        turned,
        attended,
        [first, first_x, first_y, second, second_x, second_y, third, third_x, third_y],
        [[(start + number, depth, 0, False) for number in range(3)] for start in (0, 3, 6)],
        None,
        0,
        jnp.float32,
    )
    def block_of(distance):
        return lax.rem(wa - distance + n_wa, n_wa)

    owners = jnp.stack([block_of(distance) // blocks == ta for distance in range(n_wa)])
    inner = jnp.stack([lax.rem(block_of(distance), blocks) for distance in range(n_wa)])
    place = jnp.stack([owners.astype(jnp.int32), inner], axis=1).reshape(-1)
    late, place, other_hidden = together(late, place, other_hidden)
    base, gates = pick(place, hidden, other_hidden, gate, other_gate, width)
    early, totals = mix(base, gates, sums, other_sums)

    first_far, second_far, third_far, early, totals, late = together(
        first_far, second_far, third_far, early, totals, late
    )
    late = project(
        turned,
        attended,
        [first_far, second_far, third_far],
        [[(number, depth, 0, False)] for number in range(3)],
        late,
        3 * depth,
        jnp.bfloat16,
    )
    other_late = swap(late, "ta", 1)
    place = jnp.stack(
        [lax.rem(wa - ta * blocks - block + 2 * n_wa, n_wa) for block in range(blocks)]
    )
    return finish(
        place, base, gates, picked[2:3], picked[1:2], totals, early, late, other_late
    )


def gathered(hidden, queries, keys_values, windows, out_weight, picked):
    n_ha, n_wa, n_ta = lax.axis_size("ha"), lax.axis_size("wa"), lax.axis_size("ta")
    ha, ta = lax.axis_index("ha"), lax.axis_index("ta")
    work = Tokens(queries, keys_values, windows, 1)
    vector = work.plan.vector
    work.plan.agree(work.plan.counts)
    halos = *work.halos(work.edge_rows(vector, 0)), *work.rest_halos(vector)
    sent = work.leaving(vector, 0)
    visitors = shift(sent, "wa", 1), shift(sent, "wa", -1)
    near = work.stay(vector, halos)
    for_left, for_right = work.visit(vector, visitors, halos)
    sides = shift(for_right, "wa", 1), shift(for_left, "wa", -1)
    attended = work.combine(vector, near, [*sides, *work.rest_sides(vector, halos)])
    tokens, features = attended.shape
    depth = features // n_ha
    width = out_weight.shape[1]
    share = lax.dynamic_slice_in_dim(out_weight, ha * depth, depth, 0)
    weights = lax.all_gather(share, ("ha", "wa"), axis=0, tiled=False).reshape(
        n_ha, n_wa, depth, width
    )
    partial_sums = jnp.einsum(
        "thk,hwkc->wtc",
        attended.reshape(tokens, n_ha, depth),
        weights,
        preferred_element_type=jnp.float32,
    ).astype(jnp.bfloat16)
    blocks = n_wa // n_ta
    summed = None
    for step in range(n_ta):
        target = lax.rem(ta + step, n_ta)
        piece = lax.dynamic_slice_in_dim(partial_sums, target * blocks, blocks, 0)
        if step:
            piece = turn(piece, "ta", step)
        piece = piece.astype(jnp.float32)
        summed = piece if summed is None else summed + piece
    summed = jnp.transpose(summed, (1, 0, 2)).reshape(tokens, -1)
    mixed = hidden.astype(jnp.float32) + picked[0] * summed
    sum_first, sum_second = lax.psum((jnp.sum(mixed, axis=1), jnp.sum(mixed * mixed, axis=1)), "ta")
    average = (sum_first / D)[:, None]
    variance = (sum_second / D)[:, None] - average * average
    normed = (mixed - average) * lax.rsqrt(variance + EPSILON)
    ffn_input = (normed * (1.0 + picked[2]) + picked[1]).astype(jnp.bfloat16)
    return mixed.astype(jnp.bfloat16), ffn_input


def shards(hidden_states, queries, keys_values, out_weight, mod_table, windows, step_index):
    tokens = math.prod(queries.shape[:3])
    width = hidden_states.shape[3]
    picked = lax.dynamic_index_in_dim(mod_table, step_index[0], 0, keepdims=False)
    sizes = lax.axis_size("ha"), lax.axis_size("wa"), lax.axis_size("ta")
    tuned = sizes == (4, 4, 2) and out_weight.shape[0] % (20 * LANES) == 0
    residual_out, ffn_input = (paired if tuned else gathered)(
        hidden_states.reshape(tokens, width), queries, keys_values, windows, out_weight, picked
    )
    return residual_out.reshape(hidden_states.shape), ffn_input.reshape(hidden_states.shape)


def solution(mesh):
    return jax.shard_map(
        shards,
        mesh=mesh,
        in_specs=(
            P(None, "ha", "wa", "ta"),
            P(None, "ha", "wa", "ta"),
            P(None, None, "ha", "wa", "ta"),
            P("ta", "wa"),
            P(None, None, "ta"),
            P("ta", None),
            P(),
        ),
        out_specs=(P(None, "ha", "wa", "ta"), P(None, "ha", "wa", "ta")),
        check_vma=False,
    )
```
